32 devices in a mesh: dp: 8 (over z, y), tensor: 4 (over x, core).
Axes of the slice: x: 2, y: 2, z: 4, core: 2. Of those that a mesh axis runs over, the one named last changes fastest.
Arguments:
- inputs: bfloat16 [8192, 2048], P(('dp', 'tensor')), may hold values from -6 to 6
- segment_ids: int32 [8, 1024], P('dp', 'tensor'), may hold values from 0 to 2, never falling along the last dimension, each value on 1 to 768 neighbouring positions
- expert_ids: int32 [8192, 8], P(('dp', 'tensor')), may hold values from 0 to 63, all different within a row
- gate_values: bfloat16 [8192, 8], P(('dp', 'tensor')), may hold values from 0.039794922 to 0.29882812
- attn_gain: float32 [2048], replicated, may hold values from 0.25 to 1.75
- query_gain: float32 [128], replicated, may hold values from 0.25 to 1.75
- key_gain: float32 [128], replicated, may hold values from 0.25 to 1.75
- w_query: bfloat16 [2048, 2048], P('dp', 'tensor'), may hold values from -0.125 to 0.125
- w_key: bfloat16 [2048, 2048], P('dp', 'tensor'), may hold values from -0.125 to 0.125
- w_value: bfloat16 [2048, 2048], P('dp', 'tensor'), may hold values from -0.125 to 0.125
- w_output: bfloat16 [2048, 2048], P('tensor', 'dp'), may hold values from -2 to 2
- ffn_gain: float32 [2048], replicated, may hold values from 0.25 to 1.75
- w_gate: bfloat16 [64, 2048, 1024], P('dp', None, 'tensor'), may hold values from -0.125 to 0.125
- w_up: bfloat16 [64, 2048, 1024], P('dp', None, 'tensor'), may hold values from -0.125 to 0.125
- w_down: bfloat16 [64, 1024, 2048], P('dp', 'tensor'), may hold values from -0.75 to 0.75
- cotangent: bfloat16 [8192, 2048], P(('dp', 'tensor')), may hold values from -6 to 6
Outputs:
- outputs: float32 [8192, 2048], P(('dp', 'tensor'))
- grad_inputs: float32 [8192, 2048], P(('dp', 'tensor'))
- grad_attn_gain: float32 [2048], replicated
- grad_query_gain: float32 [128], replicated
- grad_key_gain: float32 [128], replicated
- grad_w_query: float32 [2048, 2048], P('dp', 'tensor')
- grad_w_key: float32 [2048, 2048], P('dp', 'tensor')
- grad_w_value: float32 [2048, 2048], P('dp', 'tensor')
- grad_w_output: float32 [2048, 2048], P('tensor', 'dp')
- grad_ffn_gain: float32 [2048], replicated
- grad_w_gate: float32 [64, 2048, 1024], P('dp', None, 'tensor')
- grad_w_up: float32 [64, 2048, 1024], P('dp', None, 'tensor')
- grad_w_down: float32 [64, 1024, 2048], P('dp', 'tensor')
The draws below stay inside these ranges and needn't reach their ends.
Inputs may be any that keep to these rules, and one draw needn't show every extreme that they name: `segment_ids`: within a pack the ids never fall. `expert_ids`: each token names 8 different experts.
All inputs are finite; a program needn't handle non-finite values.
Results may differ from the reference program's by a relative error of at most 0.02.
Values may be sent and summed in bfloat16 or wider, within the bound.
No kernel may reach another device: no remote copies, remote signals or barrier semaphores. Data moves between devices by JAX's collectives and lax.ppermute only.
A program may use at most 512 MiB of HBM per device.

```python
import math
import jax
import jax.numpy as jnp
import numpy as np
from jax import lax

D = 2048
HEADS = 16
HD = 128
FF = 1024
EXPERTS = 64
TOP = 8
WINDOW = 1024
SEQ = 1024
CAP = 128
TOKENS = 8192
N_DP = 8
N_TENSOR = 4


def raised(drawn, own_key, source, target, parts, factor):
    owner, partner = [(jnp.arange(drawn.shape[axis_at]) // (drawn.shape[axis_at] // parts)).reshape([-1 if axis == axis_at else 1 for axis in range(drawn.ndim)]) for axis_at in (source, target)]
    chosen = jax.random.permutation(own_key, parts)[partner]
    strong = (owner == chosen) | (owner == (partner + parts // 2) % parts)
    return jnp.where(strong, factor * drawn, drawn)


def steps_of(key, shape, shards, least, top_value):
    factor_of = 1.0
    for axis_at, blocks in shards:
        steps = jax.random.uniform(jax.random.fold_in(jax.random.fold_in(key, 6), axis_at), (blocks,), jnp.float32, least / len(shards), top_value / len(shards))
        factor_of = factor_of * jnp.repeat(jnp.exp(steps), shape[axis_at] // blocks).reshape((-1,) + (1,) * (len(shape) - 1 - axis_at))
    return factor_of


def different_ones(rng, rows, count, top, lift):
    order = jax.random.permutation(jax.random.fold_in(rng, 1), count)
    pull = order
    for power in range(3):
        pull = pull * pull // count
    pull = pull * lift // count
    lots = jax.random.randint(jax.random.fold_in(rng, 2), (rows, count), 0, 4096) + pull
    holders = jax.random.permutation(jax.random.fold_in(rng, 3), rows)[jnp.arange(count) % rows]
    lots = jnp.where(jnp.arange(rows)[:, None] == holders[None, :], 1 << 14, lots)
    score = lots * count + jnp.arange(count)
    return lax.top_k(score.astype(jnp.int32), top)[1].astype(jnp.int32)


def profile(count, total, reach, skew):
    loads = [(1 << 20) // math.isqrt(rank ** skew) + 1 for rank in range(2, count + 1)]
    surplus, given = total - reach - (count - 1), [1] * (count - 1)
    while surplus > 0:
        free = [i for i in range(count - 1) if given[i] < reach]
        whole, left = sum([loads[i] for i in free]), surplus
        for i in free:
            more = min(reach - given[i], max(1, left * loads[i] // whole), surplus)
            given[i] = given[i] + more
            surplus = surplus - more
    return np.array([reach] + given)


def ragged(own_key, amount, total, most, skew):
    if amount == 2:
        one = jax.random.randint(own_key, (), max(1, total - most), min(most, total - 1) + 1)
        return jnp.stack([one, total - one])
    tallies = jnp.asarray(profile(amount, total, most, skew), jnp.int32)
    pairs = (amount - 1) // 2
    source_of, receiver = tallies[1:1 + 2 * pairs:2], tallies[2:2 + 2 * pairs:2]
    margin = jnp.minimum(source_of - 1, most - receiver)
    shifted = jax.random.randint(jax.random.fold_in(own_key, 1), (pairs,), 0, 1 << 20) % (margin + 1)
    tallies = tallies.at[1:1 + 2 * pairs:2].set(source_of - shifted).at[2:2 + 2 * pairs:2].set(receiver + shifted)
    return tallies[jax.random.permutation(jax.random.fold_in(own_key, 2), amount)]


def gaussian(key, dims, deviation, most, pieces=(), kind=jnp.bfloat16):
    drawn = jax.random.normal(key, dims, jnp.float32) * deviation
    if len(pieces) > 0:
        drawn = steps_of(key, dims, pieces, -0.22, 0.18) * drawn
    return jnp.clip(drawn, min=-most, max=most).astype(kind)


def bell_draw_with(key, shape, scale, bound, cuts, heavy, kind=jnp.bfloat16):
    drawn = scale * jax.random.normal(key, shape, jnp.float32)
    if cuts:
        drawn = drawn * steps_of(key, shape, cuts, -0.22, 0.18)
    return jnp.clip(raised(drawn, jax.random.fold_in(key, 3), *heavy), -bound, bound).astype(kind)


def setup_inputs(seed: int = 0) -> dict:
    streams_of = jax.random.split(jax.random.key(seed), 17)
    inputs = gaussian(streams_of[0], (TOKENS, D), 1.0, 6.0, ((0, 32),))
    segment_ids = jax.vmap(lambda own: jnp.searchsorted(jnp.cumsum(ragged(own, 3, SEQ, 3 * SEQ // 4, 2)), jnp.arange(SEQ), side="right"))(jax.random.split(streams_of[1], N_DP)).reshape((N_DP, SEQ)).astype(jnp.int32)
    expert_ids = different_ones(streams_of[2], TOKENS, EXPERTS, TOP, 1024)
    gate_values = jnp.clip(jnp.exp(math.log(0.29882812) - 2.0161293 * jax.random.uniform(streams_of[3], (TOKENS, TOP), jnp.float32) ** steps_of(streams_of[3], (TOKENS, TOP), ((0, 32),), -0.2, 0.2)), 0.039794922, 0.29882812).astype(jnp.bfloat16)
    attn_gain = jnp.clip(1.0 + 0.15 * jax.random.normal(streams_of[4], (D,), jnp.float32), 0.25, 1.75)
    query_gain = jnp.clip(1.0 + 0.15 * jax.random.normal(streams_of[5], (HD,), jnp.float32), 0.25, 1.75)
    key_gain = jnp.clip(1.0 + 0.15 * jax.random.normal(streams_of[6], (HD,), jnp.float32), 0.25, 1.75)
    w_query = gaussian(streams_of[7], (D, HEADS * HD), D ** -0.5, 0.125, ((0, 8), (1, 4)))
    w_key = gaussian(streams_of[8], (D, HEADS * HD), D ** -0.5, 0.125, ((0, 8), (1, 4)))
    w_value = gaussian(streams_of[9], (D, HEADS * HD), D ** -0.5, 0.125, ((0, 8), (1, 4)))
    w_output = gaussian(streams_of[10], (HEADS * HD, D), 8 ** -0.5, 2.0, ((0, 4), (1, 8)))
    ffn_gain = jnp.clip(1.0 + 0.15 * jax.random.normal(streams_of[11], (D,), jnp.float32), 0.25, 1.75)
    w_gate = gaussian(streams_of[12], (EXPERTS, D, FF), D ** -0.5, 0.125, ((0, 8), (2, 4)))
    w_up = gaussian(streams_of[13], (EXPERTS, D, FF), D ** -0.5, 0.125, ((0, 8), (2, 4)))
    w_down = gaussian(streams_of[14], (EXPERTS, FF, D), (FF // 16) ** -0.5, 0.75, ((0, 8), (1, 4)))
    cotangent = bell_draw_with(streams_of[15], (TOKENS, D), 1.0, 6.0, ((0, 32),), (0, 1, 32, 2.75))
    return {"inputs": inputs, "segment_ids": segment_ids, "expert_ids": expert_ids, "gate_values": gate_values, "attn_gain": attn_gain, "query_gain": query_gain, "key_gain": key_gain, "w_query": w_query, "w_key": w_key, "w_value": w_value, "w_output": w_output, "ffn_gain": ffn_gain, "w_gate": w_gate, "w_up": w_up, "w_down": w_down, "cotangent": cotangent}


EPSILON = 1e-06
THETA = 50000.0
NEG_FILL = -1e+30

@jax.custom_vjp
def low(v):
    return lax.optimization_barrier(v.astype(jnp.bfloat16)).astype(jnp.float32)

@jax.custom_vjp
def low_back(v):
    return v

def low_keep(v):
    return (low(v), None)

def low_pass(kept, grad):
    return (grad,)

def back_keep(v):
    return (v, None)

def back_low(kept, grad):
    return (low(grad),)
low.defvjp(low_keep, low_pass)
low_back.defvjp(back_keep, back_low)

def product(left_side, right_side):
    return jnp.dot(left_side, right_side, precision=lax.Precision.HIGHEST, preferred_element_type=jnp.float32)

def rms_scale(values, gain_vec):
    return values * lax.rsqrt(lax.optimization_barrier(jnp.mean(values * values, axis=-1, keepdims=True)) + EPSILON) * gain_vec

def rope_tables(length, head_size):
    half_size = head_size // 2
    frequency = THETA ** (-(2.0 * jnp.arange(half_size, dtype=jnp.float32)) / head_size)
    angles = jnp.arange(length, dtype=jnp.float32)[:, None] * frequency[None, :]
    return (jnp.cos(angles)[:, None, :], jnp.sin(angles)[:, None, :])

def rotate(values, cosine, sine_tab):
    half_size = values.shape[-1] // 2
    first_half = values[..., :half_size]
    second_half = values[..., half_size:]
    return jnp.concatenate([first_half * cosine - second_half * sine_tab, second_half * cosine + first_half * sine_tab], axis=-1)

def attend_pack(operands):
    queries, key_rows, value_rows, segments = operands
    length = segments.shape[0]
    places = jnp.arange(length)
    allowed = (segments[:, None] == segments[None, :]) & (jnp.abs(places[:, None] - places[None, :]) < WINDOW // 2)
    scores = jnp.einsum('qhd,khd->hqk', queries, key_rows, precision=lax.Precision.HIGHEST) * HD ** (-0.5)
    scores = jnp.where(allowed[None], low_back(scores), NEG_FILL)
    weights = low(jax.nn.softmax(scores, axis=-1))
    mixture = jnp.einsum('hqk,khd->qhd', weights, value_rows, precision=lax.Precision.HIGHEST)
    return low(low_back(mixture))

def slot_table(route_rows):
    flat_ids = route_rows.reshape(-1)
    onehot = (flat_ids[:, None] == jnp.arange(EXPERTS, dtype=jnp.int32)[None, :]).astype(jnp.int32)
    places = lax.optimization_barrier(jnp.sum((jnp.cumsum(onehot, axis=0) - onehot) * onehot, axis=1))
    return jnp.where(places < CAP, flat_ids * CAP + places, EXPERTS * CAP).astype(jnp.int32)

def dispatch_pack(operands):
    pack_rows, slot_pack = operands
    repeated = jnp.repeat(pack_rows, TOP, axis=0)
    return jnp.zeros((EXPERTS * CAP + 1, D), jnp.float32).at[slot_pack].add(repeated)[:EXPERTS * CAP]

def combine_pack(operands):
    result_pack, slot_pack, gate_pack = operands
    padded = jnp.concatenate([result_pack, jnp.zeros((1, D), jnp.float32)], axis=0)
    picked = jnp.take(padded, slot_pack, axis=0).reshape(SEQ, TOP, D)
    return lax.optimization_barrier(jnp.sum(picked * gate_pack[:, :, None], axis=1))

def expert_rows(operands):
    rows_in, gate_mat, up_mat, down_mat = operands
    group_width = FF // N_TENSOR
    summed = jnp.zeros(rows_in.shape, jnp.float32)
    for group_index in range(N_TENSOR):
        lower = group_index * group_width
        shared = low_back(rows_in)
        gated = low_back(product(shared, gate_mat[:, lower:lower + group_width]))
        lifted = low_back(product(shared, up_mat[:, lower:lower + group_width]))
        hidden = low(jax.nn.silu(gated) * lifted)
        summed = summed + low_back(low(product(hidden, down_mat[lower:lower + group_width, :])))
    return summed

def layer(inputs, attn_gain, query_gain, key_gain, w_query, w_key, w_value, w_output, ffn_gain, w_gate, w_up, w_down, segment_ids, expert_ids, gate_floats):
    pack_count = segment_ids.shape[0]
    first_in = low(rms_scale(inputs, attn_gain))
    cosine, sine_tab = rope_tables(SEQ, HD)

    def split_heads(values):
        return values.reshape(pack_count, SEQ, HEADS, HD)
    queries = low(rotate(rms_scale(split_heads(low_back(product(first_in, w_query))), query_gain), cosine, sine_tab))
    key_rows = low(rotate(rms_scale(split_heads(low_back(product(first_in, w_key))), key_gain), cosine, sine_tab))
    value_rows = split_heads(low(low_back(product(first_in, w_value))))
    mixture = lax.map(jax.checkpoint(attend_pack), (queries, key_rows, value_rows, segment_ids))
    attended = low_back(product(mixture.reshape(pack_count * SEQ, HEADS * HD), w_output))
    middle = inputs + attended
    second_in = low(rms_scale(middle, ffn_gain))
    slot_index = jax.vmap(slot_table)(expert_ids.reshape(pack_count, SEQ, TOP))
    buffers = lax.map(dispatch_pack, (second_in.reshape(pack_count, SEQ, D), slot_index))
    grouped = buffers.reshape(pack_count, EXPERTS, CAP, D).transpose(1, 0, 2, 3).reshape(EXPERTS, pack_count * CAP, D)
    results = lax.map(jax.checkpoint(expert_rows), (grouped, w_gate, w_up, w_down))
    returned = results.reshape(EXPERTS, pack_count, CAP, D).transpose(1, 0, 2, 3).reshape(pack_count, EXPERTS * CAP, D)
    combined = lax.map(combine_pack, (returned, slot_index, gate_floats.reshape(pack_count, SEQ, TOP)))
    return middle + combined.reshape(pack_count * SEQ, D)

def reference(inputs, segment_ids, expert_ids, gate_values, attn_gain, query_gain, key_gain, w_query, w_key, w_value, w_output, ffn_gain, w_gate, w_up, w_down, cotangent):
    params = tuple((operand.astype(jnp.float32) for operand in (inputs, attn_gain, query_gain, key_gain, w_query, w_key, w_value, w_output, ffn_gain, w_gate, w_up, w_down)))
    gate_floats = gate_values.astype(jnp.float32)

    def forward(weights):
        return layer(weights[0], weights[1], weights[2], weights[3], weights[4], weights[5], weights[6], weights[7], weights[8], weights[9], weights[10], weights[11], segment_ids, expert_ids, gate_floats)
    outputs, pullback = jax.vjp(forward, params)
    gradients, = pullback(cotangent.astype(jnp.float32))
    return (outputs, gradients[0], gradients[1], gradients[2], gradients[3], gradients[4], gradients[5], gradients[6], gradients[7], gradients[8], gradients[9], gradients[10], gradients[11])
```

```python
import jax
import jax.numpy as jnp
import functools

from jax import lax
from jax.experimental import pallas as pl
from jax.experimental.pallas import tpu as pltpu
from jax.sharding import PartitionSpec as P

WINDOW = 1024


EPSILON = 1e-06
THETA = 50000.0
NEG_FILL = -1e30


def matmul(left_side, right_side):
    return jnp.dot(left_side, right_side, preferred_element_type=jnp.float32)


def contract_last(left_side, right_side):
    return lax.dot_general(
        left_side, right_side, (((1,), (1,)), ((), ())), preferred_element_type=jnp.float32
    )


def contract_first(left_side, right_side):
    return lax.dot_general(
        left_side, right_side, (((0,), (0,)), ((), ())), preferred_element_type=jnp.float32
    )


def norm_parts(values):
    factor = lax.rsqrt(jnp.mean(values * values, axis=-1, keepdims=True) + EPSILON)
    return (values * factor, factor)


def norm_back(grad_out, normed, factor, gain_vec):
    scaled = grad_out * gain_vec
    return factor * (scaled - normed * jnp.mean(scaled * normed, axis=-1, keepdims=True))


def rope_tables(length, head_size):
    half_size = head_size // 2
    frequency = THETA ** (-(2.0 * jnp.arange(half_size, dtype=jnp.float32)) / head_size)
    angles = jnp.arange(length, dtype=jnp.float32)[:, None] * frequency[None, :]
    return (jnp.cos(angles)[:, None, :], jnp.sin(angles)[:, None, :])


def rotate(values, cosine, sine_tab):
    half_size = values.shape[-1] // 2
    first_half = values[..., :half_size]
    second_half = values[..., half_size:]
    return jnp.concatenate(
        [
            first_half * cosine - second_half * sine_tab,
            second_half * cosine + first_half * sine_tab,
        ],
        axis=-1,
    )


def rotate_back(grads_in, cosine, sine_tab):
    half_size = grads_in.shape[-1] // 2
    first_half = grads_in[..., :half_size]
    second_half = grads_in[..., half_size:]
    return jnp.concatenate(
        [
            first_half * cosine + second_half * sine_tab,
            second_half * cosine - first_half * sine_tab,
        ],
        axis=-1,
    )


def block_mask(segments, offset, block_rows, key_count):
    query_pos = offset + jnp.arange(block_rows)
    key_pos = jnp.arange(key_count)
    same_doc = segments[offset : offset + block_rows][:, None] == segments[None, :]
    near_pos = jnp.abs(query_pos[:, None] - key_pos[None, :]) < WINDOW // 2
    return same_doc & near_pos


def block_scores(query_block, key_low, allowed, inv_root):
    scores = (
        jnp.einsum("qhd,khd->hqk", query_block, key_low, preferred_element_type=jnp.float32)
        * inv_root
    )
    return jnp.where(allowed[None], scores, NEG_FILL)


def row_sum(term_fn, tok_rows):
    return lax.psum_scatter(
        term_fn(jnp.int32(0), lax.axis_size("tensor") * tok_rows),
        "tensor",
        scatter_dimension=0,
        tiled=True,
    )


def gather_rows(values):
    return lax.all_gather(values, "tensor", axis=0, tiled=True)


def from_experts(values):
    return lax.all_to_all(values, "dp", split_axis=1, concat_axis=1, tiled=True)


def to_experts(source_rows, slot_token, slot_gate, layout):
    picked = jnp.take(source_rows, slot_token, axis=0, mode="fill", fill_value=0)
    if slot_gate is not None:
        picked = (picked.astype(jnp.float32) * slot_gate[:, None]).astype(jnp.bfloat16)
    picked = picked.reshape(layout + (picked.shape[1],))
    return lax.all_to_all(picked, "dp", split_axis=1, concat_axis=1, tiled=True)


def pair_sum(table, weights_low, pair_slots, row_count):
    picked = jnp.take(table, pair_slots.reshape(-1), axis=0, mode="fill", fill_value=0)
    picked = picked.reshape(row_count, pair_slots.shape[1], table.shape[1])
    return jnp.einsum("rk,rkd->rd", weights_low, picked, preferred_element_type=jnp.float32)


def expert_forward(operands):
    rows_in, gate_mat, up_mat, down_mat = operands
    flat_rows = rows_in.reshape(-1, rows_in.shape[-1])
    gated = matmul(flat_rows, gate_mat)
    lifted = matmul(flat_rows, up_mat)
    hidden = (jax.nn.silu(gated) * lifted).astype(jnp.bfloat16)
    result = matmul(hidden, down_mat).astype(jnp.bfloat16)
    return (result.reshape(rows_in.shape), gated, lifted)


def expert_backward(operands):
    rows_in, grad_in, gated, lifted, gate_mat, up_mat, down_mat = operands
    flat_rows = rows_in.reshape(-1, rows_in.shape[-1])
    flat_grad = grad_in.reshape(-1, grad_in.shape[-1])
    gate_sig = jax.nn.sigmoid(gated)
    activated = jax.nn.silu(gated)
    hidden = (activated * lifted).astype(jnp.bfloat16)
    grad_hidden = contract_last(flat_grad, down_mat)
    grad_down = contract_first(hidden, flat_grad)
    grad_gated = (grad_hidden * lifted * gate_sig * (1.0 + gated * (1.0 - gate_sig))).astype(
        jnp.bfloat16
    )
    grad_lifted = (grad_hidden * activated).astype(jnp.bfloat16)
    grad_gate = contract_first(flat_rows, grad_gated)
    grad_up = contract_first(flat_rows, grad_lifted)
    grad_rows = (contract_last(grad_gated, gate_mat) + contract_last(grad_lifted, up_mat)).astype(
        jnp.bfloat16
    )
    return (grad_rows.reshape(rows_in.shape), grad_gate, grad_up, grad_down)


VMEM_BYTES = 60 * 1024 * 1024
COLUMN_CHUNK = 512


def select_rows(places_ref, gates_ref, pick_ref, capacity):
    expert_count, seq_len = places_ref.shape[1:]
    slot_range = lax.broadcasted_iota(jnp.int32, (capacity, seq_len), 0)
    for expert in range(expert_count):
        hit = places_ref[0, expert : expert + 1, :] == slot_range
        weight = 1.0 if gates_ref is None else gates_ref[0, expert : expert + 1, :]
        rows = slice(expert * capacity, (expert + 1) * capacity)
        pick_ref[rows, :] = jnp.where(hit, weight, 0.0).astype(jnp.bfloat16)


def spread_rows(places_ref, gates_ref, pick_ref, capacity):
    seq_len, expert_count = places_ref.shape[1:]
    slot_range = lax.broadcasted_iota(jnp.int32, (seq_len, capacity), 1)
    for expert in range(expert_count):
        hit = places_ref[0, :, expert : expert + 1] == slot_range
        weight = 1.0 if gates_ref is None else gates_ref[0, :, expert : expert + 1]
        columns = slice(expert * capacity, (expert + 1) * capacity)
        pick_ref[:, columns] = jnp.where(hit, weight, 0.0).astype(jnp.bfloat16)


def rows_to_slots(pick_ref, rows_ref, slots_ref, pack, capacity):
    width = rows_ref.shape[2]
    expert_count = slots_ref.shape[0]
    for start in range(0, width, COLUMN_CHUNK):
        columns = slice(start, start + COLUMN_CHUNK)
        picked = matmul(pick_ref[...], rows_ref[0, :, columns]).astype(jnp.bfloat16)
        slots_ref[:, pack, :, columns] = picked.reshape(expert_count, capacity, COLUMN_CHUNK)


def slots_to_rows(pick_ref, slots_ref, rows_ref, pack):
    width = rows_ref.shape[2]
    for start in range(0, width, COLUMN_CHUNK):
        columns = slice(start, start + COLUMN_CHUNK)
        slots = slots_ref[:, pack, :, columns].reshape(-1, COLUMN_CHUNK)
        rows_ref[0, :, columns] = matmul(pick_ref[...], slots).astype(rows_ref.dtype)


def cot_kernel(packs, experts, capacity, places, gates, rows, down, slots_out, hidden_out, slots, pick):
    step = pl.program_id(0)

    @pl.when(step < packs)
    def _():
        select_rows(places, gates, pick, capacity)
        rows_to_slots(pick, rows, slots, step, capacity)

    @pl.when(step >= packs)
    def _():
        block = slots[step - packs].reshape(packs * capacity, -1)
        slots_out[0] = block
        hidden_out[0] = contract_last(block, down[0])


def row_kernel(
    packs, experts, capacity, places, places_t, rows, gate, up, grad_hidden,
    slots_out, hidden_out, gated_out, lifted_out, rows_out, slots, grads, pick, spread,
):
    step = pl.program_id(0)

    @pl.when(step < packs)
    def _():
        select_rows(places, None, pick, capacity)
        rows_to_slots(pick, rows, slots, step, capacity)

    @pl.when((step >= packs) & (step < packs + experts))
    def _():
        expert = step - packs
        block = slots[expert].reshape(packs * capacity, -1)
        slots_out[0] = block
        gated = matmul(block, gate[0])
        lifted = matmul(block, up[0])
        sig = 1.0 / (1.0 + jnp.exp(-gated))
        active = gated * sig
        hidden_out[0] = (active * lifted).astype(jnp.bfloat16)
        above = grad_hidden[0]
        grad_gated = (above * lifted * sig * (1.0 + gated * (1.0 - sig))).astype(jnp.bfloat16)
        grad_lifted = (above * active).astype(jnp.bfloat16)
        gated_out[0] = grad_gated
        lifted_out[0] = grad_lifted
        back = contract_last(grad_gated, gate[0]) + contract_last(grad_lifted, up[0])
        grads[expert] = back.astype(jnp.bfloat16).reshape(packs, capacity, -1)

    @pl.when(step >= packs + experts)
    def _():
        spread_rows(places_t, None, spread, capacity)
        slots_to_rows(spread, grads, rows_out, step - packs - experts)


def mix_kernel(packs, experts, capacity, places_t, gates_t, hidden, down, rows_out, results, spread):
    step = pl.program_id(0)

    @pl.when(step < experts)
    def _():
        result = matmul(hidden[0], down[0])
        results[step] = result.astype(jnp.bfloat16).reshape(packs, capacity, -1)

    @pl.when(step >= experts)
    def _():
        spread_rows(places_t, gates_t, spread, capacity)
        slots_to_rows(spread, results, rows_out, step - experts)


def weight_kernel(planes, *refs):
    slots, grads, hidden, gated, lifted = (refs[i * planes : (i + 1) * planes] for i in range(5))
    gate_out, up_out, down_out = refs[5 * planes :]

    def total(left, right):
        result = contract_first(left[0][0], right[0][0])
        for index in range(1, planes):
            result = result + contract_first(left[index][0], right[index][0])
        return result

    gate_out[0] = total(slots, gated)
    up_out[0] = total(slots, lifted)
    down_out[0] = total(hidden, grads)


def block(shape, place):
    tail = (0,) * (len(shape) - 1)
    return pl.BlockSpec((1,) + tuple(shape[1:]), lambda step: (place(step),) + tail)


def staged(first, count):
    return lambda step: jnp.clip(step - first, 0, count - 1)


def shape_of(shape, kind):
    return jax.ShapeDtypeStruct(shape, kind)


def call(kernel, steps, specs, out_specs, out_shape, scratch):
    return pl.pallas_call(
        kernel,
        grid=(steps,),
        in_specs=specs,
        out_specs=out_specs,
        out_shape=out_shape,
        scratch_shapes=scratch,
        compiler_params=pltpu.CompilerParams(
            dimension_semantics=("arbitrary",), vmem_limit_bytes=VMEM_BYTES
        ),
    )


def cot_slots(places, gates, rows, down, capacity):
    packs, seq_len, width = rows.shape
    experts, hidden_width, _ = down.shape
    slot_rows = packs * capacity
    by_pack, by_expert = staged(0, packs), staged(packs, experts)
    out_shape = [
        shape_of((experts, slot_rows, width), jnp.bfloat16),
        shape_of((experts, slot_rows, hidden_width), jnp.float32),
    ]
    return call(
        functools.partial(cot_kernel, packs, experts, capacity),
        packs + experts,
        [block(places.shape, by_pack), block(gates.shape, by_pack), block(rows.shape, by_pack), block(down.shape, by_expert)],
        [block(out.shape, by_expert) for out in out_shape],
        out_shape,
        [
            pltpu.VMEM((experts, packs, capacity, width), jnp.bfloat16),
            pltpu.VMEM((experts * capacity, seq_len), jnp.bfloat16),
        ],
    )(places, gates, rows, down)


def row_slots(places, places_t, rows, gate, up, grad_hidden, capacity):
    packs, seq_len, width = rows.shape
    experts, _, hidden_width = gate.shape
    slot_rows = packs * capacity
    first, middle, last = staged(0, packs), staged(packs, experts), staged(packs + experts, packs)
    narrow = shape_of((experts, slot_rows, hidden_width), jnp.bfloat16)
    out_shape = [
        shape_of((experts, slot_rows, width), jnp.bfloat16), narrow, narrow, narrow,
        shape_of(rows.shape, jnp.bfloat16),
    ]
    return call(
        functools.partial(row_kernel, packs, experts, capacity),
        2 * packs + experts,
        [
            block(places.shape, first), block(places_t.shape, last), block(rows.shape, first),
            block(gate.shape, middle), block(up.shape, middle), block(grad_hidden.shape, middle),
        ],
        [block(out.shape, middle) for out in out_shape[:4]] + [block(rows.shape, last)],
        out_shape,
        [
            pltpu.VMEM((experts, packs, capacity, width), jnp.bfloat16),
            pltpu.VMEM((experts, packs, capacity, width), jnp.bfloat16),
            pltpu.VMEM((experts * capacity, seq_len), jnp.bfloat16),
            pltpu.VMEM((seq_len, experts * capacity), jnp.bfloat16),
        ],
    )(places, places_t, rows, gate, up, grad_hidden)


def mix_rows(places_t, gates_t, hidden, down, capacity):
    packs, seq_len, _ = places_t.shape
    experts, _, width = down.shape
    first, last = staged(0, experts), staged(experts, packs)
    out = shape_of((packs, seq_len, width), jnp.bfloat16)
    return call(
        functools.partial(mix_kernel, packs, experts, capacity),
        packs + experts,
        [
            block(places_t.shape, last), block(gates_t.shape, last),
            block(hidden.shape, first), block(down.shape, first),
        ],
        block(out.shape, last),
        out,
        [
            pltpu.VMEM((experts, packs, capacity, width), jnp.bfloat16),
            pltpu.VMEM((seq_len, experts * capacity), jnp.bfloat16),
        ],
    )(places_t, gates_t, hidden, down)


def weight_grads(slots, grads, hidden, gated, lifted):
    planes = len(slots)
    operands = [*slots, *grads, *hidden, *gated, *lifted]
    experts, _, width = slots[0].shape
    hidden_width = hidden[0].shape[2]
    each = lambda step: step
    out_shape = [
        shape_of((experts, width, hidden_width), jnp.float32),
        shape_of((experts, width, hidden_width), jnp.float32),
        shape_of((experts, hidden_width, width), jnp.float32),
    ]
    return call(
        functools.partial(weight_kernel, planes),
        experts,
        [block(operand.shape, each) for operand in operands],
        [block(out.shape, each) for out in out_shape],
        out_shape,
        [],
    )(*operands)


def routing(all_ids, all_gates, local_experts, capacity):
    seq_len = all_ids.shape[1]
    first = lax.axis_index("dp") * local_experts
    wanted = first + jnp.arange(local_experts, dtype=jnp.int32)
    matches = all_ids[:, :, :, None] == wanted
    member = jnp.any(matches, axis=2)
    gates = jnp.sum(jnp.where(matches, all_gates.astype(jnp.float32)[..., None], 0.0), axis=2)
    order = jnp.arange(seq_len, dtype=jnp.int32)
    earlier = (order[:, None] > order[None, :]).astype(jnp.bfloat16)
    before = jnp.einsum(
        "ts,pse->pte", earlier, member.astype(jnp.bfloat16), preferred_element_type=jnp.float32
    ).astype(jnp.int32)
    return jnp.where(member & (before < capacity), before, -1), gates


def experts_by_exchange(
    second_in, cotangent, expert_ids, gate_values, w_gate, w_up, w_down, middle, capacity
):
    tok_rows, model_width = second_in.shape
    tensor_count = lax.axis_size("tensor")
    data_count = lax.axis_size("dp")
    local_experts = w_gate.shape[0]
    all_experts = local_experts * data_count
    top_count = expert_ids.shape[1]
    seq_len = tok_rows * tensor_count
    pack_cot, pack_ids, pack_gates = (
        gather_rows(cotangent), gather_rows(expert_ids), gather_rows(gate_values)
    )
    pack_second = gather_rows(second_in)
    expert_range = jnp.arange(all_experts, dtype=jnp.int32)
    matches = pack_ids[:, :, None] == expert_range[None, None, :]
    token_counts = jnp.sum(matches.astype(jnp.float32), axis=1).astype(jnp.bfloat16)
    token_range = jnp.arange(seq_len, dtype=jnp.int32)
    earlier = (token_range[:, None] > token_range[None, :]).astype(jnp.bfloat16)
    before = matmul(earlier, token_counts)
    places = (
        jnp.sum(jnp.where(matches, before[:, None, :], 0.0), axis=2).astype(jnp.int32).reshape(-1)
    )
    flat_ids = pack_ids.reshape(-1)
    owners = flat_ids // local_experts
    local_index = flat_ids % local_experts
    dump_slot = all_experts * capacity
    slot_index = jnp.where(
        places < capacity,
        local_index * (data_count * capacity) + owners * capacity + places,
        dump_slot,
    ).astype(jnp.int32)
    pair_token = jnp.arange(seq_len * top_count) // top_count
    slot_token = (
        jnp.full((dump_slot + 1,), seq_len, jnp.int32).at[slot_index].set(pair_token)[:dump_slot]
    )
    pair_gates = pack_gates.astype(jnp.float32)
    slot_gate = (
        jnp.zeros((dump_slot + 1,), jnp.float32)
        .at[slot_index]
        .set(pair_gates.reshape(-1))[:dump_slot]
    )
    pair_slots = slot_index.reshape(seq_len, top_count)
    layout = (local_experts, data_count, capacity)
    arrived_rows = to_experts(pack_second, slot_token, None, layout)
    expert_out, gated_all, lifted_all = lax.map(
        expert_forward, (arrived_rows, w_gate, w_up, w_down)
    )
    returned = from_experts(expert_out).reshape(-1, model_width)

    def combine_term(offset, row_count):
        return pair_sum(returned, pack_gates, pair_slots, row_count)

    outputs = middle + row_sum(combine_term, tok_rows)
    grad_arrived = to_experts(pack_cot, slot_token, slot_gate, layout)
    grad_rows_all, grad_w_gate, grad_w_up, grad_w_down = lax.map(
        expert_backward, (arrived_rows, grad_arrived, gated_all, lifted_all, w_gate, w_up, w_down)
    )
    returned_grad = from_experts(grad_rows_all).reshape(-1, model_width)
    unit_gates = jnp.ones_like(pack_gates)

    def dispatch_term(offset, row_count):
        return pair_sum(returned_grad, unit_gates, pair_slots, row_count)

    grad_second = row_sum(dispatch_term, tok_rows)
    return outputs, grad_second, grad_w_gate, grad_w_up, grad_w_down


def experts_by_gather(
    second_in, cotangent, expert_ids, gate_values, w_gate, w_up, w_down, middle, capacity
):
    tok_rows, model_width = second_in.shape
    axes = ("dp", "tensor")
    data_count = lax.axis_size("dp")
    seq_len = tok_rows * lax.axis_size("tensor")
    local_experts = w_gate.shape[0]

    def everywhere(values):
        gathered = lax.all_gather(values, axes, axis=0, tiled=True)
        return gathered.reshape(data_count, seq_len, values.shape[1])

    places_t, gates_t = routing(
        everywhere(expert_ids), everywhere(gate_values), local_experts, capacity
    )
    places, gates = places_t.transpose(0, 2, 1), gates_t.transpose(0, 2, 1)
    per_plane = 2
    planes = data_count // per_plane
    all_cot = everywhere(cotangent)
    all_rows = everywhere(second_in)
    kept = []
    row_parts, mix_parts = [], []
    for plane in range(planes):
        packs = slice(plane * per_plane, (plane + 1) * per_plane)
        grad_slots, grad_hidden = cot_slots(
            places[packs], gates[packs], all_cot[packs], w_down, capacity
        )
        slots, hidden, grad_gated, grad_lifted, row_part = row_slots(
            places[packs], places_t[packs], all_rows[packs], w_gate, w_up, grad_hidden, capacity
        )
        row_parts.append(row_part)
        mix_parts.append(mix_rows(places_t[packs], gates_t[packs], hidden, w_down, capacity))
        kept.append((slots, grad_slots, hidden, grad_gated, grad_lifted))

    def scattered(parts):
        whole = jnp.concatenate(parts, axis=0).reshape(data_count * seq_len, model_width)
        summed = lax.psum_scatter(whole, axes, scatter_dimension=0, tiled=True)
        return summed.astype(jnp.float32)

    grad_second = scattered(row_parts)
    outputs = middle + scattered(mix_parts)
    grad_w_gate, grad_w_up, grad_w_down = weight_grads(*zip(*kept))
    return outputs, grad_second, grad_w_gate, grad_w_up, grad_w_down


def shards(
    inputs,
    segment_ids,
    expert_ids,
    gate_values,
    attn_gain,
    query_gain,
    key_gain,
    w_query,
    w_key,
    w_value,
    w_output,
    ffn_gain,
    w_gate,
    w_up,
    w_down,
    cotangent,
):
    tok_rows, model_width = inputs.shape
    head_size = query_gain.shape[0]
    tensor_count = lax.axis_size("tensor")
    data_count = lax.axis_size("dp")
    local_experts = w_gate.shape[0]
    all_experts = local_experts * data_count
    top_count = expert_ids.shape[1]
    seq_len = tok_rows * tensor_count
    capacity = seq_len * top_count // all_experts
    inv_root = head_size ** (-0.5)
    inputs_f32 = inputs.astype(jnp.float32)
    normed_one, factor_one = norm_parts(inputs_f32)
    first_in = (normed_one * attn_gain).astype(jnp.bfloat16)
    pack_in, pack_segs = (
        lax.all_gather(first_in, "tensor", axis=0, tiled=True),
        lax.all_gather(segment_ids, "tensor", axis=1, tiled=True),
    )
    full_query, full_key, full_value, full_output = (
        lax.all_gather(w_query, "dp", axis=0, tiled=True),
        lax.all_gather(w_key, "dp", axis=0, tiled=True),
        lax.all_gather(w_value, "dp", axis=0, tiled=True),
        lax.all_gather(w_output, "dp", axis=1, tiled=True),
    )
    query_pre = matmul(pack_in, full_query)
    key_pre = matmul(pack_in, full_key)
    value_low = matmul(pack_in, full_value).astype(jnp.bfloat16)
    head_count = query_pre.shape[1] // head_size
    cosine, sine_tab = rope_tables(seq_len, head_size)
    query_norm, query_factor = norm_parts(query_pre.reshape(seq_len, head_count, head_size))
    key_norm, key_factor = norm_parts(key_pre.reshape(seq_len, head_count, head_size))
    query_low = rotate(query_norm * query_gain, cosine, sine_tab).astype(jnp.bfloat16)
    key_low = rotate(key_norm * key_gain, cosine, sine_tab).astype(jnp.bfloat16)
    value_heads = value_low.reshape(seq_len, head_count, head_size)
    segments = pack_segs[0]
    block_rows = min(512, seq_len)
    block_total = seq_len // block_rows
    masks = []
    mixture_parts = []
    lse_parts = []
    for block_index in range(block_total):
        offset = block_index * block_rows
        allowed = block_mask(segments, offset, block_rows, seq_len)
        masks.append(allowed)
        scores = block_scores(query_low[offset : offset + block_rows], key_low, allowed, inv_root)
        top_score = jnp.max(scores, axis=-1, keepdims=True)
        raw_weights = jnp.exp(scores - top_score)
        totals = jnp.sum(raw_weights, axis=-1, keepdims=True)
        weights_low = (raw_weights / totals).astype(jnp.bfloat16)
        mixture_parts.append(
            jnp.einsum(
                "hqk,khd->qhd", weights_low, value_heads, preferred_element_type=jnp.float32
            ).astype(jnp.bfloat16)
        )
        lse_parts.append(top_score + jnp.log(totals))
    mixture = jnp.concatenate(mixture_parts, axis=0).reshape(seq_len, head_count * head_size)

    def attn_term(offset, row_count):
        return matmul(mixture, full_output)

    middle = inputs_f32 + row_sum(attn_term, tok_rows)
    normed_two, factor_two = norm_parts(middle)
    second_in = (normed_two * ffn_gain).astype(jnp.bfloat16)
    if seq_len <= local_experts * capacity:
        outputs, grad_second, grad_w_gate, grad_w_up, grad_w_down = experts_by_gather(
            second_in, cotangent, expert_ids, gate_values, w_gate, w_up, w_down, middle, capacity
        )
    else:
        outputs, grad_second, grad_w_gate, grad_w_up, grad_w_down = experts_by_exchange(
            second_in, cotangent, expert_ids, gate_values, w_gate, w_up, w_down, middle, capacity
        )
    ffn_gain_part = jnp.sum(grad_second * normed_two, axis=0)
    grad_middle = cotangent.astype(jnp.float32) + norm_back(
        grad_second, normed_two, factor_two, ffn_gain
    )
    pack_grad = gather_rows(grad_middle.astype(jnp.bfloat16))
    output_part = contract_first(mixture, pack_grad)
    grad_mixture = (
        contract_last(pack_grad, full_output)
        .astype(jnp.bfloat16)
        .reshape(seq_len, head_count, head_size)
    )
    grad_query_parts = []
    grad_key_sum = jnp.zeros((seq_len, head_count, head_size), jnp.float32)
    grad_value_sum = jnp.zeros((seq_len, head_count, head_size), jnp.float32)
    for block_index in range(block_total):
        offset = block_index * block_rows
        query_block = query_low[offset : offset + block_rows]
        grad_block = grad_mixture[offset : offset + block_rows]
        scores = block_scores(query_block, key_low, masks[block_index], inv_root)
        prob_rows = jnp.exp(scores - lse_parts[block_index])
        grad_probs = jnp.einsum(
            "qhd,khd->hqk", grad_block, value_heads, preferred_element_type=jnp.float32
        )
        row_delta = jnp.sum(grad_probs * prob_rows, axis=-1, keepdims=True)
        grad_scores = (prob_rows * (grad_probs - row_delta)).astype(jnp.bfloat16)
        grad_query_parts.append(
            jnp.einsum("hqk,khd->qhd", grad_scores, key_low, preferred_element_type=jnp.float32)
            * inv_root
        )
        grad_key_sum = (
            grad_key_sum
            + jnp.einsum(
                "hqk,qhd->khd", grad_scores, query_block, preferred_element_type=jnp.float32
            )
            * inv_root
        )
        grad_value_sum = grad_value_sum + jnp.einsum(
            "hqk,qhd->khd",
            prob_rows.astype(jnp.bfloat16),
            grad_block,
            preferred_element_type=jnp.float32,
        )
    grad_query_norm = rotate_back(jnp.concatenate(grad_query_parts, axis=0), cosine, sine_tab)
    grad_key_norm = rotate_back(grad_key_sum, cosine, sine_tab)
    query_gain_part = jnp.sum(grad_query_norm * query_norm, axis=(0, 1))
    key_gain_part = jnp.sum(grad_key_norm * key_norm, axis=(0, 1))
    grad_query_pre = (
        norm_back(grad_query_norm, query_norm, query_factor, query_gain)
        .reshape(seq_len, -1)
        .astype(jnp.bfloat16)
    )
    grad_key_pre = (
        norm_back(grad_key_norm, key_norm, key_factor, key_gain)
        .reshape(seq_len, -1)
        .astype(jnp.bfloat16)
    )
    grad_value_low = grad_value_sum.reshape(seq_len, -1).astype(jnp.bfloat16)
    query_part = contract_first(pack_in, grad_query_pre)
    key_part = contract_first(pack_in, grad_key_pre)
    value_part = contract_first(pack_in, grad_value_low)

    def input_term(offset, row_count):
        total_term = contract_last(grad_query_pre, full_query)
        total_term = total_term + contract_last(grad_key_pre, full_key)
        return total_term + contract_last(grad_value_low, full_value)

    grad_first = row_sum(input_term, tok_rows)
    attn_gain_part = jnp.sum(grad_first * normed_one, axis=0)
    grad_inputs = grad_middle + norm_back(grad_first, normed_one, factor_one, attn_gain)
    grad_w_query, grad_w_key, grad_w_value, grad_w_output = (
        lax.psum_scatter(
            query_part.astype(jnp.bfloat16), "dp", scatter_dimension=0, tiled=True
        ).astype(jnp.float32),
        lax.psum_scatter(
            key_part.astype(jnp.bfloat16), "dp", scatter_dimension=0, tiled=True
        ).astype(jnp.float32),
        lax.psum_scatter(
            value_part.astype(jnp.bfloat16), "dp", scatter_dimension=0, tiled=True
        ).astype(jnp.float32),
        lax.psum_scatter(
            output_part.astype(jnp.bfloat16), "dp", scatter_dimension=1, tiled=True
        ).astype(jnp.float32),
    )
    grad_attn_gain, grad_ffn_gain, grad_query_gain, grad_key_gain = lax.psum(
        (attn_gain_part, ffn_gain_part, query_gain_part, key_gain_part), ("dp", "tensor")
    )
    return (
        outputs,
        grad_inputs,
        grad_attn_gain,
        grad_query_gain,
        grad_key_gain,
        grad_w_query,
        grad_w_key,
        grad_w_value,
        grad_w_output,
        grad_ffn_gain,
        grad_w_gate,
        grad_w_up,
        grad_w_down,
    )


def solution(mesh):
    in_specs = (
        P(("dp", "tensor"), None),
        P("dp", "tensor"),
        P(("dp", "tensor"), None),
        P(("dp", "tensor"), None),
        P(),
        P(),
        P(),
        P("dp", "tensor"),
        P("dp", "tensor"),
        P("dp", "tensor"),
        P("tensor", "dp"),
        P(),
        P("dp", None, "tensor"),
        P("dp", None, "tensor"),
        P("dp", "tensor", None),
        P(("dp", "tensor"), None),
    )
    out_specs = (
        P(("dp", "tensor"), None),
        P(("dp", "tensor"), None),
        P(),
        P(),
        P(),
        P("dp", "tensor"),
        P("dp", "tensor"),
        P("dp", "tensor"),
        P("tensor", "dp"),
        P(),
        P("dp", None, "tensor"),
        P("dp", None, "tensor"),
        P("dp", "tensor", None),
    )
    return jax.shard_map(shards, mesh=mesh, in_specs=in_specs, out_specs=out_specs, check_vma=False)
```

```python
import jax
import jax.numpy as jnp
import functools

from jax import lax
from jax.experimental import pallas as pl
from jax.experimental.pallas import tpu as pltpu
from jax.sharding import PartitionSpec as P

WINDOW = 1024


EPSILON = 1e-06
THETA = 50000.0
NEG_FILL = -1e30


def matmul(left_side, right_side):
    return jnp.dot(left_side, right_side, preferred_element_type=jnp.float32)


def contract_last(left_side, right_side):
    return lax.dot_general(
        left_side, right_side, (((1,), (1,)), ((), ())), preferred_element_type=jnp.float32
    )


def contract_first(left_side, right_side):
    return lax.dot_general(
        left_side, right_side, (((0,), (0,)), ((), ())), preferred_element_type=jnp.float32
    )


def norm_parts(values):
    factor = lax.rsqrt(jnp.mean(values * values, axis=-1, keepdims=True) + EPSILON)
    return (values * factor, factor)


def norm_back(grad_out, normed, factor, gain_vec):
    scaled = grad_out * gain_vec
    return factor * (scaled - normed * jnp.mean(scaled * normed, axis=-1, keepdims=True))


def rope_tables(length, head_size):
    half_size = head_size // 2
    frequency = THETA ** (-(2.0 * jnp.arange(half_size, dtype=jnp.float32)) / head_size)
    angles = jnp.arange(length, dtype=jnp.float32)[:, None] * frequency[None, :]
    return (jnp.cos(angles)[:, None, :], jnp.sin(angles)[:, None, :])


def rotate(values, cosine, sine_tab):
    half_size = values.shape[-1] // 2
    first_half = values[..., :half_size]
    second_half = values[..., half_size:]
    return jnp.concatenate(
        [
            first_half * cosine - second_half * sine_tab,
            second_half * cosine + first_half * sine_tab,
        ],
        axis=-1,
    )


def rotate_back(grads_in, cosine, sine_tab):
    half_size = grads_in.shape[-1] // 2
    first_half = grads_in[..., :half_size]
    second_half = grads_in[..., half_size:]
    return jnp.concatenate(
        [
            first_half * cosine + second_half * sine_tab,
            second_half * cosine - first_half * sine_tab,
        ],
        axis=-1,
    )


def block_mask(segments, offset, block_rows, key_count):
    query_pos = offset + jnp.arange(block_rows)
    key_pos = jnp.arange(key_count)
    same_doc = segments[offset : offset + block_rows][:, None] == segments[None, :]
    near_pos = jnp.abs(query_pos[:, None] - key_pos[None, :]) < WINDOW // 2
    return same_doc & near_pos


def block_scores(query_block, key_low, allowed, inv_root):
    scores = (
        jnp.einsum("qhd,khd->hqk", query_block, key_low, preferred_element_type=jnp.float32)
        * inv_root
    )
    return jnp.where(allowed[None], scores, NEG_FILL)


def row_sum(term_fn, tok_rows):
    return lax.psum_scatter(
        term_fn(jnp.int32(0), lax.axis_size("tensor") * tok_rows),
        "tensor",
        scatter_dimension=0,
        tiled=True,
    )


def gather_rows(values):
    return lax.all_gather(values, "tensor", axis=0, tiled=True)


def from_experts(values):
    return lax.all_to_all(values, "dp", split_axis=1, concat_axis=1, tiled=True)


def to_experts(source_rows, slot_token, slot_gate, layout):
    picked = jnp.take(source_rows, slot_token, axis=0, mode="fill", fill_value=0)
    if slot_gate is not None:
        picked = (picked.astype(jnp.float32) * slot_gate[:, None]).astype(jnp.bfloat16)
    picked = picked.reshape(layout + (picked.shape[1],))
    return lax.all_to_all(picked, "dp", split_axis=1, concat_axis=1, tiled=True)


def pair_sum(table, weights_low, pair_slots, row_count):
    picked = jnp.take(table, pair_slots.reshape(-1), axis=0, mode="fill", fill_value=0)
    picked = picked.reshape(row_count, pair_slots.shape[1], table.shape[1])
    return jnp.einsum("rk,rkd->rd", weights_low, picked, preferred_element_type=jnp.float32)


def expert_forward(operands):
    rows_in, gate_mat, up_mat, down_mat = operands
    flat_rows = rows_in.reshape(-1, rows_in.shape[-1])
    gated = matmul(flat_rows, gate_mat)
    lifted = matmul(flat_rows, up_mat)
    hidden = (jax.nn.silu(gated) * lifted).astype(jnp.bfloat16)
    result = matmul(hidden, down_mat).astype(jnp.bfloat16)
    return (result.reshape(rows_in.shape), gated, lifted)


def expert_backward(operands):
    rows_in, grad_in, gated, lifted, gate_mat, up_mat, down_mat = operands
    flat_rows = rows_in.reshape(-1, rows_in.shape[-1])
    flat_grad = grad_in.reshape(-1, grad_in.shape[-1])
    gate_sig = jax.nn.sigmoid(gated)
    activated = jax.nn.silu(gated)
    hidden = (activated * lifted).astype(jnp.bfloat16)
    grad_hidden = contract_last(flat_grad, down_mat)
    grad_down = contract_first(hidden, flat_grad)
    grad_gated = (grad_hidden * lifted * gate_sig * (1.0 + gated * (1.0 - gate_sig))).astype(
        jnp.bfloat16
    )
    grad_lifted = (grad_hidden * activated).astype(jnp.bfloat16)
    grad_gate = contract_first(flat_rows, grad_gated)
    grad_up = contract_first(flat_rows, grad_lifted)
    grad_rows = (contract_last(grad_gated, gate_mat) + contract_last(grad_lifted, up_mat)).astype(
        jnp.bfloat16
    )
    return (grad_rows.reshape(rows_in.shape), grad_gate, grad_up, grad_down)


VMEM_BYTES = 60 * 1024 * 1024
COLUMN_CHUNK = 512


def select_rows(places_ref, gates_ref, pick_ref, capacity):
    expert_count, seq_len = places_ref.shape[1:]
    slot_range = lax.broadcasted_iota(jnp.int32, (capacity, seq_len), 0)
    for expert in range(expert_count):
        hit = places_ref[0, expert : expert + 1, :] == slot_range
        weight = 1.0 if gates_ref is None else gates_ref[0, expert : expert + 1, :]
        rows = slice(expert * capacity, (expert + 1) * capacity)
        pick_ref[rows, :] = jnp.where(hit, weight, 0.0).astype(jnp.bfloat16)


def spread_rows(places_ref, gates_ref, pick_ref, capacity):
    seq_len, expert_count = places_ref.shape[1:]
    slot_range = lax.broadcasted_iota(jnp.int32, (seq_len, capacity), 1)
    for expert in range(expert_count):
        hit = places_ref[0, :, expert : expert + 1] == slot_range
        weight = 1.0 if gates_ref is None else gates_ref[0, :, expert : expert + 1]
        columns = slice(expert * capacity, (expert + 1) * capacity)
        pick_ref[:, columns] = jnp.where(hit, weight, 0.0).astype(jnp.bfloat16)


def rows_to_slots(pick_ref, rows_ref, slots_ref, pack, capacity):
    width = rows_ref.shape[2]
    expert_count = slots_ref.shape[0]
    for start in range(0, width, COLUMN_CHUNK):
        columns = slice(start, start + COLUMN_CHUNK)
        picked = matmul(pick_ref[...], rows_ref[0, :, columns]).astype(jnp.bfloat16)
        slots_ref[:, pack, :, columns] = picked.reshape(expert_count, capacity, COLUMN_CHUNK)


def slots_to_rows(pick_ref, slots_ref, own_ref, other_ref, pack):
    width = own_ref.shape[3]
    for start in range(0, width, COLUMN_CHUNK):
        columns = slice(start, start + COLUMN_CHUNK)
        slots = slots_ref[:, pack, :, columns].reshape(-1, COLUMN_CHUNK)
        rows = matmul(pick_ref[...], slots).astype(own_ref.dtype)
        rows = rows.reshape(2, 2, own_ref.shape[2], COLUMN_CHUNK)
        own_ref[0, :, :, columns] = rows[:, 0]
        other_ref[0, :, :, columns] = rows[:, 1]


def cot_kernel(
    packs, experts, capacity, table, places, gates, rows, down, slots_out, hidden_out, slots, pick
):
    step = pl.program_id(0)

    @pl.when(step < packs)
    def _():
        select_rows(places, gates, pick, capacity)
        rows_to_slots(pick, rows, slots, step, capacity)

    @pl.when(step >= packs)
    def _():
        block = slots[step - packs].reshape(packs * capacity, -1)
        slots_out[0] = block
        hidden_out[0] = contract_last(block, down[0])


def piece_copies(own, other, rows, sems, pack):
    half_rows = own.shape[1]
    copies = []
    for far in range(2):
        for core, source in enumerate((own, other)):
            for half, index in enumerate((4 * far + pack, 2 + 4 * pack + far)):
                start = ((far * 2 + core) * 2 + half) * half_rows
                copies.append(
                    pltpu.make_async_copy(
                        source.at[index],
                        rows.at[pack, pl.ds(start, half_rows)],
                        sems.at[pack * 8 + len(copies)],
                    )
                )
    return copies


def row_kernel(
    packs, experts, capacity, places, places_t, own, other, gate, up, grad_hidden,
    slots_out, hidden_out, gated_out, lifted_out, rows_own, rows_other,
    rows, slots, grads, pick, spread, sems,
):
    step = pl.program_id(0)

    @pl.when(step == 0)
    def _():
        for pack in range(packs):
            for copy in piece_copies(own, other, rows, sems, pack):
                copy.start()

    for pack in range(packs):

        @pl.when(step == pack)
        def _(pack=pack):
            select_rows(places, None, pick, capacity)
            for copy in piece_copies(own, other, rows, sems, pack):
                copy.wait()
            rows_to_slots(pick, rows.at[pl.ds(pack, 1)], slots, pack, capacity)

    @pl.when((step >= packs) & (step < packs + experts))
    def _():
        expert = step - packs
        block = slots[expert].reshape(packs * capacity, -1)
        slots_out[0] = block
        gated = matmul(block, gate[0])
        lifted = matmul(block, up[0])
        sig = 1.0 / (1.0 + jnp.exp(-gated))
        active = gated * sig
        hidden_out[0] = (active * lifted).astype(jnp.bfloat16)
        above = grad_hidden[0]
        grad_gated = (above * lifted * sig * (1.0 + gated * (1.0 - sig))).astype(jnp.bfloat16)
        grad_lifted = (above * active).astype(jnp.bfloat16)
        gated_out[0] = grad_gated
        lifted_out[0] = grad_lifted
        back = contract_last(grad_gated, gate[0]) + contract_last(grad_lifted, up[0])
        grads[expert] = back.astype(jnp.bfloat16).reshape(packs, capacity, -1)

    @pl.when(step >= packs + experts)
    def _():
        spread_rows(places_t, None, spread, capacity)
        slots_to_rows(spread, grads, rows_own, rows_other, step - packs - experts)


def mix_kernel(
    packs, experts, capacity, places_t, gates_t, hidden, down, rows_own, rows_other, results, spread
):
    step = pl.program_id(0)

    @pl.when(step < experts)
    def _():
        result = matmul(hidden[0], down[0])
        results[step] = result.astype(jnp.bfloat16).reshape(packs, capacity, -1)

    @pl.when(step >= experts)
    def _():
        spread_rows(places_t, gates_t, spread, capacity)
        slots_to_rows(spread, results, rows_own, rows_other, step - experts)


def weight_kernel(planes, *refs):
    slots, grads, hidden, gated, lifted = (refs[i * planes : (i + 1) * planes] for i in range(5))
    gate_out, up_out, down_out = refs[5 * planes :]

    def total(left, right):
        result = contract_first(left[0][0], right[0][0])
        for index in range(1, planes):
            result = result + contract_first(left[index][0], right[index][0])
        return result

    gate_out[0] = total(slots, gated)
    up_out[0] = total(slots, lifted)
    down_out[0] = total(hidden, grads)


def block(shape, place):
    tail = (0,) * (len(shape) - 1)
    return pl.BlockSpec((1,) + tuple(shape[1:]), lambda *ids: (place(*ids),) + tail)


def staged(first, count):
    return lambda step, *rest: jnp.clip(step - first, 0, count - 1)


def shape_of(shape, kind):
    return jax.ShapeDtypeStruct(shape, kind)


def call(kernel, steps, specs, out_specs, out_shape, scratch, flops, prefetch=0):
    return pl.pallas_call(
        kernel,
        grid_spec=pltpu.PrefetchScalarGridSpec(
            num_scalar_prefetch=prefetch,
            grid=(steps,),
            in_specs=specs,
            out_specs=out_specs,
            scratch_shapes=scratch,
        ),
        out_shape=out_shape,
        cost_estimate=pl.CostEstimate(
            flops=flops, transcendentals=0, bytes_accessed=flops // 500
        ),
        compiler_params=pltpu.CompilerParams(
            dimension_semantics=("arbitrary",), vmem_limit_bytes=VMEM_BYTES
        ),
    )


def cot_slots(table, places, gates, rows, down, capacity):
    packs = table.shape[0]
    _, seq_len, width = rows.shape
    experts, hidden_width, _ = down.shape
    slot_rows = packs * capacity
    by_pack, by_expert = staged(0, packs), staged(packs, experts)
    listed = lambda step, numbers: numbers[by_pack(step)]
    out_shape = [
        shape_of((experts, slot_rows, width), jnp.bfloat16),
        shape_of((experts, slot_rows, hidden_width), jnp.float32),
    ]
    return call(
        functools.partial(cot_kernel, packs, experts, capacity),
        packs + experts,
        [
            block(places.shape, listed), block(gates.shape, listed), block(rows.shape, listed),
            block(down.shape, by_expert),
        ],
        [block(out.shape, by_expert) for out in out_shape],
        out_shape,
        [
            pltpu.VMEM((experts, packs, capacity, width), jnp.bfloat16),
            pltpu.VMEM((experts * capacity, seq_len), jnp.bfloat16),
        ],
        2 * experts * slot_rows * width * (seq_len + hidden_width),
        1,
    )(table, places, gates, rows, down)


def row_slots(places, places_t, own, other, gate, up, grad_hidden, capacity):
    packs, _, seq_len = places.shape
    experts, width, hidden_width = gate.shape
    slot_rows = packs * capacity
    first, middle, last = staged(0, packs), staged(packs, experts), staged(packs + experts, packs)
    narrow = shape_of((experts, slot_rows, hidden_width), jnp.bfloat16)
    part = shape_of((packs, 2, seq_len // 4, width), jnp.bfloat16)
    out_shape = [
        shape_of((experts, slot_rows, width), jnp.bfloat16), narrow, narrow, narrow, part, part
    ]
    anywhere = pl.BlockSpec(memory_space=pl.ANY)
    return call(
        functools.partial(row_kernel, packs, experts, capacity),
        2 * packs + experts,
        [
            block(places.shape, first), block(places_t.shape, last), anywhere, anywhere,
            block(gate.shape, middle), block(up.shape, middle), block(grad_hidden.shape, middle),
        ],
        [block(out.shape, middle) for out in out_shape[:4]] + [block(part.shape, last)] * 2,
        out_shape,
        [
            pltpu.VMEM((packs, seq_len, width), jnp.bfloat16),
            pltpu.VMEM((experts, packs, capacity, width), jnp.bfloat16),
            pltpu.VMEM((experts, packs, capacity, width), jnp.bfloat16),
            pltpu.VMEM((experts * capacity, seq_len), jnp.bfloat16),
            pltpu.VMEM((seq_len, experts * capacity), jnp.bfloat16),
            pltpu.SemaphoreType.DMA((8 * packs,)),
        ],
        4 * experts * slot_rows * width * (seq_len + 2 * hidden_width),
    )(places, places_t, own, other, gate, up, grad_hidden)


def mix_rows(places_t, gates_t, hidden, down, capacity):
    packs, seq_len, _ = places_t.shape
    experts, hidden_width, width = down.shape
    first, last = staged(0, experts), staged(experts, packs)
    part = shape_of((packs, 2, seq_len // 4, width), jnp.bfloat16)
    return call(
        functools.partial(mix_kernel, packs, experts, capacity),
        packs + experts,
        [
            block(places_t.shape, last), block(gates_t.shape, last),
            block(hidden.shape, first), block(down.shape, first),
        ],
        [block(part.shape, last)] * 2,
        [part, part],
        [
            pltpu.VMEM((experts, packs, capacity, width), jnp.bfloat16),
            pltpu.VMEM((seq_len, experts * capacity), jnp.bfloat16),
        ],
        2 * experts * packs * capacity * width * (seq_len + hidden_width),
    )(places_t, gates_t, hidden, down)


def weight_grads(slots, grads, hidden, gated, lifted):
    planes = len(slots)
    operands = [*slots, *grads, *hidden, *gated, *lifted]
    experts, _, width = slots[0].shape
    hidden_width = hidden[0].shape[2]
    each = lambda step: step
    out_shape = [
        shape_of((experts, width, hidden_width), jnp.float32),
        shape_of((experts, width, hidden_width), jnp.float32),
        shape_of((experts, hidden_width, width), jnp.float32),
    ]
    return call(
        functools.partial(weight_kernel, planes),
        experts,
        [block(operand.shape, each) for operand in operands],
        [block(out.shape, each) for out in out_shape],
        out_shape,
        [],
        6 * planes * slots[0].shape[1] * experts * width * hidden_width,
    )(*operands)


def swapped(values, axis, bit):
    count = lax.axis_size(axis)
    return lax.ppermute(values, axis, [(i, i ^ bit) for i in range(count)])


def far_side(values):
    return swapped(values, "tensor", 2)


def far_core(values):
    return swapped(values, "tensor", 1)


def far_pack(values):
    return swapped(values, "dp", 1)


def next_plane(values):
    count = lax.axis_size("dp")
    return lax.ppermute(values, "dp", [(i, (i + 2) % count) for i in range(count)])


def spread_plane(values):
    half_rows = values.shape[0] // 2
    upper, lower = values[:half_rows], values[half_rows:]
    near_upper = jnp.stack([upper, far_pack(upper)])
    near_lower = jnp.stack([lower, far_side(lower)])
    own = jnp.concatenate([near_upper, near_lower, far_side(near_upper), far_pack(near_lower)])
    return own, far_core(own)


def plane_order():
    packs = lax.axis_size("dp")
    planes = packs // 2
    index = lax.axis_index("dp")
    return jnp.stack(
        [
            ((index // 2 + planes - plane) % planes) * 2 + (index % 2 ^ near)
            for plane in range(planes)
            for near in range(2)
        ]
    )


def laid(pieces, order):
    whole = jnp.zeros((len(pieces),) + pieces[0].shape, pieces[0].dtype)
    for index, piece in enumerate(pieces):
        place = (order[index],) + (0,) * piece.ndim
        whole = lax.dynamic_update_slice(whole, piece[None], place)
    return whole


def gather_packs(values):
    pieces = []
    for plane in range(lax.axis_size("dp") // 2):
        values = next_plane(values) if plane else values
        pieces += [values, far_pack(values)]
    return laid(pieces, plane_order())


def fold_packs(values):
    order = plane_order()
    take = lambda index: lax.dynamic_index_in_dim(values, order[index], 0, keepdims=False)
    near = [added(take(2 * i), far_pack(take(2 * i + 1))) for i in range(values.shape[0] // 2)]
    summed = near[1]
    for part in near[2:]:
        summed = added(next_plane(summed), part)
    return added(next_plane(summed), near[0], jnp.float32)


def gather_sides(values):
    across = far_side(values)
    pieces = [values, far_core(values), across, far_core(across)]
    order = lax.axis_index("tensor") ^ jnp.arange(len(pieces), dtype=jnp.int32)
    return laid(pieces, order).reshape((-1,) + values.shape[1:])


def fold_sides(values):
    split = values.astype(jnp.bfloat16).reshape((4, -1) + values.shape[1:])
    take = lambda bits: lax.dynamic_index_in_dim(
        split, lax.axis_index("tensor") ^ bits, 0, keepdims=False
    )
    far = added(take(2), far_core(take(3)))
    near = added(take(0), far_core(take(1)))
    return added(near, far_side(far), jnp.float32)


def sum_everywhere(values):
    for axis in ("tensor", "dp"):
        bit = 1
        while bit < lax.axis_size(axis):
            values = values + swapped(values, axis, bit)
            bit *= 2
    return values


def added(left, right, kind=jnp.bfloat16):
    return (left.astype(jnp.float32) + right.astype(jnp.float32)).astype(kind)


def fold_plane(own, other):
    half_rows = own.shape[2] // 2
    arrived = far_core(other)
    upper, lower = slice(None, half_rows), slice(half_rows, None)
    upper_near = added(own[:, 0, upper], arrived[:, 0, upper])
    upper_far = added(own[:, 1, upper], arrived[:, 1, upper])
    lower_near = added(own[0, :, lower], arrived[0, :, lower])
    lower_far = added(own[1, :, lower], arrived[1, :, lower])
    upper_near = added(upper_near, far_side(upper_far))
    lower_near = added(lower_near, far_pack(lower_far))
    return jnp.concatenate(
        [
            added(upper_near[0], far_pack(upper_near[1])),
            added(lower_near[0], far_side(lower_near[1])),
        ]
    )


def fold_all(parts):
    summed = fold_plane(*parts[1])
    for part in parts[2:]:
        summed = added(next_plane(summed), fold_plane(*part))
    return added(next_plane(summed), fold_plane(*parts[0]), jnp.float32)


def routing(all_ids, all_gates, local_experts, capacity):
    packs = lax.axis_size("dp")
    first = lax.axis_index("dp") * local_experts
    wanted = first + jnp.arange(local_experts, dtype=jnp.int32)

    def by_pack(values):
        top_count, tok_rows = values.shape[1:]
        ordered = values.reshape(packs, -1, top_count, tok_rows).transpose(0, 2, 1, 3)
        return ordered.reshape(packs, top_count, -1)

    matches = by_pack(all_ids)[:, :, None, :] == wanted[None, None, :, None]
    pair_gates = by_pack(all_gates).astype(jnp.float32)
    member = jnp.any(matches, axis=1)
    gates = jnp.sum(jnp.where(matches, pair_gates[:, :, None, :], 0.0), axis=1)
    order = jnp.arange(member.shape[2], dtype=jnp.int32)
    earlier = (order[:, None] < order[None, :]).astype(jnp.bfloat16)
    flat = member.reshape(packs * local_experts, -1).astype(jnp.bfloat16)
    before = matmul(flat, earlier).astype(jnp.int32).reshape(member.shape)
    return jnp.where(member & (before < capacity), before, -1), gates


def experts_by_exchange(
    second_in, cotangent, expert_ids, gate_values, w_gate, w_up, w_down, middle, capacity
):
    tok_rows, model_width = second_in.shape
    tensor_count = lax.axis_size("tensor")
    data_count = lax.axis_size("dp")
    local_experts = w_gate.shape[0]
    all_experts = local_experts * data_count
    top_count = expert_ids.shape[1]
    seq_len = tok_rows * tensor_count
    pack_cot, pack_ids, pack_gates = (
        gather_rows(cotangent), gather_rows(expert_ids), gather_rows(gate_values)
    )
    pack_second = gather_rows(second_in)
    expert_range = jnp.arange(all_experts, dtype=jnp.int32)
    matches = pack_ids[:, :, None] == expert_range[None, None, :]
    token_counts = jnp.sum(matches.astype(jnp.float32), axis=1).astype(jnp.bfloat16)
    token_range = jnp.arange(seq_len, dtype=jnp.int32)
    earlier = (token_range[:, None] > token_range[None, :]).astype(jnp.bfloat16)
    before = matmul(earlier, token_counts)
    places = (
        jnp.sum(jnp.where(matches, before[:, None, :], 0.0), axis=2).astype(jnp.int32).reshape(-1)
    )
    flat_ids = pack_ids.reshape(-1)
    owners = flat_ids // local_experts
    local_index = flat_ids % local_experts
    dump_slot = all_experts * capacity
    slot_index = jnp.where(
        places < capacity,
        local_index * (data_count * capacity) + owners * capacity + places,
        dump_slot,
    ).astype(jnp.int32)
    pair_token = jnp.arange(seq_len * top_count) // top_count
    slot_token = (
        jnp.full((dump_slot + 1,), seq_len, jnp.int32).at[slot_index].set(pair_token)[:dump_slot]
    )
    pair_gates = pack_gates.astype(jnp.float32)
    slot_gate = (
        jnp.zeros((dump_slot + 1,), jnp.float32)
        .at[slot_index]
        .set(pair_gates.reshape(-1))[:dump_slot]
    )
    pair_slots = slot_index.reshape(seq_len, top_count)
    layout = (local_experts, data_count, capacity)
    arrived_rows = to_experts(pack_second, slot_token, None, layout)
    expert_out, gated_all, lifted_all = lax.map(
        expert_forward, (arrived_rows, w_gate, w_up, w_down)
    )
    returned = from_experts(expert_out).reshape(-1, model_width)

    def combine_term(offset, row_count):
        return pair_sum(returned, pack_gates, pair_slots, row_count)

    outputs = middle + row_sum(combine_term, tok_rows)
    grad_arrived = to_experts(pack_cot, slot_token, slot_gate, layout)
    grad_rows_all, grad_w_gate, grad_w_up, grad_w_down = lax.map(
        expert_backward, (arrived_rows, grad_arrived, gated_all, lifted_all, w_gate, w_up, w_down)
    )
    returned_grad = from_experts(grad_rows_all).reshape(-1, model_width)
    unit_gates = jnp.ones_like(pack_gates)

    def dispatch_term(offset, row_count):
        return pair_sum(returned_grad, unit_gates, pair_slots, row_count)

    grad_second = row_sum(dispatch_term, tok_rows)
    return outputs, grad_second, grad_w_gate, grad_w_up, grad_w_down


def experts_by_gather(second_in, all_cot, places, gates, w_gate, w_up, w_down, middle, capacity):
    packs, local_experts, seq_len = places.shape
    tensor_count = lax.axis_size("tensor")
    planes = packs // 2
    pack_order = plane_order()
    side_index = lax.axis_index("tensor")
    quarter_order = side_index ^ jnp.arange(tensor_count, dtype=jnp.int32)

    def as_met(values):
        split = values.reshape(packs, local_experts, tensor_count, -1)
        split = jnp.take(jnp.take(split, pack_order, axis=0), quarter_order, axis=2)
        return split.reshape(values.shape)

    near_places, near_gates = as_met(places), as_met(gates)
    places_t, gates_t = near_places.transpose(0, 2, 1), near_gates.transpose(0, 2, 1)
    kept = []
    row_parts, mix_parts = [], []
    travelling = second_in
    for plane in range(planes):
        pair = slice(plane * 2, plane * 2 + 2)
        grad_slots, grad_hidden = cot_slots(
            pack_order[pair], places, gates, all_cot, w_down, capacity
        )
        own, other = spread_plane(travelling)
        if plane + 1 < planes:
            travelling = next_plane(travelling)
        slots, hidden, grad_gated, grad_lifted, *row_part = row_slots(
            near_places[pair], places_t[pair], own, other, w_gate, w_up, grad_hidden, capacity
        )
        row_parts.append(row_part)
        kept.append((slots, grad_slots, hidden, grad_gated, grad_lifted))
    kept, _ = lax.optimization_barrier((kept, row_parts[-1]))
    for plane in range(planes):
        pair = slice(plane * 2, plane * 2 + 2)
        mix_parts.append(mix_rows(places_t[pair], gates_t[pair], kept[plane][2], w_down, capacity))
    grad_second, mix_parts = lax.optimization_barrier((fold_all(row_parts), mix_parts))
    outputs = middle + fold_all(mix_parts)
    grad_w_gate, grad_w_up, grad_w_down = weight_grads(*zip(*kept))
    return outputs, grad_second, grad_w_gate, grad_w_up, grad_w_down


def shards(
    inputs,
    segment_ids,
    expert_ids,
    gate_values,
    attn_gain,
    query_gain,
    key_gain,
    w_query,
    w_key,
    w_value,
    w_output,
    ffn_gain,
    w_gate,
    w_up,
    w_down,
    cotangent,
):
    tok_rows, model_width = inputs.shape
    head_size = query_gain.shape[0]
    tensor_count = lax.axis_size("tensor")
    data_count = lax.axis_size("dp")
    local_experts = w_gate.shape[0]
    all_experts = local_experts * data_count
    top_count = expert_ids.shape[1]
    seq_len = tok_rows * tensor_count
    capacity = seq_len * top_count // all_experts
    inv_root = head_size ** (-0.5)
    by_gather = (
        seq_len <= local_experts * capacity
        and tensor_count == 4
        and data_count > 2
        and data_count & (data_count - 1) == 0
    )
    if by_gather:
        axes = ("dp", "tensor")
        all_ids = lax.all_gather(expert_ids.T, axes, axis=0)
        all_gates = lax.all_gather(gate_values.T, axes, axis=0)
        pack_segs = lax.all_gather(segment_ids, "tensor", axis=1, tiled=True)
        inputs, cotangent, w_query, all_ids, all_gates, pack_segs = lax.optimization_barrier(
            (inputs, cotangent, w_query, all_ids, all_gates, pack_segs)
        )
        all_cot = lax.all_gather(cotangent, axes, axis=0, tiled=True)
        all_cot = all_cot.reshape(data_count, seq_len, model_width)
        places, gates = routing(all_ids, all_gates, local_experts, capacity)
    inputs_f32 = inputs.astype(jnp.float32)
    normed_one, factor_one = norm_parts(inputs_f32)
    first_in = (normed_one * attn_gain).astype(jnp.bfloat16)
    if by_gather:
        side_sum, side_gather = fold_sides, gather_sides
        local_width = w_query.shape[1]
        full_in = gather_packs(jnp.concatenate([w_query, w_key, w_value], axis=1))
        full_in = full_in.reshape(model_width, -1)
        full_query, full_key, full_value = (
            full_in[:, index * local_width : (index + 1) * local_width] for index in range(3)
        )
        full_output = gather_packs(w_output).transpose(1, 0, 2).reshape(w_output.shape[0], -1)
    else:
        side_sum, side_gather = lambda term: row_sum(lambda *_: term, tok_rows), gather_rows
        pack_segs = lax.all_gather(segment_ids, "tensor", axis=1, tiled=True)
        full_query, full_key, full_value, full_output = (
            lax.all_gather(w_query, "dp", axis=0, tiled=True),
            lax.all_gather(w_key, "dp", axis=0, tiled=True),
            lax.all_gather(w_value, "dp", axis=0, tiled=True),
            lax.all_gather(w_output, "dp", axis=1, tiled=True),
        )
    pack_in = side_gather(first_in)
    query_pre = matmul(pack_in, full_query)
    key_pre = matmul(pack_in, full_key)
    value_low = matmul(pack_in, full_value).astype(jnp.bfloat16)
    head_count = query_pre.shape[1] // head_size
    cosine, sine_tab = rope_tables(seq_len, head_size)
    query_norm, query_factor = norm_parts(query_pre.reshape(seq_len, head_count, head_size))
    key_norm, key_factor = norm_parts(key_pre.reshape(seq_len, head_count, head_size))
    query_low = rotate(query_norm * query_gain, cosine, sine_tab).astype(jnp.bfloat16)
    key_low = rotate(key_norm * key_gain, cosine, sine_tab).astype(jnp.bfloat16)
    value_heads = value_low.reshape(seq_len, head_count, head_size)
    segments = pack_segs[0]
    block_rows = min(512, seq_len)
    block_total = seq_len // block_rows
    masks = []
    mixture_parts = []
    lse_parts = []
    for block_index in range(block_total):
        offset = block_index * block_rows
        allowed = block_mask(segments, offset, block_rows, seq_len)
        masks.append(allowed)
        scores = block_scores(query_low[offset : offset + block_rows], key_low, allowed, inv_root)
        top_score = jnp.max(scores, axis=-1, keepdims=True)
        raw_weights = jnp.exp(scores - top_score)
        totals = jnp.sum(raw_weights, axis=-1, keepdims=True)
        weights_low = (raw_weights / totals).astype(jnp.bfloat16)
        mixture_parts.append(
            jnp.einsum(
                "hqk,khd->qhd", weights_low, value_heads, preferred_element_type=jnp.float32
            ).astype(jnp.bfloat16)
        )
        lse_parts.append(top_score + jnp.log(totals))
    mixture = jnp.concatenate(mixture_parts, axis=0).reshape(seq_len, head_count * head_size)

    middle = inputs_f32 + side_sum(matmul(mixture, full_output))
    normed_two, factor_two = norm_parts(middle)
    second_in = (normed_two * ffn_gain).astype(jnp.bfloat16)
    if by_gather:
        outputs, grad_second, grad_w_gate, grad_w_up, grad_w_down = experts_by_gather(
            second_in, all_cot, places, gates, w_gate, w_up, w_down, middle, capacity
        )
    else:
        outputs, grad_second, grad_w_gate, grad_w_up, grad_w_down = experts_by_exchange(
            second_in, cotangent, expert_ids, gate_values, w_gate, w_up, w_down, middle, capacity
        )
    ffn_gain_part = jnp.sum(grad_second * normed_two, axis=0)
    grad_middle = cotangent.astype(jnp.float32) + norm_back(
        grad_second, normed_two, factor_two, ffn_gain
    )
    pack_grad = side_gather(grad_middle.astype(jnp.bfloat16))
    output_part = contract_first(mixture, pack_grad)
    grad_mixture = (
        contract_last(pack_grad, full_output)
        .astype(jnp.bfloat16)
        .reshape(seq_len, head_count, head_size)
    )
    grad_query_parts = []
    grad_key_sum = jnp.zeros((seq_len, head_count, head_size), jnp.float32)
    grad_value_sum = jnp.zeros((seq_len, head_count, head_size), jnp.float32)
    for block_index in range(block_total):
        offset = block_index * block_rows
        query_block = query_low[offset : offset + block_rows]
        grad_block = grad_mixture[offset : offset + block_rows]
        scores = block_scores(query_block, key_low, masks[block_index], inv_root)
        prob_rows = jnp.exp(scores - lse_parts[block_index])
        grad_probs = jnp.einsum(
            "qhd,khd->hqk", grad_block, value_heads, preferred_element_type=jnp.float32
        )
        row_delta = jnp.sum(grad_probs * prob_rows, axis=-1, keepdims=True)
        grad_scores = (prob_rows * (grad_probs - row_delta)).astype(jnp.bfloat16)
        grad_query_parts.append(
            jnp.einsum("hqk,khd->qhd", grad_scores, key_low, preferred_element_type=jnp.float32)
            * inv_root
        )
        grad_key_sum = (
            grad_key_sum
            + jnp.einsum(
                "hqk,qhd->khd", grad_scores, query_block, preferred_element_type=jnp.float32
            )
            * inv_root
        )
        grad_value_sum = grad_value_sum + jnp.einsum(
            "hqk,qhd->khd",
            prob_rows.astype(jnp.bfloat16),
            grad_block,
            preferred_element_type=jnp.float32,
        )
    grad_query_norm = rotate_back(jnp.concatenate(grad_query_parts, axis=0), cosine, sine_tab)
    grad_key_norm = rotate_back(grad_key_sum, cosine, sine_tab)
    query_gain_part = jnp.sum(grad_query_norm * query_norm, axis=(0, 1))
    key_gain_part = jnp.sum(grad_key_norm * key_norm, axis=(0, 1))
    grad_query_pre = (
        norm_back(grad_query_norm, query_norm, query_factor, query_gain)
        .reshape(seq_len, -1)
        .astype(jnp.bfloat16)
    )
    grad_key_pre = (
        norm_back(grad_key_norm, key_norm, key_factor, key_gain)
        .reshape(seq_len, -1)
        .astype(jnp.bfloat16)
    )
    grad_value_low = grad_value_sum.reshape(seq_len, -1).astype(jnp.bfloat16)
    query_part = contract_first(pack_in, grad_query_pre)
    key_part = contract_first(pack_in, grad_key_pre)
    value_part = contract_first(pack_in, grad_value_low)

    total_term = contract_last(grad_query_pre, full_query)
    total_term = total_term + contract_last(grad_key_pre, full_key)
    grad_first = side_sum(total_term + contract_last(grad_value_low, full_value))
    attn_gain_part = jnp.sum(grad_first * normed_one, axis=0)
    grad_inputs = grad_middle + norm_back(grad_first, normed_one, factor_one, attn_gain)
    gain_parts = (attn_gain_part, ffn_gain_part, query_gain_part, key_gain_part)
    if by_gather:
        in_part = jnp.concatenate([query_part, key_part, value_part], axis=1)
        grad_in = fold_packs(in_part.astype(jnp.bfloat16).reshape(data_count, -1, 3 * local_width))
        grad_w_query, grad_w_key, grad_w_value = (
            grad_in[:, index * local_width : (index + 1) * local_width] for index in range(3)
        )
        by_column = output_part.astype(jnp.bfloat16).reshape(local_width, data_count, -1)
        grad_w_output = fold_packs(by_column.transpose(1, 0, 2))
        late = sum_everywhere(attn_gain_part)
        early = sum_everywhere(jnp.concatenate(gain_parts[1:]))
        splits = (model_width, model_width + head_size)
        gain_sums = (late, *jnp.split(early, splits))
    else:
        grad_w_query, grad_w_key, grad_w_value, grad_w_output = (
            lax.psum_scatter(
                part.astype(jnp.bfloat16), "dp", scatter_dimension=along, tiled=True
            ).astype(jnp.float32)
            for part, along in ((query_part, 0), (key_part, 0), (value_part, 0), (output_part, 1))
        )
        gain_sums = lax.psum(gain_parts, ("dp", "tensor"))
    grad_attn_gain, grad_ffn_gain, grad_query_gain, grad_key_gain = gain_sums
    return (
        outputs,
        grad_inputs,
        grad_attn_gain,
        grad_query_gain,
        grad_key_gain,
        grad_w_query,
        grad_w_key,
        grad_w_value,
        grad_w_output,
        grad_ffn_gain,
        grad_w_gate,
        grad_w_up,
        grad_w_down,
    )


def solution(mesh):
    in_specs = (
        P(("dp", "tensor"), None),
        P("dp", "tensor"),
        P(("dp", "tensor"), None),
        P(("dp", "tensor"), None),
        P(),
        P(),
        P(),
        P("dp", "tensor"),
        P("dp", "tensor"),
        P("dp", "tensor"),
        P("tensor", "dp"),
        P(),
        P("dp", None, "tensor"),
        P("dp", None, "tensor"),
        P("dp", "tensor", None),
        P(("dp", "tensor"), None),
    )
    out_specs = (
        P(("dp", "tensor"), None),
        P(("dp", "tensor"), None),
        P(),
        P(),
        P(),
        P("dp", "tensor"),
        P("dp", "tensor"),
        P("dp", "tensor"),
        P("tensor", "dp"),
        P(),
        P("dp", None, "tensor"),
        P("dp", None, "tensor"),
        P("dp", "tensor", None),
    )
    return jax.shard_map(shards, mesh=mesh, in_specs=in_specs, out_specs=out_specs, check_vma=False)
```

```python
import jax
import jax.numpy as jnp
import functools

from jax import lax
from jax.experimental import pallas as pl
from jax.experimental.pallas import tpu as pltpu
from jax.sharding import PartitionSpec as P

WINDOW = 1024


EPSILON = 1e-06
THETA = 50000.0
NEG_FILL = -1e30


def matmul(left_side, right_side):
    return jnp.dot(left_side, right_side, preferred_element_type=jnp.float32)


def contract_last(left_side, right_side):
    return lax.dot_general(
        left_side, right_side, (((1,), (1,)), ((), ())), preferred_element_type=jnp.float32
    )


def contract_first(left_side, right_side):
    return lax.dot_general(
        left_side, right_side, (((0,), (0,)), ((), ())), preferred_element_type=jnp.float32
    )


def norm_parts(values):
    factor = lax.rsqrt(jnp.mean(values * values, axis=-1, keepdims=True) + EPSILON)
    return (values * factor, factor)


def norm_back(grad_out, normed, factor, gain_vec):
    scaled = grad_out * gain_vec
    return factor * (scaled - normed * jnp.mean(scaled * normed, axis=-1, keepdims=True))


def rope_tables(length, head_size):
    half_size = head_size // 2
    frequency = THETA ** (-(2.0 * jnp.arange(half_size, dtype=jnp.float32)) / head_size)
    angles = jnp.arange(length, dtype=jnp.float32)[:, None] * frequency[None, :]
    return (jnp.cos(angles)[:, None, :], jnp.sin(angles)[:, None, :])


def rotate(values, cosine, sine_tab):
    half_size = values.shape[-1] // 2
    first_half = values[..., :half_size]
    second_half = values[..., half_size:]
    return jnp.concatenate(
        [
            first_half * cosine - second_half * sine_tab,
            second_half * cosine + first_half * sine_tab,
        ],
        axis=-1,
    )


def rotate_back(grads_in, cosine, sine_tab):
    half_size = grads_in.shape[-1] // 2
    first_half = grads_in[..., :half_size]
    second_half = grads_in[..., half_size:]
    return jnp.concatenate(
        [
            first_half * cosine + second_half * sine_tab,
            second_half * cosine - first_half * sine_tab,
        ],
        axis=-1,
    )


def block_mask(segments, offset, block_rows, key_count):
    query_pos = offset + jnp.arange(block_rows)
    key_pos = jnp.arange(key_count)
    same_doc = segments[offset : offset + block_rows][:, None] == segments[None, :]
    near_pos = jnp.abs(query_pos[:, None] - key_pos[None, :]) < WINDOW // 2
    return same_doc & near_pos


def block_scores(query_block, key_low, allowed, inv_root):
    scores = (
        jnp.einsum("qhd,khd->hqk", query_block, key_low, preferred_element_type=jnp.float32)
        * inv_root
    )
    return jnp.where(allowed[None], scores, NEG_FILL)


def row_sum(term_fn, tok_rows):
    return lax.psum_scatter(
        term_fn(jnp.int32(0), lax.axis_size("tensor") * tok_rows),
        "tensor",
        scatter_dimension=0,
        tiled=True,
    )


def gather_rows(values):
    return lax.all_gather(values, "tensor", axis=0, tiled=True)


def from_experts(values):
    return lax.all_to_all(values, "dp", split_axis=1, concat_axis=1, tiled=True)


def to_experts(source_rows, slot_token, slot_gate, layout):
    picked = jnp.take(source_rows, slot_token, axis=0, mode="fill", fill_value=0)
    if slot_gate is not None:
        picked = (picked.astype(jnp.float32) * slot_gate[:, None]).astype(jnp.bfloat16)
    picked = picked.reshape(layout + (picked.shape[1],))
    return lax.all_to_all(picked, "dp", split_axis=1, concat_axis=1, tiled=True)


def pair_sum(table, weights_low, pair_slots, row_count):
    picked = jnp.take(table, pair_slots.reshape(-1), axis=0, mode="fill", fill_value=0)
    picked = picked.reshape(row_count, pair_slots.shape[1], table.shape[1])
    return jnp.einsum("rk,rkd->rd", weights_low, picked, preferred_element_type=jnp.float32)


def expert_forward(operands):
    rows_in, gate_mat, up_mat, down_mat = operands
    flat_rows = rows_in.reshape(-1, rows_in.shape[-1])
    gated = matmul(flat_rows, gate_mat)
    lifted = matmul(flat_rows, up_mat)
    hidden = (jax.nn.silu(gated) * lifted).astype(jnp.bfloat16)
    result = matmul(hidden, down_mat).astype(jnp.bfloat16)
    return (result.reshape(rows_in.shape), gated, lifted)


def expert_backward(operands):
    rows_in, grad_in, gated, lifted, gate_mat, up_mat, down_mat = operands
    flat_rows = rows_in.reshape(-1, rows_in.shape[-1])
    flat_grad = grad_in.reshape(-1, grad_in.shape[-1])
    gate_sig = jax.nn.sigmoid(gated)
    activated = jax.nn.silu(gated)
    hidden = (activated * lifted).astype(jnp.bfloat16)
    grad_hidden = contract_last(flat_grad, down_mat)
    grad_down = contract_first(hidden, flat_grad)
    grad_gated = (grad_hidden * lifted * gate_sig * (1.0 + gated * (1.0 - gate_sig))).astype(
        jnp.bfloat16
    )
    grad_lifted = (grad_hidden * activated).astype(jnp.bfloat16)
    grad_gate = contract_first(flat_rows, grad_gated)
    grad_up = contract_first(flat_rows, grad_lifted)
    grad_rows = (contract_last(grad_gated, gate_mat) + contract_last(grad_lifted, up_mat)).astype(
        jnp.bfloat16
    )
    return (grad_rows.reshape(rows_in.shape), grad_gate, grad_up, grad_down)


VMEM_BYTES = 60 * 1024 * 1024
COLUMN_CHUNK = 512


def select_rows(places_ref, gates_ref, pick_ref, capacity):
    expert_count, seq_len = places_ref.shape[1:]
    slot_range = lax.broadcasted_iota(jnp.int32, (capacity, seq_len), 0)
    for expert in range(expert_count):
        hit = places_ref[0, expert : expert + 1, :] == slot_range
        weight = 1.0 if gates_ref is None else gates_ref[0, expert : expert + 1, :]
        rows = slice(expert * capacity, (expert + 1) * capacity)
        pick_ref[rows, :] = jnp.where(hit, weight, 0.0).astype(jnp.bfloat16)


def spread_rows(places_ref, gates_ref, pick_ref, capacity):
    seq_len, expert_count = places_ref.shape[1:]
    slot_range = lax.broadcasted_iota(jnp.int32, (seq_len, capacity), 1)
    for expert in range(expert_count):
        hit = places_ref[0, :, expert : expert + 1] == slot_range
        weight = 1.0 if gates_ref is None else gates_ref[0, :, expert : expert + 1]
        columns = slice(expert * capacity, (expert + 1) * capacity)
        pick_ref[:, columns] = jnp.where(hit, weight, 0.0).astype(jnp.bfloat16)


def rows_to_slots(pick_ref, rows_ref, slots_ref, pack, capacity):
    width = rows_ref.shape[2]
    expert_count = slots_ref.shape[0]
    for start in range(0, width, COLUMN_CHUNK):
        columns = slice(start, start + COLUMN_CHUNK)
        picked = matmul(pick_ref[...], rows_ref[0, :, columns]).astype(jnp.bfloat16)
        slots_ref[:, pack, :, columns] = picked.reshape(expert_count, capacity, COLUMN_CHUNK)


def slots_to_rows(pick_ref, slots_ref, own_ref, other_ref, pack):
    width = own_ref.shape[3]
    for start in range(0, width, COLUMN_CHUNK):
        columns = slice(start, start + COLUMN_CHUNK)
        slots = slots_ref[:, pack, :, columns].reshape(-1, COLUMN_CHUNK)
        rows = matmul(pick_ref[...], slots).astype(own_ref.dtype)
        rows = rows.reshape(2, 2, own_ref.shape[2], COLUMN_CHUNK)
        own_ref[0, :, :, columns] = rows[:, 0]
        other_ref[0, :, :, columns] = rows[:, 1]


def cot_kernel(
    packs, experts, capacity, table, places, gates, rows, down, slots_out, hidden_out, slots, pick
):
    step = pl.program_id(0)

    @pl.when(step < packs)
    def _():
        select_rows(places, gates, pick, capacity)
        rows_to_slots(pick, rows, slots, step, capacity)

    @pl.when(step >= packs)
    def _():
        block = slots[step - packs].reshape(packs * capacity, -1)
        slots_out[0] = block
        hidden_out[0] = contract_last(block, down[0])


def piece_copies(own, other, rows, sems, pack):
    half_rows = own.shape[1]
    copies = []
    for far in range(2):
        for core, source in enumerate((own, other)):
            for half, index in enumerate((4 * far + pack, 2 + 4 * pack + far)):
                start = ((far * 2 + core) * 2 + half) * half_rows
                copies.append(
                    pltpu.make_async_copy(
                        source.at[index],
                        rows.at[pack, pl.ds(start, half_rows)],
                        sems.at[pack * 8 + len(copies)],
                    )
                )
    return copies


def row_kernel(
    packs, experts, capacity, places, places_t, own, other, gate, up, grad_hidden,
    slots_out, hidden_out, gated_out, lifted_out, rows_own, rows_other,
    rows, slots, grads, pick, spread, sems,
):
    step = pl.program_id(0)

    @pl.when(step == 0)
    def _():
        for pack in range(packs):
            for copy in piece_copies(own, other, rows, sems, pack):
                copy.start()

    for pack in range(packs):

        @pl.when(step == pack)
        def _(pack=pack):
            select_rows(places, None, pick, capacity)
            for copy in piece_copies(own, other, rows, sems, pack):
                copy.wait()
            rows_to_slots(pick, rows.at[pl.ds(pack, 1)], slots, pack, capacity)

    @pl.when((step >= packs) & (step < packs + experts))
    def _():
        expert = step - packs
        block = slots[expert].reshape(packs * capacity, -1)
        slots_out[0] = block
        gated = matmul(block, gate[0])
        lifted = matmul(block, up[0])
        sig = 1.0 / (1.0 + jnp.exp(-gated))
        active = gated * sig
        hidden_out[0] = (active * lifted).astype(jnp.bfloat16)
        above = grad_hidden[0]
        grad_gated = (above * lifted * sig * (1.0 + gated * (1.0 - sig))).astype(jnp.bfloat16)
        grad_lifted = (above * active).astype(jnp.bfloat16)
        gated_out[0] = grad_gated
        lifted_out[0] = grad_lifted
        back = contract_last(grad_gated, gate[0]) + contract_last(grad_lifted, up[0])
        grads[expert] = back.astype(jnp.bfloat16).reshape(packs, capacity, -1)

    @pl.when(step >= packs + experts)
    def _():
        spread_rows(places_t, None, spread, capacity)
        slots_to_rows(spread, grads, rows_own, rows_other, step - packs - experts)


def mix_kernel(
    packs, experts, capacity, places_t, gates_t, hidden, down, rows_own, rows_other, results, spread
):
    step = pl.program_id(0)

    @pl.when(step < experts)
    def _():
        result = matmul(hidden[0], down[0])
        results[step] = result.astype(jnp.bfloat16).reshape(packs, capacity, -1)

    @pl.when(step >= experts)
    def _():
        spread_rows(places_t, gates_t, spread, capacity)
        slots_to_rows(spread, results, rows_own, rows_other, step - experts)


def weight_kernel(planes, *refs):
    slots, grads, hidden, gated, lifted = (refs[i * planes : (i + 1) * planes] for i in range(5))
    gate_out, up_out, down_out = refs[5 * planes :]

    def total(left, right):
        result = contract_first(left[0][0], right[0][0])
        for index in range(1, planes):
            result = result + contract_first(left[index][0], right[index][0])
        return result

    gate_out[0] = total(slots, gated)
    up_out[0] = total(slots, lifted)
    down_out[0] = total(hidden, grads)


def block(shape, place):
    tail = (0,) * (len(shape) - 1)
    return pl.BlockSpec((1,) + tuple(shape[1:]), lambda *ids: (place(*ids),) + tail)


def staged(first, count):
    return lambda step, *rest: jnp.clip(step - first, 0, count - 1)


def shape_of(shape, kind):
    return jax.ShapeDtypeStruct(shape, kind)


def call(kernel, steps, specs, out_specs, out_shape, scratch, flops, prefetch=0):
    return pl.pallas_call(
        kernel,
        grid_spec=pltpu.PrefetchScalarGridSpec(
            num_scalar_prefetch=prefetch,
            grid=(steps,),
            in_specs=specs,
            out_specs=out_specs,
            scratch_shapes=scratch,
        ),
        out_shape=out_shape,
        cost_estimate=pl.CostEstimate(
            flops=flops, transcendentals=0, bytes_accessed=flops // 500
        ),
        compiler_params=pltpu.CompilerParams(
            dimension_semantics=("arbitrary",), vmem_limit_bytes=VMEM_BYTES
        ),
    )


def cot_slots(table, places, gates, rows, down, capacity):
    packs = table.shape[0]
    _, seq_len, width = rows.shape
    experts, hidden_width, _ = down.shape
    slot_rows = packs * capacity
    by_pack, by_expert = staged(0, packs), staged(packs, experts)
    listed = lambda step, numbers: numbers[by_pack(step)]
    out_shape = [
        shape_of((experts, slot_rows, width), jnp.bfloat16),
        shape_of((experts, slot_rows, hidden_width), jnp.float32),
    ]
    return call(
        functools.partial(cot_kernel, packs, experts, capacity),
        packs + experts,
        [
            block(places.shape, listed), block(gates.shape, listed), block(rows.shape, listed),
            block(down.shape, by_expert),
        ],
        [block(out.shape, by_expert) for out in out_shape],
        out_shape,
        [
            pltpu.VMEM((experts, packs, capacity, width), jnp.bfloat16),
            pltpu.VMEM((experts * capacity, seq_len), jnp.bfloat16),
        ],
        2 * experts * slot_rows * width * (seq_len + hidden_width),
        1,
    )(table, places, gates, rows, down)


def row_slots(places, places_t, own, other, gate, up, grad_hidden, capacity):
    packs, _, seq_len = places.shape
    experts, width, hidden_width = gate.shape
    slot_rows = packs * capacity
    first, middle, last = staged(0, packs), staged(packs, experts), staged(packs + experts, packs)
    narrow = shape_of((experts, slot_rows, hidden_width), jnp.bfloat16)
    part = shape_of((packs, 2, seq_len // 4, width), jnp.bfloat16)
    out_shape = [
        shape_of((experts, slot_rows, width), jnp.bfloat16), narrow, narrow, narrow, part, part
    ]
    anywhere = pl.BlockSpec(memory_space=pl.ANY)
    return call(
        functools.partial(row_kernel, packs, experts, capacity),
        2 * packs + experts,
        [
            block(places.shape, first), block(places_t.shape, last), anywhere, anywhere,
            block(gate.shape, middle), block(up.shape, middle), block(grad_hidden.shape, middle),
        ],
        [block(out.shape, middle) for out in out_shape[:4]] + [block(part.shape, last)] * 2,
        out_shape,
        [
            pltpu.VMEM((packs, seq_len, width), jnp.bfloat16),
            pltpu.VMEM((experts, packs, capacity, width), jnp.bfloat16),
            pltpu.VMEM((experts, packs, capacity, width), jnp.bfloat16),
            pltpu.VMEM((experts * capacity, seq_len), jnp.bfloat16),
            pltpu.VMEM((seq_len, experts * capacity), jnp.bfloat16),
            pltpu.SemaphoreType.DMA((8 * packs,)),
        ],
        4 * experts * slot_rows * width * (seq_len + 2 * hidden_width),
    )(places, places_t, own, other, gate, up, grad_hidden)


def mix_rows(places_t, gates_t, hidden, down, capacity):
    packs, seq_len, _ = places_t.shape
    experts, hidden_width, width = down.shape
    first, last = staged(0, experts), staged(experts, packs)
    part = shape_of((packs, 2, seq_len // 4, width), jnp.bfloat16)
    return call(
        functools.partial(mix_kernel, packs, experts, capacity),
        packs + experts,
        [
            block(places_t.shape, last), block(gates_t.shape, last),
            block(hidden.shape, first), block(down.shape, first),
        ],
        [block(part.shape, last)] * 2,
        [part, part],
        [
            pltpu.VMEM((experts, packs, capacity, width), jnp.bfloat16),
            pltpu.VMEM((seq_len, experts * capacity), jnp.bfloat16),
        ],
        2 * experts * packs * capacity * width * (seq_len + hidden_width),
    )(places_t, gates_t, hidden, down)


def weight_grads(slots, grads, hidden, gated, lifted):
    planes = len(slots)
    operands = [*slots, *grads, *hidden, *gated, *lifted]
    experts, _, width = slots[0].shape
    hidden_width = hidden[0].shape[2]
    each = lambda step: step
    out_shape = [
        shape_of((experts, width, hidden_width), jnp.float32),
        shape_of((experts, width, hidden_width), jnp.float32),
        shape_of((experts, hidden_width, width), jnp.float32),
    ]
    return call(
        functools.partial(weight_kernel, planes),
        experts,
        [block(operand.shape, each) for operand in operands],
        [block(out.shape, each) for out in out_shape],
        out_shape,
        [],
        6 * planes * slots[0].shape[1] * experts * width * hidden_width,
    )(*operands)


def swapped(values, axis, bit):
    count = lax.axis_size(axis)
    return lax.ppermute(values, axis, [(i, i ^ bit) for i in range(count)])


def far_side(values):
    return swapped(values, "tensor", 2)


def far_core(values):
    return swapped(values, "tensor", 1)


def far_pack(values):
    return swapped(values, "dp", 1)


def next_plane(values):
    count = lax.axis_size("dp")
    return lax.ppermute(values, "dp", [(i, (i + 2) % count) for i in range(count)])


def spread_plane(values):
    half_rows = values.shape[0] // 2
    upper, lower = values[:half_rows], values[half_rows:]
    near_upper = jnp.stack([upper, far_pack(upper)])
    near_lower = jnp.stack([lower, far_side(lower)])
    own = jnp.concatenate([near_upper, near_lower, far_side(near_upper), far_pack(near_lower)])
    return own, far_core(own)


def plane_order():
    packs = lax.axis_size("dp")
    planes = packs // 2
    index = lax.axis_index("dp")
    return jnp.stack(
        [
            ((index // 2 + planes - plane) % planes) * 2 + (index % 2 ^ near)
            for plane in range(planes)
            for near in range(2)
        ]
    )


def place_kernel(by_column, order, *refs):
    *pieces, whole, sems = refs
    copies = []
    for index, piece in enumerate(pieces):
        target = whole.at[order[index]]
        if by_column:
            width = piece.shape[1]
            target = whole.at[:, pl.ds(pl.multiple_of(order[index] * width, 128), width)]
        copies.append(pltpu.make_async_copy(piece, target, sems.at[index]))
        copies[-1].start()
    for copy in copies:
        copy.wait()


def laid(pieces, order, by_column=False):
    count = len(pieces)
    rows, columns = pieces[0].shape
    shape = (rows, count * columns) if by_column else (count, rows, columns)
    anywhere = pl.BlockSpec(memory_space=pl.ANY)
    return call(
        functools.partial(place_kernel, by_column),
        1,
        [anywhere] * count,
        anywhere,
        shape_of(shape, pieces[0].dtype),
        [pltpu.SemaphoreType.DMA((count,))],
        1000,
        1,
    )(order, *pieces)


def gather_packs(values, by_column=False):
    pieces = []
    for plane in range(lax.axis_size("dp") // 2):
        values = next_plane(values) if plane else values
        pieces += [values, far_pack(values)]
    return laid(pieces, plane_order(), by_column)


def fold_packs(values):
    order = plane_order()
    take = lambda index: lax.dynamic_index_in_dim(values, order[index], 0, keepdims=False)
    near = [added(take(2 * i), far_pack(take(2 * i + 1))) for i in range(values.shape[0] // 2)]
    summed = near[1]
    for part in near[2:]:
        summed = added(next_plane(summed), part)
    return added(next_plane(summed), near[0], jnp.float32)


def gather_sides(values):
    across = far_side(values)
    pieces = [values, far_core(values), across, far_core(across)]
    order = lax.axis_index("tensor") ^ jnp.arange(len(pieces), dtype=jnp.int32)
    return laid(pieces, order).reshape((-1,) + values.shape[1:])


def fold_sides(values):
    split = values.astype(jnp.bfloat16).reshape((4, -1) + values.shape[1:])
    take = lambda bits: lax.dynamic_index_in_dim(
        split, lax.axis_index("tensor") ^ bits, 0, keepdims=False
    )
    far = added(take(2), far_core(take(3)))
    near = added(take(0), far_core(take(1)))
    return added(near, far_side(far), jnp.float32)


def sum_everywhere(values):
    for axis in ("tensor", "dp"):
        bit = 1
        while bit < lax.axis_size(axis):
            values = values + swapped(values, axis, bit)
            bit *= 2
    return values


def added(left, right, kind=jnp.bfloat16):
    return (left.astype(jnp.float32) + right.astype(jnp.float32)).astype(kind)


def fold_first(own, arrived):
    half_rows = own.shape[2] // 2
    upper, lower = slice(None, half_rows), slice(half_rows, None)
    return (
        added(own[:, 0, upper], arrived[:, 0, upper]),
        added(own[0, :, lower], arrived[0, :, lower]),
        added(own[:, 1, upper], arrived[:, 1, upper]),
        added(own[1, :, lower], arrived[1, :, lower]),
    )


def fold_second(upper, lower, upper_far, lower_far):
    upper = added(upper, far_side(upper_far))
    lower = added(lower, far_pack(lower_far))
    return upper[0], lower[0], upper[1], lower[1]


def fold_third(upper, lower, upper_far, lower_far):
    return jnp.concatenate(
        [added(upper, far_pack(upper_far)), added(lower, far_side(lower_far))]
    )


def tied(small, values):
    return lax.optimization_barrier((small, values))


def gather_tables(expert_ids, gate_values, segment_ids):
    top_count = expert_ids.shape[1]
    tables = jnp.concatenate(
        [expert_ids.T.astype(jnp.bfloat16), gate_values.T, segment_ids.astype(jnp.bfloat16)]
    )[None]
    for axis in ("tensor", "dp"):
        bit = 1
        while bit < lax.axis_size(axis):
            tables = jnp.concatenate([tables, swapped(tables, axis, bit)])
            bit *= 2
        if axis == "tensor":
            sides = jnp.arange(tables.shape[0], dtype=jnp.int32) ^ lax.axis_index("tensor")
            segments = jnp.take(tables[:, -1], sides, axis=0).reshape(-1)
    devices = jnp.arange(tables.shape[0], dtype=jnp.int32)
    own = lax.axis_index("dp") * lax.axis_size("tensor") + lax.axis_index("tensor")
    tables = jnp.take(tables, devices ^ own, axis=0)
    all_ids, all_gates = tables[:, :top_count], tables[:, top_count : 2 * top_count]
    return all_ids.astype(jnp.int32), all_gates, segments.astype(jnp.int32)


def routing(all_ids, all_gates, local_experts, capacity):
    packs = lax.axis_size("dp")
    first = lax.axis_index("dp") * local_experts
    wanted = first + jnp.arange(local_experts, dtype=jnp.int32)

    def by_pack(values):
        top_count, tok_rows = values.shape[1:]
        ordered = values.reshape(packs, -1, top_count, tok_rows).transpose(0, 2, 1, 3)
        return ordered.reshape(packs, top_count, -1)

    matches = by_pack(all_ids)[:, :, None, :] == wanted[None, None, :, None]
    pair_gates = by_pack(all_gates).astype(jnp.float32)
    member = jnp.any(matches, axis=1)
    gates = jnp.sum(jnp.where(matches, pair_gates[:, :, None, :], 0.0), axis=1)
    order = jnp.arange(member.shape[2], dtype=jnp.int32)
    earlier = (order[:, None] < order[None, :]).astype(jnp.bfloat16)
    flat = member.reshape(packs * local_experts, -1).astype(jnp.bfloat16)
    before = matmul(flat, earlier).astype(jnp.int32).reshape(member.shape)
    return jnp.where(member & (before < capacity), before, -1), gates


def experts_by_exchange(
    second_in, cotangent, expert_ids, gate_values, w_gate, w_up, w_down, middle, capacity
):
    tok_rows, model_width = second_in.shape
    tensor_count = lax.axis_size("tensor")
    data_count = lax.axis_size("dp")
    local_experts = w_gate.shape[0]
    all_experts = local_experts * data_count
    top_count = expert_ids.shape[1]
    seq_len = tok_rows * tensor_count
    pack_cot, pack_ids, pack_gates = (
        gather_rows(cotangent), gather_rows(expert_ids), gather_rows(gate_values)
    )
    pack_second = gather_rows(second_in)
    expert_range = jnp.arange(all_experts, dtype=jnp.int32)
    matches = pack_ids[:, :, None] == expert_range[None, None, :]
    token_counts = jnp.sum(matches.astype(jnp.float32), axis=1).astype(jnp.bfloat16)
    token_range = jnp.arange(seq_len, dtype=jnp.int32)
    earlier = (token_range[:, None] > token_range[None, :]).astype(jnp.bfloat16)
    before = matmul(earlier, token_counts)
    places = (
        jnp.sum(jnp.where(matches, before[:, None, :], 0.0), axis=2).astype(jnp.int32).reshape(-1)
    )
    flat_ids = pack_ids.reshape(-1)
    owners = flat_ids // local_experts
    local_index = flat_ids % local_experts
    dump_slot = all_experts * capacity
    slot_index = jnp.where(
        places < capacity,
        local_index * (data_count * capacity) + owners * capacity + places,
        dump_slot,
    ).astype(jnp.int32)
    pair_token = jnp.arange(seq_len * top_count) // top_count
    slot_token = (
        jnp.full((dump_slot + 1,), seq_len, jnp.int32).at[slot_index].set(pair_token)[:dump_slot]
    )
    pair_gates = pack_gates.astype(jnp.float32)
    slot_gate = (
        jnp.zeros((dump_slot + 1,), jnp.float32)
        .at[slot_index]
        .set(pair_gates.reshape(-1))[:dump_slot]
    )
    pair_slots = slot_index.reshape(seq_len, top_count)
    layout = (local_experts, data_count, capacity)
    arrived_rows = to_experts(pack_second, slot_token, None, layout)
    expert_out, gated_all, lifted_all = lax.map(
        expert_forward, (arrived_rows, w_gate, w_up, w_down)
    )
    returned = from_experts(expert_out).reshape(-1, model_width)

    def combine_term(offset, row_count):
        return pair_sum(returned, pack_gates, pair_slots, row_count)

    outputs = middle + row_sum(combine_term, tok_rows)
    grad_arrived = to_experts(pack_cot, slot_token, slot_gate, layout)
    grad_rows_all, grad_w_gate, grad_w_up, grad_w_down = lax.map(
        expert_backward, (arrived_rows, grad_arrived, gated_all, lifted_all, w_gate, w_up, w_down)
    )
    returned_grad = from_experts(grad_rows_all).reshape(-1, model_width)
    unit_gates = jnp.ones_like(pack_gates)

    def dispatch_term(offset, row_count):
        return pair_sum(returned_grad, unit_gates, pair_slots, row_count)

    grad_second = row_sum(dispatch_term, tok_rows)
    return outputs, grad_second, grad_w_gate, grad_w_up, grad_w_down


class Folding:
    def __init__(self, order):
        self.order, self.waiting = order, {}
        self.summed, self.count, self.total = None, 0, None

    def begin(self, plane, own, other):
        self.waiting[plane] = (0, (own, far_core(other)))

    def step(self, small):
        made = {}
        for plane, (stage, values) in self.waiting.items():
            if stage < 3:
                made[plane] = (fold_first, fold_second, fold_third)[stage](*values)
        ready = {plane: values for plane, (stage, values) in self.waiting.items() if stage == 3}
        following = self.order[self.count] if self.count < len(self.order) else None
        passed = None
        if following in ready:
            last = self.count + 1 == len(self.order)
            kind = jnp.float32 if last else jnp.bfloat16
            passed = ready[following]
            if self.summed is not None:
                passed = added(next_plane(self.summed), passed, kind)
            del self.waiting[following]
            self.count += 1
            if last:
                self.total = passed
        small, (made, passed) = tied(small, (made, passed))
        for plane, values in made.items():
            self.waiting[plane] = (self.waiting[plane][0] + 1, values)
        if passed is not None:
            self.summed = passed
        return small


def experts_by_gather(second_in, all_cot, places, gates, w_gate, w_up, w_down, capacity):
    packs, local_experts, seq_len = places.shape
    tensor_count = lax.axis_size("tensor")
    planes = packs // 2
    pack_order = plane_order()
    side_index = lax.axis_index("tensor")
    quarter_order = side_index ^ jnp.arange(tensor_count, dtype=jnp.int32)

    def as_met(values):
        split = values.reshape(packs, local_experts, tensor_count, -1)
        split = jnp.take(jnp.take(split, pack_order, axis=0), quarter_order, axis=2)
        return split.reshape(values.shape)

    near_places, near_gates = as_met(places), as_met(gates)
    places_t, gates_t = near_places.transpose(0, 2, 1), near_gates.transpose(0, 2, 1)
    pieces, travelling = [], second_in
    for plane in range(planes):
        travelling = next_plane(travelling) if plane else travelling
        pieces.append(spread_plane(travelling))
    pairs = [slice(plane * 2, plane * 2 + 2) for plane in range(planes)]
    order = [*range(1, planes), 0]
    kept, folding, mixing = {}, Folding(order), Folding(order)
    for plane in range(planes):
        pair = pairs[plane]
        grad_slots, grad_hidden = cot_slots(
            pack_order[pair], places, gates, all_cot, w_down, capacity
        )
        near = folding.step(near_places[pair]) if plane > 1 else near_places[pair]
        slots, hidden, grad_gated, grad_lifted, *part = row_slots(
            near, places_t[pair], *pieces[plane], w_gate, w_up, grad_hidden, capacity
        )
        folding.begin(plane, *part)
        kept[plane] = (slots, grad_slots, hidden, grad_gated, grad_lifted)
    for plane in order:
        near_t = folding.step(places_t[pairs[plane]])
        part = mix_rows(near_t, gates_t[pairs[plane]], kept[plane][2], w_down, capacity)
        mixing.begin(plane, *part)
    while folding.total is None:
        folding.step(pack_order)
    return folding.total, mixing, [kept[plane] for plane in range(planes)]


def shards(
    inputs,
    segment_ids,
    expert_ids,
    gate_values,
    attn_gain,
    query_gain,
    key_gain,
    w_query,
    w_key,
    w_value,
    w_output,
    ffn_gain,
    w_gate,
    w_up,
    w_down,
    cotangent,
):
    tok_rows, model_width = inputs.shape
    head_size = query_gain.shape[0]
    tensor_count = lax.axis_size("tensor")
    data_count = lax.axis_size("dp")
    local_experts = w_gate.shape[0]
    all_experts = local_experts * data_count
    top_count = expert_ids.shape[1]
    seq_len = tok_rows * tensor_count
    capacity = seq_len * top_count // all_experts
    inv_root = head_size ** (-0.5)
    by_gather = (
        seq_len <= local_experts * capacity
        and tensor_count == 4
        and data_count > 2
        and data_count & (data_count - 1) == 0
        and all_experts <= 256
    )
    if by_gather:
        axes = ("dp", "tensor")
        all_ids, all_gates, segments = gather_tables(expert_ids, gate_values, segment_ids)
        all_cot = lax.all_gather(cotangent, axes, axis=0, tiled=True)
        all_cot = all_cot.reshape(data_count, seq_len, model_width)
        places, gates = routing(all_ids, all_gates, local_experts, capacity)
    inputs_f32 = inputs.astype(jnp.float32)
    normed_one, factor_one = norm_parts(inputs_f32)
    first_in = (normed_one * attn_gain).astype(jnp.bfloat16)
    if by_gather:
        side_sum, side_gather = fold_sides, gather_sides
        local_width = w_query.shape[1]
        full_in = gather_packs(jnp.concatenate([w_query, w_key, w_value], axis=1))
        full_in = full_in.reshape(model_width, -1)
        full_query, full_key, full_value = (
            full_in[:, index * local_width : (index + 1) * local_width] for index in range(3)
        )
        full_output = gather_packs(w_output, True)
    else:
        side_sum, side_gather = lambda term: row_sum(lambda *_: term, tok_rows), gather_rows
        segments = lax.all_gather(segment_ids, "tensor", axis=1, tiled=True)[0]
        full_query, full_key, full_value, full_output = (
            lax.all_gather(w_query, "dp", axis=0, tiled=True),
            lax.all_gather(w_key, "dp", axis=0, tiled=True),
            lax.all_gather(w_value, "dp", axis=0, tiled=True),
            lax.all_gather(w_output, "dp", axis=1, tiled=True),
        )
    pack_in = side_gather(first_in)
    query_pre = matmul(pack_in, full_query)
    key_pre = matmul(pack_in, full_key)
    value_low = matmul(pack_in, full_value).astype(jnp.bfloat16)
    head_count = query_pre.shape[1] // head_size
    cosine, sine_tab = rope_tables(seq_len, head_size)
    query_norm, query_factor = norm_parts(query_pre.reshape(seq_len, head_count, head_size))
    key_norm, key_factor = norm_parts(key_pre.reshape(seq_len, head_count, head_size))
    query_low = rotate(query_norm * query_gain, cosine, sine_tab).astype(jnp.bfloat16)
    key_low = rotate(key_norm * key_gain, cosine, sine_tab).astype(jnp.bfloat16)
    value_heads = value_low.reshape(seq_len, head_count, head_size)
    block_rows = min(512, seq_len)
    block_total = seq_len // block_rows
    masks = []
    mixture_parts = []
    lse_parts = []
    for block_index in range(block_total):
        offset = block_index * block_rows
        allowed = block_mask(segments, offset, block_rows, seq_len)
        masks.append(allowed)
        scores = block_scores(query_low[offset : offset + block_rows], key_low, allowed, inv_root)
        top_score = jnp.max(scores, axis=-1, keepdims=True)
        raw_weights = jnp.exp(scores - top_score)
        totals = jnp.sum(raw_weights, axis=-1, keepdims=True)
        weights_low = (raw_weights / totals).astype(jnp.bfloat16)
        mixture_parts.append(
            jnp.einsum(
                "hqk,khd->qhd", weights_low, value_heads, preferred_element_type=jnp.float32
            ).astype(jnp.bfloat16)
        )
        lse_parts.append(top_score + jnp.log(totals))
    mixture = jnp.concatenate(mixture_parts, axis=0).reshape(seq_len, head_count * head_size)

    middle = inputs_f32 + side_sum(matmul(mixture, full_output))
    normed_two, factor_two = norm_parts(middle)
    second_in = (normed_two * ffn_gain).astype(jnp.bfloat16)
    if by_gather:
        grad_second, mixing, kept = experts_by_gather(
            second_in, all_cot, places, gates, w_gate, w_up, w_down, capacity
        )
        mix_step = mixing.step
    else:
        outputs, grad_second, grad_w_gate, grad_w_up, grad_w_down = experts_by_exchange(
            second_in, cotangent, expert_ids, gate_values, w_gate, w_up, w_down, middle, capacity
        )
        mix_step = lambda values: values
    ffn_gain_part = jnp.sum(grad_second * normed_two, axis=0)
    grad_middle = cotangent.astype(jnp.float32) + norm_back(
        grad_second, normed_two, factor_two, ffn_gain
    )
    pack_grad = mix_step(side_gather(grad_middle.astype(jnp.bfloat16)))
    output_part = contract_first(mixture, pack_grad)
    grad_mixture = (
        contract_last(pack_grad, full_output)
        .astype(jnp.bfloat16)
        .reshape(seq_len, head_count, head_size)
    )
    grad_mixture = mix_step(grad_mixture)
    grad_query_parts = []
    grad_key_sum = jnp.zeros((seq_len, head_count, head_size), jnp.float32)
    grad_value_sum = jnp.zeros((seq_len, head_count, head_size), jnp.float32)
    for block_index in range(block_total):
        offset = block_index * block_rows
        query_block = mix_step(query_low[offset : offset + block_rows])
        grad_block = grad_mixture[offset : offset + block_rows]
        scores = block_scores(query_block, key_low, masks[block_index], inv_root)
        prob_rows = jnp.exp(scores - lse_parts[block_index])
        grad_probs = jnp.einsum(
            "qhd,khd->hqk", grad_block, value_heads, preferred_element_type=jnp.float32
        )
        row_delta = jnp.sum(grad_probs * prob_rows, axis=-1, keepdims=True)
        grad_scores = (prob_rows * (grad_probs - row_delta)).astype(jnp.bfloat16)
        grad_query_parts.append(
            jnp.einsum("hqk,khd->qhd", grad_scores, key_low, preferred_element_type=jnp.float32)
            * inv_root
        )
        grad_key_sum = (
            grad_key_sum
            + jnp.einsum(
                "hqk,qhd->khd", grad_scores, query_block, preferred_element_type=jnp.float32
            )
            * inv_root
        )
        grad_value_sum = grad_value_sum + jnp.einsum(
            "hqk,qhd->khd",
            prob_rows.astype(jnp.bfloat16),
            grad_block,
            preferred_element_type=jnp.float32,
        )
    grad_query_norm = rotate_back(jnp.concatenate(grad_query_parts, axis=0), cosine, sine_tab)
    grad_key_norm = rotate_back(grad_key_sum, cosine, sine_tab)
    query_gain_part = jnp.sum(grad_query_norm * query_norm, axis=(0, 1))
    key_gain_part = jnp.sum(grad_key_norm * key_norm, axis=(0, 1))
    grad_query_norm = mix_step(grad_query_norm)
    grad_query_pre = (
        norm_back(grad_query_norm, query_norm, query_factor, query_gain)
        .reshape(seq_len, -1)
        .astype(jnp.bfloat16)
    )
    grad_key_pre = (
        norm_back(grad_key_norm, key_norm, key_factor, key_gain)
        .reshape(seq_len, -1)
        .astype(jnp.bfloat16)
    )
    grad_value_low = grad_value_sum.reshape(seq_len, -1).astype(jnp.bfloat16)
    query_part = contract_first(pack_in, grad_query_pre)
    key_part = contract_first(pack_in, grad_key_pre)
    value_part = contract_first(pack_in, grad_value_low)

    total_term = contract_last(grad_query_pre, full_query)
    total_term = total_term + contract_last(grad_key_pre, full_key)
    grad_first = side_sum(total_term + contract_last(grad_value_low, full_value))
    attn_gain_part = jnp.sum(grad_first * normed_one, axis=0)
    grad_inputs = grad_middle + norm_back(grad_first, normed_one, factor_one, attn_gain)
    gain_parts = (attn_gain_part, ffn_gain_part, query_gain_part, key_gain_part)
    if by_gather:
        in_part = jnp.concatenate([query_part, key_part, value_part], axis=1)
        grad_in = fold_packs(in_part.astype(jnp.bfloat16).reshape(data_count, -1, 3 * local_width))
        grad_w_query, grad_w_key, grad_w_value = (
            grad_in[:, index * local_width : (index + 1) * local_width] for index in range(3)
        )
        by_column = output_part.astype(jnp.bfloat16).reshape(local_width, data_count, -1)
        grad_w_output = fold_packs(by_column.transpose(1, 0, 2))
        kept, _ = lax.optimization_barrier((kept, in_part))
        grad_w_gate, grad_w_up, grad_w_down = weight_grads(*zip(*kept))
        while mixing.total is None:
            mixing.step(attn_gain)
        outputs = middle + mixing.total
        late = sum_everywhere(attn_gain_part)
        early = sum_everywhere(jnp.concatenate(gain_parts[1:]))
        splits = (model_width, model_width + head_size)
        gain_sums = (late, *jnp.split(early, splits))
    else:
        grad_w_query, grad_w_key, grad_w_value, grad_w_output = (
            lax.psum_scatter(
                part.astype(jnp.bfloat16), "dp", scatter_dimension=along, tiled=True
            ).astype(jnp.float32)
            for part, along in ((query_part, 0), (key_part, 0), (value_part, 0), (output_part, 1))
        )
        gain_sums = lax.psum(gain_parts, ("dp", "tensor"))
    grad_attn_gain, grad_ffn_gain, grad_query_gain, grad_key_gain = gain_sums
    return (
        outputs,
        grad_inputs,
        grad_attn_gain,
        grad_query_gain,
        grad_key_gain,
        grad_w_query,
        grad_w_key,
        grad_w_value,
        grad_w_output,
        grad_ffn_gain,
        grad_w_gate,
        grad_w_up,
        grad_w_down,
    )


def solution(mesh):
    in_specs = (
        P(("dp", "tensor"), None),
        P("dp", "tensor"),
        P(("dp", "tensor"), None),
        P(("dp", "tensor"), None),
        P(),
        P(),
        P(),
        P("dp", "tensor"),
        P("dp", "tensor"),
        P("dp", "tensor"),
        P("tensor", "dp"),
        P(),
        P("dp", None, "tensor"),
        P("dp", None, "tensor"),
        P("dp", "tensor", None),
        P(("dp", "tensor"), None),
    )
    out_specs = (
        P(("dp", "tensor"), None),
        P(("dp", "tensor"), None),
        P(),
        P(),
        P(),
        P("dp", "tensor"),
        P("dp", "tensor"),
        P("dp", "tensor"),
        P("tensor", "dp"),
        P(),
        P("dp", None, "tensor"),
        P("dp", None, "tensor"),
        P("dp", "tensor", None),
    )
    return jax.shard_map(shards, mesh=mesh, in_specs=in_specs, out_specs=out_specs, check_vma=False)
```

```python
import jax
import jax.numpy as jnp
import functools

from jax import lax
from jax.experimental import pallas as pl
from jax.experimental.pallas import tpu as pltpu
from jax.sharding import PartitionSpec as P

WINDOW = 1024


EPSILON = 1e-06
THETA = 50000.0
NEG_FILL = -1e30


def matmul(left_side, right_side):
    return jnp.dot(left_side, right_side, preferred_element_type=jnp.float32)


def contract_last(left_side, right_side):
    return lax.dot_general(
        left_side, right_side, (((1,), (1,)), ((), ())), preferred_element_type=jnp.float32
    )


def contract_first(left_side, right_side):
    return lax.dot_general(
        left_side, right_side, (((0,), (0,)), ((), ())), preferred_element_type=jnp.float32
    )


def norm_parts(values):
    factor = lax.rsqrt(jnp.mean(values * values, axis=-1, keepdims=True) + EPSILON)
    return (values * factor, factor)


def norm_back(grad_out, normed, factor, gain_vec):
    scaled = grad_out * gain_vec
    return factor * (scaled - normed * jnp.mean(scaled * normed, axis=-1, keepdims=True))


def rope_tables(length, head_size):
    half_size = head_size // 2
    frequency = THETA ** (-(2.0 * jnp.arange(half_size, dtype=jnp.float32)) / head_size)
    angles = jnp.arange(length, dtype=jnp.float32)[:, None] * frequency[None, :]
    return (jnp.cos(angles)[:, None, :], jnp.sin(angles)[:, None, :])


def rotate(values, cosine, sine_tab):
    half_size = values.shape[-1] // 2
    first_half = values[..., :half_size]
    second_half = values[..., half_size:]
    return jnp.concatenate(
        [
            first_half * cosine - second_half * sine_tab,
            second_half * cosine + first_half * sine_tab,
        ],
        axis=-1,
    )


def rotate_back(grads_in, cosine, sine_tab):
    half_size = grads_in.shape[-1] // 2
    first_half = grads_in[..., :half_size]
    second_half = grads_in[..., half_size:]
    return jnp.concatenate(
        [
            first_half * cosine + second_half * sine_tab,
            second_half * cosine - first_half * sine_tab,
        ],
        axis=-1,
    )


def block_mask(segments, offset, block_rows, key_count):
    query_pos = offset + jnp.arange(block_rows)
    key_pos = jnp.arange(key_count)
    same_doc = segments[offset : offset + block_rows][:, None] == segments[None, :]
    near_pos = jnp.abs(query_pos[:, None] - key_pos[None, :]) < WINDOW // 2
    return same_doc & near_pos


def block_scores(query_block, key_low, allowed, inv_root):
    scores = (
        jnp.einsum("qhd,khd->hqk", query_block, key_low, preferred_element_type=jnp.float32)
        * inv_root
    )
    return jnp.where(allowed[None], scores, NEG_FILL)


def row_sum(term_fn, tok_rows):
    return lax.psum_scatter(
        term_fn(jnp.int32(0), lax.axis_size("tensor") * tok_rows),
        "tensor",
        scatter_dimension=0,
        tiled=True,
    )


def gather_rows(values):
    return lax.all_gather(values, "tensor", axis=0, tiled=True)


def from_experts(values):
    return lax.all_to_all(values, "dp", split_axis=1, concat_axis=1, tiled=True)


def to_experts(source_rows, slot_token, slot_gate, layout):
    picked = jnp.take(source_rows, slot_token, axis=0, mode="fill", fill_value=0)
    if slot_gate is not None:
        picked = (picked.astype(jnp.float32) * slot_gate[:, None]).astype(jnp.bfloat16)
    picked = picked.reshape(layout + (picked.shape[1],))
    return lax.all_to_all(picked, "dp", split_axis=1, concat_axis=1, tiled=True)


def pair_sum(table, weights_low, pair_slots, row_count):
    picked = jnp.take(table, pair_slots.reshape(-1), axis=0, mode="fill", fill_value=0)
    picked = picked.reshape(row_count, pair_slots.shape[1], table.shape[1])
    return jnp.einsum("rk,rkd->rd", weights_low, picked, preferred_element_type=jnp.float32)


def expert_forward(operands):
    rows_in, gate_mat, up_mat, down_mat = operands
    flat_rows = rows_in.reshape(-1, rows_in.shape[-1])
    gated = matmul(flat_rows, gate_mat)
    lifted = matmul(flat_rows, up_mat)
    hidden = (jax.nn.silu(gated) * lifted).astype(jnp.bfloat16)
    result = matmul(hidden, down_mat).astype(jnp.bfloat16)
    return (result.reshape(rows_in.shape), gated, lifted)


def expert_backward(operands):
    rows_in, grad_in, gated, lifted, gate_mat, up_mat, down_mat = operands
    flat_rows = rows_in.reshape(-1, rows_in.shape[-1])
    flat_grad = grad_in.reshape(-1, grad_in.shape[-1])
    gate_sig = jax.nn.sigmoid(gated)
    activated = jax.nn.silu(gated)
    hidden = (activated * lifted).astype(jnp.bfloat16)
    grad_hidden = contract_last(flat_grad, down_mat)
    grad_down = contract_first(hidden, flat_grad)
    grad_gated = (grad_hidden * lifted * gate_sig * (1.0 + gated * (1.0 - gate_sig))).astype(
        jnp.bfloat16
    )
    grad_lifted = (grad_hidden * activated).astype(jnp.bfloat16)
    grad_gate = contract_first(flat_rows, grad_gated)
    grad_up = contract_first(flat_rows, grad_lifted)
    grad_rows = (contract_last(grad_gated, gate_mat) + contract_last(grad_lifted, up_mat)).astype(
        jnp.bfloat16
    )
    return (grad_rows.reshape(rows_in.shape), grad_gate, grad_up, grad_down)


VMEM_BYTES = 60 * 1024 * 1024
COLUMN_CHUNK = 512


def select_rows(places_ref, gates_ref, pick_ref, capacity):
    expert_count, seq_len = places_ref.shape[1:]
    slot_range = lax.broadcasted_iota(jnp.int32, (capacity, seq_len), 0)
    for expert in range(expert_count):
        hit = places_ref[0, expert : expert + 1, :] == slot_range
        weight = 1.0 if gates_ref is None else gates_ref[0, expert : expert + 1, :]
        rows = slice(expert * capacity, (expert + 1) * capacity)
        pick_ref[rows, :] = jnp.where(hit, weight, 0.0).astype(jnp.bfloat16)


def spread_rows(places_ref, gates_ref, pick_ref, capacity):
    seq_len, expert_count = places_ref.shape[1:]
    slot_range = lax.broadcasted_iota(jnp.int32, (seq_len, capacity), 1)
    for expert in range(expert_count):
        hit = places_ref[0, :, expert : expert + 1] == slot_range
        weight = 1.0 if gates_ref is None else gates_ref[0, :, expert : expert + 1]
        columns = slice(expert * capacity, (expert + 1) * capacity)
        pick_ref[:, columns] = jnp.where(hit, weight, 0.0).astype(jnp.bfloat16)


def rows_to_slots(pick_ref, rows_ref, slots_ref, pack, capacity):
    width = rows_ref.shape[2]
    expert_count = slots_ref.shape[0]
    for start in range(0, width, COLUMN_CHUNK):
        columns = slice(start, start + COLUMN_CHUNK)
        picked = matmul(pick_ref[...], rows_ref[0, :, columns]).astype(jnp.bfloat16)
        slots_ref[:, pack, :, columns] = picked.reshape(expert_count, capacity, COLUMN_CHUNK)


def slots_to_rows(pick_ref, slots_ref, own_ref, other_ref, pack):
    width = own_ref.shape[3]
    for start in range(0, width, COLUMN_CHUNK):
        columns = slice(start, start + COLUMN_CHUNK)
        slots = slots_ref[:, pack, :, columns].reshape(-1, COLUMN_CHUNK)
        rows = matmul(pick_ref[...], slots).astype(own_ref.dtype)
        rows = rows.reshape(2, 2, own_ref.shape[2], COLUMN_CHUNK)
        own_ref[0, :, :, columns] = rows[:, 0]
        other_ref[0, :, :, columns] = rows[:, 1]


def cot_kernel(
    packs, experts, capacity, table, places, gates, rows, down, slots_out, hidden_out, slots, pick
):
    step = pl.program_id(0)

    @pl.when(step < packs)
    def _():
        select_rows(places, gates, pick, capacity)
        rows_to_slots(pick, rows, slots, step, capacity)

    @pl.when(step >= packs)
    def _():
        block = slots[step - packs].reshape(packs * capacity, -1)
        slots_out[0] = block
        hidden_out[0] = contract_last(block, down[0])


def piece_copies(own, other, rows, sems, pack):
    half_rows = own.shape[1]
    copies = []
    for far in range(2):
        for core, source in enumerate((own, other)):
            for half, index in enumerate((4 * far + pack, 2 + 4 * pack + far)):
                start = ((far * 2 + core) * 2 + half) * half_rows
                copies.append(
                    pltpu.make_async_copy(
                        source.at[index],
                        rows.at[pack, pl.ds(start, half_rows)],
                        sems.at[pack * 8 + len(copies)],
                    )
                )
    return copies


def row_kernel(
    packs, experts, capacity, places, places_t, own, other, gate, up, grad_hidden,
    slots_out, hidden_out, gated_out, lifted_out, rows_own, rows_other,
    rows, slots, grads, pick, spread, sems,
):
    step = pl.program_id(0)

    @pl.when(step == 0)
    def _():
        for pack in range(packs):
            for copy in piece_copies(own, other, rows, sems, pack):
                copy.start()

    for pack in range(packs):

        @pl.when(step == pack)
        def _(pack=pack):
            select_rows(places, None, pick, capacity)
            for copy in piece_copies(own, other, rows, sems, pack):
                copy.wait()
            rows_to_slots(pick, rows.at[pl.ds(pack, 1)], slots, pack, capacity)

    @pl.when((step >= packs) & (step < packs + experts))
    def _():
        expert = step - packs
        block = slots[expert].reshape(packs * capacity, -1)
        slots_out[0] = block
        gated = matmul(block, gate[0])
        lifted = matmul(block, up[0])
        sig = 1.0 / (1.0 + jnp.exp(-gated))
        active = gated * sig
        hidden_out[0] = (active * lifted).astype(jnp.bfloat16)
        above = grad_hidden[0]
        grad_gated = (above * lifted * sig * (1.0 + gated * (1.0 - sig))).astype(jnp.bfloat16)
        grad_lifted = (above * active).astype(jnp.bfloat16)
        gated_out[0] = grad_gated
        lifted_out[0] = grad_lifted
        back = contract_last(grad_gated, gate[0]) + contract_last(grad_lifted, up[0])
        grads[expert] = back.astype(jnp.bfloat16).reshape(packs, capacity, -1)

    @pl.when(step >= packs + experts)
    def _():
        spread_rows(places_t, None, spread, capacity)
        slots_to_rows(spread, grads, rows_own, rows_other, step - packs - experts)


def mix_kernel(
    packs, experts, capacity, places_t, gates_t, hidden, down, rows_own, rows_other, results, spread
):
    step = pl.program_id(0)

    @pl.when(step < experts)
    def _():
        result = matmul(hidden[0], down[0])
        results[step] = result.astype(jnp.bfloat16).reshape(packs, capacity, -1)

    @pl.when(step >= experts)
    def _():
        spread_rows(places_t, gates_t, spread, capacity)
        slots_to_rows(spread, results, rows_own, rows_other, step - experts)


def weight_kernel(planes, *refs):
    slots, grads, hidden, gated, lifted = (refs[i * planes : (i + 1) * planes] for i in range(5))
    gate_out, up_out, down_out = refs[5 * planes :]

    def total(left, right):
        result = contract_first(left[0][0], right[0][0])
        for index in range(1, planes):
            result = result + contract_first(left[index][0], right[index][0])
        return result

    gate_out[0] = total(slots, gated)
    up_out[0] = total(slots, lifted)
    down_out[0] = total(hidden, grads)


def block(shape, place):
    tail = (0,) * (len(shape) - 1)
    return pl.BlockSpec((1,) + tuple(shape[1:]), lambda *ids: (place(*ids),) + tail)


def staged(first, count):
    return lambda step, *rest: jnp.clip(step - first, 0, count - 1)


def shape_of(shape, kind):
    return jax.ShapeDtypeStruct(shape, kind)


def call(kernel, steps, specs, out_specs, out_shape, scratch, flops, prefetch=0):
    return pl.pallas_call(
        kernel,
        grid_spec=pltpu.PrefetchScalarGridSpec(
            num_scalar_prefetch=prefetch,
            grid=(steps,),
            in_specs=specs,
            out_specs=out_specs,
            scratch_shapes=scratch,
        ),
        out_shape=out_shape,
        cost_estimate=pl.CostEstimate(
            flops=flops, transcendentals=0, bytes_accessed=flops // 500
        ),
        compiler_params=pltpu.CompilerParams(
            dimension_semantics=("arbitrary",), vmem_limit_bytes=VMEM_BYTES
        ),
    )


def cot_slots(table, places, gates, rows, down, capacity):
    packs = table.shape[0]
    _, seq_len, width = rows.shape
    experts, hidden_width, _ = down.shape
    slot_rows = packs * capacity
    by_pack, by_expert = staged(0, packs), staged(packs, experts)
    listed = lambda step, numbers: numbers[by_pack(step)]
    out_shape = [
        shape_of((experts, slot_rows, width), jnp.bfloat16),
        shape_of((experts, slot_rows, hidden_width), jnp.float32),
    ]
    return call(
        functools.partial(cot_kernel, packs, experts, capacity),
        packs + experts,
        [
            block(places.shape, listed), block(gates.shape, listed), block(rows.shape, listed),
            block(down.shape, by_expert),
        ],
        [block(out.shape, by_expert) for out in out_shape],
        out_shape,
        [
            pltpu.VMEM((experts, packs, capacity, width), jnp.bfloat16),
            pltpu.VMEM((experts * capacity, seq_len), jnp.bfloat16),
        ],
        2 * experts * slot_rows * width * (seq_len + hidden_width),
        1,
    )(table, places, gates, rows, down)


def row_slots(places, places_t, own, other, gate, up, grad_hidden, capacity):
    packs, _, seq_len = places.shape
    experts, width, hidden_width = gate.shape
    slot_rows = packs * capacity
    first, middle, last = staged(0, packs), staged(packs, experts), staged(packs + experts, packs)
    narrow = shape_of((experts, slot_rows, hidden_width), jnp.bfloat16)
    part = shape_of((packs, 2, seq_len // 4, width), jnp.bfloat16)
    out_shape = [
        shape_of((experts, slot_rows, width), jnp.bfloat16), narrow, narrow, narrow, part, part
    ]
    anywhere = pl.BlockSpec(memory_space=pl.ANY)
    return call(
        functools.partial(row_kernel, packs, experts, capacity),
        2 * packs + experts,
        [
            block(places.shape, first), block(places_t.shape, last), anywhere, anywhere,
            block(gate.shape, middle), block(up.shape, middle), block(grad_hidden.shape, middle),
        ],
        [block(out.shape, middle) for out in out_shape[:4]] + [block(part.shape, last)] * 2,
        out_shape,
        [
            pltpu.VMEM((packs, seq_len, width), jnp.bfloat16),
            pltpu.VMEM((experts, packs, capacity, width), jnp.bfloat16),
            pltpu.VMEM((experts, packs, capacity, width), jnp.bfloat16),
            pltpu.VMEM((experts * capacity, seq_len), jnp.bfloat16),
            pltpu.VMEM((seq_len, experts * capacity), jnp.bfloat16),
            pltpu.SemaphoreType.DMA((8 * packs,)),
        ],
        4 * experts * slot_rows * width * (seq_len + 2 * hidden_width),
    )(places, places_t, own, other, gate, up, grad_hidden)


def mix_rows(places_t, gates_t, hidden, down, capacity):
    packs, seq_len, _ = places_t.shape
    experts, hidden_width, width = down.shape
    first, last = staged(0, experts), staged(experts, packs)
    part = shape_of((packs, 2, seq_len // 4, width), jnp.bfloat16)
    return call(
        functools.partial(mix_kernel, packs, experts, capacity),
        packs + experts,
        [
            block(places_t.shape, last), block(gates_t.shape, last),
            block(hidden.shape, first), block(down.shape, first),
        ],
        [block(part.shape, last)] * 2,
        [part, part],
        [
            pltpu.VMEM((experts, packs, capacity, width), jnp.bfloat16),
            pltpu.VMEM((seq_len, experts * capacity), jnp.bfloat16),
        ],
        2 * experts * packs * capacity * width * (seq_len + hidden_width),
    )(places_t, gates_t, hidden, down)


def weight_grads(slots, grads, hidden, gated, lifted):
    planes = len(slots)
    operands = [*slots, *grads, *hidden, *gated, *lifted]
    experts, _, width = slots[0].shape
    hidden_width = hidden[0].shape[2]
    each = lambda step: step
    out_shape = [
        shape_of((experts, width, hidden_width), jnp.float32),
        shape_of((experts, width, hidden_width), jnp.float32),
        shape_of((experts, hidden_width, width), jnp.float32),
    ]
    return call(
        functools.partial(weight_kernel, planes),
        experts,
        [block(operand.shape, each) for operand in operands],
        [block(out.shape, each) for out in out_shape],
        out_shape,
        [],
        6 * planes * slots[0].shape[1] * experts * width * hidden_width,
    )(*operands)


def swapped(values, axis, bit):
    count = lax.axis_size(axis)
    return lax.ppermute(values, axis, [(i, i ^ bit) for i in range(count)])


def far_side(values):
    return swapped(values, "tensor", 2)


def far_core(values):
    return swapped(values, "tensor", 1)


def far_pack(values):
    return swapped(values, "dp", 1)


def next_plane(values):
    count = lax.axis_size("dp")
    return lax.ppermute(values, "dp", [(i, (i + 2) % count) for i in range(count)])


def spread_plane(values, beside):
    half_rows = values.shape[0] // 2
    upper, lower = values[:half_rows], values[half_rows:]
    near_upper = jnp.stack([upper, far_pack(upper)])
    near_lower = jnp.stack([lower, far_side(lower)])
    near, made = beside((near_upper, near_lower))
    own = jnp.concatenate([*near, far_side(near[0]), far_pack(near[1])])
    own, made = lax.optimization_barrier((own, made))
    return own, far_core(own), made


def plane_order():
    packs = lax.axis_size("dp")
    planes = packs // 2
    index = lax.axis_index("dp")
    return jnp.stack(
        [
            ((index // 2 + planes - plane) % planes) * 2 + (index % 2 ^ near)
            for plane in range(planes)
            for near in range(2)
        ]
    )


def place_kernel(by_column, order, *refs):
    *pieces, whole, sems = refs
    copies = []
    for index, piece in enumerate(pieces):
        target = None if by_column else whole.at[order[index]]
        if by_column:
            width = piece.shape[1]
            target = whole.at[:, pl.ds(pl.multiple_of(order[index] * width, 128), width)]
        copies.append(pltpu.make_async_copy(piece, target, sems.at[index]))
        copies[-1].start()
    for copy in copies:
        copy.wait()


def laid(pieces, order, by_column=False):
    count = len(pieces)
    rows, columns = pieces[0].shape
    shape = (rows, count * columns) if by_column else (count, rows, columns)
    anywhere = pl.BlockSpec(memory_space=pl.ANY)
    return call(
        functools.partial(place_kernel, by_column),
        1,
        [anywhere] * count,
        pl.BlockSpec(memory_space=pltpu.VMEM),
        shape_of(shape, pieces[0].dtype),
        [pltpu.SemaphoreType.DMA((count,))],
        1000,
        1,
    )(order, *pieces)


def gather_packs(values, by_column=False):
    pieces = []
    for plane in range(lax.axis_size("dp") // 2):
        values = next_plane(values) if plane else values
        pieces += [values, far_pack(values)]
    return laid(pieces, plane_order(), by_column)


def fold_packs(values):
    order = plane_order()
    take = lambda index: lax.dynamic_index_in_dim(values, order[index], 0, keepdims=False)
    near = [added(take(2 * i), far_pack(take(2 * i + 1))) for i in range(values.shape[0] // 2)]
    summed = near[1]
    for part in near[2:]:
        summed = added(next_plane(summed), part)
    return added(next_plane(summed), near[0], jnp.float32)


def gather_sides(values):
    across = far_side(values)
    pieces = [values, far_core(values), across, far_core(across)]
    order = lax.axis_index("tensor") ^ jnp.arange(len(pieces), dtype=jnp.int32)
    return laid(pieces, order).reshape((-1,) + values.shape[1:])


def fold_sides(values):
    split = values.astype(jnp.bfloat16).reshape((4, -1) + values.shape[1:])
    take = lambda bits: lax.dynamic_index_in_dim(
        split, lax.axis_index("tensor") ^ bits, 0, keepdims=False
    )
    far = added(take(2), far_core(take(3)))
    near = added(take(0), far_core(take(1)))
    return added(near, far_side(far), jnp.float32)


def sum_everywhere(values):
    for axis in ("tensor", "dp"):
        bit = 1
        while bit < lax.axis_size(axis):
            values = values + swapped(values, axis, bit)
            bit *= 2
    return values


def added(left, right, kind=jnp.bfloat16):
    return (left.astype(jnp.float32) + right.astype(jnp.float32)).astype(kind)


def fold_first(own, arrived):
    half_rows = own.shape[2] // 2
    upper, lower = slice(None, half_rows), slice(half_rows, None)
    return (
        added(own[:, 0, upper], arrived[:, 0, upper]),
        added(own[0, :, lower], arrived[0, :, lower]),
        added(own[:, 1, upper], arrived[:, 1, upper]),
        added(own[1, :, lower], arrived[1, :, lower]),
    )


def fold_second(upper, lower, upper_far, lower_far):
    upper = added(upper, far_side(upper_far))
    lower = added(lower, far_pack(lower_far))
    return upper[0], lower[0], upper[1], lower[1]


def fold_third(upper, lower, upper_far, lower_far):
    return jnp.concatenate(
        [added(upper, far_pack(upper_far)), added(lower, far_side(lower_far))]
    )


def tied(small, values):
    return lax.optimization_barrier((small, values))


def gather_tables(expert_ids, gate_values, segment_ids):
    top_count = expert_ids.shape[1]
    tables = jnp.concatenate(
        [expert_ids.T.astype(jnp.bfloat16), gate_values.T, segment_ids.astype(jnp.bfloat16)]
    )[None]
    for axis in ("tensor", "dp"):
        bit = 1
        while bit < lax.axis_size(axis):
            tables = jnp.concatenate([tables, swapped(tables, axis, bit)])
            bit *= 2
        if axis == "tensor":
            sides = jnp.arange(tables.shape[0], dtype=jnp.int32) ^ lax.axis_index("tensor")
            segments = jnp.take(tables[:, -1], sides, axis=0).reshape(-1)
    devices = jnp.arange(tables.shape[0], dtype=jnp.int32)
    own = lax.axis_index("dp") * lax.axis_size("tensor") + lax.axis_index("tensor")
    tables = jnp.take(tables, devices ^ own, axis=0)
    all_ids, all_gates = tables[:, :top_count], tables[:, top_count : 2 * top_count]
    return all_ids.astype(jnp.int32), all_gates, segments.astype(jnp.int32)


def routing(all_ids, all_gates, local_experts, capacity):
    packs = lax.axis_size("dp")
    first = lax.axis_index("dp") * local_experts
    wanted = first + jnp.arange(local_experts, dtype=jnp.int32)

    def by_pack(values):
        top_count, tok_rows = values.shape[1:]
        ordered = values.reshape(packs, -1, top_count, tok_rows).transpose(0, 2, 1, 3)
        return ordered.reshape(packs, top_count, -1)

    matches = by_pack(all_ids)[:, :, None, :] == wanted[None, None, :, None]
    pair_gates = by_pack(all_gates).astype(jnp.float32)
    member = jnp.any(matches, axis=1)
    gates = jnp.sum(jnp.where(matches, pair_gates[:, :, None, :], 0.0), axis=1)
    order = jnp.arange(member.shape[2], dtype=jnp.int32)
    earlier = (order[:, None] < order[None, :]).astype(jnp.bfloat16)
    flat = member.reshape(packs * local_experts, -1).astype(jnp.bfloat16)
    before = matmul(flat, earlier).astype(jnp.int32).reshape(member.shape)
    return jnp.where(member & (before < capacity), before, -1), gates


def experts_by_exchange(
    second_in, cotangent, expert_ids, gate_values, w_gate, w_up, w_down, middle, capacity
):
    tok_rows, model_width = second_in.shape
    tensor_count = lax.axis_size("tensor")
    data_count = lax.axis_size("dp")
    local_experts = w_gate.shape[0]
    all_experts = local_experts * data_count
    top_count = expert_ids.shape[1]
    seq_len = tok_rows * tensor_count
    pack_cot, pack_ids, pack_gates = (
        gather_rows(cotangent), gather_rows(expert_ids), gather_rows(gate_values)
    )
    pack_second = gather_rows(second_in)
    expert_range = jnp.arange(all_experts, dtype=jnp.int32)
    matches = pack_ids[:, :, None] == expert_range[None, None, :]
    token_counts = jnp.sum(matches.astype(jnp.float32), axis=1).astype(jnp.bfloat16)
    token_range = jnp.arange(seq_len, dtype=jnp.int32)
    earlier = (token_range[:, None] > token_range[None, :]).astype(jnp.bfloat16)
    before = matmul(earlier, token_counts)
    places = (
        jnp.sum(jnp.where(matches, before[:, None, :], 0.0), axis=2).astype(jnp.int32).reshape(-1)
    )
    flat_ids = pack_ids.reshape(-1)
    owners = flat_ids // local_experts
    local_index = flat_ids % local_experts
    dump_slot = all_experts * capacity
    slot_index = jnp.where(
        places < capacity,
        local_index * (data_count * capacity) + owners * capacity + places,
        dump_slot,
    ).astype(jnp.int32)
    pair_token = jnp.arange(seq_len * top_count) // top_count
    slot_token = (
        jnp.full((dump_slot + 1,), seq_len, jnp.int32).at[slot_index].set(pair_token)[:dump_slot]
    )
    pair_gates = pack_gates.astype(jnp.float32)
    slot_gate = (
        jnp.zeros((dump_slot + 1,), jnp.float32)
        .at[slot_index]
        .set(pair_gates.reshape(-1))[:dump_slot]
    )
    pair_slots = slot_index.reshape(seq_len, top_count)
    layout = (local_experts, data_count, capacity)
    arrived_rows = to_experts(pack_second, slot_token, None, layout)
    expert_out, gated_all, lifted_all = lax.map(
        expert_forward, (arrived_rows, w_gate, w_up, w_down)
    )
    returned = from_experts(expert_out).reshape(-1, model_width)

    def combine_term(offset, row_count):
        return pair_sum(returned, pack_gates, pair_slots, row_count)

    outputs = middle + row_sum(combine_term, tok_rows)
    grad_arrived = to_experts(pack_cot, slot_token, slot_gate, layout)
    grad_rows_all, grad_w_gate, grad_w_up, grad_w_down = lax.map(
        expert_backward, (arrived_rows, grad_arrived, gated_all, lifted_all, w_gate, w_up, w_down)
    )
    returned_grad = from_experts(grad_rows_all).reshape(-1, model_width)
    unit_gates = jnp.ones_like(pack_gates)

    def dispatch_term(offset, row_count):
        return pair_sum(returned_grad, unit_gates, pair_slots, row_count)

    grad_second = row_sum(dispatch_term, tok_rows)
    return outputs, grad_second, grad_w_gate, grad_w_up, grad_w_down


class Folding:
    def __init__(self, order):
        self.order, self.waiting, self.fresh = order, {}, {}
        self.summed, self.count, self.total = None, 0, None

    def begin(self, plane, own, other):
        self.fresh[plane] = (0, (own, far_core(other)))

    def step(self, small):
        made = {}
        for plane, (stage, values) in self.waiting.items():
            if stage < 3:
                made[plane] = (fold_first, fold_second, fold_third)[stage](*values)
        ready = {plane: values for plane, (stage, values) in self.waiting.items() if stage == 3}
        following = self.order[self.count] if self.count < len(self.order) else None
        passed = None
        if following in ready:
            last = self.count + 1 == len(self.order)
            kind = jnp.float32 if last else jnp.bfloat16
            passed = ready[following]
            if self.summed is not None:
                passed = added(next_plane(self.summed), passed, kind)
            del self.waiting[following]
            self.count += 1
            if last:
                self.total = passed
        small, (made, passed) = tied(small, (made, passed))
        self.waiting.update(self.fresh)
        self.fresh = {}
        for plane, values in made.items():
            self.waiting[plane] = (self.waiting[plane][0] + 1, values)
        if passed is not None:
            self.summed = passed
        return small


def experts_by_gather(second_in, all_cot, places, gates, w_gate, w_up, w_down, capacity):
    packs, local_experts, seq_len = places.shape
    tensor_count = lax.axis_size("tensor")
    planes = packs // 2
    pack_order = plane_order()
    side_index = lax.axis_index("tensor")
    quarter_order = side_index ^ jnp.arange(tensor_count, dtype=jnp.int32)

    def as_met(values):
        split = values.reshape(packs, local_experts, tensor_count, -1)
        split = jnp.take(jnp.take(split, pack_order, axis=0), quarter_order, axis=2)
        return split.reshape(values.shape)

    near_places, near_gates = as_met(places), as_met(gates)
    places_t, gates_t = near_places.transpose(0, 2, 1), near_gates.transpose(0, 2, 1)
    pieces, travelling = [], second_in
    for plane in range(planes):
        travelling = next_plane(travelling) if plane else travelling

        def beside(near, listed=pack_order[plane * 2 : plane * 2 + 2]):
            listed, near = tied(listed, near)
            return near, cot_slots(listed, places, gates, all_cot, w_down, capacity)

        pieces.append(spread_plane(travelling, beside))
    pairs = [slice(plane * 2, plane * 2 + 2) for plane in range(planes)]
    order = [*range(1, planes), 0]
    kept, folding, mixing = {}, Folding(order), Folding(order)
    for plane in range(planes):
        pair = pairs[plane]
        own, other, (grad_slots, grad_hidden) = pieces[plane]
        near = folding.step(near_places[pair]) if plane > 1 else near_places[pair]
        slots, hidden, grad_gated, grad_lifted, *part = row_slots(
            near, places_t[pair], own, other, w_gate, w_up, grad_hidden, capacity
        )
        folding.begin(plane, *part)
        kept[plane] = (slots, grad_slots, hidden, grad_gated, grad_lifted)
    for plane in order:
        near_t = folding.step(places_t[pairs[plane]])
        part = mix_rows(near_t, gates_t[pairs[plane]], kept[plane][2], w_down, capacity)
        mixing.begin(plane, *part)
    while folding.total is None:
        folding.step(pack_order)
    return folding.total, mixing, [kept[plane] for plane in range(planes)]


def shards(
    inputs,
    segment_ids,
    expert_ids,
    gate_values,
    attn_gain,
    query_gain,
    key_gain,
    w_query,
    w_key,
    w_value,
    w_output,
    ffn_gain,
    w_gate,
    w_up,
    w_down,
    cotangent,
):
    tok_rows, model_width = inputs.shape
    head_size = query_gain.shape[0]
    tensor_count = lax.axis_size("tensor")
    data_count = lax.axis_size("dp")
    local_experts = w_gate.shape[0]
    all_experts = local_experts * data_count
    top_count = expert_ids.shape[1]
    seq_len = tok_rows * tensor_count
    capacity = seq_len * top_count // all_experts
    inv_root = head_size ** (-0.5)
    by_gather = (
        seq_len <= local_experts * capacity
        and tensor_count == 4
        and data_count > 2
        and data_count & (data_count - 1) == 0
        and all_experts <= 256
    )
    if by_gather:
        axes = ("dp", "tensor")
        all_ids, all_gates, segments = gather_tables(expert_ids, gate_values, segment_ids)
        all_cot = lax.all_gather(cotangent, axes, axis=0, tiled=True)
        all_cot = all_cot.reshape(data_count, seq_len, model_width)
        places, gates = routing(all_ids, all_gates, local_experts, capacity)
    inputs_f32 = inputs.astype(jnp.float32)
    normed_one, factor_one = norm_parts(inputs_f32)
    first_in = (normed_one * attn_gain).astype(jnp.bfloat16)
    if by_gather:
        side_sum, side_gather = fold_sides, gather_sides
        local_width = w_query.shape[1]
        full_in = gather_packs(jnp.concatenate([w_query, w_key, w_value], axis=1))
        full_in = full_in.reshape(model_width, -1)
        full_query, full_key, full_value = (
            full_in[:, index * local_width : (index + 1) * local_width] for index in range(3)
        )
        full_output = gather_packs(w_output, True)
    else:
        side_sum, side_gather = lambda term: row_sum(lambda *_: term, tok_rows), gather_rows
        segments = lax.all_gather(segment_ids, "tensor", axis=1, tiled=True)[0]
        full_query, full_key, full_value, full_output = (
            lax.all_gather(w_query, "dp", axis=0, tiled=True),
            lax.all_gather(w_key, "dp", axis=0, tiled=True),
            lax.all_gather(w_value, "dp", axis=0, tiled=True),
            lax.all_gather(w_output, "dp", axis=1, tiled=True),
        )
    pack_in = side_gather(first_in)
    query_pre = matmul(pack_in, full_query)
    key_pre = matmul(pack_in, full_key)
    value_low = matmul(pack_in, full_value).astype(jnp.bfloat16)
    head_count = query_pre.shape[1] // head_size
    cosine, sine_tab = rope_tables(seq_len, head_size)
    query_norm, query_factor = norm_parts(query_pre.reshape(seq_len, head_count, head_size))
    key_norm, key_factor = norm_parts(key_pre.reshape(seq_len, head_count, head_size))
    query_low = rotate(query_norm * query_gain, cosine, sine_tab).astype(jnp.bfloat16)
    key_low = rotate(key_norm * key_gain, cosine, sine_tab).astype(jnp.bfloat16)
    value_heads = value_low.reshape(seq_len, head_count, head_size)
    block_rows = min(512, seq_len)
    block_total = seq_len // block_rows
    masks = []
    mixture_parts = []
    lse_parts = []
    for block_index in range(block_total):
        offset = block_index * block_rows
        allowed = block_mask(segments, offset, block_rows, seq_len)
        masks.append(allowed)
        scores = block_scores(query_low[offset : offset + block_rows], key_low, allowed, inv_root)
        top_score = jnp.max(scores, axis=-1, keepdims=True)
        raw_weights = jnp.exp(scores - top_score)
        totals = jnp.sum(raw_weights, axis=-1, keepdims=True)
        weights_low = (raw_weights / totals).astype(jnp.bfloat16)
        mixture_parts.append(
            jnp.einsum(
                "hqk,khd->qhd", weights_low, value_heads, preferred_element_type=jnp.float32
            ).astype(jnp.bfloat16)
        )
        lse_parts.append(top_score + jnp.log(totals))
    mixture = jnp.concatenate(mixture_parts, axis=0).reshape(seq_len, head_count * head_size)

    middle = inputs_f32 + side_sum(matmul(mixture, full_output))
    normed_two, factor_two = norm_parts(middle)
    second_in = (normed_two * ffn_gain).astype(jnp.bfloat16)
    if by_gather:
        grad_second, mixing, kept = experts_by_gather(
            second_in, all_cot, places, gates, w_gate, w_up, w_down, capacity
        )
        mix_step = mixing.step
    else:
        outputs, grad_second, grad_w_gate, grad_w_up, grad_w_down = experts_by_exchange(
            second_in, cotangent, expert_ids, gate_values, w_gate, w_up, w_down, middle, capacity
        )
        mix_step = lambda values: values
    ffn_gain_part = jnp.sum(grad_second * normed_two, axis=0)
    grad_middle = cotangent.astype(jnp.float32) + norm_back(
        grad_second, normed_two, factor_two, ffn_gain
    )
    pack_grad = mix_step(side_gather(grad_middle.astype(jnp.bfloat16)))
    output_part = contract_first(mixture, pack_grad)
    grad_mixture = (
        contract_last(pack_grad, full_output)
        .astype(jnp.bfloat16)
        .reshape(seq_len, head_count, head_size)
    )
    grad_query_parts = []
    grad_key_sum = jnp.zeros((seq_len, head_count, head_size), jnp.float32)
    grad_value_sum = jnp.zeros((seq_len, head_count, head_size), jnp.float32)
    for block_index in range(block_total):
        offset = block_index * block_rows
        query_block = query_low[offset : offset + block_rows]
        if block_index:
            query_block = mix_step(query_block)
        grad_block = grad_mixture[offset : offset + block_rows]
        scores = block_scores(query_block, key_low, masks[block_index], inv_root)
        prob_rows = jnp.exp(scores - lse_parts[block_index])
        grad_probs = jnp.einsum(
            "qhd,khd->hqk", grad_block, value_heads, preferred_element_type=jnp.float32
        )
        row_delta = jnp.sum(grad_probs * prob_rows, axis=-1, keepdims=True)
        grad_scores = (prob_rows * (grad_probs - row_delta)).astype(jnp.bfloat16)
        grad_query_parts.append(
            jnp.einsum("hqk,khd->qhd", grad_scores, key_low, preferred_element_type=jnp.float32)
            * inv_root
        )
        grad_key_sum = (
            grad_key_sum
            + jnp.einsum(
                "hqk,qhd->khd", grad_scores, query_block, preferred_element_type=jnp.float32
            )
            * inv_root
        )
        grad_value_sum = grad_value_sum + jnp.einsum(
            "hqk,qhd->khd",
            prob_rows.astype(jnp.bfloat16),
            grad_block,
            preferred_element_type=jnp.float32,
        )
    grad_query_norm = rotate_back(jnp.concatenate(grad_query_parts, axis=0), cosine, sine_tab)
    grad_key_norm = rotate_back(grad_key_sum, cosine, sine_tab)
    query_gain_part = jnp.sum(grad_query_norm * query_norm, axis=(0, 1))
    key_gain_part = jnp.sum(grad_key_norm * key_norm, axis=(0, 1))
    grad_query_norm = mix_step(grad_query_norm)
    grad_query_pre = (
        norm_back(grad_query_norm, query_norm, query_factor, query_gain)
        .reshape(seq_len, -1)
        .astype(jnp.bfloat16)
    )
    grad_key_pre = (
        norm_back(grad_key_norm, key_norm, key_factor, key_gain)
        .reshape(seq_len, -1)
        .astype(jnp.bfloat16)
    )
    grad_value_low = grad_value_sum.reshape(seq_len, -1).astype(jnp.bfloat16)
    query_part = contract_first(pack_in, grad_query_pre)
    key_part = contract_first(pack_in, grad_key_pre)
    value_part = contract_first(pack_in, grad_value_low)

    total_term = contract_last(grad_query_pre, full_query)
    total_term = total_term + contract_last(grad_key_pre, full_key)
    grad_first = side_sum(total_term + contract_last(grad_value_low, full_value))
    attn_gain_part = jnp.sum(grad_first * normed_one, axis=0)
    grad_inputs = grad_middle + norm_back(grad_first, normed_one, factor_one, attn_gain)
    gain_parts = (attn_gain_part, ffn_gain_part, query_gain_part, key_gain_part)
    if by_gather:
        in_part = jnp.concatenate([query_part, key_part, value_part], axis=1)
        grad_in = fold_packs(in_part.astype(jnp.bfloat16).reshape(data_count, -1, 3 * local_width))
        grad_w_query, grad_w_key, grad_w_value = (
            grad_in[:, index * local_width : (index + 1) * local_width] for index in range(3)
        )
        by_column = output_part.astype(jnp.bfloat16).reshape(local_width, data_count, -1)
        grad_w_output = fold_packs(by_column.transpose(1, 0, 2))
        kept, _ = lax.optimization_barrier((kept, in_part))
        grad_w_gate, grad_w_up, grad_w_down = weight_grads(*zip(*kept))
        while mixing.total is None:
            mixing.step(attn_gain)
        outputs = middle + mixing.total
        late = sum_everywhere(attn_gain_part)
        early = sum_everywhere(jnp.concatenate(gain_parts[1:]))
        splits = (model_width, model_width + head_size)
        gain_sums = (late, *jnp.split(early, splits))
    else:
        grad_w_query, grad_w_key, grad_w_value, grad_w_output = (
            lax.psum_scatter(
                part.astype(jnp.bfloat16), "dp", scatter_dimension=along, tiled=True
            ).astype(jnp.float32)
            for part, along in ((query_part, 0), (key_part, 0), (value_part, 0), (output_part, 1))
        )
        gain_sums = lax.psum(gain_parts, ("dp", "tensor"))
    grad_attn_gain, grad_ffn_gain, grad_query_gain, grad_key_gain = gain_sums
    return (
        outputs,
        grad_inputs,
        grad_attn_gain,
        grad_query_gain,
        grad_key_gain,
        grad_w_query,
        grad_w_key,
        grad_w_value,
        grad_w_output,
        grad_ffn_gain,
        grad_w_gate,
        grad_w_up,
        grad_w_down,
    )


def solution(mesh):
    in_specs = (
        P(("dp", "tensor"), None),
        P("dp", "tensor"),
        P(("dp", "tensor"), None),
        P(("dp", "tensor"), None),
        P(),
        P(),
        P(),
        P("dp", "tensor"),
        P("dp", "tensor"),
        P("dp", "tensor"),
        P("tensor", "dp"),
        P(),
        P("dp", None, "tensor"),
        P("dp", None, "tensor"),
        P("dp", "tensor", None),
        P(("dp", "tensor"), None),
    )
    out_specs = (
        P(("dp", "tensor"), None),
        P(("dp", "tensor"), None),
        P(),
        P(),
        P(),
        P("dp", "tensor"),
        P("dp", "tensor"),
        P("dp", "tensor"),
        P("tensor", "dp"),
        P(),
        P("dp", None, "tensor"),
        P("dp", None, "tensor"),
        P("dp", "tensor", None),
    )
    return jax.shard_map(shards, mesh=mesh, in_specs=in_specs, out_specs=out_specs, check_vma=False)
```

```python
import jax
import jax.numpy as jnp
import functools
import math

from jax import lax
from jax.experimental import pallas as pl
from jax.experimental.pallas import tpu as pltpu
from jax.sharding import PartitionSpec as P

WINDOW = 1024


EPSILON = 1e-06
THETA = 50000.0
NEG_FILL = -1e30


def matmul(left_side, right_side):
    return jnp.dot(left_side, right_side, preferred_element_type=jnp.float32)


def contract_last(left_side, right_side):
    return lax.dot_general(
        left_side, right_side, (((1,), (1,)), ((), ())), preferred_element_type=jnp.float32
    )


def contract_first(left_side, right_side):
    return lax.dot_general(
        left_side, right_side, (((0,), (0,)), ((), ())), preferred_element_type=jnp.float32
    )


def norm_parts(values):
    factor = lax.rsqrt(jnp.mean(values * values, axis=-1, keepdims=True) + EPSILON)
    return (values * factor, factor)


def norm_back(grad_out, normed, factor, gain_vec):
    scaled = grad_out * gain_vec
    return factor * (scaled - normed * jnp.mean(scaled * normed, axis=-1, keepdims=True))


def rope_tables(length, head_size):
    half_size = head_size // 2
    frequency = THETA ** (-(2.0 * jnp.arange(half_size, dtype=jnp.float32)) / head_size)
    angles = jnp.arange(length, dtype=jnp.float32)[:, None] * frequency[None, :]
    return (jnp.cos(angles)[:, None, :], jnp.sin(angles)[:, None, :])


def rotate(values, cosine, sine_tab):
    half_size = values.shape[-1] // 2
    first_half = values[..., :half_size]
    second_half = values[..., half_size:]
    return jnp.concatenate(
        [
            first_half * cosine - second_half * sine_tab,
            second_half * cosine + first_half * sine_tab,
        ],
        axis=-1,
    )


def rotate_back(grads_in, cosine, sine_tab):
    half_size = grads_in.shape[-1] // 2
    first_half = grads_in[..., :half_size]
    second_half = grads_in[..., half_size:]
    return jnp.concatenate(
        [
            first_half * cosine + second_half * sine_tab,
            second_half * cosine - first_half * sine_tab,
        ],
        axis=-1,
    )


def block_mask(segments, offset, block_rows, key_count):
    query_pos = offset + jnp.arange(block_rows)
    key_pos = jnp.arange(key_count)
    same_doc = segments[offset : offset + block_rows][:, None] == segments[None, :]
    near_pos = jnp.abs(query_pos[:, None] - key_pos[None, :]) < WINDOW // 2
    return same_doc & near_pos


def block_scores(query_block, key_low, allowed, inv_root):
    scores = (
        jnp.einsum("qhd,khd->hqk", query_block, key_low, preferred_element_type=jnp.float32)
        * inv_root
    )
    return jnp.where(allowed[None], scores, NEG_FILL)


def row_sum(term_fn, tok_rows):
    return lax.psum_scatter(
        term_fn(jnp.int32(0), lax.axis_size("tensor") * tok_rows),
        "tensor",
        scatter_dimension=0,
        tiled=True,
    )


def gather_rows(values):
    return lax.all_gather(values, "tensor", axis=0, tiled=True)


def from_experts(values):
    return lax.all_to_all(values, "dp", split_axis=1, concat_axis=1, tiled=True)


def to_experts(source_rows, slot_token, slot_gate, layout):
    picked = jnp.take(source_rows, slot_token, axis=0, mode="fill", fill_value=0)
    if slot_gate is not None:
        picked = (picked.astype(jnp.float32) * slot_gate[:, None]).astype(jnp.bfloat16)
    picked = picked.reshape(layout + (picked.shape[1],))
    return lax.all_to_all(picked, "dp", split_axis=1, concat_axis=1, tiled=True)


def pair_sum(table, weights_low, pair_slots, row_count):
    picked = jnp.take(table, pair_slots.reshape(-1), axis=0, mode="fill", fill_value=0)
    picked = picked.reshape(row_count, pair_slots.shape[1], table.shape[1])
    return jnp.einsum("rk,rkd->rd", weights_low, picked, preferred_element_type=jnp.float32)


def expert_forward(operands):
    rows_in, gate_mat, up_mat, down_mat = operands
    flat_rows = rows_in.reshape(-1, rows_in.shape[-1])
    gated = matmul(flat_rows, gate_mat)
    lifted = matmul(flat_rows, up_mat)
    hidden = (jax.nn.silu(gated) * lifted).astype(jnp.bfloat16)
    result = matmul(hidden, down_mat).astype(jnp.bfloat16)
    return (result.reshape(rows_in.shape), gated, lifted)


def expert_backward(operands):
    rows_in, grad_in, gated, lifted, gate_mat, up_mat, down_mat = operands
    flat_rows = rows_in.reshape(-1, rows_in.shape[-1])
    flat_grad = grad_in.reshape(-1, grad_in.shape[-1])
    gate_sig = jax.nn.sigmoid(gated)
    activated = jax.nn.silu(gated)
    hidden = (activated * lifted).astype(jnp.bfloat16)
    grad_hidden = contract_last(flat_grad, down_mat)
    grad_down = contract_first(hidden, flat_grad)
    grad_gated = (grad_hidden * lifted * gate_sig * (1.0 + gated * (1.0 - gate_sig))).astype(
        jnp.bfloat16
    )
    grad_lifted = (grad_hidden * activated).astype(jnp.bfloat16)
    grad_gate = contract_first(flat_rows, grad_gated)
    grad_up = contract_first(flat_rows, grad_lifted)
    grad_rows = (contract_last(grad_gated, gate_mat) + contract_last(grad_lifted, up_mat)).astype(
        jnp.bfloat16
    )
    return (grad_rows.reshape(rows_in.shape), grad_gate, grad_up, grad_down)


VMEM_BYTES = 60 * 1024 * 1024
COLUMN_CHUNK = 512
GROUP = 2


def select_rows(places_ref, gates_ref, pick_ref, capacity):
    expert_count, seq_len = places_ref.shape[1:]
    slot_range = lax.broadcasted_iota(jnp.int32, (capacity, seq_len), 0).astype(jnp.bfloat16)
    nothing = jnp.zeros((capacity, seq_len), jnp.bfloat16)
    for expert in range(expert_count):
        hit = places_ref[0, expert : expert + 1, :] == slot_range
        if gates_ref is None:
            weight = jnp.ones((capacity, seq_len), jnp.bfloat16)
        else:
            weight = jnp.broadcast_to(gates_ref[0, expert : expert + 1, :], (capacity, seq_len))
        rows = slice(expert * capacity, (expert + 1) * capacity)
        pick_ref[rows, :] = jnp.where(hit, weight, nothing)


def rows_to_slots(pick_ref, rows_ref, slots_ref, pack, capacity):
    width = rows_ref.shape[2]
    expert_count = slots_ref.shape[0]
    for start in range(0, width, COLUMN_CHUNK):
        columns = slice(start, start + COLUMN_CHUNK)
        picked = matmul(pick_ref[...], rows_ref[0, :, columns]).astype(jnp.bfloat16)
        slots_ref[:, pack, :, columns] = picked.reshape(expert_count, capacity, COLUMN_CHUNK)


def slots_to_rows(pick_ref, slots_ref, own_ref, other_ref, pack):
    width = own_ref.shape[3]
    for start in range(0, width, COLUMN_CHUNK):
        columns = slice(start, start + COLUMN_CHUNK)
        slots = slots_ref[:, pack, :, columns].reshape(-1, COLUMN_CHUNK)
        rows = contract_first(pick_ref[...], slots).astype(own_ref.dtype)
        rows = rows.reshape(2, 2, own_ref.shape[2], COLUMN_CHUNK)
        own_ref[0, :, :, columns] = rows[:, 0]
        other_ref[0, :, :, columns] = rows[:, 1]


def cot_kernel(
    packs, steps, capacity, table, places, gates, rows, down, slots_out, hidden_out, slots, pick
):
    step = pl.program_id(0)

    @pl.when(step < packs)
    def _():
        select_rows(places, gates, pick, capacity)
        rows_to_slots(pick, rows, slots, step, capacity)

    @pl.when(step >= packs)
    def _():
        for member in range(down.shape[0]):
            block = slots[(step - packs) * down.shape[0] + member].reshape(packs * capacity, -1)
            slots_out[member] = block
            hidden_out[member] = contract_last(block, down[member])


def piece_copies(own, other, rows, sems, pack):
    half_rows = own.shape[1]
    copies = []
    for far in range(2):
        for core, source in enumerate((own, other)):
            for half, index in enumerate((4 * far + pack, 2 + 4 * pack + far)):
                start = ((far * 2 + core) * 2 + half) * half_rows
                copies.append(
                    pltpu.make_async_copy(
                        source.at[index],
                        rows.at[pack, pl.ds(start, half_rows)],
                        sems.at[pack * 8 + len(copies)],
                    )
                )
    return copies


def row_kernel(
    packs, steps, capacity, places, own, other, both, grad_hidden,
    slots_out, hidden_out, grads_out, rows_own, rows_other,
    rows, slots, grads, pick, sems,
):
    step = pl.program_id(0)
    half = hidden_out.shape[2]

    @pl.when(step == 0)
    def _():
        for pack in range(packs):
            for copy in piece_copies(own, other, rows, sems, pack):
                copy.start()
        for pack in range(packs):
            select_rows(places.at[pl.ds(pack, 1)], None, pick.at[pack], capacity)

    for pack in range(packs):

        @pl.when(step == pack)
        def _(pack=pack):
            for copy in piece_copies(own, other, rows, sems, pack):
                copy.wait()
            rows_to_slots(pick.at[pack], rows.at[pl.ds(pack, 1)], slots, pack, capacity)

    @pl.when((step >= packs) & (step < packs + steps))
    def _():
        for member in range(both.shape[0]):
            expert = (step - packs) * both.shape[0] + member
            block = slots[expert].reshape(packs * capacity, -1)
            slots_out[member] = block
            product = matmul(block, both[member])
            gated, lifted = product[:, :half], product[:, half:]
            sig = 1.0 / (1.0 + jnp.exp(-gated))
            active = gated * sig
            hidden_out[member] = (active * lifted).astype(jnp.bfloat16)
            above = grad_hidden[member]
            grad_gated = above * lifted * sig * (1.0 + gated * (1.0 - sig))
            joined = jnp.concatenate([grad_gated, above * active], axis=1).astype(jnp.bfloat16)
            grads_out[member] = joined
            back = contract_last(joined, both[member])
            grads[expert] = back.astype(jnp.bfloat16).reshape(packs, capacity, -1)

    for pack in range(packs):

        @pl.when(step == packs + steps + pack)
        def _(pack=pack):
            slots_to_rows(pick.at[pack], grads, rows_own, rows_other, pack)


def mix_kernel(packs, steps, capacity, places, gates, hidden, down, rows_own, rows_other, results, pick):
    step = pl.program_id(0)

    @pl.when(step < steps)
    def _():
        for member in range(down.shape[0]):
            result = matmul(hidden[member], down[member]).astype(jnp.bfloat16)
            results[step * down.shape[0] + member] = result.reshape(packs, capacity, -1)

    @pl.when(step >= steps)
    def _():
        select_rows(places, gates, pick, capacity)
        slots_to_rows(pick, results, rows_own, rows_other, step - steps)


def weight_kernel(planes, *refs):
    slots, grads, hidden, above = (
        jnp.concatenate([ref[0] for ref in refs[i * planes : (i + 1) * planes]]) for i in range(4)
    )
    gate_out, up_out, down_out = refs[-3:]
    half = gate_out.shape[2]
    both = contract_first(slots, above)
    gate_out[0] = both[:, :half]
    up_out[0] = both[:, half:]
    down_out[0] = contract_first(hidden, grads)


def block(shape, place, count=1):
    tail = (0,) * (len(shape) - 1)
    return pl.BlockSpec((count,) + tuple(shape[1:]), lambda *ids: (place(*ids),) + tail)


def staged(first, count):
    return lambda step, *rest: jnp.clip(step - first, 0, count - 1)


def shape_of(shape, kind):
    return jax.ShapeDtypeStruct(shape, kind)


def call(kernel, steps, specs, out_specs, out_shape, scratch, flops, prefetch=0, aliases={}):
    return pl.pallas_call(
        kernel,
        grid_spec=pltpu.PrefetchScalarGridSpec(
            num_scalar_prefetch=prefetch,
            grid=(steps,),
            in_specs=specs,
            out_specs=out_specs,
            scratch_shapes=scratch,
        ),
        out_shape=out_shape,
        input_output_aliases=aliases,
        cost_estimate=pl.CostEstimate(
            flops=flops, transcendentals=0, bytes_accessed=flops // 500
        ),
        compiler_params=pltpu.CompilerParams(
            dimension_semantics=("arbitrary",), vmem_limit_bytes=VMEM_BYTES
        ),
    )


def cot_slots(table, places, gates, rows, down, capacity):
    packs = table.shape[0]
    _, seq_len, width = rows.shape
    experts, hidden_width, _ = down.shape
    slot_rows = packs * capacity
    group = math.gcd(experts, GROUP)
    steps = experts // group
    by_pack, by_expert = staged(0, packs), staged(packs, steps)
    listed = lambda step, numbers: numbers[by_pack(step)]
    out_shape = [
        shape_of((experts, slot_rows, width), jnp.bfloat16),
        shape_of((experts, slot_rows, hidden_width), jnp.float32),
    ]
    return call(
        functools.partial(cot_kernel, packs, steps, capacity),
        packs + steps,
        [
            block(places.shape, listed), block(gates.shape, listed), block(rows.shape, listed),
            block(down.shape, by_expert, group),
        ],
        [block(out.shape, by_expert, group) for out in out_shape],
        out_shape,
        [
            pltpu.VMEM((experts, packs, capacity, width), jnp.bfloat16),
            pltpu.VMEM((experts * capacity, seq_len), jnp.bfloat16),
        ],
        2 * experts * slot_rows * width * (seq_len + hidden_width),
        1,
    )(table, places, gates, rows, down)


def row_slots(places, own, other, both, grad_hidden, capacity):
    packs, _, seq_len = places.shape
    experts, width, hidden_width = both.shape
    slot_rows = packs * capacity
    group = math.gcd(experts, GROUP)
    steps = experts // group
    middle, last = staged(packs, steps), staged(packs + steps, packs)
    part = shape_of((packs, 2, seq_len // 4, width), jnp.bfloat16)
    out_shape = [
        shape_of((experts, slot_rows, width), jnp.bfloat16),
        shape_of((experts, slot_rows, hidden_width // 2), jnp.bfloat16),
        shape_of((experts, slot_rows, hidden_width), jnp.bfloat16),
        part, part,
    ]
    anywhere = pl.BlockSpec(memory_space=pl.ANY)
    return call(
        functools.partial(row_kernel, packs, steps, capacity),
        2 * packs + steps,
        [
            block(places.shape, lambda step: 0, packs), anywhere, anywhere,
            block(both.shape, middle, group), block(grad_hidden.shape, middle, group),
        ],
        [block(out.shape, middle, group) for out in out_shape[:3]] + [block(part.shape, last)] * 2,
        out_shape,
        [
            pltpu.VMEM((packs, seq_len, width), jnp.bfloat16),
            pltpu.VMEM((experts, packs, capacity, width), jnp.bfloat16),
            pltpu.VMEM((experts, packs, capacity, width), jnp.bfloat16),
            pltpu.VMEM((packs, experts * capacity, seq_len), jnp.bfloat16),
            pltpu.SemaphoreType.DMA((8 * packs,)),
        ],
        4 * experts * slot_rows * width * (seq_len + hidden_width),
    )(places, own, other, both, grad_hidden)


def mix_rows(places, gates, hidden, down, capacity):
    packs, _, seq_len = places.shape
    experts, hidden_width, width = down.shape
    group = math.gcd(experts, GROUP)
    steps = experts // group
    first, last = staged(0, steps), staged(steps, packs)
    part = shape_of((packs, 2, seq_len // 4, width), jnp.bfloat16)
    return call(
        functools.partial(mix_kernel, packs, steps, capacity),
        packs + steps,
        [
            block(places.shape, last), block(gates.shape, last),
            block(hidden.shape, first, group), block(down.shape, first, group),
        ],
        [block(part.shape, last)] * 2,
        [part, part],
        [
            pltpu.VMEM((experts, packs, capacity, width), jnp.bfloat16),
            pltpu.VMEM((experts * capacity, seq_len), jnp.bfloat16),
        ],
        2 * experts * packs * capacity * width * (seq_len + hidden_width),
    )(places, gates, hidden, down)


def weight_grads(first, count, slots, grads, hidden, above, earlier=()):
    planes = len(slots)
    operands = [*slots, *grads, *hidden, *above]
    experts, _, width = slots[0].shape
    hidden_width = hidden[0].shape[2]
    each = lambda step: step + first
    out_shape = [
        shape_of((experts, width, hidden_width), jnp.float32),
        shape_of((experts, width, hidden_width), jnp.float32),
        shape_of((experts, hidden_width, width), jnp.float32),
    ]
    return call(
        functools.partial(weight_kernel, planes),
        count,
        [block(operand.shape, each) for operand in operands]
        + [pl.BlockSpec(memory_space=pl.ANY)] * len(earlier),
        [block(out.shape, each) for out in out_shape],
        out_shape,
        [],
        6 * planes * slots[0].shape[1] * count * width * hidden_width,
        aliases={len(operands) + index: index for index in range(len(earlier))},
    )(*operands, *earlier)


def swapped(values, axis, bit):
    count = lax.axis_size(axis)
    return lax.ppermute(values, axis, [(i, i ^ bit) for i in range(count)])


def far_side(values):
    return swapped(values, "tensor", 2)


def far_core(values):
    return swapped(values, "tensor", 1)


def far_pack(values):
    return swapped(values, "dp", 1)


def next_plane(values):
    count = lax.axis_size("dp")
    return lax.ppermute(values, "dp", [(i, (i + 2) % count) for i in range(count)])


def spread_plane(values, beside):
    half_rows = values.shape[0] // 2
    upper, lower = values[:half_rows], values[half_rows:]
    near_upper = jnp.stack([upper, far_pack(upper)])
    near_lower = jnp.stack([lower, far_side(lower)])
    near, made = beside((near_upper, near_lower))
    own = jnp.concatenate([*near, far_side(near[0]), far_pack(near[1])])
    own, made = lax.optimization_barrier((own, made))
    return own, far_core(own), made


def plane_order():
    packs = lax.axis_size("dp")
    planes = packs // 2
    index = lax.axis_index("dp")
    return jnp.stack(
        [
            ((index // 2 + planes - plane) % planes) * 2 + (index % 2 ^ near)
            for plane in range(planes)
            for near in range(2)
        ]
    )


def place_kernel(by_column, order, *refs):
    *pieces, whole, sems = refs
    copies = []
    for index, piece in enumerate(pieces):
        target = None if by_column else whole.at[order[index]]
        if by_column:
            width = piece.shape[1]
            target = whole.at[:, pl.ds(pl.multiple_of(order[index] * width, 128), width)]
        copies.append(pltpu.make_async_copy(piece, target, sems.at[index]))
        copies[-1].start()
    for copy in copies:
        copy.wait()


def laid(pieces, order, by_column=False):
    count = len(pieces)
    rows, columns = pieces[0].shape
    shape = (rows, count * columns) if by_column else (count, rows, columns)
    anywhere = pl.BlockSpec(memory_space=pl.ANY)
    return call(
        functools.partial(place_kernel, by_column),
        1,
        [anywhere] * count,
        pl.BlockSpec(memory_space=pltpu.VMEM),
        shape_of(shape, pieces[0].dtype),
        [pltpu.SemaphoreType.DMA((count,))],
        1000,
        1,
    )(order, *pieces)


def gather_packs(values, by_column=False):
    pieces = []
    for plane in range(lax.axis_size("dp") // 2):
        values = next_plane(values) if plane else values
        pieces += [values, far_pack(values)]
    return laid(pieces, plane_order(), by_column)


def fold_packs(values):
    order = plane_order()
    take = lambda index: lax.dynamic_index_in_dim(values, order[index], 0, keepdims=False)
    near = [added(take(2 * i), far_pack(take(2 * i + 1))) for i in range(values.shape[0] // 2)]
    summed = near[1]
    for part in near[2:]:
        summed = added(next_plane(summed), part)
    return added(next_plane(summed), near[0], jnp.float32)


def gather_sides(values):
    across = far_side(values)
    pieces = [values, far_core(values), across, far_core(across)]
    order = lax.axis_index("tensor") ^ jnp.arange(len(pieces), dtype=jnp.int32)
    return laid(pieces, order).reshape((-1,) + values.shape[1:])


def fold_sides(values):
    split = values.astype(jnp.bfloat16).reshape((4, -1) + values.shape[1:])
    take = lambda bits: lax.dynamic_index_in_dim(
        split, lax.axis_index("tensor") ^ bits, 0, keepdims=False
    )
    far = added(take(2), far_core(take(3)))
    near = added(take(0), far_core(take(1)))
    return added(near, far_side(far), jnp.float32)


def sum_everywhere(values):
    for axis in ("tensor", "dp"):
        bit = 1
        while bit < lax.axis_size(axis):
            values = values + swapped(values, axis, bit)
            bit *= 2
    return values


def added(left, right, kind=jnp.bfloat16):
    return (left.astype(jnp.float32) + right.astype(jnp.float32)).astype(kind)


def fold_first(own, arrived):
    half_rows = own.shape[2] // 2
    upper, lower = slice(None, half_rows), slice(half_rows, None)
    return (
        added(own[:, 0, upper], arrived[:, 0, upper]),
        added(own[0, :, lower], arrived[0, :, lower]),
        added(own[:, 1, upper], arrived[:, 1, upper]),
        added(own[1, :, lower], arrived[1, :, lower]),
    )


def fold_second(upper, lower, upper_far, lower_far):
    upper = added(upper, far_side(upper_far))
    lower = added(lower, far_pack(lower_far))
    return upper[0], lower[0], upper[1], lower[1]


def fold_third(upper, lower, upper_far, lower_far):
    return jnp.concatenate(
        [added(upper, far_pack(upper_far)), added(lower, far_side(lower_far))]
    )


def tied(small, values):
    return lax.optimization_barrier((small, values))


def gather_tables(expert_ids, gate_values, segment_ids):
    top_count = expert_ids.shape[1]
    tables = jnp.concatenate(
        [expert_ids.T.astype(jnp.bfloat16), gate_values.T, segment_ids.astype(jnp.bfloat16)]
    )[None]
    for axis in ("tensor", "dp"):
        bit = 1
        while bit < lax.axis_size(axis):
            tables = jnp.concatenate([tables, swapped(tables, axis, bit)])
            bit *= 2
        if axis == "tensor":
            sides = jnp.arange(tables.shape[0], dtype=jnp.int32) ^ lax.axis_index("tensor")
            segments = jnp.take(tables[:, -1], sides, axis=0).reshape(-1)
    devices = jnp.arange(tables.shape[0], dtype=jnp.int32)
    own = lax.axis_index("dp") * lax.axis_size("tensor") + lax.axis_index("tensor")
    tables = jnp.take(tables, devices ^ own, axis=0)
    all_ids, all_gates = tables[:, :top_count], tables[:, top_count : 2 * top_count]
    return all_ids.astype(jnp.int32), all_gates, segments.astype(jnp.int32)


def routing(all_ids, all_gates, local_experts, capacity):
    packs = lax.axis_size("dp")
    first = lax.axis_index("dp") * local_experts
    wanted = first + jnp.arange(local_experts, dtype=jnp.int32)

    def by_pack(values):
        top_count, tok_rows = values.shape[1:]
        ordered = values.reshape(packs, -1, top_count, tok_rows).transpose(0, 2, 1, 3)
        return ordered.reshape(packs, top_count, -1)

    matches = by_pack(all_ids)[:, :, None, :] == wanted[None, None, :, None]
    pair_gates = by_pack(all_gates).astype(jnp.float32)
    member = jnp.any(matches, axis=1)
    gates = jnp.sum(jnp.where(matches, pair_gates[:, :, None, :], 0.0), axis=1)
    order = jnp.arange(member.shape[2], dtype=jnp.int32)
    earlier = (order[:, None] < order[None, :]).astype(jnp.bfloat16)
    flat = member.reshape(packs * local_experts, -1).astype(jnp.bfloat16)
    before = matmul(flat, earlier).astype(jnp.int32).reshape(member.shape)
    places = jnp.where(member & (before < capacity), before, -1)
    return places.astype(jnp.bfloat16), gates.astype(jnp.bfloat16)


def experts_by_exchange(
    second_in, cotangent, expert_ids, gate_values, w_gate, w_up, w_down, middle, capacity
):
    tok_rows, model_width = second_in.shape
    tensor_count = lax.axis_size("tensor")
    data_count = lax.axis_size("dp")
    local_experts = w_gate.shape[0]
    all_experts = local_experts * data_count
    top_count = expert_ids.shape[1]
    seq_len = tok_rows * tensor_count
    pack_cot, pack_ids, pack_gates = (
        gather_rows(cotangent), gather_rows(expert_ids), gather_rows(gate_values)
    )
    pack_second = gather_rows(second_in)
    expert_range = jnp.arange(all_experts, dtype=jnp.int32)
    matches = pack_ids[:, :, None] == expert_range[None, None, :]
    token_counts = jnp.sum(matches.astype(jnp.float32), axis=1).astype(jnp.bfloat16)
    token_range = jnp.arange(seq_len, dtype=jnp.int32)
    earlier = (token_range[:, None] > token_range[None, :]).astype(jnp.bfloat16)
    before = matmul(earlier, token_counts)
    places = (
        jnp.sum(jnp.where(matches, before[:, None, :], 0.0), axis=2).astype(jnp.int32).reshape(-1)
    )
    flat_ids = pack_ids.reshape(-1)
    owners = flat_ids // local_experts
    local_index = flat_ids % local_experts
    dump_slot = all_experts * capacity
    slot_index = jnp.where(
        places < capacity,
        local_index * (data_count * capacity) + owners * capacity + places,
        dump_slot,
    ).astype(jnp.int32)
    pair_token = jnp.arange(seq_len * top_count) // top_count
    slot_token = (
        jnp.full((dump_slot + 1,), seq_len, jnp.int32).at[slot_index].set(pair_token)[:dump_slot]
    )
    pair_gates = pack_gates.astype(jnp.float32)
    slot_gate = (
        jnp.zeros((dump_slot + 1,), jnp.float32)
        .at[slot_index]
        .set(pair_gates.reshape(-1))[:dump_slot]
    )
    pair_slots = slot_index.reshape(seq_len, top_count)
    layout = (local_experts, data_count, capacity)
    arrived_rows = to_experts(pack_second, slot_token, None, layout)
    expert_out, gated_all, lifted_all = lax.map(
        expert_forward, (arrived_rows, w_gate, w_up, w_down)
    )
    returned = from_experts(expert_out).reshape(-1, model_width)

    def combine_term(offset, row_count):
        return pair_sum(returned, pack_gates, pair_slots, row_count)

    outputs = middle + row_sum(combine_term, tok_rows)
    grad_arrived = to_experts(pack_cot, slot_token, slot_gate, layout)
    grad_rows_all, grad_w_gate, grad_w_up, grad_w_down = lax.map(
        expert_backward, (arrived_rows, grad_arrived, gated_all, lifted_all, w_gate, w_up, w_down)
    )
    returned_grad = from_experts(grad_rows_all).reshape(-1, model_width)
    unit_gates = jnp.ones_like(pack_gates)

    def dispatch_term(offset, row_count):
        return pair_sum(returned_grad, unit_gates, pair_slots, row_count)

    grad_second = row_sum(dispatch_term, tok_rows)
    return outputs, grad_second, grad_w_gate, grad_w_up, grad_w_down


class Folding:
    def __init__(self, order):
        self.order, self.waiting, self.fresh = order, {}, {}
        self.summed, self.count = None, 0

    def begin(self, plane, own, other):
        self.fresh[plane] = (0, (own, far_core(other)))

    def step(self, small):
        made = {}
        for plane, (stage, values) in self.waiting.items():
            if stage < 3:
                made[plane] = (fold_first, fold_second, fold_third)[stage](*values)
        ready = {plane: values for plane, (stage, values) in self.waiting.items() if stage == 3}
        passed = None
        if self.order[self.count] in ready:
            passed = self.passed_on(ready[self.order[self.count]])
            del self.waiting[self.order[self.count]]
            self.count += 1
        small, (made, passed) = tied(small, (made, passed))
        self.waiting.update(self.fresh)
        self.fresh = {}
        for plane, values in made.items():
            self.waiting[plane] = (self.waiting[plane][0] + 1, values)
        if passed is not None:
            self.summed = passed
        return small

    def passed_on(self, values):
        kind = jnp.float32 if self.count + 1 == len(self.order) else jnp.bfloat16
        return values if self.summed is None else added(next_plane(self.summed), values, kind)

    def finish(self):
        self.waiting.update(self.fresh)
        for plane in self.order[self.count :]:
            stage, values = self.waiting[plane]
            for fold in (fold_first, fold_second, fold_third)[stage:]:
                values = fold(*values)
            self.summed = self.passed_on(values)
            self.count += 1
        return self.summed


def experts_by_gather(second_in, all_cot, places, gates, w_gate, w_up, w_down, capacity):
    packs, local_experts, seq_len = places.shape
    tensor_count = lax.axis_size("tensor")
    planes = packs // 2
    pack_order = plane_order()
    side_index = lax.axis_index("tensor")
    quarter_order = side_index ^ jnp.arange(tensor_count, dtype=jnp.int32)

    def as_met(values):
        split = values.reshape(packs, local_experts, tensor_count, -1)
        split = jnp.take(jnp.take(split, pack_order, axis=0), quarter_order, axis=2)
        return split.reshape(values.shape)

    near_places, near_gates = as_met(places), as_met(gates)
    w_both = jnp.concatenate([w_gate, w_up], axis=2)
    pieces, travelling = [], second_in
    for plane in range(planes):
        travelling = next_plane(travelling) if plane else travelling

        def beside(near, listed=pack_order[plane * 2 : plane * 2 + 2]):
            listed, near = tied(listed, near)
            return near, cot_slots(listed, places, gates, all_cot, w_down, capacity)

        pieces.append(spread_plane(travelling, beside))
    pairs = [slice(plane * 2, plane * 2 + 2) for plane in range(planes)]
    order = [*range(1, planes), 0]
    kept, folding, mixing = {}, Folding(order), Folding(order)
    for plane in range(planes):
        pair = pairs[plane]
        own, other, (grad_slots, grad_hidden) = pieces[plane]
        near = folding.step(near_places[pair]) if plane else near_places[pair]
        slots, hidden, above, *part = row_slots(near, own, other, w_both, grad_hidden, capacity)
        folding.begin(plane, *part)
        kept[plane] = (slots, grad_slots, hidden, above)
    for plane in order:
        near = folding.step(near_places[pairs[plane]])
        part = mix_rows(near, near_gates[pairs[plane]], kept[plane][2], w_down, capacity)
        mixing.begin(plane, *part)
    return folding.finish(), mixing, [kept[plane] for plane in range(planes)]


def shards(
    inputs,
    segment_ids,
    expert_ids,
    gate_values,
    attn_gain,
    query_gain,
    key_gain,
    w_query,
    w_key,
    w_value,
    w_output,
    ffn_gain,
    w_gate,
    w_up,
    w_down,
    cotangent,
):
    tok_rows, model_width = inputs.shape
    head_size = query_gain.shape[0]
    tensor_count = lax.axis_size("tensor")
    data_count = lax.axis_size("dp")
    local_experts = w_gate.shape[0]
    all_experts = local_experts * data_count
    top_count = expert_ids.shape[1]
    seq_len = tok_rows * tensor_count
    capacity = seq_len * top_count // all_experts
    inv_root = head_size ** (-0.5)
    by_gather = (
        seq_len <= local_experts * capacity
        and tensor_count == 4
        and data_count > 2
        and data_count & (data_count - 1) == 0
        and all_experts <= 256
    )
    if by_gather:
        axes = ("dp", "tensor")
        all_ids, all_gates, segments = gather_tables(expert_ids, gate_values, segment_ids)
        places, gates = routing(all_ids, all_gates, local_experts, capacity)
    inputs_f32 = inputs.astype(jnp.float32)
    normed_one, factor_one = norm_parts(inputs_f32)
    first_in = (normed_one * attn_gain).astype(jnp.bfloat16)
    if by_gather:
        side_sum, side_gather = fold_sides, gather_sides
        local_width = w_query.shape[1]
        full_in = gather_packs(jnp.concatenate([w_query, w_key, w_value], axis=1))
        full_in, cotangent = tied(full_in, cotangent)
        all_cot = lax.all_gather(cotangent, axes, axis=0, tiled=True)
        all_cot = all_cot.reshape(data_count, seq_len, model_width)
        full_in = full_in.reshape(model_width, -1)
        full_query, full_key, full_value = (
            full_in[:, index * local_width : (index + 1) * local_width] for index in range(3)
        )
        full_output = gather_packs(w_output, True)
    else:
        side_sum, side_gather = lambda term: row_sum(lambda *_: term, tok_rows), gather_rows
        segments = lax.all_gather(segment_ids, "tensor", axis=1, tiled=True)[0]
        full_query, full_key, full_value, full_output = (
            lax.all_gather(w_query, "dp", axis=0, tiled=True),
            lax.all_gather(w_key, "dp", axis=0, tiled=True),
            lax.all_gather(w_value, "dp", axis=0, tiled=True),
            lax.all_gather(w_output, "dp", axis=1, tiled=True),
        )
    pack_in = side_gather(first_in)
    query_pre = matmul(pack_in, full_query)
    key_pre = matmul(pack_in, full_key)
    value_low = matmul(pack_in, full_value).astype(jnp.bfloat16)
    head_count = query_pre.shape[1] // head_size
    cosine, sine_tab = rope_tables(seq_len, head_size)
    query_norm, query_factor = norm_parts(query_pre.reshape(seq_len, head_count, head_size))
    key_norm, key_factor = norm_parts(key_pre.reshape(seq_len, head_count, head_size))
    query_low = rotate(query_norm * query_gain, cosine, sine_tab).astype(jnp.bfloat16)
    key_low = rotate(key_norm * key_gain, cosine, sine_tab).astype(jnp.bfloat16)
    value_heads = value_low.reshape(seq_len, head_count, head_size)
    block_rows = min(512, seq_len)
    block_total = seq_len // block_rows
    masks = []
    mixture_parts = []
    lse_parts = []
    for block_index in range(block_total):
        offset = block_index * block_rows
        allowed = block_mask(segments, offset, block_rows, seq_len)
        masks.append(allowed)
        scores = block_scores(query_low[offset : offset + block_rows], key_low, allowed, inv_root)
        top_score = jnp.max(scores, axis=-1, keepdims=True)
        raw_weights = jnp.exp(scores - top_score)
        totals = jnp.sum(raw_weights, axis=-1, keepdims=True)
        weights_low = (raw_weights / totals).astype(jnp.bfloat16)
        mixture_parts.append(
            jnp.einsum(
                "hqk,khd->qhd", weights_low, value_heads, preferred_element_type=jnp.float32
            ).astype(jnp.bfloat16)
        )
        lse_parts.append(top_score + jnp.log(totals))
    mixture = jnp.concatenate(mixture_parts, axis=0).reshape(seq_len, head_count * head_size)

    middle = inputs_f32 + side_sum(matmul(mixture, full_output))
    normed_two, factor_two = norm_parts(middle)
    second_in = (normed_two * ffn_gain).astype(jnp.bfloat16)
    if by_gather:
        grad_second, mixing, kept = experts_by_gather(
            second_in, all_cot, places, gates, w_gate, w_up, w_down, capacity
        )
        mix_step = mixing.step
    else:
        outputs, grad_second, grad_w_gate, grad_w_up, grad_w_down = experts_by_exchange(
            second_in, cotangent, expert_ids, gate_values, w_gate, w_up, w_down, middle, capacity
        )
        mix_step = lambda values: values
    ffn_gain_part = jnp.sum(grad_second * normed_two, axis=0)
    grad_middle = cotangent.astype(jnp.float32) + norm_back(
        grad_second, normed_two, factor_two, ffn_gain
    )
    grad_attended = grad_middle.astype(jnp.bfloat16)
    if by_gather:
        kept, grad_attended = tied(kept, grad_attended)
        part_size = math.gcd(local_experts, GROUP)
        weight_parts = ()
        for first in range(0, local_experts // 2, part_size):
            weight_parts = weight_grads(first, part_size, *zip(*kept), weight_parts)
        weight_parts, pack_grad = tied(weight_parts, side_gather(grad_attended))
    else:
        pack_grad = side_gather(grad_attended)
    pack_grad = mix_step(pack_grad)
    output_part = contract_first(mixture, pack_grad)
    grad_mixture = (
        contract_last(pack_grad, full_output)
        .astype(jnp.bfloat16)
        .reshape(seq_len, head_count, head_size)
    )
    grad_query_parts = []
    grad_key_sum = jnp.zeros((seq_len, head_count, head_size), jnp.float32)
    grad_value_sum = jnp.zeros((seq_len, head_count, head_size), jnp.float32)
    for block_index in range(block_total):
        offset = block_index * block_rows
        query_block = query_low[offset : offset + block_rows]
        if block_index:
            query_block = mix_step(query_block)
        grad_block = grad_mixture[offset : offset + block_rows]
        scores = block_scores(query_block, key_low, masks[block_index], inv_root)
        prob_rows = jnp.exp(scores - lse_parts[block_index])
        grad_probs = jnp.einsum(
            "qhd,khd->hqk", grad_block, value_heads, preferred_element_type=jnp.float32
        )
        row_delta = jnp.sum(grad_probs * prob_rows, axis=-1, keepdims=True)
        grad_scores = (prob_rows * (grad_probs - row_delta)).astype(jnp.bfloat16)
        grad_query_parts.append(
            jnp.einsum("hqk,khd->qhd", grad_scores, key_low, preferred_element_type=jnp.float32)
            * inv_root
        )
        grad_key_sum = (
            grad_key_sum
            + jnp.einsum(
                "hqk,qhd->khd", grad_scores, query_block, preferred_element_type=jnp.float32
            )
            * inv_root
        )
        grad_value_sum = grad_value_sum + jnp.einsum(
            "hqk,qhd->khd",
            prob_rows.astype(jnp.bfloat16),
            grad_block,
            preferred_element_type=jnp.float32,
        )
    grad_query_norm = rotate_back(jnp.concatenate(grad_query_parts, axis=0), cosine, sine_tab)
    grad_key_norm = rotate_back(grad_key_sum, cosine, sine_tab)
    query_gain_part = jnp.sum(grad_query_norm * query_norm, axis=(0, 1))
    key_gain_part = jnp.sum(grad_key_norm * key_norm, axis=(0, 1))
    grad_query_norm = mix_step(grad_query_norm)
    grad_query_pre = (
        norm_back(grad_query_norm, query_norm, query_factor, query_gain)
        .reshape(seq_len, -1)
        .astype(jnp.bfloat16)
    )
    grad_key_pre = (
        norm_back(grad_key_norm, key_norm, key_factor, key_gain)
        .reshape(seq_len, -1)
        .astype(jnp.bfloat16)
    )
    grad_value_low = grad_value_sum.reshape(seq_len, -1).astype(jnp.bfloat16)
    query_part = contract_first(pack_in, grad_query_pre)
    key_part = contract_first(pack_in, grad_key_pre)
    value_part = contract_first(pack_in, grad_value_low)

    total_term = contract_last(grad_query_pre, full_query)
    total_term = total_term + contract_last(grad_key_pre, full_key)
    grad_first = side_sum(total_term + contract_last(grad_value_low, full_value))
    attn_gain_part = jnp.sum(grad_first * normed_one, axis=0)
    grad_inputs = grad_middle + norm_back(grad_first, normed_one, factor_one, attn_gain)
    gain_parts = (attn_gain_part, ffn_gain_part, query_gain_part, key_gain_part)
    if by_gather:
        in_part = jnp.concatenate([query_part, key_part, value_part], axis=1)
        grad_in = fold_packs(in_part.astype(jnp.bfloat16).reshape(data_count, -1, 3 * local_width))
        grad_w_query, grad_w_key, grad_w_value = (
            grad_in[:, index * local_width : (index + 1) * local_width] for index in range(3)
        )
        by_column = output_part.astype(jnp.bfloat16).reshape(local_width, data_count, -1)
        grad_w_output = fold_packs(by_column.transpose(1, 0, 2))
        kept, _ = tied(kept, in_part)
        for first in range(local_experts // 2 // part_size * part_size, local_experts, part_size):
            weight_parts = weight_grads(first, part_size, *zip(*kept), weight_parts)
        grad_w_gate, grad_w_up, grad_w_down = weight_parts
        outputs = middle + mixing.finish()
        late = sum_everywhere(attn_gain_part)
        early = sum_everywhere(jnp.concatenate(gain_parts[1:]))
        splits = (model_width, model_width + head_size)
        gain_sums = (late, *jnp.split(early, splits))
    else:
        grad_w_query, grad_w_key, grad_w_value, grad_w_output = (
            lax.psum_scatter(
                part.astype(jnp.bfloat16), "dp", scatter_dimension=along, tiled=True
            ).astype(jnp.float32)
            for part, along in ((query_part, 0), (key_part, 0), (value_part, 0), (output_part, 1))
        )
        gain_sums = lax.psum(gain_parts, ("dp", "tensor"))
    grad_attn_gain, grad_ffn_gain, grad_query_gain, grad_key_gain = gain_sums
    return (
        outputs,
        grad_inputs,
        grad_attn_gain,
        grad_query_gain,
        grad_key_gain,
        grad_w_query,
        grad_w_key,
        grad_w_value,
        grad_w_output,
        grad_ffn_gain,
        grad_w_gate,
        grad_w_up,
        grad_w_down,
    )


def solution(mesh):
    in_specs = (
        P(("dp", "tensor"), None),
        P("dp", "tensor"),
        P(("dp", "tensor"), None),
        P(("dp", "tensor"), None),
        P(),
        P(),
        P(),
        P("dp", "tensor"),
        P("dp", "tensor"),
        P("dp", "tensor"),
        P("tensor", "dp"),
        P(),
        P("dp", None, "tensor"),
        P("dp", None, "tensor"),
        P("dp", "tensor", None),
        P(("dp", "tensor"), None),
    )
    out_specs = (
        P(("dp", "tensor"), None),
        P(("dp", "tensor"), None),
        P(),
        P(),
        P(),
        P("dp", "tensor"),
        P("dp", "tensor"),
        P("dp", "tensor"),
        P("tensor", "dp"),
        P(),
        P("dp", None, "tensor"),
        P("dp", None, "tensor"),
        P("dp", "tensor", None),
    )
    return jax.shard_map(shards, mesh=mesh, in_specs=in_specs, out_specs=out_specs, check_vma=False)
```

```python
import jax
import jax.numpy as jnp
import functools
import math

from jax import lax
from jax.experimental import pallas as pl
from jax.experimental.pallas import tpu as pltpu
from jax.sharding import PartitionSpec as P

WINDOW = 1024
DP = ("plane", "pack")
TENSOR = ("side", "core")


EPSILON = 1e-06
THETA = 50000.0
NEG_FILL = -1e30


def matmul(left_side, right_side):
    return jnp.dot(left_side, right_side, preferred_element_type=jnp.float32)


def contract_last(left_side, right_side):
    return lax.dot_general(
        left_side, right_side, (((1,), (1,)), ((), ())), preferred_element_type=jnp.float32
    )


def contract_first(left_side, right_side):
    return lax.dot_general(
        left_side, right_side, (((0,), (0,)), ((), ())), preferred_element_type=jnp.float32
    )


def norm_parts(values):
    factor = lax.rsqrt(jnp.mean(values * values, axis=-1, keepdims=True) + EPSILON)
    return (values * factor, factor)


def norm_back(grad_out, normed, factor, gain_vec):
    scaled = grad_out * gain_vec
    return factor * (scaled - normed * jnp.mean(scaled * normed, axis=-1, keepdims=True))


def rope_tables(length, head_size):
    half_size = head_size // 2
    frequency = THETA ** (-(2.0 * jnp.arange(half_size, dtype=jnp.float32)) / head_size)
    angles = jnp.arange(length, dtype=jnp.float32)[:, None] * frequency[None, :]
    return (jnp.cos(angles)[:, None, :], jnp.sin(angles)[:, None, :])


def rotate(values, cosine, sine_tab):
    half_size = values.shape[-1] // 2
    first_half = values[..., :half_size]
    second_half = values[..., half_size:]
    return jnp.concatenate(
        [
            first_half * cosine - second_half * sine_tab,
            second_half * cosine + first_half * sine_tab,
        ],
        axis=-1,
    )


def rotate_back(grads_in, cosine, sine_tab):
    half_size = grads_in.shape[-1] // 2
    first_half = grads_in[..., :half_size]
    second_half = grads_in[..., half_size:]
    return jnp.concatenate(
        [
            first_half * cosine + second_half * sine_tab,
            second_half * cosine - first_half * sine_tab,
        ],
        axis=-1,
    )


def block_mask(segments, offset, block_rows, key_count):
    query_pos = offset + jnp.arange(block_rows)
    key_pos = jnp.arange(key_count)
    same_doc = segments[offset : offset + block_rows][:, None] == segments[None, :]
    near_pos = jnp.abs(query_pos[:, None] - key_pos[None, :]) < WINDOW // 2
    return same_doc & near_pos


def block_scores(query_block, key_low, allowed, inv_root):
    scores = (
        jnp.einsum("qhd,khd->hqk", query_block, key_low, preferred_element_type=jnp.float32)
        * inv_root
    )
    return jnp.where(allowed[None], scores, NEG_FILL)


def row_sum(term_fn, tok_rows):
    return lax.psum_scatter(
        term_fn(jnp.int32(0), lax.axis_size(TENSOR) * tok_rows),
        TENSOR,
        scatter_dimension=0,
        tiled=True,
    )


def gather_rows(values):
    return lax.all_gather(values, TENSOR, axis=0, tiled=True)


def from_experts(values):
    return lax.all_to_all(values, DP, split_axis=1, concat_axis=1, tiled=True)


def to_experts(source_rows, slot_token, slot_gate, layout):
    picked = jnp.take(source_rows, slot_token, axis=0, mode="fill", fill_value=0)
    if slot_gate is not None:
        picked = (picked.astype(jnp.float32) * slot_gate[:, None]).astype(jnp.bfloat16)
    picked = picked.reshape(layout + (picked.shape[1],))
    return lax.all_to_all(picked, DP, split_axis=1, concat_axis=1, tiled=True)


def pair_sum(table, weights_low, pair_slots, row_count):
    picked = jnp.take(table, pair_slots.reshape(-1), axis=0, mode="fill", fill_value=0)
    picked = picked.reshape(row_count, pair_slots.shape[1], table.shape[1])
    return jnp.einsum("rk,rkd->rd", weights_low, picked, preferred_element_type=jnp.float32)


def expert_forward(operands):
    rows_in, gate_mat, up_mat, down_mat = operands
    flat_rows = rows_in.reshape(-1, rows_in.shape[-1])
    gated = matmul(flat_rows, gate_mat)
    lifted = matmul(flat_rows, up_mat)
    hidden = (jax.nn.silu(gated) * lifted).astype(jnp.bfloat16)
    result = matmul(hidden, down_mat).astype(jnp.bfloat16)
    return (result.reshape(rows_in.shape), gated, lifted)


def expert_backward(operands):
    rows_in, grad_in, gated, lifted, gate_mat, up_mat, down_mat = operands
    flat_rows = rows_in.reshape(-1, rows_in.shape[-1])
    flat_grad = grad_in.reshape(-1, grad_in.shape[-1])
    gate_sig = jax.nn.sigmoid(gated)
    activated = jax.nn.silu(gated)
    hidden = (activated * lifted).astype(jnp.bfloat16)
    grad_hidden = contract_last(flat_grad, down_mat)
    grad_down = contract_first(hidden, flat_grad)
    grad_gated = (grad_hidden * lifted * gate_sig * (1.0 + gated * (1.0 - gate_sig))).astype(
        jnp.bfloat16
    )
    grad_lifted = (grad_hidden * activated).astype(jnp.bfloat16)
    grad_gate = contract_first(flat_rows, grad_gated)
    grad_up = contract_first(flat_rows, grad_lifted)
    grad_rows = (contract_last(grad_gated, gate_mat) + contract_last(grad_lifted, up_mat)).astype(
        jnp.bfloat16
    )
    return (grad_rows.reshape(rows_in.shape), grad_gate, grad_up, grad_down)


VMEM_BYTES = 60 * 1024 * 1024
COLUMN_CHUNK = 512
GROUP = 2


def select_rows(places_ref, gates_ref, pick_ref, capacity):
    expert_count, seq_len = places_ref.shape[1:]
    slot_range = lax.broadcasted_iota(jnp.int32, (capacity, seq_len), 0).astype(jnp.bfloat16)
    nothing = jnp.zeros((capacity, seq_len), jnp.bfloat16)
    for expert in range(expert_count):
        hit = places_ref[0, expert : expert + 1, :] == slot_range
        if gates_ref is None:
            weight = jnp.ones((capacity, seq_len), jnp.bfloat16)
        else:
            weight = jnp.broadcast_to(gates_ref[0, expert : expert + 1, :], (capacity, seq_len))
        rows = slice(expert * capacity, (expert + 1) * capacity)
        pick_ref[rows, :] = jnp.where(hit, weight, nothing)


def rows_to_slots(pick_ref, rows_ref, slots_ref, pack, capacity):
    width = rows_ref.shape[2]
    expert_count = slots_ref.shape[0]
    for start in range(0, width, COLUMN_CHUNK):
        columns = slice(start, start + COLUMN_CHUNK)
        picked = matmul(pick_ref[...], rows_ref[0, :, columns]).astype(jnp.bfloat16)
        slots_ref[:, pack, :, columns] = picked.reshape(expert_count, capacity, COLUMN_CHUNK)


def slots_to_rows(pick_ref, slots_ref, own_ref, other_ref, pack):
    width = own_ref.shape[3]
    for start in range(0, width, COLUMN_CHUNK):
        columns = slice(start, start + COLUMN_CHUNK)
        slots = slots_ref[:, pack, :, columns].reshape(-1, COLUMN_CHUNK)
        rows = contract_first(pick_ref[...], slots).astype(own_ref.dtype)
        rows = rows.reshape(2, 2, own_ref.shape[2], COLUMN_CHUNK)
        own_ref[0, :, :, columns] = rows[:, 0]
        other_ref[0, :, :, columns] = rows[:, 1]


def cot_kernel(
    packs, steps, capacity, table, places, gates, rows, down, slots_out, hidden_out, slots, pick
):
    step = pl.program_id(0)

    @pl.when(step < packs)
    def _():
        select_rows(places, gates, pick, capacity)
        rows_to_slots(pick, rows, slots, step, capacity)

    @pl.when(step >= packs)
    def _():
        for member in range(down.shape[0]):
            block = slots[(step - packs) * down.shape[0] + member].reshape(packs * capacity, -1)
            slots_out[member] = block
            hidden_out[member] = contract_last(block, down[member])


def piece_copies(own, other, rows, sems, pack):
    half_rows = own.shape[1]
    copies = []
    for far in range(2):
        for core, source in enumerate((own, other)):
            for half, index in enumerate((4 * far + pack, 2 + 4 * pack + far)):
                start = ((far * 2 + core) * 2 + half) * half_rows
                copies.append(
                    pltpu.make_async_copy(
                        source.at[index],
                        rows.at[pack, pl.ds(start, half_rows)],
                        sems.at[pack * 8 + len(copies)],
                    )
                )
    return copies


def row_kernel(
    packs, steps, capacity, places, own, other, both, grad_hidden,
    slots_out, hidden_out, grads_out, rows_own, rows_other,
    rows, slots, grads, pick, sems,
):
    step = pl.program_id(0)
    half = hidden_out.shape[2]

    @pl.when(step == 0)
    def _():
        for pack in range(packs):
            for copy in piece_copies(own, other, rows, sems, pack):
                copy.start()
        for pack in range(packs):
            select_rows(places.at[pl.ds(pack, 1)], None, pick.at[pack], capacity)

    for pack in range(packs):

        @pl.when(step == pack)
        def _(pack=pack):
            for copy in piece_copies(own, other, rows, sems, pack):
                copy.wait()
            rows_to_slots(pick.at[pack], rows.at[pl.ds(pack, 1)], slots, pack, capacity)

    @pl.when((step >= packs) & (step < packs + steps))
    def _():
        for member in range(both.shape[0]):
            expert = (step - packs) * both.shape[0] + member
            block = slots[expert].reshape(packs * capacity, -1)
            slots_out[member] = block
            product = matmul(block, both[member])
            gated, lifted = product[:, :half], product[:, half:]
            sig = 1.0 / (1.0 + jnp.exp(-gated))
            active = gated * sig
            hidden_out[member] = (active * lifted).astype(jnp.bfloat16)
            above = grad_hidden[member]
            grad_gated = above * lifted * sig * (1.0 + gated * (1.0 - sig))
            joined = jnp.concatenate([grad_gated, above * active], axis=1).astype(jnp.bfloat16)
            grads_out[member] = joined
            back = contract_last(joined, both[member])
            grads[expert] = back.astype(jnp.bfloat16).reshape(packs, capacity, -1)

    for pack in range(packs):

        @pl.when(step == packs + steps + pack)
        def _(pack=pack):
            slots_to_rows(pick.at[pack], grads, rows_own, rows_other, pack)


def mix_kernel(packs, steps, capacity, table, places, gates, hidden, down, *refs):
    rows_own, rows_other, results, pick = refs[-4:]
    step = pl.program_id(0)

    @pl.when(step < steps)
    def _():
        for member in range(down.shape[0]):
            result = matmul(hidden[member], down[member]).astype(jnp.bfloat16)
            results[step * down.shape[0] + member] = result.reshape(packs, capacity, -1)

    @pl.when(step >= steps)
    def _():
        select_rows(places, gates, pick, capacity)
        pack = (step - steps) ^ table[1]
        slots_to_rows(pick, results, rows_own.at[0], rows_other.at[0], pack)


def weight_kernel(planes, *refs):
    slots, grads, hidden, above = (
        jnp.concatenate([ref[0] for ref in refs[i * planes : (i + 1) * planes]]) for i in range(4)
    )
    gate_out, up_out, down_out = refs[-3:]
    half = gate_out.shape[2]
    both = contract_first(slots, above)
    gate_out[0] = both[:, :half]
    up_out[0] = both[:, half:]
    down_out[0] = contract_first(hidden, grads)


def block(shape, place, count=1):
    tail = (0,) * (len(shape) - 1)
    return pl.BlockSpec((count,) + tuple(shape[1:]), lambda *ids: (place(*ids),) + tail)


def staged(first, count):
    return lambda step, *rest: jnp.clip(step - first, 0, count - 1)


def shape_of(shape, kind):
    return jax.ShapeDtypeStruct(shape, kind)


def call(kernel, steps, specs, out_specs, out_shape, scratch, flops, prefetch=0, aliases={}):
    return pl.pallas_call(
        kernel,
        grid_spec=pltpu.PrefetchScalarGridSpec(
            num_scalar_prefetch=prefetch,
            grid=(steps,),
            in_specs=specs,
            out_specs=out_specs,
            scratch_shapes=scratch,
        ),
        out_shape=out_shape,
        input_output_aliases=aliases,
        cost_estimate=pl.CostEstimate(
            flops=flops, transcendentals=0, bytes_accessed=flops // 500
        ),
        compiler_params=pltpu.CompilerParams(
            dimension_semantics=("arbitrary",), vmem_limit_bytes=VMEM_BYTES
        ),
    )


def cot_slots(table, places, gates, rows, down, capacity):
    packs = table.shape[0]
    _, seq_len, width = rows.shape
    experts, hidden_width, _ = down.shape
    slot_rows = packs * capacity
    group = math.gcd(experts, GROUP)
    steps = experts // group
    by_pack, by_expert = staged(0, packs), staged(packs, steps)
    listed = lambda step, numbers: numbers[by_pack(step)]
    out_shape = [
        shape_of((experts, slot_rows, width), jnp.bfloat16),
        shape_of((experts, slot_rows, hidden_width), jnp.float32),
    ]
    return call(
        functools.partial(cot_kernel, packs, steps, capacity),
        packs + steps,
        [
            block(places.shape, listed), block(gates.shape, listed), block(rows.shape, listed),
            block(down.shape, by_expert, group),
        ],
        [block(out.shape, by_expert, group) for out in out_shape],
        out_shape,
        [
            pltpu.VMEM((experts, packs, capacity, width), jnp.bfloat16),
            pltpu.VMEM((experts * capacity, seq_len), jnp.bfloat16),
        ],
        2 * experts * slot_rows * width * (seq_len + hidden_width),
        1,
    )(table, places, gates, rows, down)


def row_slots(places, own, other, both, grad_hidden, capacity):
    packs, _, seq_len = places.shape
    experts, width, hidden_width = both.shape
    slot_rows = packs * capacity
    group = math.gcd(experts, GROUP)
    steps = experts // group
    middle, last = staged(packs, steps), staged(packs + steps, packs)
    part = shape_of((packs, 2, seq_len // 4, width), jnp.bfloat16)
    out_shape = [
        shape_of((experts, slot_rows, width), jnp.bfloat16),
        shape_of((experts, slot_rows, hidden_width // 2), jnp.bfloat16),
        shape_of((experts, slot_rows, hidden_width), jnp.bfloat16),
        part, part,
    ]
    anywhere = pl.BlockSpec(memory_space=pl.ANY)
    return call(
        functools.partial(row_kernel, packs, steps, capacity),
        2 * packs + steps,
        [
            block(places.shape, lambda step: 0, packs), anywhere, anywhere,
            block(both.shape, middle, group), block(grad_hidden.shape, middle, group),
        ],
        [block(out.shape, middle, group) for out in out_shape[:3]] + [block(part.shape, last)] * 2,
        out_shape,
        [
            pltpu.VMEM((packs, seq_len, width), jnp.bfloat16),
            pltpu.VMEM((experts, packs, capacity, width), jnp.bfloat16),
            pltpu.VMEM((experts, packs, capacity, width), jnp.bfloat16),
            pltpu.VMEM((packs, experts * capacity, seq_len), jnp.bfloat16),
            pltpu.SemaphoreType.DMA((8 * packs,)),
        ],
        4 * experts * slot_rows * width * (seq_len + hidden_width),
    )(places, own, other, both, grad_hidden)


def mix_rows(table, places, gates, hidden, down, planes, capacity, earlier=()):
    packs, _, seq_len = places.shape
    experts, hidden_width, width = down.shape
    group = math.gcd(experts, GROUP)
    steps = experts // group
    first, last = staged(0, steps), staged(steps, packs)
    part = shape_of((planes, packs, 2, seq_len // 4, width), jnp.bfloat16)
    out_spec = pl.BlockSpec(
        (1, 1) + part.shape[2:], lambda step, numbers: (numbers[0], last(step), 0, 0, 0)
    )
    return call(
        functools.partial(mix_kernel, packs, steps, capacity),
        packs + steps,
        [
            block(places.shape, last), block(gates.shape, last),
            block(hidden.shape, first, group), block(down.shape, first, group),
        ]
        + [pl.BlockSpec(memory_space=pl.ANY)] * len(earlier),
        [out_spec] * 2,
        [part, part],
        [
            pltpu.VMEM((experts, packs, capacity, width), jnp.bfloat16),
            pltpu.VMEM((experts * capacity, seq_len), jnp.bfloat16),
        ],
        2 * experts * packs * capacity * width * (seq_len + hidden_width),
        1,
        aliases={5 + index: index for index in range(len(earlier))},
    )(table, places, gates, hidden, down, *earlier)


def weight_grads(first, count, slots, hidden, grads, above, earlier=()):
    planes = len(slots)
    operands = [*slots, *grads, *hidden, *above]
    experts, _, width = slots[0].shape
    hidden_width = hidden[0].shape[2]
    each = lambda step: step + first
    out_shape = [
        shape_of((experts, width, hidden_width), jnp.float32),
        shape_of((experts, width, hidden_width), jnp.float32),
        shape_of((experts, hidden_width, width), jnp.float32),
    ]
    return call(
        functools.partial(weight_kernel, planes),
        count,
        [block(operand.shape, each) for operand in operands]
        + [pl.BlockSpec(memory_space=pl.ANY)] * len(earlier),
        [block(out.shape, each) for out in out_shape],
        out_shape,
        [],
        6 * planes * slots[0].shape[1] * count * width * hidden_width,
        aliases={len(operands) + index: index for index in range(len(earlier))},
    )(*operands, *earlier)


def swapped(values, axis, bit):
    count = lax.axis_size(axis)
    return lax.ppermute(values, axis, [(i, i ^ bit) for i in range(count)])


def far_side(values):
    return swapped(values, TENSOR, 2)


def far_core(values):
    return swapped(values, TENSOR, 1)


def far_pack(values):
    return swapped(values, DP, 1)


def next_plane(values):
    count = lax.axis_size(DP)
    return lax.ppermute(values, DP, [(i, (i + 2) % count) for i in range(count)])


def spread_plane(values, beside):
    half_rows = values.shape[0] // 2
    upper, lower = values[:half_rows], values[half_rows:]
    near_upper = jnp.stack([upper, far_pack(upper)])
    near_lower = jnp.stack([lower, far_side(lower)])
    near, made = beside((near_upper, near_lower))
    own = jnp.concatenate([*near, far_side(near[0]), far_pack(near[1])])
    own, made = lax.optimization_barrier((own, made))
    return own, far_core(own), made


def plane_order():
    packs = lax.axis_size(DP)
    planes = packs // 2
    index = lax.axis_index(DP)
    return jnp.stack(
        [
            ((index // 2 + planes - plane) % planes) * 2 + (index % 2 ^ near)
            for plane in range(planes)
            for near in range(2)
        ]
    )


def place_kernel(by_column, order, *refs):
    *pieces, whole, sems = refs
    copies = []
    for index, piece in enumerate(pieces):
        target = None if by_column else whole.at[order[index]]
        if by_column:
            width = piece.shape[1]
            target = whole.at[:, pl.ds(pl.multiple_of(order[index] * width, 128), width)]
        copies.append(pltpu.make_async_copy(piece, target, sems.at[index]))
        copies[-1].start()
    for copy in copies:
        copy.wait()


def laid(pieces, order, by_column=False):
    count = len(pieces)
    rows, columns = pieces[0].shape
    shape = (rows, count * columns) if by_column else (count, rows, columns)
    anywhere = pl.BlockSpec(memory_space=pl.ANY)
    return call(
        functools.partial(place_kernel, by_column),
        1,
        [anywhere] * count,
        pl.BlockSpec(memory_space=pltpu.VMEM),
        shape_of(shape, pieces[0].dtype),
        [pltpu.SemaphoreType.DMA((count,))],
        1000,
        1,
    )(order, *pieces)


def gather_packs(values, by_column=False):
    pieces = []
    planes = lax.axis_size("plane")
    for plane in range(planes):
        moved = [far_pack(values), next_plane(values) if plane + 1 < planes else ()]
        across, following = lax.optimization_barrier(moved)
        pieces += [values, across]
        values = following
    return laid(pieces, plane_order(), by_column)


def fold_packs(values):
    order = plane_order()
    take = lambda index: lax.dynamic_index_in_dim(values, order[index], 0, keepdims=False)
    near = [added(take(2 * i), far_pack(take(2 * i + 1))) for i in range(values.shape[0] // 2)]
    summed = near[1]
    for part in near[2:]:
        summed = added(next_plane(summed), part)
    return added(next_plane(summed), near[0], jnp.float32)


def laid_sides(pieces):
    order = lax.axis_index(TENSOR) ^ jnp.arange(len(pieces), dtype=jnp.int32)
    return laid(pieces, order).reshape((-1,) + pieces[0].shape[1:])


def gather_sides(values):
    across = far_side(values)
    return laid_sides([values, far_core(values), across, far_core(across)])


def fold_sides(values):
    split = values.astype(jnp.bfloat16).reshape((4, -1) + values.shape[1:])
    take = lambda bits: lax.dynamic_index_in_dim(
        split, lax.axis_index(TENSOR) ^ bits, 0, keepdims=False
    )
    far = added(take(2), far_core(take(3)))
    near = added(take(0), far_core(take(1)))
    return added(near, far_side(far), jnp.float32)


def gather_both(weights, rows):
    pieces, row_pieces, values = [], [rows], weights
    planes = lax.axis_size("plane")
    for plane in range(planes):
        moved = [far_pack(values), next_plane(values) if plane + 1 < planes else ()]
        if plane == 0:
            moved += [far_core(rows), far_side(rows)]
        if plane == 1:
            moved += [far_core(row_pieces[2])]
        across, following, *arrived = lax.optimization_barrier(moved)
        pieces += [values, across]
        row_pieces += arrived
        values = following
    return laid(pieces, plane_order()), laid_sides(row_pieces)


def sum_everywhere(values):
    for axis in (TENSOR, DP):
        bit = 1
        while bit < lax.axis_size(axis):
            values = values + swapped(values, axis, bit)
            bit *= 2
    return values


def added(left, right, kind=jnp.bfloat16):
    return (left.astype(jnp.float32) + right.astype(jnp.float32)).astype(kind)


def fold_first(own, arrived):
    half_rows = own.shape[2] // 2
    upper, lower = slice(None, half_rows), slice(half_rows, None)
    return (
        added(own[:, 0, upper], arrived[:, 0, upper]),
        added(own[0, :, lower], arrived[0, :, lower]),
        added(own[:, 1, upper], arrived[:, 1, upper]),
        added(own[1, :, lower], arrived[1, :, lower]),
    )


def fold_second(upper, lower, upper_far, lower_far):
    upper = added(upper, far_side(upper_far))
    lower = added(lower, far_pack(lower_far))
    return upper[0], lower[0], upper[1], lower[1]


def fold_third(upper, lower, upper_far, lower_far):
    return jnp.concatenate(
        [added(upper, far_pack(upper_far)), added(lower, far_side(lower_far))]
    )


def tied(small, values):
    return lax.optimization_barrier((small, values))


def gather_tables(expert_ids, gate_values, segment_ids):
    top_count = expert_ids.shape[1]
    tables = jnp.concatenate(
        [expert_ids.T.astype(jnp.bfloat16), gate_values.T, segment_ids.astype(jnp.bfloat16)]
    )[None]
    for axis in (TENSOR, DP):
        bit = 1
        while bit < lax.axis_size(axis):
            tables = jnp.concatenate([tables, swapped(tables, axis, bit)])
            bit *= 2
        if axis == TENSOR:
            sides = jnp.arange(tables.shape[0], dtype=jnp.int32) ^ lax.axis_index(TENSOR)
            segments = jnp.take(tables[:, -1], sides, axis=0).reshape(-1)
    devices = jnp.arange(tables.shape[0], dtype=jnp.int32)
    own = lax.axis_index(DP) * lax.axis_size(TENSOR) + lax.axis_index(TENSOR)
    tables = jnp.take(tables, devices ^ own, axis=0)
    all_ids, all_gates = tables[:, :top_count], tables[:, top_count : 2 * top_count]
    return all_ids.astype(jnp.int32), all_gates, segments.astype(jnp.int32)


def routing(all_ids, all_gates, local_experts, capacity):
    packs = lax.axis_size(DP)
    first = lax.axis_index(DP) * local_experts
    wanted = first + jnp.arange(local_experts, dtype=jnp.int32)

    def by_pack(values):
        top_count, tok_rows = values.shape[1:]
        ordered = values.reshape(packs, -1, top_count, tok_rows).transpose(0, 2, 1, 3)
        return ordered.reshape(packs, top_count, -1)

    matches = by_pack(all_ids)[:, :, None, :] == wanted[None, None, :, None]
    pair_gates = by_pack(all_gates).astype(jnp.float32)
    member = jnp.any(matches, axis=1)
    gates = jnp.sum(jnp.where(matches, pair_gates[:, :, None, :], 0.0), axis=1)
    order = jnp.arange(member.shape[2], dtype=jnp.int32)
    earlier = (order[:, None] < order[None, :]).astype(jnp.bfloat16)
    flat = member.reshape(packs * local_experts, -1).astype(jnp.bfloat16)
    before = matmul(flat, earlier).astype(jnp.int32).reshape(member.shape)
    places = jnp.where(member & (before < capacity), before, -1)
    return places.astype(jnp.bfloat16), gates.astype(jnp.bfloat16)


def experts_by_exchange(
    second_in, cotangent, expert_ids, gate_values, w_gate, w_up, w_down, middle, capacity
):
    tok_rows, model_width = second_in.shape
    tensor_count = lax.axis_size(TENSOR)
    data_count = lax.axis_size(DP)
    local_experts = w_gate.shape[0]
    all_experts = local_experts * data_count
    top_count = expert_ids.shape[1]
    seq_len = tok_rows * tensor_count
    pack_cot, pack_ids, pack_gates = (
        gather_rows(cotangent), gather_rows(expert_ids), gather_rows(gate_values)
    )
    pack_second = gather_rows(second_in)
    expert_range = jnp.arange(all_experts, dtype=jnp.int32)
    matches = pack_ids[:, :, None] == expert_range[None, None, :]
    token_counts = jnp.sum(matches.astype(jnp.float32), axis=1).astype(jnp.bfloat16)
    token_range = jnp.arange(seq_len, dtype=jnp.int32)
    earlier = (token_range[:, None] > token_range[None, :]).astype(jnp.bfloat16)
    before = matmul(earlier, token_counts)
    places = (
        jnp.sum(jnp.where(matches, before[:, None, :], 0.0), axis=2).astype(jnp.int32).reshape(-1)
    )
    flat_ids = pack_ids.reshape(-1)
    owners = flat_ids // local_experts
    local_index = flat_ids % local_experts
    dump_slot = all_experts * capacity
    slot_index = jnp.where(
        places < capacity,
        local_index * (data_count * capacity) + owners * capacity + places,
        dump_slot,
    ).astype(jnp.int32)
    pair_token = jnp.arange(seq_len * top_count) // top_count
    slot_token = (
        jnp.full((dump_slot + 1,), seq_len, jnp.int32).at[slot_index].set(pair_token)[:dump_slot]
    )
    pair_gates = pack_gates.astype(jnp.float32)
    slot_gate = (
        jnp.zeros((dump_slot + 1,), jnp.float32)
        .at[slot_index]
        .set(pair_gates.reshape(-1))[:dump_slot]
    )
    pair_slots = slot_index.reshape(seq_len, top_count)
    layout = (local_experts, data_count, capacity)
    arrived_rows = to_experts(pack_second, slot_token, None, layout)
    expert_out, gated_all, lifted_all = lax.map(
        expert_forward, (arrived_rows, w_gate, w_up, w_down)
    )
    returned = from_experts(expert_out).reshape(-1, model_width)

    def combine_term(offset, row_count):
        return pair_sum(returned, pack_gates, pair_slots, row_count)

    outputs = middle + row_sum(combine_term, tok_rows)
    grad_arrived = to_experts(pack_cot, slot_token, slot_gate, layout)
    grad_rows_all, grad_w_gate, grad_w_up, grad_w_down = lax.map(
        expert_backward, (arrived_rows, grad_arrived, gated_all, lifted_all, w_gate, w_up, w_down)
    )
    returned_grad = from_experts(grad_rows_all).reshape(-1, model_width)
    unit_gates = jnp.ones_like(pack_gates)

    def dispatch_term(offset, row_count):
        return pair_sum(returned_grad, unit_gates, pair_slots, row_count)

    grad_second = row_sum(dispatch_term, tok_rows)
    return outputs, grad_second, grad_w_gate, grad_w_up, grad_w_down


class Folding:
    def __init__(self, order):
        self.order, self.waiting, self.fresh = order, {}, {}
        self.summed, self.count = None, 0

    def begin(self, plane, own, other):
        self.fresh[plane] = (0, (own, far_core(other)))

    def step(self, small):
        made = {}
        for plane, (stage, values) in self.waiting.items():
            if stage < 3:
                made[plane] = (fold_first, fold_second, fold_third)[stage](*values)
        ready = {plane: values for plane, (stage, values) in self.waiting.items() if stage == 3}
        passed = None
        if self.order[self.count] in ready:
            passed = self.passed_on(ready[self.order[self.count]])
            del self.waiting[self.order[self.count]]
            self.count += 1
        small, (made, passed) = tied(small, (made, passed))
        self.waiting.update(self.fresh)
        self.fresh = {}
        for plane, values in made.items():
            self.waiting[plane] = (self.waiting[plane][0] + 1, values)
        if passed is not None:
            self.summed = passed
        return small

    def passed_on(self, values):
        kind = jnp.float32 if self.count + 1 == len(self.order) else jnp.bfloat16
        return values if self.summed is None else added(next_plane(self.summed), values, kind)

    def finish(self):
        self.waiting.update(self.fresh)
        for plane in self.order[self.count :]:
            stage, values = self.waiting[plane]
            for fold in (fold_first, fold_second, fold_third)[stage:]:
                values = fold(*values)
            self.summed = self.passed_on(values)
            self.count += 1
        return self.summed


def experts_by_gather(second_in, all_cot, places, gates, w_gate, w_up, w_down, capacity):
    packs, local_experts, seq_len = places.shape
    tensor_count = lax.axis_size(TENSOR)
    planes = packs // 2
    pack_order = plane_order()
    side_index = lax.axis_index(TENSOR)
    quarter_order = side_index ^ jnp.arange(tensor_count, dtype=jnp.int32)

    def as_met(values, by_pack, by_quarter):
        split = values.reshape(packs, local_experts, tensor_count, -1)
        split = jnp.take(jnp.take(split, by_pack, axis=0), by_quarter, axis=2)
        return split.reshape(values.shape)

    near_places = as_met(places, pack_order, quarter_order)
    plane_index = pack_order[::2] // 2
    whole_order = (plane_index[:, None] * 2 + jnp.arange(2, dtype=jnp.int32)).reshape(-1)
    core_order = lax.axis_index("core") ^ jnp.arange(tensor_count, dtype=jnp.int32)
    mix_places = as_met(places, whole_order, core_order)
    mix_gates = as_met(gates, whole_order, core_order)
    w_both = jnp.concatenate([w_gate, w_up], axis=2)
    pieces, travelling = [], second_in
    for plane in range(planes):
        travelling = next_plane(travelling) if plane else travelling

        def beside(near, listed=pack_order[plane * 2 : plane * 2 + 2]):
            listed, near = tied(listed, near)
            return near, cot_slots(listed, places, gates, all_cot, w_down, capacity)

        pieces.append(spread_plane(travelling, beside))
    pairs = [slice(plane * 2, plane * 2 + 2) for plane in range(planes)]
    order = [*range(1, planes), 0]
    kept, folding = {}, Folding(order)
    for plane in range(planes):
        pair = pairs[plane]
        own, other, (grad_slots, grad_hidden) = pieces[plane]
        near = folding.step(near_places[pair]) if plane else near_places[pair]
        slots, hidden, above, *part = row_slots(near, own, other, w_both, grad_hidden, capacity)
        folding.begin(plane, *part)
        kept[plane] = (slots, hidden, grad_slots, above)
    mixed = ()
    for index, plane in enumerate(order):
        pair = pairs[plane]
        near = mix_places[pair] if index % 2 else folding.step(mix_places[pair])
        table = jnp.stack([plane_index[plane], lax.axis_index("pack")])
        mixed = mix_rows(
            table, near, mix_gates[pair], kept[plane][1], w_down, planes, capacity, mixed
        )
    own, other = mixed
    whole = added(own, far_core(other)).reshape(planes, -1, own.shape[-1])
    whole = lax.psum_scatter(whole, ("pack", "side"), scatter_dimension=1, tiled=True)
    whole = lax.psum_scatter(whole, "plane", scatter_dimension=0, tiled=True)
    return folding.finish(), whole[0].astype(jnp.float32), [kept[plane] for plane in range(planes)]


def shards(
    inputs,
    segment_ids,
    expert_ids,
    gate_values,
    attn_gain,
    query_gain,
    key_gain,
    w_query,
    w_key,
    w_value,
    w_output,
    ffn_gain,
    w_gate,
    w_up,
    w_down,
    cotangent,
):
    tok_rows, model_width = inputs.shape
    head_size = query_gain.shape[0]
    tensor_count = lax.axis_size(TENSOR)
    data_count = lax.axis_size(DP)
    local_experts = w_gate.shape[0]
    all_experts = local_experts * data_count
    top_count = expert_ids.shape[1]
    seq_len = tok_rows * tensor_count
    capacity = seq_len * top_count // all_experts
    inv_root = head_size ** (-0.5)
    by_gather = (
        seq_len <= local_experts * capacity
        and tensor_count == 4
        and data_count > 2
        and data_count & (data_count - 1) == 0
        and all_experts <= 256
    )
    if by_gather:
        axes = (*DP, *TENSOR)
        all_ids, all_gates, segments = gather_tables(expert_ids, gate_values, segment_ids)
        places, gates = routing(all_ids, all_gates, local_experts, capacity)
    inputs_f32 = inputs.astype(jnp.float32)
    normed_one, factor_one = norm_parts(inputs_f32)
    first_in = (normed_one * attn_gain).astype(jnp.bfloat16)
    if by_gather:
        side_sum, side_gather = fold_sides, gather_sides
        local_width = w_query.shape[1]
        w_in = jnp.concatenate([w_query, w_key, w_value], axis=1)
        full_in, pack_in = gather_both(w_in, first_in)
        full_in, cotangent, w_output = lax.optimization_barrier((full_in, cotangent, w_output))
        all_cot = lax.all_gather(cotangent, axes, axis=0, tiled=True)
        all_cot = all_cot.reshape(data_count, seq_len, model_width)
        full_in = full_in.reshape(model_width, -1)
        full_query, full_key, full_value = (
            full_in[:, index * local_width : (index + 1) * local_width] for index in range(3)
        )
        full_output = gather_packs(w_output, True)
    else:
        side_sum, side_gather = lambda term: row_sum(lambda *_: term, tok_rows), gather_rows
        segments = lax.all_gather(segment_ids, TENSOR, axis=1, tiled=True)[0]
        full_query, full_key, full_value, full_output = (
            lax.all_gather(w_query, DP, axis=0, tiled=True),
            lax.all_gather(w_key, DP, axis=0, tiled=True),
            lax.all_gather(w_value, DP, axis=0, tiled=True),
            lax.all_gather(w_output, DP, axis=1, tiled=True),
        )
        pack_in = side_gather(first_in)
    query_pre = matmul(pack_in, full_query)
    key_pre = matmul(pack_in, full_key)
    value_low = matmul(pack_in, full_value).astype(jnp.bfloat16)
    head_count = query_pre.shape[1] // head_size
    cosine, sine_tab = rope_tables(seq_len, head_size)
    query_norm, query_factor = norm_parts(query_pre.reshape(seq_len, head_count, head_size))
    key_norm, key_factor = norm_parts(key_pre.reshape(seq_len, head_count, head_size))
    query_low = rotate(query_norm * query_gain, cosine, sine_tab).astype(jnp.bfloat16)
    key_low = rotate(key_norm * key_gain, cosine, sine_tab).astype(jnp.bfloat16)
    value_heads = value_low.reshape(seq_len, head_count, head_size)
    block_rows = min(512, seq_len)
    block_total = seq_len // block_rows
    masks = []
    mixture_parts = []
    lse_parts = []
    for block_index in range(block_total):
        offset = block_index * block_rows
        allowed = block_mask(segments, offset, block_rows, seq_len)
        masks.append(allowed)
        scores = block_scores(query_low[offset : offset + block_rows], key_low, allowed, inv_root)
        top_score = jnp.max(scores, axis=-1, keepdims=True)
        raw_weights = jnp.exp(scores - top_score)
        totals = jnp.sum(raw_weights, axis=-1, keepdims=True)
        weights_low = (raw_weights / totals).astype(jnp.bfloat16)
        mixture_parts.append(
            jnp.einsum(
                "hqk,khd->qhd", weights_low, value_heads, preferred_element_type=jnp.float32
            ).astype(jnp.bfloat16)
        )
        lse_parts.append(top_score + jnp.log(totals))
    mixture = jnp.concatenate(mixture_parts, axis=0).reshape(seq_len, head_count * head_size)

    middle = inputs_f32 + side_sum(matmul(mixture, full_output))
    normed_two, factor_two = norm_parts(middle)
    second_in = (normed_two * ffn_gain).astype(jnp.bfloat16)
    if by_gather:
        grad_second, mixed, kept = experts_by_gather(
            second_in, all_cot, places, gates, w_gate, w_up, w_down, capacity
        )
    else:
        outputs, grad_second, grad_w_gate, grad_w_up, grad_w_down = experts_by_exchange(
            second_in, cotangent, expert_ids, gate_values, w_gate, w_up, w_down, middle, capacity
        )
    ffn_gain_part = jnp.sum(grad_second * normed_two, axis=0)
    grad_middle = cotangent.astype(jnp.float32) + norm_back(
        grad_second, normed_two, factor_two, ffn_gain
    )
    grad_attended = grad_middle.astype(jnp.bfloat16)
    if by_gather:
        kept, grad_attended = tied(kept, grad_attended)
        part_size = math.gcd(local_experts, GROUP)
        weight_parts = ()
        for first in range(0, local_experts // 2, part_size):
            weight_parts = weight_grads(first, part_size, *zip(*kept), weight_parts)
        weight_parts, pack_grad = tied(weight_parts, side_gather(grad_attended))
    else:
        pack_grad = side_gather(grad_attended)
    output_part = contract_first(mixture, pack_grad)
    grad_mixture = (
        contract_last(pack_grad, full_output)
        .astype(jnp.bfloat16)
        .reshape(seq_len, head_count, head_size)
    )
    grad_query_parts = []
    grad_key_sum = jnp.zeros((seq_len, head_count, head_size), jnp.float32)
    grad_value_sum = jnp.zeros((seq_len, head_count, head_size), jnp.float32)
    for block_index in range(block_total):
        offset = block_index * block_rows
        query_block = query_low[offset : offset + block_rows]
        grad_block = grad_mixture[offset : offset + block_rows]
        scores = block_scores(query_block, key_low, masks[block_index], inv_root)
        prob_rows = jnp.exp(scores - lse_parts[block_index])
        grad_probs = jnp.einsum(
            "qhd,khd->hqk", grad_block, value_heads, preferred_element_type=jnp.float32
        )
        row_delta = jnp.sum(grad_probs * prob_rows, axis=-1, keepdims=True)
        grad_scores = (prob_rows * (grad_probs - row_delta)).astype(jnp.bfloat16)
        grad_query_parts.append(
            jnp.einsum("hqk,khd->qhd", grad_scores, key_low, preferred_element_type=jnp.float32)
            * inv_root
        )
        grad_key_sum = (
            grad_key_sum
            + jnp.einsum(
                "hqk,qhd->khd", grad_scores, query_block, preferred_element_type=jnp.float32
            )
            * inv_root
        )
        grad_value_sum = grad_value_sum + jnp.einsum(
            "hqk,qhd->khd",
            prob_rows.astype(jnp.bfloat16),
            grad_block,
            preferred_element_type=jnp.float32,
        )
    grad_query_norm = rotate_back(jnp.concatenate(grad_query_parts, axis=0), cosine, sine_tab)
    grad_key_norm = rotate_back(grad_key_sum, cosine, sine_tab)
    query_gain_part = jnp.sum(grad_query_norm * query_norm, axis=(0, 1))
    key_gain_part = jnp.sum(grad_key_norm * key_norm, axis=(0, 1))
    grad_query_pre = (
        norm_back(grad_query_norm, query_norm, query_factor, query_gain)
        .reshape(seq_len, -1)
        .astype(jnp.bfloat16)
    )
    grad_key_pre = (
        norm_back(grad_key_norm, key_norm, key_factor, key_gain)
        .reshape(seq_len, -1)
        .astype(jnp.bfloat16)
    )
    grad_value_low = grad_value_sum.reshape(seq_len, -1).astype(jnp.bfloat16)
    query_part = contract_first(pack_in, grad_query_pre)
    key_part = contract_first(pack_in, grad_key_pre)
    value_part = contract_first(pack_in, grad_value_low)

    total_term = contract_last(grad_query_pre, full_query)
    total_term = total_term + contract_last(grad_key_pre, full_key)
    grad_first = side_sum(total_term + contract_last(grad_value_low, full_value))
    attn_gain_part = jnp.sum(grad_first * normed_one, axis=0)
    grad_inputs = grad_middle + norm_back(grad_first, normed_one, factor_one, attn_gain)
    gain_parts = (attn_gain_part, ffn_gain_part, query_gain_part, key_gain_part)
    if by_gather:
        in_part = jnp.concatenate([query_part, key_part, value_part], axis=1)
        grad_in = fold_packs(in_part.astype(jnp.bfloat16).reshape(data_count, -1, 3 * local_width))
        grad_w_query, grad_w_key, grad_w_value = (
            grad_in[:, index * local_width : (index + 1) * local_width] for index in range(3)
        )
        by_column = output_part.astype(jnp.bfloat16).reshape(local_width, data_count, -1)
        grad_w_output = fold_packs(by_column.transpose(1, 0, 2))
        kept, _ = tied(kept, in_part)
        for first in range(local_experts // 2 // part_size * part_size, local_experts, part_size):
            weight_parts = weight_grads(first, part_size, *zip(*kept), weight_parts)
        grad_w_gate, grad_w_up, grad_w_down = weight_parts
        outputs = middle + mixed
        late = sum_everywhere(attn_gain_part)
        early = sum_everywhere(jnp.concatenate(gain_parts[1:]))
        splits = (model_width, model_width + head_size)
        gain_sums = (late, *jnp.split(early, splits))
    else:
        grad_w_query, grad_w_key, grad_w_value, grad_w_output = (
            lax.psum_scatter(
                part.astype(jnp.bfloat16), DP, scatter_dimension=along, tiled=True
            ).astype(jnp.float32)
            for part, along in ((query_part, 0), (key_part, 0), (value_part, 0), (output_part, 1))
        )
        gain_sums = lax.psum(gain_parts, (*DP, *TENSOR))
    grad_attn_gain, grad_ffn_gain, grad_query_gain, grad_key_gain = gain_sums
    return (
        outputs,
        grad_inputs,
        grad_attn_gain,
        grad_query_gain,
        grad_key_gain,
        grad_w_query,
        grad_w_key,
        grad_w_value,
        grad_w_output,
        grad_ffn_gain,
        grad_w_gate,
        grad_w_up,
        grad_w_down,
    )


def solution(mesh):
    rows, columns = mesh.devices.shape
    split = jax.sharding.Mesh(
        mesh.devices.reshape(rows // 2, 2, columns // 2, 2), (*DP, *TENSOR)
    )
    in_specs = (
        P((*DP, *TENSOR), None),
        P(DP, TENSOR),
        P((*DP, *TENSOR), None),
        P((*DP, *TENSOR), None),
        P(),
        P(),
        P(),
        P(DP, TENSOR),
        P(DP, TENSOR),
        P(DP, TENSOR),
        P(TENSOR, DP),
        P(),
        P(DP, None, TENSOR),
        P(DP, None, TENSOR),
        P(DP, TENSOR, None),
        P((*DP, *TENSOR), None),
    )
    out_specs = (
        P((*DP, *TENSOR), None),
        P((*DP, *TENSOR), None),
        P(),
        P(),
        P(),
        P(DP, TENSOR),
        P(DP, TENSOR),
        P(DP, TENSOR),
        P(TENSOR, DP),
        P(),
        P(DP, None, TENSOR),
        P(DP, None, TENSOR),
        P(DP, TENSOR, None),
    )
    return jax.shard_map(shards, mesh=split, in_specs=in_specs, out_specs=out_specs, check_vma=False)
```

```python
import jax
import jax.numpy as jnp
import functools
import math

from jax import lax
from jax.experimental import pallas as pl
from jax.experimental.pallas import tpu as pltpu
from jax.sharding import PartitionSpec as P

WINDOW = 1024
DP = ("plane", "pack")
TENSOR = ("side", "core")


EPSILON = 1e-06
THETA = 50000.0
NEG_FILL = -1e30


def matmul(left_side, right_side):
    return jnp.dot(left_side, right_side, preferred_element_type=jnp.float32)


def contract_last(left_side, right_side):
    return lax.dot_general(
        left_side, right_side, (((1,), (1,)), ((), ())), preferred_element_type=jnp.float32
    )


def contract_first(left_side, right_side):
    return lax.dot_general(
        left_side, right_side, (((0,), (0,)), ((), ())), preferred_element_type=jnp.float32
    )


def norm_parts(values):
    factor = lax.rsqrt(jnp.mean(values * values, axis=-1, keepdims=True) + EPSILON)
    return (values * factor, factor)


def norm_back(grad_out, normed, factor, gain_vec):
    scaled = grad_out * gain_vec
    return factor * (scaled - normed * jnp.mean(scaled * normed, axis=-1, keepdims=True))


def rope_tables(length, head_size):
    half_size = head_size // 2
    frequency = THETA ** (-(2.0 * jnp.arange(half_size, dtype=jnp.float32)) / head_size)
    angles = jnp.arange(length, dtype=jnp.float32)[:, None] * frequency[None, :]
    return (jnp.cos(angles)[:, None, :], jnp.sin(angles)[:, None, :])


def rotate(values, cosine, sine_tab):
    half_size = values.shape[-1] // 2
    first_half = values[..., :half_size]
    second_half = values[..., half_size:]
    return jnp.concatenate(
        [
            first_half * cosine - second_half * sine_tab,
            second_half * cosine + first_half * sine_tab,
        ],
        axis=-1,
    )


def rotate_back(grads_in, cosine, sine_tab):
    half_size = grads_in.shape[-1] // 2
    first_half = grads_in[..., :half_size]
    second_half = grads_in[..., half_size:]
    return jnp.concatenate(
        [
            first_half * cosine + second_half * sine_tab,
            second_half * cosine - first_half * sine_tab,
        ],
        axis=-1,
    )


def block_mask(segments, offset, block_rows, key_count):
    query_pos = offset + jnp.arange(block_rows)
    key_pos = jnp.arange(key_count)
    same_doc = segments[offset : offset + block_rows][:, None] == segments[None, :]
    near_pos = jnp.abs(query_pos[:, None] - key_pos[None, :]) < WINDOW // 2
    return same_doc & near_pos


def block_scores(query_block, key_low, allowed, inv_root):
    scores = (
        jnp.einsum("qhd,khd->hqk", query_block, key_low, preferred_element_type=jnp.float32)
        * inv_root
    )
    return jnp.where(allowed[None], scores, NEG_FILL)


def row_sum(term_fn, tok_rows):
    return lax.psum_scatter(
        term_fn(jnp.int32(0), lax.axis_size(TENSOR) * tok_rows),
        TENSOR,
        scatter_dimension=0,
        tiled=True,
    )


def gather_rows(values):
    return lax.all_gather(values, TENSOR, axis=0, tiled=True)


def from_experts(values):
    return lax.all_to_all(values, DP, split_axis=1, concat_axis=1, tiled=True)


def to_experts(source_rows, slot_token, slot_gate, layout):
    picked = jnp.take(source_rows, slot_token, axis=0, mode="fill", fill_value=0)
    if slot_gate is not None:
        picked = (picked.astype(jnp.float32) * slot_gate[:, None]).astype(jnp.bfloat16)
    picked = picked.reshape(layout + (picked.shape[1],))
    return lax.all_to_all(picked, DP, split_axis=1, concat_axis=1, tiled=True)


def pair_sum(table, weights_low, pair_slots, row_count):
    picked = jnp.take(table, pair_slots.reshape(-1), axis=0, mode="fill", fill_value=0)
    picked = picked.reshape(row_count, pair_slots.shape[1], table.shape[1])
    return jnp.einsum("rk,rkd->rd", weights_low, picked, preferred_element_type=jnp.float32)


def expert_forward(operands):
    rows_in, gate_mat, up_mat, down_mat = operands
    flat_rows = rows_in.reshape(-1, rows_in.shape[-1])
    gated = matmul(flat_rows, gate_mat)
    lifted = matmul(flat_rows, up_mat)
    hidden = (jax.nn.silu(gated) * lifted).astype(jnp.bfloat16)
    result = matmul(hidden, down_mat).astype(jnp.bfloat16)
    return (result.reshape(rows_in.shape), gated, lifted)


def expert_backward(operands):
    rows_in, grad_in, gated, lifted, gate_mat, up_mat, down_mat = operands
    flat_rows = rows_in.reshape(-1, rows_in.shape[-1])
    flat_grad = grad_in.reshape(-1, grad_in.shape[-1])
    gate_sig = jax.nn.sigmoid(gated)
    activated = jax.nn.silu(gated)
    hidden = (activated * lifted).astype(jnp.bfloat16)
    grad_hidden = contract_last(flat_grad, down_mat)
    grad_down = contract_first(hidden, flat_grad)
    grad_gated = (grad_hidden * lifted * gate_sig * (1.0 + gated * (1.0 - gate_sig))).astype(
        jnp.bfloat16
    )
    grad_lifted = (grad_hidden * activated).astype(jnp.bfloat16)
    grad_gate = contract_first(flat_rows, grad_gated)
    grad_up = contract_first(flat_rows, grad_lifted)
    grad_rows = (contract_last(grad_gated, gate_mat) + contract_last(grad_lifted, up_mat)).astype(
        jnp.bfloat16
    )
    return (grad_rows.reshape(rows_in.shape), grad_gate, grad_up, grad_down)


VMEM_BYTES = 60 * 1024 * 1024
COLUMN_CHUNK = 512
GROUP = 2


def select_rows(places_ref, gates_ref, pick_ref, capacity):
    expert_count, seq_len = places_ref.shape[1:]
    slot_range = lax.broadcasted_iota(jnp.int32, (capacity, seq_len), 0).astype(jnp.bfloat16)
    nothing = jnp.zeros((capacity, seq_len), jnp.bfloat16)
    for expert in range(expert_count):
        hit = places_ref[0, expert : expert + 1, :] == slot_range
        if gates_ref is None:
            weight = jnp.ones((capacity, seq_len), jnp.bfloat16)
        else:
            weight = jnp.broadcast_to(gates_ref[0, expert : expert + 1, :], (capacity, seq_len))
        rows = slice(expert * capacity, (expert + 1) * capacity)
        pick_ref[rows, :] = jnp.where(hit, weight, nothing)


def rows_to_slots(pick_ref, rows_ref, slots_ref, pack, capacity):
    width = rows_ref.shape[2]
    expert_count = slots_ref.shape[0]
    for start in range(0, width, COLUMN_CHUNK):
        columns = slice(start, start + COLUMN_CHUNK)
        picked = matmul(pick_ref[...], rows_ref[0, :, columns]).astype(jnp.bfloat16)
        slots_ref[:, pack, :, columns] = picked.reshape(expert_count, capacity, COLUMN_CHUNK)


def slots_to_rows(pick_ref, slots_ref, own_ref, other_ref, pack):
    width = own_ref.shape[3]
    for start in range(0, width, COLUMN_CHUNK):
        columns = slice(start, start + COLUMN_CHUNK)
        slots = slots_ref[:, pack, :, columns].reshape(-1, COLUMN_CHUNK)
        rows = contract_first(pick_ref[...], slots).astype(own_ref.dtype)
        rows = rows.reshape(2, 2, own_ref.shape[2], COLUMN_CHUNK)
        own_ref[0, :, :, columns] = rows[:, 0]
        other_ref[0, :, :, columns] = rows[:, 1]


def cot_kernel(
    packs, steps, capacity, table, places, gates, rows, down, slots_out, hidden_out, slots, pick
):
    step = pl.program_id(0)

    @pl.when(step < packs)
    def _():
        select_rows(places, gates, pick, capacity)
        rows_to_slots(pick, rows, slots, step, capacity)

    @pl.when(step >= packs)
    def _():
        for member in range(down.shape[0]):
            block = slots[(step - packs) * down.shape[0] + member].reshape(packs * capacity, -1)
            slots_out[member] = block
            hidden_out[member] = contract_last(block, down[member])


def piece_copies(own, other, rows, sems, pack):
    half_rows = own.shape[1]
    copies = []
    for far in range(2):
        for core, source in enumerate((own, other)):
            for half, index in enumerate((4 * far + pack, 2 + 4 * pack + far)):
                start = ((far * 2 + core) * 2 + half) * half_rows
                copies.append(
                    pltpu.make_async_copy(
                        source.at[index],
                        rows.at[pack, pl.ds(start, half_rows)],
                        sems.at[pack * 8 + len(copies)],
                    )
                )
    return copies


def row_kernel(
    packs, steps, capacity, places, own, other, both, grad_hidden,
    slots_out, hidden_out, grads_out, rows_own, rows_other,
    rows, slots, grads, pick, sems,
):
    step = pl.program_id(0)
    half = hidden_out.shape[2]

    @pl.when(step == 0)
    def _():
        for pack in range(packs):
            for copy in piece_copies(own, other, rows, sems, pack):
                copy.start()
        for pack in range(packs):
            select_rows(places.at[pl.ds(pack, 1)], None, pick.at[pack], capacity)

    for pack in range(packs):

        @pl.when(step == pack)
        def _(pack=pack):
            for copy in piece_copies(own, other, rows, sems, pack):
                copy.wait()
            rows_to_slots(pick.at[pack], rows.at[pl.ds(pack, 1)], slots, pack, capacity)

    @pl.when((step >= packs) & (step < packs + steps))
    def _():
        for member in range(both.shape[0]):
            expert = (step - packs) * both.shape[0] + member
            block = slots[expert].reshape(packs * capacity, -1)
            slots_out[member] = block
            product = matmul(block, both[member])
            gated, lifted = product[:, :half], product[:, half:]
            sig = 1.0 / (1.0 + jnp.exp(-gated))
            active = gated * sig
            hidden_out[member] = (active * lifted).astype(jnp.bfloat16)
            above = grad_hidden[member]
            grad_gated = above * lifted * sig * (1.0 + gated * (1.0 - sig))
            joined = jnp.concatenate([grad_gated, above * active], axis=1).astype(jnp.bfloat16)
            grads_out[member] = joined
            back = contract_last(joined, both[member])
            grads[expert] = back.astype(jnp.bfloat16).reshape(packs, capacity, -1)

    for pack in range(packs):

        @pl.when(step == packs + steps + pack)
        def _(pack=pack):
            slots_to_rows(pick.at[pack], grads, rows_own, rows_other, pack)


def mix_kernel(
    packs, steps, capacity, table, places, gates, hidden, down, rows_own, rows_other, results, pick
):
    step = pl.program_id(0)

    @pl.when(step < steps)
    def _():
        for member in range(down.shape[0]):
            result = matmul(hidden[member], down[member]).astype(jnp.bfloat16)
            results[step * down.shape[0] + member] = result.reshape(packs, capacity, -1)

    @pl.when(step >= steps)
    def _():
        select_rows(places, gates, pick, capacity)
        slots_to_rows(pick, results, rows_own, rows_other, (step - steps) ^ table[0])


def weight_kernel(planes, *refs):
    slots, grads, hidden, above = (
        jnp.concatenate([ref[0] for ref in refs[i * planes : (i + 1) * planes]]) for i in range(4)
    )
    gate_out, up_out, down_out = refs[-3:]
    half = gate_out.shape[2]
    both = contract_first(slots, above)
    gate_out[0] = both[:, :half]
    up_out[0] = both[:, half:]
    down_out[0] = contract_first(hidden, grads)


def block(shape, place, count=1):
    tail = (0,) * (len(shape) - 1)
    return pl.BlockSpec((count,) + tuple(shape[1:]), lambda *ids: (place(*ids),) + tail)


def staged(first, count):
    return lambda step, *rest: jnp.clip(step - first, 0, count - 1)


def shape_of(shape, kind):
    return jax.ShapeDtypeStruct(shape, kind)


def call(kernel, steps, specs, out_specs, out_shape, scratch, flops, prefetch=0, aliases={}):
    return pl.pallas_call(
        kernel,
        grid_spec=pltpu.PrefetchScalarGridSpec(
            num_scalar_prefetch=prefetch,
            grid=(steps,),
            in_specs=specs,
            out_specs=out_specs,
            scratch_shapes=scratch,
        ),
        out_shape=out_shape,
        input_output_aliases=aliases,
        cost_estimate=pl.CostEstimate(
            flops=flops, transcendentals=0, bytes_accessed=flops // 500
        ),
        compiler_params=pltpu.CompilerParams(
            dimension_semantics=("arbitrary",), vmem_limit_bytes=VMEM_BYTES
        ),
    )


def cot_slots(table, places, gates, rows, down, capacity):
    packs = table.shape[0]
    _, seq_len, width = rows.shape
    experts, hidden_width, _ = down.shape
    slot_rows = packs * capacity
    group = math.gcd(experts, GROUP)
    steps = experts // group
    by_pack, by_expert = staged(0, packs), staged(packs, steps)
    listed = lambda step, numbers: numbers[by_pack(step)]
    out_shape = [
        shape_of((experts, slot_rows, width), jnp.bfloat16),
        shape_of((experts, slot_rows, hidden_width), jnp.float32),
    ]
    return call(
        functools.partial(cot_kernel, packs, steps, capacity),
        packs + steps,
        [
            block(places.shape, listed), block(gates.shape, listed), block(rows.shape, listed),
            block(down.shape, by_expert, group),
        ],
        [block(out.shape, by_expert, group) for out in out_shape],
        out_shape,
        [
            pltpu.VMEM((experts, packs, capacity, width), jnp.bfloat16),
            pltpu.VMEM((experts * capacity, seq_len), jnp.bfloat16),
        ],
        2 * experts * slot_rows * width * (seq_len + hidden_width),
        1,
    )(table, places, gates, rows, down)


def row_slots(places, own, other, both, grad_hidden, capacity):
    packs, _, seq_len = places.shape
    experts, width, hidden_width = both.shape
    slot_rows = packs * capacity
    group = math.gcd(experts, GROUP)
    steps = experts // group
    middle, last = staged(packs, steps), staged(packs + steps, packs)
    part = shape_of((packs, 2, seq_len // 4, width), jnp.bfloat16)
    out_shape = [
        shape_of((experts, slot_rows, width), jnp.bfloat16),
        shape_of((experts, slot_rows, hidden_width // 2), jnp.bfloat16),
        shape_of((experts, slot_rows, hidden_width), jnp.bfloat16),
        part, part,
    ]
    anywhere = pl.BlockSpec(memory_space=pl.ANY)
    return call(
        functools.partial(row_kernel, packs, steps, capacity),
        2 * packs + steps,
        [
            block(places.shape, lambda step: 0, packs), anywhere, anywhere,
            block(both.shape, middle, group), block(grad_hidden.shape, middle, group),
        ],
        [block(out.shape, middle, group) for out in out_shape[:3]] + [block(part.shape, last)] * 2,
        out_shape,
        [
            pltpu.VMEM((packs, seq_len, width), jnp.bfloat16),
            pltpu.VMEM((experts, packs, capacity, width), jnp.bfloat16),
            pltpu.VMEM((experts, packs, capacity, width), jnp.bfloat16),
            pltpu.VMEM((packs, experts * capacity, seq_len), jnp.bfloat16),
            pltpu.SemaphoreType.DMA((8 * packs,)),
        ],
        4 * experts * slot_rows * width * (seq_len + hidden_width),
    )(places, own, other, both, grad_hidden)


def mix_rows(table, places, gates, hidden, down, capacity):
    packs, _, seq_len = places.shape
    experts, hidden_width, width = down.shape
    group = math.gcd(experts, GROUP)
    steps = experts // group
    first, last = staged(0, steps), staged(steps, packs)
    listed = lambda step, numbers: numbers[1] * steps + first(step)
    part = shape_of((packs, 2, seq_len // 4, width), jnp.bfloat16)
    return call(
        functools.partial(mix_kernel, packs, steps, capacity),
        packs + steps,
        [
            block(places.shape, last), block(gates.shape, last),
            block(hidden.shape, listed, group), block(down.shape, first, group),
        ],
        [block(part.shape, last)] * 2,
        [part, part],
        [
            pltpu.VMEM((experts, packs, capacity, width), jnp.bfloat16),
            pltpu.VMEM((experts * capacity, seq_len), jnp.bfloat16),
        ],
        2 * experts * packs * capacity * width * (seq_len + hidden_width),
        1,
    )(table, places, gates, hidden, down)


def weight_grads(first, count, slots, hidden, grads, above, earlier=()):
    planes = len(slots)
    operands = [*slots, *grads, *hidden, *above]
    experts, _, width = slots[0].shape
    hidden_width = hidden[0].shape[2]
    each = lambda step: step + first
    out_shape = [
        shape_of((experts, width, hidden_width), jnp.float32),
        shape_of((experts, width, hidden_width), jnp.float32),
        shape_of((experts, hidden_width, width), jnp.float32),
    ]
    return call(
        functools.partial(weight_kernel, planes),
        count,
        [block(operand.shape, each) for operand in operands]
        + [pl.BlockSpec(memory_space=pl.ANY)] * len(earlier),
        [block(out.shape, each) for out in out_shape],
        out_shape,
        [],
        6 * planes * slots[0].shape[1] * count * width * hidden_width,
        aliases={len(operands) + index: index for index in range(len(earlier))},
    )(*operands, *earlier)


def swapped(values, axis, bit):
    count = lax.axis_size(axis)
    return lax.ppermute(values, axis, [(i, i ^ bit) for i in range(count)])


def far_side(values):
    return swapped(values, TENSOR, 2)


def far_core(values):
    return swapped(values, TENSOR, 1)


def far_pack(values):
    return swapped(values, DP, 1)


def next_plane(values):
    count = lax.axis_size(DP)
    return lax.ppermute(values, DP, [(i, (i + 2) % count) for i in range(count)])


def spread_all(values, small, work):
    planes = lax.axis_size("plane")
    half_rows = values.shape[0] // 2
    first = lambda rows: (far_pack(rows[:half_rows]), far_side(rows[half_rows:]))
    small, values = tied(small, values)
    (across_pack, across_side), following = lax.optimization_barrier(
        (first(values), next_plane(values))
    )
    pieces, made = [], []
    for plane in range(planes):
        upper = jnp.stack([values[:half_rows], across_pack])
        lower = jnp.stack([values[half_rows:], across_side])
        small, (upper, lower, values) = tied(small, (upper, lower, following))
        moved = [
            far_side(upper),
            far_pack(lower),
            first(values) if plane + 1 < planes else ((), ()),
            next_plane(values) if plane + 2 < planes else (),
            far_core(pieces[-1]) if plane else (),
            work(plane, small),
        ]
        upper_far, lower_far, (across_pack, across_side), following, other, result = (
            lax.optimization_barrier(moved)
        )
        if plane:
            pieces[-1] = (pieces[-1], other)
        made.append(result)
        pieces.append(jnp.concatenate([upper, lower, upper_far, lower_far]))
    pieces[-1] = (pieces[-1], far_core(pieces[-1]))
    return pieces, made


def plane_order():
    packs = lax.axis_size(DP)
    planes = packs // 2
    index = lax.axis_index(DP)
    return jnp.stack(
        [
            ((index // 2 + planes - plane) % planes) * 2 + (index % 2 ^ near)
            for plane in range(planes)
            for near in range(2)
        ]
    )


def place_kernel(by_column, order, *refs):
    *pieces, whole, sems = refs
    copies = []
    for index, piece in enumerate(pieces):
        target = None if by_column else whole.at[order[index]]
        if by_column:
            width = piece.shape[1]
            target = whole.at[:, pl.ds(pl.multiple_of(order[index] * width, 128), width)]
        copies.append(pltpu.make_async_copy(piece, target, sems.at[index]))
        copies[-1].start()
    for copy in copies:
        copy.wait()


def laid(pieces, order, by_column=False):
    count = len(pieces)
    rows, columns = pieces[0].shape
    shape = (rows, count * columns) if by_column else (count, rows, columns)
    anywhere = pl.BlockSpec(memory_space=pl.ANY)
    return call(
        functools.partial(place_kernel, by_column),
        1,
        [anywhere] * count,
        pl.BlockSpec(memory_space=pltpu.VMEM),
        shape_of(shape, pieces[0].dtype),
        [pltpu.SemaphoreType.DMA((count,))],
        1000,
        1,
    )(order, *pieces)


def fold_packs(values):
    order = plane_order()
    take = lambda index: lax.dynamic_index_in_dim(values, order[index], 0, keepdims=False)
    near = [added(take(2 * i), far_pack(take(2 * i + 1))) for i in range(values.shape[0] // 2)]
    summed = near[1]
    for part in near[2:]:
        summed = added(next_plane(summed), part)
    return added(next_plane(summed), near[0], jnp.float32)


def laid_sides(pieces):
    order = lax.axis_index(TENSOR) ^ jnp.arange(len(pieces), dtype=jnp.int32)
    return laid(pieces, order).reshape((-1,) + pieces[0].shape[1:])


def gather_sides(values):
    across = far_side(values)
    return laid_sides([values, far_core(values), across, far_core(across)])


def fold_sides(values):
    split = values.astype(jnp.bfloat16).reshape((4, -1) + values.shape[1:])
    take = lambda bits: lax.dynamic_index_in_dim(
        split, lax.axis_index(TENSOR) ^ bits, 0, keepdims=False
    )
    far = added(take(2), far_core(take(3)))
    near = added(take(0), far_core(take(1)))
    return added(near, far_side(far), jnp.float32)


def fold_both(weights, rows):
    order = plane_order()
    planes = weights.shape[0] // 2
    take = lambda index: lax.dynamic_index_in_dim(weights, order[index], 0, keepdims=False)
    split = rows.astype(jnp.bfloat16).reshape((4, -1) + rows.shape[1:])
    mine = lax.axis_index(TENSOR)
    pick = lambda bits: lax.dynamic_index_in_dim(split, mine ^ bits, 0, keepdims=False)
    summed, total = None, None
    for turn, plane in enumerate([*range(1, planes), 0]):
        moved = [far_pack(take(2 * plane + 1)), () if summed is None else next_plane(summed)]
        if turn == 0:
            moved += [far_core(pick(3)), far_core(pick(1))]
        if turn == 1:
            moved += [far_side(far)]
        across, passed, *arrived = lax.optimization_barrier(moved)
        if turn == 0:
            far, close = added(pick(2), arrived[0]), added(pick(0), arrived[1])
        if turn == 1:
            total = added(close, arrived[0], jnp.float32)
        near = added(take(2 * plane), across)
        kind = jnp.float32 if turn + 1 == planes else jnp.bfloat16
        summed = near if turn == 0 else added(passed, near, kind)
    return summed, total


def gather_both(weights, outer, rows):
    pieces, outer_pieces, row_pieces, values = [], [], [rows], (weights, outer)
    planes = lax.axis_size("plane")
    for plane in range(planes):
        moved = [tuple(far_pack(value) for value in values), ()]
        if plane + 1 < planes:
            moved[1] = tuple(next_plane(value) for value in values)
        if plane == 0:
            moved += [far_core(rows), far_side(rows)]
        if plane == 1:
            moved += [far_core(row_pieces[2])]
        across, following, *arrived = lax.optimization_barrier(moved)
        pieces += [values[0], across[0]]
        outer_pieces += [values[1], across[1]]
        row_pieces += arrived
        values = following
    order = plane_order()
    return laid(pieces, order), laid(outer_pieces, order, True), laid_sides(row_pieces)


def sum_everywhere(values):
    for axis in (TENSOR, DP):
        bit = 1
        while bit < lax.axis_size(axis):
            values = values + swapped(values, axis, bit)
            bit *= 2
    return values


def added(left, right, kind=jnp.bfloat16):
    return (left.astype(jnp.float32) + right.astype(jnp.float32)).astype(kind)


def fold_first(own, arrived):
    half_rows = own.shape[2] // 2
    upper, lower = slice(None, half_rows), slice(half_rows, None)
    return (
        added(own[:, 0, upper], arrived[:, 0, upper]),
        added(own[0, :, lower], arrived[0, :, lower]),
        added(own[:, 1, upper], arrived[:, 1, upper]),
        added(own[1, :, lower], arrived[1, :, lower]),
    )


def tied(small, values):
    return lax.optimization_barrier((small, values))


def gather_tables(expert_ids, gate_values, segment_ids):
    top_count = expert_ids.shape[1]
    tables = jnp.concatenate(
        [expert_ids.T.astype(jnp.bfloat16), gate_values.T, segment_ids.astype(jnp.bfloat16)]
    )[None]
    for axis in (TENSOR, DP):
        bit = 1
        while bit < lax.axis_size(axis):
            tables = jnp.concatenate([tables, swapped(tables, axis, bit)])
            bit *= 2
        if axis == TENSOR:
            sides = jnp.arange(tables.shape[0], dtype=jnp.int32) ^ lax.axis_index(TENSOR)
            segments = jnp.take(tables[:, -1], sides, axis=0).reshape(-1)
    devices = jnp.arange(tables.shape[0], dtype=jnp.int32)
    own = lax.axis_index(DP) * lax.axis_size(TENSOR) + lax.axis_index(TENSOR)
    tables = jnp.take(tables, devices ^ own, axis=0)
    all_ids, all_gates = tables[:, :top_count], tables[:, top_count : 2 * top_count]
    return all_ids.astype(jnp.int32), all_gates, segments.astype(jnp.int32)


def routing(all_ids, all_gates, local_experts, capacity):
    packs = lax.axis_size(DP)
    first = lax.axis_index(DP) * local_experts
    wanted = first + jnp.arange(local_experts, dtype=jnp.int32)

    def by_pack(values):
        top_count, tok_rows = values.shape[1:]
        ordered = values.reshape(packs, -1, top_count, tok_rows).transpose(0, 2, 1, 3)
        return ordered.reshape(packs, top_count, -1)

    matches = by_pack(all_ids)[:, :, None, :] == wanted[None, None, :, None]
    pair_gates = by_pack(all_gates).astype(jnp.float32)
    member = jnp.any(matches, axis=1)
    gates = jnp.sum(jnp.where(matches, pair_gates[:, :, None, :], 0.0), axis=1)
    order = jnp.arange(member.shape[2], dtype=jnp.int32)
    earlier = (order[:, None] < order[None, :]).astype(jnp.bfloat16)
    flat = member.reshape(packs * local_experts, -1).astype(jnp.bfloat16)
    before = matmul(flat, earlier).astype(jnp.int32).reshape(member.shape)
    places = jnp.where(member & (before < capacity), before, -1)
    return places.astype(jnp.bfloat16), gates.astype(jnp.bfloat16)


def experts_by_exchange(
    second_in, cotangent, expert_ids, gate_values, w_gate, w_up, w_down, middle, capacity
):
    tok_rows, model_width = second_in.shape
    tensor_count = lax.axis_size(TENSOR)
    data_count = lax.axis_size(DP)
    local_experts = w_gate.shape[0]
    all_experts = local_experts * data_count
    top_count = expert_ids.shape[1]
    seq_len = tok_rows * tensor_count
    pack_cot, pack_ids, pack_gates = (
        gather_rows(cotangent), gather_rows(expert_ids), gather_rows(gate_values)
    )
    pack_second = gather_rows(second_in)
    expert_range = jnp.arange(all_experts, dtype=jnp.int32)
    matches = pack_ids[:, :, None] == expert_range[None, None, :]
    token_counts = jnp.sum(matches.astype(jnp.float32), axis=1).astype(jnp.bfloat16)
    token_range = jnp.arange(seq_len, dtype=jnp.int32)
    earlier = (token_range[:, None] > token_range[None, :]).astype(jnp.bfloat16)
    before = matmul(earlier, token_counts)
    places = (
        jnp.sum(jnp.where(matches, before[:, None, :], 0.0), axis=2).astype(jnp.int32).reshape(-1)
    )
    flat_ids = pack_ids.reshape(-1)
    owners = flat_ids // local_experts
    local_index = flat_ids % local_experts
    dump_slot = all_experts * capacity
    slot_index = jnp.where(
        places < capacity,
        local_index * (data_count * capacity) + owners * capacity + places,
        dump_slot,
    ).astype(jnp.int32)
    pair_token = jnp.arange(seq_len * top_count) // top_count
    slot_token = (
        jnp.full((dump_slot + 1,), seq_len, jnp.int32).at[slot_index].set(pair_token)[:dump_slot]
    )
    pair_gates = pack_gates.astype(jnp.float32)
    slot_gate = (
        jnp.zeros((dump_slot + 1,), jnp.float32)
        .at[slot_index]
        .set(pair_gates.reshape(-1))[:dump_slot]
    )
    pair_slots = slot_index.reshape(seq_len, top_count)
    layout = (local_experts, data_count, capacity)
    arrived_rows = to_experts(pack_second, slot_token, None, layout)
    expert_out, gated_all, lifted_all = lax.map(
        expert_forward, (arrived_rows, w_gate, w_up, w_down)
    )
    returned = from_experts(expert_out).reshape(-1, model_width)

    def combine_term(offset, row_count):
        return pair_sum(returned, pack_gates, pair_slots, row_count)

    outputs = middle + row_sum(combine_term, tok_rows)
    grad_arrived = to_experts(pack_cot, slot_token, slot_gate, layout)
    grad_rows_all, grad_w_gate, grad_w_up, grad_w_down = lax.map(
        expert_backward, (arrived_rows, grad_arrived, gated_all, lifted_all, w_gate, w_up, w_down)
    )
    returned_grad = from_experts(grad_rows_all).reshape(-1, model_width)
    unit_gates = jnp.ones_like(pack_gates)

    def dispatch_term(offset, row_count):
        return pair_sum(returned_grad, unit_gates, pair_slots, row_count)

    grad_second = row_sum(dispatch_term, tok_rows)
    return outputs, grad_second, grad_w_gate, grad_w_up, grad_w_down


class Folding:
    def __init__(self, order):
        self.order, self.planes, self.ready = order, {}, {}
        self.summed, self.count = None, 0

    def begin(self, plane, own, other):
        self.planes[plane] = (0, (own, other))

    def turn(self, small, work):
        small, (planes, summed) = tied(
            small, ({plane: values for plane, (_, values) in self.planes.items()}, self.summed)
        )
        sent = {}
        for plane, values in planes.items():
            stage = self.planes[plane][0]
            if stage == 0:
                sent[plane] = (far_core(values[1]),)
            elif stage == 1:
                sent[plane] = (far_side(values[2]), far_pack(values[3]))
            else:
                sent[plane] = (far_pack(values[2]), far_side(values[3]))
        passed = None if summed is None else next_plane(summed)
        sent, passed, result = lax.optimization_barrier((sent, passed, work(small)))
        for plane, values in planes.items():
            stage, arrived = self.planes[plane][0], sent[plane]
            if stage == 0:
                made = fold_first(values[0], *arrived)
            elif stage == 1:
                upper, lower = added(values[0], arrived[0]), added(values[1], arrived[1])
                made = (upper[0], lower[0], upper[1], lower[1])
            else:
                self.ready[plane] = jnp.concatenate(
                    [added(values[0], arrived[0]), added(values[1], arrived[1])]
                )
            if stage < 2:
                self.planes[plane] = (stage + 1, made)
            else:
                del self.planes[plane]
        following = self.order[self.count] if self.count < len(self.order) else None
        if following in self.ready:
            last = self.count + 1 == len(self.order)
            self.summed = self.ready[following]
            if passed is not None:
                kind = jnp.float32 if last else jnp.bfloat16
                self.summed = added(passed, self.summed, kind)
            self.count += 1
        return result

    def done(self):
        return self.count == len(self.order)


def experts_by_gather(second_in, all_cot, places, gates, w_gate, w_up, w_down, capacity):
    packs, local_experts, seq_len = places.shape
    tensor_count = lax.axis_size(TENSOR)
    planes = packs // 2
    pack_order = plane_order()
    side_index = lax.axis_index(TENSOR)
    quarter_order = side_index ^ jnp.arange(tensor_count, dtype=jnp.int32)

    def as_met(values, by_pack, by_quarter):
        split = values.reshape(packs, local_experts, tensor_count, -1)
        split = jnp.take(jnp.take(split, by_pack, axis=0), by_quarter, axis=2)
        return split.reshape(values.shape)

    near_places = as_met(places, pack_order, quarter_order)
    core_order = lax.axis_index("core") ^ jnp.arange(tensor_count, dtype=jnp.int32)
    mix_places = as_met(places, jnp.arange(packs, dtype=jnp.int32), core_order)
    mix_gates = as_met(gates, jnp.arange(packs, dtype=jnp.int32), core_order)
    w_both = jnp.concatenate([w_gate, w_up], axis=2)
    pairs = [slice(plane * 2, plane * 2 + 2) for plane in range(planes)]

    def cot_work(plane, order):
        return cot_slots(order[pairs[plane]], places, gates, all_cot, w_down, capacity)

    pieces, made = spread_all(second_in, pack_order, cot_work)
    order = [*range(1, planes), 0]
    kept, parts, folding = {}, {}, Folding(order)

    def row_work(plane, near):
        return row_slots(near, *pieces[plane], w_both, made[plane][1], capacity)

    for plane in range(planes):
        near = near_places[pairs[plane]]
        if plane:
            result = folding.turn(near, functools.partial(row_work, plane))
        else:
            result = row_work(plane, near)
        slots, hidden, above, *part = result
        folding.begin(plane, *part)
        kept[plane] = (slots, hidden, made[plane][0], above)
    hidden_all = jnp.concatenate([kept[plane][1] for plane in range(planes)])
    tables = jnp.stack(
        [
            jnp.stack([lax.axis_index("pack"), (lax.axis_index("plane") + planes - plane) % planes])
            for plane in range(planes)
        ]
    )

    def mix_work(plane, table):
        pair = pairs[plane]
        return mix_rows(table[plane], mix_places[pair], mix_gates[pair], hidden_all, w_down, capacity)

    def cross():
        return [far_core(parts[plane][1]) for plane in parts if plane not in crossed]

    def mix_turn(some, table):
        return [mix_work(plane, table) for plane in some], cross()

    crossed = {}
    for start in range(0, planes, 2):
        some = order[start : start + 2]
        waiting = [plane for plane in parts if plane not in crossed]
        results, arrived = folding.turn(tables, functools.partial(mix_turn, some))
        crossed.update(zip(waiting, arrived))
        parts.update(zip(some, results))
    kept = [kept[plane] for plane in range(planes)]
    weight_parts, next_expert = (), 0
    part_size = math.gcd(local_experts, GROUP)

    def weight_turn(count, small):
        state, (held, weights) = next_expert, small
        for _ in range(count):
            if state < local_experts:
                weights = weight_grads(state, part_size, *zip(*held), weights)
                state += part_size
        return weights, cross()

    for count in (2, 1, *[0] * planes):
        if folding.done():
            break
        waiting = [plane for plane in parts if plane not in crossed]
        weight_parts, arrived = folding.turn(
            (kept, weight_parts), functools.partial(weight_turn, count)
        )
        next_expert = min(next_expert + count * part_size, local_experts)
        crossed.update(zip(waiting, arrived))
        if len(crossed) == planes and waiting:
            whole = jnp.stack(
                [added(parts[plane][0], crossed[plane]) for plane in range(planes)]
            )
            whole = whole.reshape(planes, -1, whole.shape[-1])
            whole = lax.psum_scatter(whole, ("pack", "side"), scatter_dimension=1, tiled=True)
    rest = (kept, weight_parts, next_expert, part_size)
    return folding.summed, whole, rest


def shards(
    inputs,
    segment_ids,
    expert_ids,
    gate_values,
    attn_gain,
    query_gain,
    key_gain,
    w_query,
    w_key,
    w_value,
    w_output,
    ffn_gain,
    w_gate,
    w_up,
    w_down,
    cotangent,
):
    tok_rows, model_width = inputs.shape
    head_size = query_gain.shape[0]
    tensor_count = lax.axis_size(TENSOR)
    data_count = lax.axis_size(DP)
    local_experts = w_gate.shape[0]
    all_experts = local_experts * data_count
    top_count = expert_ids.shape[1]
    seq_len = tok_rows * tensor_count
    capacity = seq_len * top_count // all_experts
    inv_root = head_size ** (-0.5)
    by_gather = (
        seq_len <= local_experts * capacity
        and tensor_count == 4
        and data_count > 2
        and data_count & (data_count - 1) == 0
        and all_experts <= 256
    )
    if by_gather:
        axes = (*DP, *TENSOR)
        all_ids, all_gates, segments = gather_tables(expert_ids, gate_values, segment_ids)
        places, gates = routing(all_ids, all_gates, local_experts, capacity)
    inputs_f32 = inputs.astype(jnp.float32)
    normed_one, factor_one = norm_parts(inputs_f32)
    first_in = (normed_one * attn_gain).astype(jnp.bfloat16)
    if by_gather:
        side_sum, side_gather = fold_sides, gather_sides
        local_width = w_query.shape[1]
        w_in = jnp.concatenate([w_query, w_key, w_value], axis=1)
        full_in, full_output, pack_in = gather_both(w_in, w_output, first_in)
        full_in, cotangent = tied(full_in, cotangent)
        all_cot = lax.all_gather(cotangent, axes, axis=0, tiled=True)
        all_cot = all_cot.reshape(data_count, seq_len, model_width)
        full_in = full_in.reshape(model_width, -1)
        full_query, full_key, full_value = (
            full_in[:, index * local_width : (index + 1) * local_width] for index in range(3)
        )
    else:
        side_sum, side_gather = lambda term: row_sum(lambda *_: term, tok_rows), gather_rows
        segments = lax.all_gather(segment_ids, TENSOR, axis=1, tiled=True)[0]
        full_query, full_key, full_value, full_output = (
            lax.all_gather(w_query, DP, axis=0, tiled=True),
            lax.all_gather(w_key, DP, axis=0, tiled=True),
            lax.all_gather(w_value, DP, axis=0, tiled=True),
            lax.all_gather(w_output, DP, axis=1, tiled=True),
        )
        pack_in = side_gather(first_in)
    query_pre = matmul(pack_in, full_query)
    key_pre = matmul(pack_in, full_key)
    value_low = matmul(pack_in, full_value).astype(jnp.bfloat16)
    head_count = query_pre.shape[1] // head_size
    cosine, sine_tab = rope_tables(seq_len, head_size)
    query_norm, query_factor = norm_parts(query_pre.reshape(seq_len, head_count, head_size))
    key_norm, key_factor = norm_parts(key_pre.reshape(seq_len, head_count, head_size))
    query_low = rotate(query_norm * query_gain, cosine, sine_tab).astype(jnp.bfloat16)
    key_low = rotate(key_norm * key_gain, cosine, sine_tab).astype(jnp.bfloat16)
    value_heads = value_low.reshape(seq_len, head_count, head_size)
    block_rows = min(512, seq_len)
    block_total = seq_len // block_rows
    masks = []
    mixture_parts = []
    lse_parts = []
    for block_index in range(block_total):
        offset = block_index * block_rows
        allowed = block_mask(segments, offset, block_rows, seq_len)
        masks.append(allowed)
        scores = block_scores(query_low[offset : offset + block_rows], key_low, allowed, inv_root)
        top_score = jnp.max(scores, axis=-1, keepdims=True)
        raw_weights = jnp.exp(scores - top_score)
        totals = jnp.sum(raw_weights, axis=-1, keepdims=True)
        weights_low = (raw_weights / totals).astype(jnp.bfloat16)
        mixture_parts.append(
            jnp.einsum(
                "hqk,khd->qhd", weights_low, value_heads, preferred_element_type=jnp.float32
            ).astype(jnp.bfloat16)
        )
        lse_parts.append(top_score + jnp.log(totals))
    mixture = jnp.concatenate(mixture_parts, axis=0).reshape(seq_len, head_count * head_size)

    middle = inputs_f32 + side_sum(matmul(mixture, full_output))
    normed_two, factor_two = norm_parts(middle)
    second_in = (normed_two * ffn_gain).astype(jnp.bfloat16)
    if by_gather:
        grad_second, mixed, rest = experts_by_gather(
            second_in, all_cot, places, gates, w_gate, w_up, w_down, capacity
        )
    else:
        outputs, grad_second, grad_w_gate, grad_w_up, grad_w_down = experts_by_exchange(
            second_in, cotangent, expert_ids, gate_values, w_gate, w_up, w_down, middle, capacity
        )
    ffn_gain_part = jnp.sum(grad_second * normed_two, axis=0)
    grad_middle = cotangent.astype(jnp.float32) + norm_back(
        grad_second, normed_two, factor_two, ffn_gain
    )
    grad_attended = grad_middle.astype(jnp.bfloat16)
    if by_gather:
        kept, weight_parts, next_expert, part_size = rest
        (kept, weight_parts), grad_attended = tied((kept, weight_parts), grad_attended)
        moved = [far_core(grad_attended), far_side(grad_attended)]
        for first in range(next_expert, local_experts, part_size):
            weight_parts = weight_grads(first, part_size, *zip(*kept), weight_parts)
        grad_w_gate, grad_w_up, grad_w_down = weight_parts
        near, across, weight_parts = lax.optimization_barrier((*moved, weight_parts))
        grad_w_gate, grad_w_up, grad_w_down = weight_parts
        pack_grad = laid_sides([grad_attended, near, across, far_core(across)])
    else:
        pack_grad = side_gather(grad_attended)
    output_part = contract_first(mixture, pack_grad)
    grad_mixture = (
        contract_last(pack_grad, full_output)
        .astype(jnp.bfloat16)
        .reshape(seq_len, head_count, head_size)
    )
    grad_query_parts = []
    grad_key_sum = jnp.zeros((seq_len, head_count, head_size), jnp.float32)
    grad_value_sum = jnp.zeros((seq_len, head_count, head_size), jnp.float32)
    for block_index in range(block_total):
        offset = block_index * block_rows
        query_block = query_low[offset : offset + block_rows]
        grad_block = grad_mixture[offset : offset + block_rows]
        scores = block_scores(query_block, key_low, masks[block_index], inv_root)
        prob_rows = jnp.exp(scores - lse_parts[block_index])
        grad_probs = jnp.einsum(
            "qhd,khd->hqk", grad_block, value_heads, preferred_element_type=jnp.float32
        )
        row_delta = jnp.sum(grad_probs * prob_rows, axis=-1, keepdims=True)
        grad_scores = (prob_rows * (grad_probs - row_delta)).astype(jnp.bfloat16)
        grad_query_parts.append(
            jnp.einsum("hqk,khd->qhd", grad_scores, key_low, preferred_element_type=jnp.float32)
            * inv_root
        )
        grad_key_sum = (
            grad_key_sum
            + jnp.einsum(
                "hqk,qhd->khd", grad_scores, query_block, preferred_element_type=jnp.float32
            )
            * inv_root
        )
        grad_value_sum = grad_value_sum + jnp.einsum(
            "hqk,qhd->khd",
            prob_rows.astype(jnp.bfloat16),
            grad_block,
            preferred_element_type=jnp.float32,
        )
    grad_query_norm = rotate_back(jnp.concatenate(grad_query_parts, axis=0), cosine, sine_tab)
    grad_key_norm = rotate_back(grad_key_sum, cosine, sine_tab)
    query_gain_part = jnp.sum(grad_query_norm * query_norm, axis=(0, 1))
    key_gain_part = jnp.sum(grad_key_norm * key_norm, axis=(0, 1))
    grad_query_pre = (
        norm_back(grad_query_norm, query_norm, query_factor, query_gain)
        .reshape(seq_len, -1)
        .astype(jnp.bfloat16)
    )
    grad_key_pre = (
        norm_back(grad_key_norm, key_norm, key_factor, key_gain)
        .reshape(seq_len, -1)
        .astype(jnp.bfloat16)
    )
    grad_value_low = grad_value_sum.reshape(seq_len, -1).astype(jnp.bfloat16)
    query_part = contract_first(pack_in, grad_query_pre)
    key_part = contract_first(pack_in, grad_key_pre)
    value_part = contract_first(pack_in, grad_value_low)

    total_term = contract_last(grad_query_pre, full_query)
    total_term = total_term + contract_last(grad_key_pre, full_key)
    total_term = total_term + contract_last(grad_value_low, full_value)
    if by_gather:
        by_column = output_part.astype(jnp.bfloat16).reshape(local_width, data_count, -1)
        grad_w_output = fold_packs(by_column.transpose(1, 0, 2))
        in_part = jnp.concatenate([query_part, key_part, value_part], axis=1)
        in_part = in_part.astype(jnp.bfloat16).reshape(data_count, -1, 3 * local_width)
        mixed, in_part = tied(mixed, in_part)
        mixed = lax.psum_scatter(mixed, "plane", scatter_dimension=0, tiled=True)
        grad_in, grad_first = fold_both(in_part, total_term)
        mixed, grad_in = tied(mixed, grad_in)
    else:
        grad_first = side_sum(total_term)
    attn_gain_part = jnp.sum(grad_first * normed_one, axis=0)
    grad_inputs = grad_middle + norm_back(grad_first, normed_one, factor_one, attn_gain)
    gain_parts = (attn_gain_part, ffn_gain_part, query_gain_part, key_gain_part)
    if by_gather:
        grad_w_query, grad_w_key, grad_w_value = (
            grad_in[:, index * local_width : (index + 1) * local_width] for index in range(3)
        )
        outputs = middle + mixed[0].astype(jnp.float32)
        late = sum_everywhere(attn_gain_part)
        early = sum_everywhere(jnp.concatenate(gain_parts[1:]))
        splits = (model_width, model_width + head_size)
        gain_sums = (late, *jnp.split(early, splits))
    else:
        grad_w_query, grad_w_key, grad_w_value, grad_w_output = (
            lax.psum_scatter(
                part.astype(jnp.bfloat16), DP, scatter_dimension=along, tiled=True
            ).astype(jnp.float32)
            for part, along in ((query_part, 0), (key_part, 0), (value_part, 0), (output_part, 1))
        )
        gain_sums = lax.psum(gain_parts, (*DP, *TENSOR))
    grad_attn_gain, grad_ffn_gain, grad_query_gain, grad_key_gain = gain_sums
    return (
        outputs,
        grad_inputs,
        grad_attn_gain,
        grad_query_gain,
        grad_key_gain,
        grad_w_query,
        grad_w_key,
        grad_w_value,
        grad_w_output,
        grad_ffn_gain,
        grad_w_gate,
        grad_w_up,
        grad_w_down,
    )


def solution(mesh):
    rows, columns = mesh.devices.shape
    split = jax.sharding.Mesh(
        mesh.devices.reshape(rows // 2, 2, columns // 2, 2), (*DP, *TENSOR)
    )
    in_specs = (
        P((*DP, *TENSOR), None),
        P(DP, TENSOR),
        P((*DP, *TENSOR), None),
        P((*DP, *TENSOR), None),
        P(),
        P(),
        P(),
        P(DP, TENSOR),
        P(DP, TENSOR),
        P(DP, TENSOR),
        P(TENSOR, DP),
        P(),
        P(DP, None, TENSOR),
        P(DP, None, TENSOR),
        P(DP, TENSOR, None),
        P((*DP, *TENSOR), None),
    )
    out_specs = (
        P((*DP, *TENSOR), None),
        P((*DP, *TENSOR), None),
        P(),
        P(),
        P(),
        P(DP, TENSOR),
        P(DP, TENSOR),
        P(DP, TENSOR),
        P(TENSOR, DP),
        P(),
        P(DP, None, TENSOR),
        P(DP, None, TENSOR),
        P(DP, TENSOR, None),
    )
    return jax.shard_map(shards, mesh=split, in_specs=in_specs, out_specs=out_specs, check_vma=False)
```

```python
import jax
import jax.numpy as jnp
import functools
import math

from jax import lax
from jax.experimental import pallas as pl
from jax.experimental.pallas import tpu as pltpu
from jax.sharding import PartitionSpec as P

WINDOW = 1024
DP = ("plane", "pack")
TENSOR = ("side", "core")


EPSILON = 1e-06
THETA = 50000.0
NEG_FILL = -1e30


def matmul(left_side, right_side):
    return jnp.dot(left_side, right_side, preferred_element_type=jnp.float32)


def contract_last(left_side, right_side):
    return lax.dot_general(
        left_side, right_side, (((1,), (1,)), ((), ())), preferred_element_type=jnp.float32
    )


def contract_first(left_side, right_side):
    return lax.dot_general(
        left_side, right_side, (((0,), (0,)), ((), ())), preferred_element_type=jnp.float32
    )


def norm_parts(values):
    factor = lax.rsqrt(jnp.mean(values * values, axis=-1, keepdims=True) + EPSILON)
    return (values * factor, factor)


def norm_back(grad_out, normed, factor, gain_vec):
    scaled = grad_out * gain_vec
    return factor * (scaled - normed * jnp.mean(scaled * normed, axis=-1, keepdims=True))


def rope_tables(length, head_size):
    half_size = head_size // 2
    frequency = THETA ** (-(2.0 * jnp.arange(half_size, dtype=jnp.float32)) / head_size)
    angles = jnp.arange(length, dtype=jnp.float32)[:, None] * frequency[None, :]
    return (jnp.cos(angles)[:, None, :], jnp.sin(angles)[:, None, :])


def rotate(values, cosine, sine_tab):
    half_size = values.shape[-1] // 2
    first_half = values[..., :half_size]
    second_half = values[..., half_size:]
    return jnp.concatenate(
        [
            first_half * cosine - second_half * sine_tab,
            second_half * cosine + first_half * sine_tab,
        ],
        axis=-1,
    )


def rotate_back(grads_in, cosine, sine_tab):
    half_size = grads_in.shape[-1] // 2
    first_half = grads_in[..., :half_size]
    second_half = grads_in[..., half_size:]
    return jnp.concatenate(
        [
            first_half * cosine + second_half * sine_tab,
            second_half * cosine - first_half * sine_tab,
        ],
        axis=-1,
    )


def block_mask(segments, offset, block_rows, key_count):
    query_pos = offset + jnp.arange(block_rows)
    key_pos = jnp.arange(key_count)
    same_doc = segments[offset : offset + block_rows][:, None] == segments[None, :]
    near_pos = jnp.abs(query_pos[:, None] - key_pos[None, :]) < WINDOW // 2
    return same_doc & near_pos


def block_scores(query_block, key_low, allowed, inv_root):
    scores = (
        jnp.einsum("qhd,khd->hqk", query_block, key_low, preferred_element_type=jnp.float32)
        * inv_root
    )
    return jnp.where(allowed[None], scores, NEG_FILL)


def row_sum(term_fn, tok_rows):
    return lax.psum_scatter(
        term_fn(jnp.int32(0), lax.axis_size(TENSOR) * tok_rows),
        TENSOR,
        scatter_dimension=0,
        tiled=True,
    )


def gather_rows(values):
    return lax.all_gather(values, TENSOR, axis=0, tiled=True)


def from_experts(values):
    return lax.all_to_all(values, DP, split_axis=1, concat_axis=1, tiled=True)


def to_experts(source_rows, slot_token, slot_gate, layout):
    picked = jnp.take(source_rows, slot_token, axis=0, mode="fill", fill_value=0)
    if slot_gate is not None:
        picked = (picked.astype(jnp.float32) * slot_gate[:, None]).astype(jnp.bfloat16)
    picked = picked.reshape(layout + (picked.shape[1],))
    return lax.all_to_all(picked, DP, split_axis=1, concat_axis=1, tiled=True)


def pair_sum(table, weights_low, pair_slots, row_count):
    picked = jnp.take(table, pair_slots.reshape(-1), axis=0, mode="fill", fill_value=0)
    picked = picked.reshape(row_count, pair_slots.shape[1], table.shape[1])
    return jnp.einsum("rk,rkd->rd", weights_low, picked, preferred_element_type=jnp.float32)


def expert_forward(operands):
    rows_in, gate_mat, up_mat, down_mat = operands
    flat_rows = rows_in.reshape(-1, rows_in.shape[-1])
    gated = matmul(flat_rows, gate_mat)
    lifted = matmul(flat_rows, up_mat)
    hidden = (jax.nn.silu(gated) * lifted).astype(jnp.bfloat16)
    result = matmul(hidden, down_mat).astype(jnp.bfloat16)
    return (result.reshape(rows_in.shape), gated, lifted)


def expert_backward(operands):
    rows_in, grad_in, gated, lifted, gate_mat, up_mat, down_mat = operands
    flat_rows = rows_in.reshape(-1, rows_in.shape[-1])
    flat_grad = grad_in.reshape(-1, grad_in.shape[-1])
    gate_sig = jax.nn.sigmoid(gated)
    activated = jax.nn.silu(gated)
    hidden = (activated * lifted).astype(jnp.bfloat16)
    grad_hidden = contract_last(flat_grad, down_mat)
    grad_down = contract_first(hidden, flat_grad)
    grad_gated = (grad_hidden * lifted * gate_sig * (1.0 + gated * (1.0 - gate_sig))).astype(
        jnp.bfloat16
    )
    grad_lifted = (grad_hidden * activated).astype(jnp.bfloat16)
    grad_gate = contract_first(flat_rows, grad_gated)
    grad_up = contract_first(flat_rows, grad_lifted)
    grad_rows = (contract_last(grad_gated, gate_mat) + contract_last(grad_lifted, up_mat)).astype(
        jnp.bfloat16
    )
    return (grad_rows.reshape(rows_in.shape), grad_gate, grad_up, grad_down)


VMEM_BYTES = 60 * 1024 * 1024
COLUMN_CHUNK = 512
GROUP = 2


def select_rows(places_ref, gates_ref, pick_ref, capacity):
    expert_count, seq_len = places_ref.shape[1:]
    slot_range = lax.broadcasted_iota(jnp.int32, (capacity, seq_len), 0).astype(jnp.bfloat16)
    nothing = jnp.zeros((capacity, seq_len), jnp.bfloat16)
    for expert in range(expert_count):
        hit = places_ref[0, expert : expert + 1, :] == slot_range
        if gates_ref is None:
            weight = jnp.ones((capacity, seq_len), jnp.bfloat16)
        else:
            weight = jnp.broadcast_to(gates_ref[0, expert : expert + 1, :], (capacity, seq_len))
        rows = slice(expert * capacity, (expert + 1) * capacity)
        pick_ref[rows, :] = jnp.where(hit, weight, nothing)


def rows_to_slots(pick_ref, rows_ref, slots_ref, pack, capacity):
    width = rows_ref.shape[2]
    expert_count = slots_ref.shape[0]
    for start in range(0, width, COLUMN_CHUNK):
        columns = slice(start, start + COLUMN_CHUNK)
        picked = matmul(pick_ref[...], rows_ref[0, :, columns]).astype(jnp.bfloat16)
        slots_ref[:, pack, :, columns] = picked.reshape(expert_count, capacity, COLUMN_CHUNK)


def slots_to_rows(pick_ref, slots_ref, own_ref, other_ref, pack):
    width = own_ref.shape[3]
    for start in range(0, width, COLUMN_CHUNK):
        columns = slice(start, start + COLUMN_CHUNK)
        slots = slots_ref[:, pack, :, columns].reshape(-1, COLUMN_CHUNK)
        rows = contract_first(pick_ref[...], slots).astype(own_ref.dtype)
        rows = rows.reshape(2, 2, own_ref.shape[2], COLUMN_CHUNK)
        own_ref[0, :, :, columns] = rows[:, 0]
        other_ref[0, :, :, columns] = rows[:, 1]


def cot_kernel(
    packs, steps, capacity, table, places, gates, rows, down, slots_out, hidden_out, slots, pick
):
    step = pl.program_id(0)

    @pl.when(step < packs)
    def _():
        select_rows(places, gates, pick, capacity)
        rows_to_slots(pick, rows, slots, step, capacity)

    @pl.when(step >= packs)
    def _():
        for member in range(down.shape[0]):
            block = slots[(step - packs) * down.shape[0] + member].reshape(packs * capacity, -1)
            slots_out[member] = block
            hidden_out[member] = contract_last(block, down[member])


def piece_copies(own, other, rows, sems, pack):
    half_rows = own.shape[1]
    copies = []
    for far in range(2):
        for core, source in enumerate((own, other)):
            for half, index in enumerate((4 * far + pack, 2 + 4 * pack + far)):
                start = ((far * 2 + core) * 2 + half) * half_rows
                copies.append(
                    pltpu.make_async_copy(
                        source.at[index],
                        rows.at[pack, pl.ds(start, half_rows)],
                        sems.at[pack * 8 + len(copies)],
                    )
                )
    return copies


def row_kernel(
    packs, steps, capacity, places, own, other, both, grad_hidden,
    slots_out, hidden_out, grads_out, rows_own, rows_other,
    rows, slots, grads, pick, sems,
):
    step = pl.program_id(0)
    half = hidden_out.shape[2]

    @pl.when(step == 0)
    def _():
        for pack in range(packs):
            for copy in piece_copies(own, other, rows, sems, pack):
                copy.start()
        for pack in range(packs):
            select_rows(places.at[pl.ds(pack, 1)], None, pick.at[pack], capacity)

    for pack in range(packs):

        @pl.when(step == pack)
        def _(pack=pack):
            for copy in piece_copies(own, other, rows, sems, pack):
                copy.wait()
            rows_to_slots(pick.at[pack], rows.at[pl.ds(pack, 1)], slots, pack, capacity)

    @pl.when((step >= packs) & (step < packs + steps))
    def _():
        for member in range(both.shape[0]):
            expert = (step - packs) * both.shape[0] + member
            block = slots[expert].reshape(packs * capacity, -1)
            slots_out[member] = block
            product = matmul(block, both[member])
            gated, lifted = product[:, :half], product[:, half:]
            sig = 1.0 / (1.0 + jnp.exp(-gated))
            active = gated * sig
            hidden_out[member] = (active * lifted).astype(jnp.bfloat16)
            above = grad_hidden[member]
            grad_gated = above * lifted * sig * (1.0 + gated * (1.0 - sig))
            joined = jnp.concatenate([grad_gated, above * active], axis=1).astype(jnp.bfloat16)
            grads_out[member] = joined
            back = contract_last(joined, both[member])
            grads[expert] = back.astype(jnp.bfloat16).reshape(packs, capacity, -1)

    for pack in range(packs):

        @pl.when(step == packs + steps + pack)
        def _(pack=pack):
            slots_to_rows(pick.at[pack], grads, rows_own, rows_other, pack)


def mix_kernel(
    packs, steps, capacity, table, places, gates, hidden, down, rows_own, rows_other, results, pick
):
    step = pl.program_id(0)

    @pl.when(step < steps)
    def _():
        for member in range(down.shape[0]):
            result = matmul(hidden[member], down[member]).astype(jnp.bfloat16)
            results[step * down.shape[0] + member] = result.reshape(packs, capacity, -1)

    @pl.when(step >= steps)
    def _():
        select_rows(places, gates, pick, capacity)
        slots_to_rows(pick, results, rows_own, rows_other, (step - steps) ^ table[0])


def weight_kernel(planes, *refs):
    slots, grads, hidden, above = (
        jnp.concatenate([ref[0] for ref in refs[i * planes : (i + 1) * planes]]) for i in range(4)
    )
    gate_out, up_out, down_out = refs[-3:]
    half = gate_out.shape[2]
    both = contract_first(slots, above)
    gate_out[0] = both[:, :half]
    up_out[0] = both[:, half:]
    down_out[0] = contract_first(hidden, grads)


def block(shape, place, count=1):
    tail = (0,) * (len(shape) - 1)
    return pl.BlockSpec((count,) + tuple(shape[1:]), lambda *ids: (place(*ids),) + tail)


def staged(first, count):
    return lambda step, *rest: jnp.clip(step - first, 0, count - 1)


def shape_of(shape, kind):
    return jax.ShapeDtypeStruct(shape, kind)


def call(kernel, steps, specs, out_specs, out_shape, scratch, flops, prefetch=0, aliases={}):
    return pl.pallas_call(
        kernel,
        grid_spec=pltpu.PrefetchScalarGridSpec(
            num_scalar_prefetch=prefetch,
            grid=(steps,),
            in_specs=specs,
            out_specs=out_specs,
            scratch_shapes=scratch,
        ),
        out_shape=out_shape,
        input_output_aliases=aliases,
        cost_estimate=pl.CostEstimate(
            flops=flops, transcendentals=0, bytes_accessed=flops // 500
        ),
        compiler_params=pltpu.CompilerParams(
            dimension_semantics=("arbitrary",), vmem_limit_bytes=VMEM_BYTES
        ),
    )


def cot_slots(table, places, gates, rows, down, capacity):
    packs = table.shape[0]
    _, seq_len, width = rows.shape
    experts, hidden_width, _ = down.shape
    slot_rows = packs * capacity
    group = math.gcd(experts, GROUP)
    steps = experts // group
    by_pack, by_expert = staged(0, packs), staged(packs, steps)
    listed = lambda step, numbers: numbers[by_pack(step)]
    out_shape = [
        shape_of((experts, slot_rows, width), jnp.bfloat16),
        shape_of((experts, slot_rows, hidden_width), jnp.float32),
    ]
    return call(
        functools.partial(cot_kernel, packs, steps, capacity),
        packs + steps,
        [
            block(places.shape, listed), block(gates.shape, listed), block(rows.shape, listed),
            block(down.shape, by_expert, group),
        ],
        [block(out.shape, by_expert, group) for out in out_shape],
        out_shape,
        [
            pltpu.VMEM((experts, packs, capacity, width), jnp.bfloat16),
            pltpu.VMEM((experts * capacity, seq_len), jnp.bfloat16),
        ],
        2 * experts * slot_rows * width * (seq_len + hidden_width),
        1,
    )(table, places, gates, rows, down)


def row_slots(places, own, other, both, grad_hidden, capacity):
    packs, _, seq_len = places.shape
    experts, width, hidden_width = both.shape
    slot_rows = packs * capacity
    group = math.gcd(experts, GROUP)
    steps = experts // group
    middle, last = staged(packs, steps), staged(packs + steps, packs)
    part = shape_of((packs, 2, seq_len // 4, width), jnp.bfloat16)
    out_shape = [
        shape_of((experts, slot_rows, width), jnp.bfloat16),
        shape_of((experts, slot_rows, hidden_width // 2), jnp.bfloat16),
        shape_of((experts, slot_rows, hidden_width), jnp.bfloat16),
        part, part,
    ]
    anywhere = pl.BlockSpec(memory_space=pl.ANY)
    return call(
        functools.partial(row_kernel, packs, steps, capacity),
        2 * packs + steps,
        [
            block(places.shape, lambda step: 0, packs), anywhere, anywhere,
            block(both.shape, middle, group), block(grad_hidden.shape, middle, group),
        ],
        [block(out.shape, middle, group) for out in out_shape[:3]] + [block(part.shape, last)] * 2,
        out_shape,
        [
            pltpu.VMEM((packs, seq_len, width), jnp.bfloat16),
            pltpu.VMEM((experts, packs, capacity, width), jnp.bfloat16),
            pltpu.VMEM((experts, packs, capacity, width), jnp.bfloat16),
            pltpu.VMEM((packs, experts * capacity, seq_len), jnp.bfloat16),
            pltpu.SemaphoreType.DMA((8 * packs,)),
        ],
        4 * experts * slot_rows * width * (seq_len + hidden_width),
    )(places, own, other, both, grad_hidden)


def mix_rows(table, places, gates, hidden, down, capacity):
    packs, _, seq_len = places.shape
    experts, hidden_width, width = down.shape
    group = math.gcd(experts, GROUP)
    steps = experts // group
    first, last = staged(0, steps), staged(steps, packs)
    listed = lambda step, numbers: numbers[1] * steps + first(step)
    part = shape_of((packs, 2, seq_len // 4, width), jnp.bfloat16)
    return call(
        functools.partial(mix_kernel, packs, steps, capacity),
        packs + steps,
        [
            block(places.shape, last), block(gates.shape, last),
            block(hidden.shape, listed, group), block(down.shape, first, group),
        ],
        [block(part.shape, last)] * 2,
        [part, part],
        [
            pltpu.VMEM((experts, packs, capacity, width), jnp.bfloat16),
            pltpu.VMEM((experts * capacity, seq_len), jnp.bfloat16),
        ],
        2 * experts * packs * capacity * width * (seq_len + hidden_width),
        1,
    )(table, places, gates, hidden, down)


def weight_grads(first, count, slots, hidden, grads, above, earlier=()):
    planes = len(slots)
    operands = [*slots, *grads, *hidden, *above]
    experts, _, width = slots[0].shape
    hidden_width = hidden[0].shape[2]
    each = lambda step: step + first
    out_shape = [
        shape_of((experts, width, hidden_width), jnp.float32),
        shape_of((experts, width, hidden_width), jnp.float32),
        shape_of((experts, hidden_width, width), jnp.float32),
    ]
    return call(
        functools.partial(weight_kernel, planes),
        count,
        [block(operand.shape, each) for operand in operands]
        + [pl.BlockSpec(memory_space=pl.ANY)] * len(earlier),
        [block(out.shape, each) for out in out_shape],
        out_shape,
        [],
        6 * planes * slots[0].shape[1] * count * width * hidden_width,
        aliases={len(operands) + index: index for index in range(len(earlier))},
    )(*operands, *earlier)


def swapped(values, axis, bit):
    count = lax.axis_size(axis)
    return lax.ppermute(values, axis, [(i, i ^ bit) for i in range(count)])


def far_side(values):
    return swapped(values, TENSOR, 2)


def far_core(values):
    return swapped(values, TENSOR, 1)


def far_pack(values):
    return swapped(values, DP, 1)


def next_plane(values):
    count = lax.axis_size(DP)
    return lax.ppermute(values, DP, [(i, (i + 2) % count) for i in range(count)])


def spread_all(values, small, work):
    planes = lax.axis_size("plane")
    half_rows = values.shape[0] // 2
    first = lambda rows: (far_pack(rows[:half_rows]), far_side(rows[half_rows:]))
    small, values = tied(small, values)
    (across_pack, across_side), following = lax.optimization_barrier(
        (first(values), next_plane(values))
    )
    pieces, made = [], []
    for plane in range(planes):
        upper = jnp.stack([values[:half_rows], across_pack])
        lower = jnp.stack([values[half_rows:], across_side])
        small, (upper, lower, values) = tied(small, (upper, lower, following))
        moved = [
            far_side(upper),
            far_pack(lower),
            first(values) if plane + 1 < planes else ((), ()),
            next_plane(values) if plane + 2 < planes else (),
            far_core(pieces[-1]) if plane else (),
            work(plane - 2, small) if plane > 1 else (),
        ]
        upper_far, lower_far, (across_pack, across_side), following, other, result = (
            lax.optimization_barrier(moved)
        )
        if plane:
            pieces[-1] = (pieces[-1], other)
        if plane > 1:
            made.append(result)
        pieces.append(jnp.concatenate([upper, lower, upper_far, lower_far]))
    pieces[-1] = (pieces[-1], far_core(pieces[-1]))
    return pieces, made


def plane_order():
    packs = lax.axis_size(DP)
    planes = packs // 2
    index = lax.axis_index(DP)
    return jnp.stack(
        [
            ((index // 2 + planes - plane) % planes) * 2 + (index % 2 ^ near)
            for plane in range(planes)
            for near in range(2)
        ]
    )


def place_kernel(by_column, order, *refs):
    *pieces, whole, sems = refs
    copies = []
    for index, piece in enumerate(pieces):
        target = None if by_column else whole.at[order[index]]
        if by_column:
            width = piece.shape[1]
            target = whole.at[:, pl.ds(pl.multiple_of(order[index] * width, 128), width)]
        copies.append(pltpu.make_async_copy(piece, target, sems.at[index]))
        copies[-1].start()
    for copy in copies:
        copy.wait()


def laid(pieces, order, by_column=False):
    count = len(pieces)
    rows, columns = pieces[0].shape
    shape = (rows, count * columns) if by_column else (count, rows, columns)
    anywhere = pl.BlockSpec(memory_space=pl.ANY)
    return call(
        functools.partial(place_kernel, by_column),
        1,
        [anywhere] * count,
        pl.BlockSpec(memory_space=pltpu.VMEM),
        shape_of(shape, pieces[0].dtype),
        [pltpu.SemaphoreType.DMA((count,))],
        1000,
        1,
    )(order, *pieces)


class FoldPacks:
    def __init__(self, values):
        order = plane_order()
        take = lambda index: lax.dynamic_index_in_dim(values, order[index], 0, keepdims=False)
        planes = values.shape[0] // 2
        self.turns = [*range(1, planes), 0]
        self.near = {plane: take(2 * plane) for plane in self.turns}
        self.moving = {plane: far_pack(take(2 * plane + 1)) for plane in self.turns}
        self.summed, self.count = None, 0

    def step(self, other):
        if self.count >= len(self.turns):
            return other
        self.moving, other = tied(self.moving, other)
        if self.summed is None:
            self.near = {plane: added(self.near[plane], self.moving[plane]) for plane in self.turns}
            self.summed = self.near[self.turns[0]]
        else:
            kind = jnp.float32 if self.count + 1 == len(self.turns) else jnp.bfloat16
            self.summed = added(self.moving, self.near[self.turns[self.count]], kind)
        self.count += 1
        if self.count < len(self.turns):
            self.moving = next_plane(self.summed)
        return other

    def finish(self):
        for plane in self.turns[self.count :]:
            kind = jnp.float32 if plane == 0 else jnp.bfloat16
            self.summed = added(self.moving, self.near[plane], kind)
            self.moving = next_plane(self.summed) if plane else None
        return self.summed


def laid_sides(pieces):
    order = lax.axis_index(TENSOR) ^ jnp.arange(len(pieces), dtype=jnp.int32)
    return laid(pieces, order).reshape((-1,) + pieces[0].shape[1:])


def gather_sides(values):
    across = far_side(values)
    return laid_sides([values, far_core(values), across, far_core(across)])


def fold_sides(values):
    split = values.astype(jnp.bfloat16).reshape((4, -1) + values.shape[1:])
    take = lambda bits: lax.dynamic_index_in_dim(
        split, lax.axis_index(TENSOR) ^ bits, 0, keepdims=False
    )
    far = added(take(2), far_core(take(3)))
    near = added(take(0), far_core(take(1)))
    return added(near, far_side(far), jnp.float32)


def fold_both(weights, rows):
    order = plane_order()
    planes = weights.shape[0] // 2
    take = lambda index: lax.dynamic_index_in_dim(weights, order[index], 0, keepdims=False)
    split = rows.astype(jnp.bfloat16).reshape((4, -1) + rows.shape[1:])
    mine = lax.axis_index(TENSOR)
    pick = lambda bits: lax.dynamic_index_in_dim(split, mine ^ bits, 0, keepdims=False)
    summed, total = None, None
    for turn, plane in enumerate([*range(1, planes), 0]):
        moved = [far_pack(take(2 * plane + 1)), () if summed is None else next_plane(summed)]
        if turn == 0:
            moved += [far_core(pick(3)), far_core(pick(1))]
        if turn == 1:
            moved += [far_side(far)]
        across, passed, *arrived = lax.optimization_barrier(moved)
        if turn == 0:
            far, close = added(pick(2), arrived[0]), added(pick(0), arrived[1])
        if turn == 1:
            total = added(close, arrived[0], jnp.float32)
        near = added(take(2 * plane), across)
        kind = jnp.float32 if turn + 1 == planes else jnp.bfloat16
        summed = near if turn == 0 else added(passed, near, kind)
    return summed, total


def gather_both(weights, outer, rows, gate, up):
    pieces, outer_pieces, row_pieces, values = [], [], [rows], (weights, outer)
    planes = lax.axis_size("plane")
    for plane in range(planes):
        moved = [tuple(far_pack(value) for value in values), ()]
        if plane + 1 < planes:
            moved[1] = tuple(next_plane(value) for value in values)
        if plane == 0:
            moved += [far_core(rows), far_side(rows)]
        if plane == 1:
            moved += [far_core(row_pieces[2])]
        if plane == 0:
            moved.insert(2, jnp.concatenate([gate, up], axis=2))
        across, following, *arrived = lax.optimization_barrier(moved)
        if plane == 0:
            joined = arrived.pop(0)
        pieces += [values[0], across[0]]
        outer_pieces += [values[1], across[1]]
        row_pieces += arrived
        values = following
    order = plane_order()
    return laid(pieces, order), laid(outer_pieces, order, True), laid_sides(row_pieces), joined


def sum_everywhere(values):
    for axis in (TENSOR, DP):
        bit = 1
        while bit < lax.axis_size(axis):
            values = values + swapped(values, axis, bit)
            bit *= 2
    return values


def added(left, right, kind=jnp.bfloat16):
    return (left.astype(jnp.float32) + right.astype(jnp.float32)).astype(kind)


def fold_first(own, arrived):
    half_rows = own.shape[2] // 2
    upper, lower = slice(None, half_rows), slice(half_rows, None)
    return (
        added(own[:, 0, upper], arrived[:, 0, upper]),
        added(own[0, :, lower], arrived[0, :, lower]),
        added(own[:, 1, upper], arrived[:, 1, upper]),
        added(own[1, :, lower], arrived[1, :, lower]),
    )


def tied(small, values):
    return lax.optimization_barrier((small, values))


def gather_tables(expert_ids, gate_values, segment_ids):
    top_count = expert_ids.shape[1]
    tables = jnp.concatenate(
        [expert_ids.T.astype(jnp.bfloat16), gate_values.T, segment_ids.astype(jnp.bfloat16)]
    )[None]
    for axis in (TENSOR, DP):
        bit = 1
        while bit < lax.axis_size(axis):
            tables = jnp.concatenate([tables, swapped(tables, axis, bit)])
            bit *= 2
        if axis == TENSOR:
            sides = jnp.arange(tables.shape[0], dtype=jnp.int32) ^ lax.axis_index(TENSOR)
            segments = jnp.take(tables[:, -1], sides, axis=0).reshape(-1)
    devices = jnp.arange(tables.shape[0], dtype=jnp.int32)
    own = lax.axis_index(DP) * lax.axis_size(TENSOR) + lax.axis_index(TENSOR)
    tables = jnp.take(tables, devices ^ own, axis=0)
    all_ids, all_gates = tables[:, :top_count], tables[:, top_count : 2 * top_count]
    return all_ids.astype(jnp.int32), all_gates, segments.astype(jnp.int32)


def routing(all_ids, all_gates, local_experts, capacity):
    packs = lax.axis_size(DP)
    first = lax.axis_index(DP) * local_experts
    wanted = first + jnp.arange(local_experts, dtype=jnp.int32)

    def by_pack(values):
        top_count, tok_rows = values.shape[1:]
        ordered = values.reshape(packs, -1, top_count, tok_rows).transpose(0, 2, 1, 3)
        return ordered.reshape(packs, top_count, -1)

    matches = by_pack(all_ids)[:, :, None, :] == wanted[None, None, :, None]
    pair_gates = by_pack(all_gates).astype(jnp.float32)
    member = jnp.any(matches, axis=1)
    gates = jnp.sum(jnp.where(matches, pair_gates[:, :, None, :], 0.0), axis=1)
    order = jnp.arange(member.shape[2], dtype=jnp.int32)
    earlier = (order[:, None] < order[None, :]).astype(jnp.bfloat16)
    flat = member.reshape(packs * local_experts, -1).astype(jnp.bfloat16)
    before = matmul(flat, earlier).astype(jnp.int32).reshape(member.shape)
    places = jnp.where(member & (before < capacity), before, -1)
    return places.astype(jnp.bfloat16), gates.astype(jnp.bfloat16)


def experts_by_exchange(
    second_in, cotangent, expert_ids, gate_values, w_gate, w_up, w_down, middle, capacity
):
    tok_rows, model_width = second_in.shape
    tensor_count = lax.axis_size(TENSOR)
    data_count = lax.axis_size(DP)
    local_experts = w_gate.shape[0]
    all_experts = local_experts * data_count
    top_count = expert_ids.shape[1]
    seq_len = tok_rows * tensor_count
    pack_cot, pack_ids, pack_gates = (
        gather_rows(cotangent), gather_rows(expert_ids), gather_rows(gate_values)
    )
    pack_second = gather_rows(second_in)
    expert_range = jnp.arange(all_experts, dtype=jnp.int32)
    matches = pack_ids[:, :, None] == expert_range[None, None, :]
    token_counts = jnp.sum(matches.astype(jnp.float32), axis=1).astype(jnp.bfloat16)
    token_range = jnp.arange(seq_len, dtype=jnp.int32)
    earlier = (token_range[:, None] > token_range[None, :]).astype(jnp.bfloat16)
    before = matmul(earlier, token_counts)
    places = (
        jnp.sum(jnp.where(matches, before[:, None, :], 0.0), axis=2).astype(jnp.int32).reshape(-1)
    )
    flat_ids = pack_ids.reshape(-1)
    owners = flat_ids // local_experts
    local_index = flat_ids % local_experts
    dump_slot = all_experts * capacity
    slot_index = jnp.where(
        places < capacity,
        local_index * (data_count * capacity) + owners * capacity + places,
        dump_slot,
    ).astype(jnp.int32)
    pair_token = jnp.arange(seq_len * top_count) // top_count
    slot_token = (
        jnp.full((dump_slot + 1,), seq_len, jnp.int32).at[slot_index].set(pair_token)[:dump_slot]
    )
    pair_gates = pack_gates.astype(jnp.float32)
    slot_gate = (
        jnp.zeros((dump_slot + 1,), jnp.float32)
        .at[slot_index]
        .set(pair_gates.reshape(-1))[:dump_slot]
    )
    pair_slots = slot_index.reshape(seq_len, top_count)
    layout = (local_experts, data_count, capacity)
    arrived_rows = to_experts(pack_second, slot_token, None, layout)
    expert_out, gated_all, lifted_all = lax.map(
        expert_forward, (arrived_rows, w_gate, w_up, w_down)
    )
    returned = from_experts(expert_out).reshape(-1, model_width)

    def combine_term(offset, row_count):
        return pair_sum(returned, pack_gates, pair_slots, row_count)

    outputs = middle + row_sum(combine_term, tok_rows)
    grad_arrived = to_experts(pack_cot, slot_token, slot_gate, layout)
    grad_rows_all, grad_w_gate, grad_w_up, grad_w_down = lax.map(
        expert_backward, (arrived_rows, grad_arrived, gated_all, lifted_all, w_gate, w_up, w_down)
    )
    returned_grad = from_experts(grad_rows_all).reshape(-1, model_width)
    unit_gates = jnp.ones_like(pack_gates)

    def dispatch_term(offset, row_count):
        return pair_sum(returned_grad, unit_gates, pair_slots, row_count)

    grad_second = row_sum(dispatch_term, tok_rows)
    return outputs, grad_second, grad_w_gate, grad_w_up, grad_w_down


class Folding:
    def __init__(self, order):
        self.order, self.planes, self.ready = order, {}, {}
        self.summed, self.count = None, 0

    def begin(self, plane, own, other):
        self.planes[plane] = (0, (own, other))

    def turn(self, small, work):
        small, (planes, summed) = tied(
            small, ({plane: values for plane, (_, values) in self.planes.items()}, self.summed)
        )
        sent = {}
        for plane, values in planes.items():
            stage = self.planes[plane][0]
            if stage == 0:
                sent[plane] = (far_core(values[1]),)
            elif stage == 1:
                sent[plane] = (far_side(values[2]), far_pack(values[3]))
            else:
                sent[plane] = (far_pack(values[2]), far_side(values[3]))
        passed = None if summed is None else next_plane(summed)
        sent, passed, result = lax.optimization_barrier((sent, passed, work(small)))
        for plane, values in planes.items():
            stage, arrived = self.planes[plane][0], sent[plane]
            if stage == 0:
                made = fold_first(values[0], *arrived)
            elif stage == 1:
                upper, lower = added(values[0], arrived[0]), added(values[1], arrived[1])
                made = (upper[0], lower[0], upper[1], lower[1])
            else:
                self.ready[plane] = jnp.concatenate(
                    [added(values[0], arrived[0]), added(values[1], arrived[1])]
                )
            if stage < 2:
                self.planes[plane] = (stage + 1, made)
            else:
                del self.planes[plane]
        following = self.order[self.count] if self.count < len(self.order) else None
        if following in self.ready:
            last = self.count + 1 == len(self.order)
            self.summed = self.ready[following]
            if passed is not None:
                kind = jnp.float32 if last else jnp.bfloat16
                self.summed = added(passed, self.summed, kind)
            self.count += 1
        return result

    def done(self):
        return self.count == len(self.order)


def experts_by_gather(second_in, all_cot, places, gates, w_both, w_down, capacity):
    packs, local_experts, seq_len = places.shape
    tensor_count = lax.axis_size(TENSOR)
    planes = packs // 2
    pack_order = plane_order()
    side_index = lax.axis_index(TENSOR)
    quarter_order = side_index ^ jnp.arange(tensor_count, dtype=jnp.int32)

    def as_met(values, by_pack, by_quarter):
        split = values.reshape(packs, local_experts, tensor_count, -1)
        split = jnp.take(jnp.take(split, by_pack, axis=0), by_quarter, axis=2)
        return split.reshape(values.shape)

    near_places = as_met(places, pack_order, quarter_order)
    core_order = lax.axis_index("core") ^ jnp.arange(tensor_count, dtype=jnp.int32)
    mix_places = as_met(places, jnp.arange(packs, dtype=jnp.int32), core_order)
    mix_gates = as_met(gates, jnp.arange(packs, dtype=jnp.int32), core_order)
    pairs = [slice(plane * 2, plane * 2 + 2) for plane in range(planes)]
    tables = [
        jnp.stack([lax.axis_index("pack"), (lax.axis_index("plane") + planes - plane) % planes])
        for plane in range(planes)
    ]
    prepared = [
        [table[pair] for pair in pairs] for table in (near_places, mix_places, mix_gates, pack_order)
    ]
    prepared, second_in = tied((prepared, tables, places, gates), second_in)
    (near_places, mix_places, mix_gates, pack_order), tables, places, gates = prepared

    def cot_work(plane, order):
        return cot_slots(order[plane], places, gates, all_cot, w_down, capacity)

    pieces, made = spread_all(second_in, pack_order, cot_work)
    order = [*range(1, planes), 0]
    kept, parts, folding = {}, {}, Folding(order)

    def row_work(plane, near):
        return row_slots(near, *pieces[plane], w_both, made[plane][1], capacity)

    for plane in range(planes):
        if plane:
            result = folding.turn(near_places[plane], functools.partial(row_work, plane))
        else:
            result = row_work(plane, near_places[plane])
        slots, hidden, above, *part = result
        folding.begin(plane, *part)
        kept[plane] = (slots, hidden, made[plane][0], above)
        if len(made) < planes:
            made.append(folding.turn(pack_order, functools.partial(cot_work, len(made))))
    hidden_all = jnp.concatenate([kept[plane][1] for plane in range(planes)])
    def mix_work(plane, table):
        return mix_rows(
            table[plane], mix_places[plane], mix_gates[plane], hidden_all, w_down, capacity
        )

    def cross():
        return [far_core(parts[plane][1]) for plane in parts if plane not in crossed]

    def mix_turn(some, table):
        return [mix_work(plane, table) for plane in some], cross()

    crossed = {}
    for start in range(0, planes, 2):
        some = order[start : start + 2]
        waiting = [plane for plane in parts if plane not in crossed]
        results, arrived = folding.turn(tables, functools.partial(mix_turn, some))
        crossed.update(zip(waiting, arrived))
        parts.update(zip(some, results))
    kept = [kept[plane] for plane in range(planes)]
    weight_parts, next_expert = (), 0
    part_size = math.gcd(local_experts, GROUP)

    def weight_turn(count, small):
        state, (held, weights) = next_expert, small
        for _ in range(count):
            if state < local_experts:
                weights = weight_grads(state, part_size, *zip(*held), weights)
                state += part_size
        return weights, cross()

    for count in (2, 1, *[0] * planes):
        if folding.done():
            break
        waiting = [plane for plane in parts if plane not in crossed]
        weight_parts, arrived = folding.turn(
            (kept, weight_parts), functools.partial(weight_turn, count)
        )
        next_expert = min(next_expert + count * part_size, local_experts)
        crossed.update(zip(waiting, arrived))
        if len(crossed) == planes and waiting:
            whole = jnp.stack(
                [added(parts[plane][0], crossed[plane]) for plane in range(planes)]
            )
            whole = whole.reshape(planes, -1, whole.shape[-1])
            whole = lax.psum_scatter(whole, ("pack", "side"), scatter_dimension=1, tiled=True)
    rest = (kept, weight_parts, next_expert, part_size)
    return folding.summed, whole, rest


def shards(
    inputs,
    segment_ids,
    expert_ids,
    gate_values,
    attn_gain,
    query_gain,
    key_gain,
    w_query,
    w_key,
    w_value,
    w_output,
    ffn_gain,
    w_gate,
    w_up,
    w_down,
    cotangent,
):
    tok_rows, model_width = inputs.shape
    head_size = query_gain.shape[0]
    tensor_count = lax.axis_size(TENSOR)
    data_count = lax.axis_size(DP)
    local_experts = w_gate.shape[0]
    all_experts = local_experts * data_count
    top_count = expert_ids.shape[1]
    seq_len = tok_rows * tensor_count
    capacity = seq_len * top_count // all_experts
    inv_root = head_size ** (-0.5)
    by_gather = (
        seq_len <= local_experts * capacity
        and tensor_count == 4
        and data_count > 2
        and data_count & (data_count - 1) == 0
        and all_experts <= 256
    )
    if by_gather:
        axes = (*DP, *TENSOR)
        all_ids, all_gates, segments = gather_tables(expert_ids, gate_values, segment_ids)
        places, gates = routing(all_ids, all_gates, local_experts, capacity)
    inputs_f32 = inputs.astype(jnp.float32)
    normed_one, factor_one = norm_parts(inputs_f32)
    first_in = (normed_one * attn_gain).astype(jnp.bfloat16)
    if by_gather:
        side_sum, side_gather = fold_sides, gather_sides
        local_width = w_query.shape[1]
        w_in = jnp.concatenate([w_query, w_key, w_value], axis=1)
        full_in, full_output, pack_in, w_both = gather_both(
            w_in, w_output, first_in, w_gate, w_up
        )
        full_in, cotangent = tied(full_in, cotangent)
        all_cot = lax.all_gather(cotangent, axes, axis=0, tiled=True)
        all_cot = all_cot.reshape(data_count, seq_len, model_width)
        full_in = full_in.reshape(model_width, -1)
        full_query, full_key, full_value = (
            full_in[:, index * local_width : (index + 1) * local_width] for index in range(3)
        )
    else:
        side_sum, side_gather = lambda term: row_sum(lambda *_: term, tok_rows), gather_rows
        segments = lax.all_gather(segment_ids, TENSOR, axis=1, tiled=True)[0]
        full_query, full_key, full_value, full_output = (
            lax.all_gather(w_query, DP, axis=0, tiled=True),
            lax.all_gather(w_key, DP, axis=0, tiled=True),
            lax.all_gather(w_value, DP, axis=0, tiled=True),
            lax.all_gather(w_output, DP, axis=1, tiled=True),
        )
        pack_in = side_gather(first_in)
    query_pre = matmul(pack_in, full_query)
    key_pre = matmul(pack_in, full_key)
    value_low = matmul(pack_in, full_value).astype(jnp.bfloat16)
    head_count = query_pre.shape[1] // head_size
    cosine, sine_tab = rope_tables(seq_len, head_size)
    query_norm, query_factor = norm_parts(query_pre.reshape(seq_len, head_count, head_size))
    key_norm, key_factor = norm_parts(key_pre.reshape(seq_len, head_count, head_size))
    query_low = rotate(query_norm * query_gain, cosine, sine_tab).astype(jnp.bfloat16)
    key_low = rotate(key_norm * key_gain, cosine, sine_tab).astype(jnp.bfloat16)
    value_heads = value_low.reshape(seq_len, head_count, head_size)
    block_rows = min(512, seq_len)
    block_total = seq_len // block_rows
    masks = []
    mixture_parts = []
    lse_parts = []
    for block_index in range(block_total):
        offset = block_index * block_rows
        allowed = block_mask(segments, offset, block_rows, seq_len)
        masks.append(allowed)
        scores = block_scores(query_low[offset : offset + block_rows], key_low, allowed, inv_root)
        top_score = jnp.max(scores, axis=-1, keepdims=True)
        raw_weights = jnp.exp(scores - top_score)
        totals = jnp.sum(raw_weights, axis=-1, keepdims=True)
        weights_low = (raw_weights / totals).astype(jnp.bfloat16)
        mixture_parts.append(
            jnp.einsum(
                "hqk,khd->qhd", weights_low, value_heads, preferred_element_type=jnp.float32
            ).astype(jnp.bfloat16)
        )
        lse_parts.append(top_score + jnp.log(totals))
    mixture = jnp.concatenate(mixture_parts, axis=0).reshape(seq_len, head_count * head_size)

    middle = inputs_f32 + side_sum(matmul(mixture, full_output))
    normed_two, factor_two = norm_parts(middle)
    second_in = (normed_two * ffn_gain).astype(jnp.bfloat16)
    if by_gather:
        grad_second, mixed, rest = experts_by_gather(
            second_in, all_cot, places, gates, w_both, w_down, capacity
        )
    else:
        outputs, grad_second, grad_w_gate, grad_w_up, grad_w_down = experts_by_exchange(
            second_in, cotangent, expert_ids, gate_values, w_gate, w_up, w_down, middle, capacity
        )
    ffn_gain_part = jnp.sum(grad_second * normed_two, axis=0)
    grad_middle = cotangent.astype(jnp.float32) + norm_back(
        grad_second, normed_two, factor_two, ffn_gain
    )
    grad_attended = grad_middle.astype(jnp.bfloat16)
    if by_gather:
        kept, weight_parts, next_expert, part_size = rest
        (kept, weight_parts), grad_attended = tied((kept, weight_parts), grad_attended)
        moved = [far_core(grad_attended), far_side(grad_attended)]
        for first in range(next_expert, local_experts, part_size):
            weight_parts = weight_grads(first, part_size, *zip(*kept), weight_parts)
        grad_w_gate, grad_w_up, grad_w_down = weight_parts
        near, across, weight_parts = lax.optimization_barrier((*moved, weight_parts))
        grad_w_gate, grad_w_up, grad_w_down = weight_parts
        pack_grad = laid_sides([grad_attended, near, across, far_core(across)])
    else:
        pack_grad = side_gather(grad_attended)
    output_part = contract_first(mixture, pack_grad)
    fold_step = lambda other: other
    if by_gather:
        by_column = output_part.astype(jnp.bfloat16).reshape(local_width, data_count, -1)
        folded = FoldPacks(by_column.transpose(1, 0, 2))
        fold_step = folded.step
    grad_mixture = (
        contract_last(pack_grad, full_output)
        .astype(jnp.bfloat16)
        .reshape(seq_len, head_count, head_size)
    )
    grad_query_parts = []
    grad_key_sum = jnp.zeros((seq_len, head_count, head_size), jnp.float32)
    grad_value_sum = jnp.zeros((seq_len, head_count, head_size), jnp.float32)
    for block_index in range(block_total):
        offset = block_index * block_rows
        query_block = query_low[offset : offset + block_rows]
        if block_index:
            query_block = fold_step(query_block)
        grad_block = grad_mixture[offset : offset + block_rows]
        scores = block_scores(query_block, key_low, masks[block_index], inv_root)
        prob_rows = jnp.exp(scores - lse_parts[block_index])
        grad_probs = jnp.einsum(
            "qhd,khd->hqk", grad_block, value_heads, preferred_element_type=jnp.float32
        )
        row_delta = jnp.sum(grad_probs * prob_rows, axis=-1, keepdims=True)
        grad_scores = (prob_rows * (grad_probs - row_delta)).astype(jnp.bfloat16)
        grad_query_parts.append(
            jnp.einsum("hqk,khd->qhd", grad_scores, key_low, preferred_element_type=jnp.float32)
            * inv_root
        )
        grad_key_sum = (
            grad_key_sum
            + jnp.einsum(
                "hqk,qhd->khd", grad_scores, query_block, preferred_element_type=jnp.float32
            )
            * inv_root
        )
        grad_value_sum = grad_value_sum + jnp.einsum(
            "hqk,qhd->khd",
            prob_rows.astype(jnp.bfloat16),
            grad_block,
            preferred_element_type=jnp.float32,
        )
    grad_query_norm = rotate_back(jnp.concatenate(grad_query_parts, axis=0), cosine, sine_tab)
    grad_key_norm = rotate_back(grad_key_sum, cosine, sine_tab)
    grad_query_norm = fold_step(grad_query_norm)
    grad_key_norm = fold_step(grad_key_norm)
    query_gain_part = jnp.sum(grad_query_norm * query_norm, axis=(0, 1))
    key_gain_part = jnp.sum(grad_key_norm * key_norm, axis=(0, 1))
    grad_query_pre = (
        norm_back(grad_query_norm, query_norm, query_factor, query_gain)
        .reshape(seq_len, -1)
        .astype(jnp.bfloat16)
    )
    grad_key_pre = (
        norm_back(grad_key_norm, key_norm, key_factor, key_gain)
        .reshape(seq_len, -1)
        .astype(jnp.bfloat16)
    )
    grad_value_low = grad_value_sum.reshape(seq_len, -1).astype(jnp.bfloat16)
    query_part = contract_first(pack_in, grad_query_pre)
    key_part = contract_first(pack_in, grad_key_pre)
    value_part = contract_first(pack_in, grad_value_low)

    total_term = contract_last(grad_query_pre, full_query)
    total_term = total_term + contract_last(grad_key_pre, full_key)
    total_term = total_term + contract_last(grad_value_low, full_value)
    if by_gather:
        in_part = jnp.concatenate([query_part, key_part, value_part], axis=1)
        in_part = in_part.astype(jnp.bfloat16).reshape(data_count, -1, 3 * local_width)
        in_part = fold_step(in_part)
        grad_w_output = folded.finish()
        mixed, in_part = tied(mixed, in_part)
        mixed = lax.psum_scatter(mixed, "plane", scatter_dimension=0, tiled=True)
        grad_in, grad_first = fold_both(in_part, total_term)
        mixed, grad_in = tied(mixed, grad_in)
    else:
        grad_first = side_sum(total_term)
    attn_gain_part = jnp.sum(grad_first * normed_one, axis=0)
    grad_inputs = grad_middle + norm_back(grad_first, normed_one, factor_one, attn_gain)
    gain_parts = (attn_gain_part, ffn_gain_part, query_gain_part, key_gain_part)
    if by_gather:
        grad_w_query, grad_w_key, grad_w_value = (
            grad_in[:, index * local_width : (index + 1) * local_width] for index in range(3)
        )
        outputs = middle + mixed[0].astype(jnp.float32)
        splits = (model_width, 2 * model_width, 2 * model_width + head_size)
        gain_sums = jnp.split(sum_everywhere(jnp.concatenate(gain_parts)), splits)
    else:
        grad_w_query, grad_w_key, grad_w_value, grad_w_output = (
            lax.psum_scatter(
                part.astype(jnp.bfloat16), DP, scatter_dimension=along, tiled=True
            ).astype(jnp.float32)
            for part, along in ((query_part, 0), (key_part, 0), (value_part, 0), (output_part, 1))
        )
        gain_sums = lax.psum(gain_parts, (*DP, *TENSOR))
    grad_attn_gain, grad_ffn_gain, grad_query_gain, grad_key_gain = gain_sums
    return (
        outputs,
        grad_inputs,
        grad_attn_gain,
        grad_query_gain,
        grad_key_gain,
        grad_w_query,
        grad_w_key,
        grad_w_value,
        grad_w_output,
        grad_ffn_gain,
        grad_w_gate,
        grad_w_up,
        grad_w_down,
    )


def solution(mesh):
    rows, columns = mesh.devices.shape
    split = jax.sharding.Mesh(
        mesh.devices.reshape(rows // 2, 2, columns // 2, 2), (*DP, *TENSOR)
    )
    in_specs = (
        P((*DP, *TENSOR), None),
        P(DP, TENSOR),
        P((*DP, *TENSOR), None),
        P((*DP, *TENSOR), None),
        P(),
        P(),
        P(),
        P(DP, TENSOR),
        P(DP, TENSOR),
        P(DP, TENSOR),
        P(TENSOR, DP),
        P(),
        P(DP, None, TENSOR),
        P(DP, None, TENSOR),
        P(DP, TENSOR, None),
        P((*DP, *TENSOR), None),
    )
    out_specs = (
        P((*DP, *TENSOR), None),
        P((*DP, *TENSOR), None),
        P(),
        P(),
        P(),
        P(DP, TENSOR),
        P(DP, TENSOR),
        P(DP, TENSOR),
        P(TENSOR, DP),
        P(),
        P(DP, None, TENSOR),
        P(DP, None, TENSOR),
        P(DP, TENSOR, None),
    )
    return jax.shard_map(shards, mesh=split, in_specs=in_specs, out_specs=out_specs, check_vma=False)
```

```python
import jax
import jax.numpy as jnp
import functools
import math

from jax import lax
from jax.experimental import pallas as pl
from jax.experimental.pallas import tpu as pltpu
from jax.sharding import PartitionSpec as P

WINDOW = 1024
DP = ("plane", "pack")
TENSOR = ("side", "core")


EPSILON = 1e-06
THETA = 50000.0
NEG_FILL = -1e30


def matmul(left_side, right_side):
    return jnp.dot(left_side, right_side, preferred_element_type=jnp.float32)


def contract_last(left_side, right_side):
    return lax.dot_general(
        left_side, right_side, (((1,), (1,)), ((), ())), preferred_element_type=jnp.float32
    )


def contract_first(left_side, right_side):
    return lax.dot_general(
        left_side, right_side, (((0,), (0,)), ((), ())), preferred_element_type=jnp.float32
    )


def norm_parts(values):
    factor = lax.rsqrt(jnp.mean(values * values, axis=-1, keepdims=True) + EPSILON)
    return (values * factor, factor)


def norm_back(grad_out, normed, factor, gain_vec):
    scaled = grad_out * gain_vec
    return factor * (scaled - normed * jnp.mean(scaled * normed, axis=-1, keepdims=True))


def rope_tables(length, head_size):
    half_size = head_size // 2
    frequency = THETA ** (-(2.0 * jnp.arange(half_size, dtype=jnp.float32)) / head_size)
    angles = jnp.arange(length, dtype=jnp.float32)[:, None] * frequency[None, :]
    return (jnp.cos(angles)[:, None, :], jnp.sin(angles)[:, None, :])


def rotate(values, cosine, sine_tab):
    half_size = values.shape[-1] // 2
    first_half = values[..., :half_size]
    second_half = values[..., half_size:]
    return jnp.concatenate(
        [
            first_half * cosine - second_half * sine_tab,
            second_half * cosine + first_half * sine_tab,
        ],
        axis=-1,
    )


def rotate_back(grads_in, cosine, sine_tab):
    half_size = grads_in.shape[-1] // 2
    first_half = grads_in[..., :half_size]
    second_half = grads_in[..., half_size:]
    return jnp.concatenate(
        [
            first_half * cosine + second_half * sine_tab,
            second_half * cosine - first_half * sine_tab,
        ],
        axis=-1,
    )


def block_mask(segments, offset, block_rows, key_count):
    query_pos = offset + jnp.arange(block_rows)
    key_pos = jnp.arange(key_count)
    same_doc = segments[offset : offset + block_rows][:, None] == segments[None, :]
    near_pos = jnp.abs(query_pos[:, None] - key_pos[None, :]) < WINDOW // 2
    return same_doc & near_pos


def block_scores(query_block, key_low, allowed, inv_root):
    scores = (
        jnp.einsum("qhd,khd->hqk", query_block, key_low, preferred_element_type=jnp.float32)
        * inv_root
    )
    return jnp.where(allowed[None], scores, NEG_FILL)


def row_sum(term_fn, tok_rows):
    return lax.psum_scatter(
        term_fn(jnp.int32(0), lax.axis_size(TENSOR) * tok_rows),
        TENSOR,
        scatter_dimension=0,
        tiled=True,
    )


def gather_rows(values):
    return lax.all_gather(values, TENSOR, axis=0, tiled=True)


def from_experts(values):
    return lax.all_to_all(values, DP, split_axis=1, concat_axis=1, tiled=True)


def to_experts(source_rows, slot_token, slot_gate, layout):
    picked = jnp.take(source_rows, slot_token, axis=0, mode="fill", fill_value=0)
    if slot_gate is not None:
        picked = (picked.astype(jnp.float32) * slot_gate[:, None]).astype(jnp.bfloat16)
    picked = picked.reshape(layout + (picked.shape[1],))
    return lax.all_to_all(picked, DP, split_axis=1, concat_axis=1, tiled=True)


def pair_sum(table, weights_low, pair_slots, row_count):
    picked = jnp.take(table, pair_slots.reshape(-1), axis=0, mode="fill", fill_value=0)
    picked = picked.reshape(row_count, pair_slots.shape[1], table.shape[1])
    return jnp.einsum("rk,rkd->rd", weights_low, picked, preferred_element_type=jnp.float32)


def expert_forward(operands):
    rows_in, gate_mat, up_mat, down_mat = operands
    flat_rows = rows_in.reshape(-1, rows_in.shape[-1])
    gated = matmul(flat_rows, gate_mat)
    lifted = matmul(flat_rows, up_mat)
    hidden = (jax.nn.silu(gated) * lifted).astype(jnp.bfloat16)
    result = matmul(hidden, down_mat).astype(jnp.bfloat16)
    return (result.reshape(rows_in.shape), gated, lifted)


def expert_backward(operands):
    rows_in, grad_in, gated, lifted, gate_mat, up_mat, down_mat = operands
    flat_rows = rows_in.reshape(-1, rows_in.shape[-1])
    flat_grad = grad_in.reshape(-1, grad_in.shape[-1])
    gate_sig = jax.nn.sigmoid(gated)
    activated = jax.nn.silu(gated)
    hidden = (activated * lifted).astype(jnp.bfloat16)
    grad_hidden = contract_last(flat_grad, down_mat)
    grad_down = contract_first(hidden, flat_grad)
    grad_gated = (grad_hidden * lifted * gate_sig * (1.0 + gated * (1.0 - gate_sig))).astype(
        jnp.bfloat16
    )
    grad_lifted = (grad_hidden * activated).astype(jnp.bfloat16)
    grad_gate = contract_first(flat_rows, grad_gated)
    grad_up = contract_first(flat_rows, grad_lifted)
    grad_rows = (contract_last(grad_gated, gate_mat) + contract_last(grad_lifted, up_mat)).astype(
        jnp.bfloat16
    )
    return (grad_rows.reshape(rows_in.shape), grad_gate, grad_up, grad_down)


VMEM_BYTES = 60 * 1024 * 1024
COLUMN_CHUNK = 512
GROUP = 2


def select_rows(places_ref, gates_ref, pick_ref, capacity):
    expert_count, seq_len = places_ref.shape[1:]
    slot_range = lax.broadcasted_iota(jnp.int32, (capacity, seq_len), 0).astype(jnp.bfloat16)
    nothing = jnp.zeros((capacity, seq_len), jnp.bfloat16)
    for expert in range(expert_count):
        hit = places_ref[0, expert : expert + 1, :] == slot_range
        if gates_ref is None:
            weight = jnp.ones((capacity, seq_len), jnp.bfloat16)
        else:
            weight = jnp.broadcast_to(gates_ref[0, expert : expert + 1, :], (capacity, seq_len))
        rows = slice(expert * capacity, (expert + 1) * capacity)
        pick_ref[rows, :] = jnp.where(hit, weight, nothing)


def rows_to_slots(pick_ref, rows_ref, slots_ref, pack, capacity):
    width = rows_ref.shape[2]
    expert_count = slots_ref.shape[0]
    for start in range(0, width, COLUMN_CHUNK):
        columns = slice(start, start + COLUMN_CHUNK)
        picked = matmul(pick_ref[...], rows_ref[0, :, columns]).astype(jnp.bfloat16)
        slots_ref[:, pack, :, columns] = picked.reshape(expert_count, capacity, COLUMN_CHUNK)


def slots_to_rows(pick_ref, slots_ref, own_ref, other_ref, pack):
    width = own_ref.shape[3]
    for start in range(0, width, COLUMN_CHUNK):
        columns = slice(start, start + COLUMN_CHUNK)
        slots = slots_ref[:, pack, :, columns].reshape(-1, COLUMN_CHUNK)
        rows = contract_first(pick_ref[...], slots).astype(own_ref.dtype)
        rows = rows.reshape(2, 2, own_ref.shape[2], COLUMN_CHUNK)
        own_ref[0, :, :, columns] = rows[:, 0]
        other_ref[0, :, :, columns] = rows[:, 1]


def cot_kernel(
    packs, steps, capacity, table, places, gates, rows, down, slots_out, hidden_out, slots, pick
):
    step = pl.program_id(0)

    @pl.when(step < packs)
    def _():
        select_rows(places, gates, pick, capacity)
        rows_to_slots(pick, rows, slots, step, capacity)

    @pl.when(step >= packs)
    def _():
        for member in range(down.shape[0]):
            block = slots[(step - packs) * down.shape[0] + member].reshape(packs * capacity, -1)
            slots_out[member] = block
            hidden_out[member] = contract_last(block, down[member])


def piece_copies(own, other, rows, sems, pack):
    half_rows = own.shape[1]
    copies = []
    for far in range(2):
        for core, source in enumerate((own, other)):
            for half, index in enumerate((4 * far + pack, 2 + 4 * pack + far)):
                start = ((far * 2 + core) * 2 + half) * half_rows
                copies.append(
                    pltpu.make_async_copy(
                        source.at[index],
                        rows.at[pack, pl.ds(start, half_rows)],
                        sems.at[pack * 8 + len(copies)],
                    )
                )
    return copies


def row_kernel(
    packs, steps, capacity, places, own, other, both, grad_hidden,
    slots_out, hidden_out, grads_out, rows_own, rows_other,
    rows, slots, grads, pick, sems,
):
    step = pl.program_id(0)
    half = hidden_out.shape[2]

    @pl.when(step == 0)
    def _():
        for pack in range(packs):
            for copy in piece_copies(own, other, rows, sems, pack):
                copy.start()
        for pack in range(packs):
            select_rows(places.at[pl.ds(pack, 1)], None, pick.at[pack], capacity)

    for pack in range(packs):

        @pl.when(step == pack)
        def _(pack=pack):
            for copy in piece_copies(own, other, rows, sems, pack):
                copy.wait()
            rows_to_slots(pick.at[pack], rows.at[pl.ds(pack, 1)], slots, pack, capacity)

    @pl.when((step >= packs) & (step < packs + steps))
    def _():
        for member in range(both.shape[0]):
            expert = (step - packs) * both.shape[0] + member
            block = slots[expert].reshape(packs * capacity, -1)
            slots_out[member] = block
            product = matmul(block, both[member])
            gated, lifted = product[:, :half], product[:, half:]
            sig = 1.0 / (1.0 + jnp.exp(-gated))
            active = gated * sig
            hidden_out[member] = (active * lifted).astype(jnp.bfloat16)
            above = grad_hidden[member]
            grad_gated = above * lifted * sig * (1.0 + gated * (1.0 - sig))
            joined = jnp.concatenate([grad_gated, above * active], axis=1).astype(jnp.bfloat16)
            grads_out[member] = joined
            back = contract_last(joined, both[member])
            grads[expert] = back.astype(jnp.bfloat16).reshape(packs, capacity, -1)

    for pack in range(packs):

        @pl.when(step == packs + steps + pack)
        def _(pack=pack):
            slots_to_rows(pick.at[pack], grads, rows_own, rows_other, pack)


def mix_kernel(packs, steps, capacity, table, places, gates, hidden, down, *refs):
    rows, results, pick = refs[-3:]
    step = pl.program_id(0)

    @pl.when(step < steps)
    def _():
        for member in range(down.shape[0]):
            result = matmul(hidden[member], down[member]).astype(jnp.bfloat16)
            results[step * down.shape[0] + member] = result.reshape(packs, capacity, -1)

    @pl.when(step >= steps)
    def _():
        select_rows(places, gates, pick, capacity)
        pack = (step - steps) ^ table[0]
        for start in range(0, rows.shape[3], COLUMN_CHUNK):
            columns = slice(start, start + COLUMN_CHUNK)
            slots = results[:, pack, :, columns].reshape(-1, COLUMN_CHUNK)
            rows[0, 0, :, columns] = contract_first(pick[...], slots).astype(rows.dtype)


def weight_kernel(planes, *refs):
    slots, grads, hidden, above = (
        jnp.concatenate([ref[0] for ref in refs[i * planes : (i + 1) * planes]]) for i in range(4)
    )
    gate_out, up_out, down_out = refs[-3:]
    half = gate_out.shape[2]
    both = contract_first(slots, above)
    gate_out[0] = both[:, :half]
    up_out[0] = both[:, half:]
    down_out[0] = contract_first(hidden, grads)


def block(shape, place, count=1):
    tail = (0,) * (len(shape) - 1)
    return pl.BlockSpec((count,) + tuple(shape[1:]), lambda *ids: (place(*ids),) + tail)


def staged(first, count):
    return lambda step, *rest: jnp.clip(step - first, 0, count - 1)


def shape_of(shape, kind):
    return jax.ShapeDtypeStruct(shape, kind)


def call(kernel, steps, specs, out_specs, out_shape, scratch, flops, prefetch=0, aliases={}):
    return pl.pallas_call(
        kernel,
        grid_spec=pltpu.PrefetchScalarGridSpec(
            num_scalar_prefetch=prefetch,
            grid=(steps,),
            in_specs=specs,
            out_specs=out_specs,
            scratch_shapes=scratch,
        ),
        out_shape=out_shape,
        input_output_aliases=aliases,
        cost_estimate=pl.CostEstimate(
            flops=flops, transcendentals=0, bytes_accessed=flops // 500
        ),
        compiler_params=pltpu.CompilerParams(
            dimension_semantics=("arbitrary",), vmem_limit_bytes=VMEM_BYTES
        ),
    )


def cot_slots(table, places, gates, rows, down, capacity):
    packs = table.shape[0]
    _, seq_len, width = rows.shape
    experts, hidden_width, _ = down.shape
    slot_rows = packs * capacity
    group = math.gcd(experts, GROUP)
    steps = experts // group
    by_pack, by_expert = staged(0, packs), staged(packs, steps)
    listed = lambda step, numbers: numbers[by_pack(step)]
    out_shape = [
        shape_of((experts, slot_rows, width), jnp.bfloat16),
        shape_of((experts, slot_rows, hidden_width), jnp.float32),
    ]
    return call(
        functools.partial(cot_kernel, packs, steps, capacity),
        packs + steps,
        [
            block(places.shape, listed), block(gates.shape, listed), block(rows.shape, listed),
            block(down.shape, by_expert, group),
        ],
        [block(out.shape, by_expert, group) for out in out_shape],
        out_shape,
        [
            pltpu.VMEM((experts, packs, capacity, width), jnp.bfloat16),
            pltpu.VMEM((experts * capacity, seq_len), jnp.bfloat16),
        ],
        2 * experts * slot_rows * width * (seq_len + hidden_width),
        1,
    )(table, places, gates, rows, down)


def row_slots(places, own, other, both, grad_hidden, capacity):
    packs, _, seq_len = places.shape
    experts, width, hidden_width = both.shape
    slot_rows = packs * capacity
    group = math.gcd(experts, GROUP)
    steps = experts // group
    middle, last = staged(packs, steps), staged(packs + steps, packs)
    part = shape_of((packs, 2, seq_len // 4, width), jnp.bfloat16)
    out_shape = [
        shape_of((experts, slot_rows, width), jnp.bfloat16),
        shape_of((experts, slot_rows, hidden_width // 2), jnp.bfloat16),
        shape_of((experts, slot_rows, hidden_width), jnp.bfloat16),
        part, part,
    ]
    anywhere = pl.BlockSpec(memory_space=pl.ANY)
    return call(
        functools.partial(row_kernel, packs, steps, capacity),
        2 * packs + steps,
        [
            block(places.shape, lambda step: 0, packs), anywhere, anywhere,
            block(both.shape, middle, group), block(grad_hidden.shape, middle, group),
        ],
        [block(out.shape, middle, group) for out in out_shape[:3]] + [block(part.shape, last)] * 2,
        out_shape,
        [
            pltpu.VMEM((packs, seq_len, width), jnp.bfloat16),
            pltpu.VMEM((experts, packs, capacity, width), jnp.bfloat16),
            pltpu.VMEM((experts, packs, capacity, width), jnp.bfloat16),
            pltpu.VMEM((packs, experts * capacity, seq_len), jnp.bfloat16),
            pltpu.SemaphoreType.DMA((8 * packs,)),
        ],
        4 * experts * slot_rows * width * (seq_len + hidden_width),
    )(places, own, other, both, grad_hidden)


def mix_rows(plane, planes, table, places, gates, hidden, down, capacity, earlier=()):
    packs, _, seq_len = places.shape
    experts, hidden_width, width = down.shape
    group = math.gcd(experts, GROUP)
    steps = experts // group
    first, last = staged(0, steps), staged(steps, packs)
    listed = lambda step, numbers: numbers[1] * steps + first(step)
    return call(
        functools.partial(mix_kernel, packs, steps, capacity),
        packs + steps,
        [
            block(places.shape, last), block(gates.shape, last),
            block(hidden.shape, listed, group), block(down.shape, first, group),
        ]
        + [pl.BlockSpec(memory_space=pl.ANY)] * len(earlier),
        [pl.BlockSpec((1, 1, seq_len, width), lambda step, numbers: (plane, last(step), 0, 0))],
        [shape_of((planes, packs, seq_len, width), jnp.bfloat16)],
        [
            pltpu.VMEM((experts, packs, capacity, width), jnp.bfloat16),
            pltpu.VMEM((experts * capacity, seq_len), jnp.bfloat16),
        ],
        2 * experts * packs * capacity * width * (seq_len + hidden_width),
        1,
        aliases={5 + index: index for index in range(len(earlier))},
    )(table, places, gates, hidden, down, *earlier)


def weight_grads(first, count, slots, hidden, grads, above, earlier=()):
    planes = len(slots)
    operands = [*slots, *grads, *hidden, *above]
    experts, _, width = slots[0].shape
    hidden_width = hidden[0].shape[2]
    each = lambda step: step + first
    out_shape = [
        shape_of((experts, width, hidden_width), jnp.float32),
        shape_of((experts, width, hidden_width), jnp.float32),
        shape_of((experts, hidden_width, width), jnp.float32),
    ]
    return call(
        functools.partial(weight_kernel, planes),
        count,
        [block(operand.shape, each) for operand in operands]
        + [pl.BlockSpec(memory_space=pl.ANY)] * len(earlier),
        [block(out.shape, each) for out in out_shape],
        out_shape,
        [],
        6 * planes * slots[0].shape[1] * count * width * hidden_width,
        aliases={len(operands) + index: index for index in range(len(earlier))},
    )(*operands, *earlier)


def swapped(values, axis, bit):
    count = lax.axis_size(axis)
    return lax.ppermute(values, axis, [(i, i ^ bit) for i in range(count)])


def far_side(values):
    return swapped(values, TENSOR, 2)


def far_core(values):
    return swapped(values, TENSOR, 1)


def far_pack(values):
    return swapped(values, DP, 1)


def next_plane(values):
    count = lax.axis_size(DP)
    return lax.ppermute(values, DP, [(i, (i + 2) % count) for i in range(count)])


def spread_all(values, small, work):
    planes = lax.axis_size("plane")
    half_rows = values.shape[0] // 2
    first = lambda rows: (far_pack(rows[:half_rows]), far_side(rows[half_rows:]))
    small, values = tied(small, values)
    (across_pack, across_side), following = lax.optimization_barrier(
        (first(values), next_plane(values))
    )
    pieces, made = [], []
    for plane in range(planes):
        upper = jnp.stack([values[:half_rows], across_pack])
        lower = jnp.stack([values[half_rows:], across_side])
        small, (upper, lower, values) = tied(small, (upper, lower, following))
        moved = [
            far_side(upper),
            far_pack(lower),
            first(values) if plane + 1 < planes else ((), ()),
            next_plane(values) if plane + 2 < planes else (),
            far_core(pieces[-1]) if plane else (),
            work(plane - 2, small) if plane > 1 else (),
        ]
        upper_far, lower_far, (across_pack, across_side), following, other, result = (
            lax.optimization_barrier(moved)
        )
        if plane:
            pieces[-1] = (pieces[-1], other)
        if plane > 1:
            made.append(result)
        pieces.append(jnp.concatenate([upper, lower, upper_far, lower_far]))
    pieces[-1] = (pieces[-1], far_core(pieces[-1]))
    return pieces, made


def plane_order():
    packs = lax.axis_size(DP)
    planes = packs // 2
    index = lax.axis_index(DP)
    return jnp.stack(
        [
            ((index // 2 + planes - plane) % planes) * 2 + (index % 2 ^ near)
            for plane in range(planes)
            for near in range(2)
        ]
    )


def place_kernel(by_column, order, *refs):
    *pieces, whole, sems = refs
    copies = []
    for index, piece in enumerate(pieces):
        target = None if by_column else whole.at[order[index]]
        if by_column:
            width = piece.shape[1]
            target = whole.at[:, pl.ds(pl.multiple_of(order[index] * width, 128), width)]
        copies.append(pltpu.make_async_copy(piece, target, sems.at[index]))
        copies[-1].start()
    for copy in copies:
        copy.wait()


def laid(pieces, order, by_column=False):
    count = len(pieces)
    rows, columns = pieces[0].shape
    shape = (rows, count * columns) if by_column else (count, rows, columns)
    anywhere = pl.BlockSpec(memory_space=pl.ANY)
    return call(
        functools.partial(place_kernel, by_column),
        1,
        [anywhere] * count,
        pl.BlockSpec(memory_space=pltpu.VMEM),
        shape_of(shape, pieces[0].dtype),
        [pltpu.SemaphoreType.DMA((count,))],
        1000,
        1,
    )(order, *pieces)


class FoldPacks:
    def __init__(self, values):
        order = plane_order()
        take = lambda index: lax.dynamic_index_in_dim(values, order[index], 0, keepdims=False)
        planes = values.shape[0] // 2
        self.turns = [*range(1, planes), 0]
        self.near = {plane: take(2 * plane) for plane in self.turns}
        self.moving = {plane: far_pack(take(2 * plane + 1)) for plane in self.turns}
        self.summed, self.count = None, 0

    def step(self, other):
        if self.count >= len(self.turns):
            return other
        self.moving, other = tied(self.moving, other)
        if self.summed is None:
            self.near = {plane: added(self.near[plane], self.moving[plane]) for plane in self.turns}
            self.summed = self.near[self.turns[0]]
        else:
            kind = jnp.float32 if self.count + 1 == len(self.turns) else jnp.bfloat16
            self.summed = added(self.moving, self.near[self.turns[self.count]], kind)
        self.count += 1
        if self.count < len(self.turns):
            self.moving = next_plane(self.summed)
        return other

    def finish(self):
        for plane in self.turns[self.count :]:
            kind = jnp.float32 if plane == 0 else jnp.bfloat16
            self.summed = added(self.moving, self.near[plane], kind)
            self.moving = next_plane(self.summed) if plane else None
        return self.summed


def laid_sides(pieces):
    order = lax.axis_index(TENSOR) ^ jnp.arange(len(pieces), dtype=jnp.int32)
    return laid(pieces, order).reshape((-1,) + pieces[0].shape[1:])


def gather_sides(values):
    across = far_side(values)
    return laid_sides([values, far_core(values), across, far_core(across)])


def fold_sides(values):
    split = values.astype(jnp.bfloat16).reshape((4, -1) + values.shape[1:])
    take = lambda bits: lax.dynamic_index_in_dim(
        split, lax.axis_index(TENSOR) ^ bits, 0, keepdims=False
    )
    far = added(take(2), far_core(take(3)))
    near = added(take(0), far_core(take(1)))
    return added(near, far_side(far), jnp.float32)


def fold_both(weights, rows):
    order = plane_order()
    planes = weights.shape[0] // 2
    take = lambda index: lax.dynamic_index_in_dim(weights, order[index], 0, keepdims=False)
    split = rows.astype(jnp.bfloat16).reshape((4, -1) + rows.shape[1:])
    mine = lax.axis_index(TENSOR)
    pick = lambda bits: lax.dynamic_index_in_dim(split, mine ^ bits, 0, keepdims=False)
    summed, total = None, None
    for turn, plane in enumerate([*range(1, planes), 0]):
        moved = [far_pack(take(2 * plane + 1)), () if summed is None else next_plane(summed)]
        if turn == 0:
            moved += [far_core(pick(3)), far_core(pick(1))]
        if turn == 1:
            moved += [far_side(far)]
        across, passed, *arrived = lax.optimization_barrier(moved)
        if turn == 0:
            far, close = added(pick(2), arrived[0]), added(pick(0), arrived[1])
        if turn == 1:
            total = added(close, arrived[0], jnp.float32)
        near = added(take(2 * plane), across)
        kind = jnp.float32 if turn + 1 == planes else jnp.bfloat16
        summed = near if turn == 0 else added(passed, near, kind)
    return summed, total


def gather_both(weights, outer, rows, gate, up, tables):
    hops = table_hops()
    pieces, outer_pieces, row_pieces, values = [], [], [rows], (weights, outer)
    planes = lax.axis_size("plane")
    for plane in range(planes):
        moved = [tuple(far_pack(value) for value in values), ()]
        if plane + 1 < planes:
            moved[1] = tuple(next_plane(value) for value in values)
        if plane == 0:
            moved += [far_core(rows), far_side(rows)]
        if plane == 1:
            moved += [far_core(row_pieces[2])]
        if plane == 0:
            moved.insert(2, jnp.concatenate([gate, up], axis=2))
        moved.insert(2, swapped(tables, *hops[plane]) if plane < len(hops) else ())
        across, following, more, *arrived = lax.optimization_barrier(moved)
        if plane < len(hops):
            tables = jnp.concatenate([tables, more])
        if plane == 0:
            joined = arrived.pop(0)
        pieces += [values[0], across[0]]
        outer_pieces += [values[1], across[1]]
        row_pieces += arrived
        values = following
    order = plane_order()
    for hop in hops[planes:]:
        tables = jnp.concatenate([tables, swapped(tables, *hop)])
    laid_rows = laid_sides(row_pieces)
    return laid(pieces, order), laid(outer_pieces, order, True), laid_rows, joined, tables


def sum_everywhere(values):
    for axis in (TENSOR, DP):
        bit = 1
        while bit < lax.axis_size(axis):
            values = values + swapped(values, axis, bit)
            bit *= 2
    return values


def added(left, right, kind=jnp.bfloat16):
    return (left.astype(jnp.float32) + right.astype(jnp.float32)).astype(kind)


def fold_first(own, arrived):
    half_rows = own.shape[2] // 2
    upper, lower = slice(None, half_rows), slice(half_rows, None)
    return (
        added(own[:, 0, upper], arrived[:, 0, upper]),
        added(own[0, :, lower], arrived[0, :, lower]),
        added(own[:, 1, upper], arrived[:, 1, upper]),
        added(own[1, :, lower], arrived[1, :, lower]),
    )


def tied(small, values):
    return lax.optimization_barrier((small, values))


def table_hops():
    hops = []
    for axis in (TENSOR, DP):
        bit = 1
        while bit < lax.axis_size(axis):
            hops.append((axis, bit))
            bit *= 2
    return hops


def read_tables(tables, top_count):
    own = lax.axis_index(DP) * lax.axis_size(TENSOR) + lax.axis_index(TENSOR)
    sides = jnp.arange(lax.axis_size(TENSOR), dtype=jnp.int32) ^ lax.axis_index(TENSOR)
    segments = jnp.take(tables[: sides.shape[0], -1], sides, axis=0).reshape(-1)
    devices = jnp.arange(tables.shape[0], dtype=jnp.int32)
    tables = jnp.take(tables, devices ^ own, axis=0)
    all_ids, all_gates = tables[:, :top_count], tables[:, top_count : 2 * top_count]
    return all_ids.astype(jnp.int32), all_gates, segments.astype(jnp.int32)


def routing(all_ids, all_gates, local_experts, capacity):
    packs = lax.axis_size(DP)
    first = lax.axis_index(DP) * local_experts
    wanted = first + jnp.arange(local_experts, dtype=jnp.int32)

    def by_pack(values):
        top_count, tok_rows = values.shape[1:]
        ordered = values.reshape(packs, -1, top_count, tok_rows).transpose(0, 2, 1, 3)
        return ordered.reshape(packs, top_count, -1)

    matches = by_pack(all_ids)[:, :, None, :] == wanted[None, None, :, None]
    pair_gates = by_pack(all_gates).astype(jnp.float32)
    member = jnp.any(matches, axis=1)
    gates = jnp.sum(jnp.where(matches, pair_gates[:, :, None, :], 0.0), axis=1)
    order = jnp.arange(member.shape[2], dtype=jnp.int32)
    earlier = (order[:, None] < order[None, :]).astype(jnp.bfloat16)
    flat = member.reshape(packs * local_experts, -1).astype(jnp.bfloat16)
    before = matmul(flat, earlier).astype(jnp.int32).reshape(member.shape)
    places = jnp.where(member & (before < capacity), before, -1)
    return places.astype(jnp.bfloat16), gates.astype(jnp.bfloat16)


def experts_by_exchange(
    second_in, cotangent, expert_ids, gate_values, w_gate, w_up, w_down, middle, capacity
):
    tok_rows, model_width = second_in.shape
    tensor_count = lax.axis_size(TENSOR)
    data_count = lax.axis_size(DP)
    local_experts = w_gate.shape[0]
    all_experts = local_experts * data_count
    top_count = expert_ids.shape[1]
    seq_len = tok_rows * tensor_count
    pack_cot, pack_ids, pack_gates = (
        gather_rows(cotangent), gather_rows(expert_ids), gather_rows(gate_values)
    )
    pack_second = gather_rows(second_in)
    expert_range = jnp.arange(all_experts, dtype=jnp.int32)
    matches = pack_ids[:, :, None] == expert_range[None, None, :]
    token_counts = jnp.sum(matches.astype(jnp.float32), axis=1).astype(jnp.bfloat16)
    token_range = jnp.arange(seq_len, dtype=jnp.int32)
    earlier = (token_range[:, None] > token_range[None, :]).astype(jnp.bfloat16)
    before = matmul(earlier, token_counts)
    places = (
        jnp.sum(jnp.where(matches, before[:, None, :], 0.0), axis=2).astype(jnp.int32).reshape(-1)
    )
    flat_ids = pack_ids.reshape(-1)
    owners = flat_ids // local_experts
    local_index = flat_ids % local_experts
    dump_slot = all_experts * capacity
    slot_index = jnp.where(
        places < capacity,
        local_index * (data_count * capacity) + owners * capacity + places,
        dump_slot,
    ).astype(jnp.int32)
    pair_token = jnp.arange(seq_len * top_count) // top_count
    slot_token = (
        jnp.full((dump_slot + 1,), seq_len, jnp.int32).at[slot_index].set(pair_token)[:dump_slot]
    )
    pair_gates = pack_gates.astype(jnp.float32)
    slot_gate = (
        jnp.zeros((dump_slot + 1,), jnp.float32)
        .at[slot_index]
        .set(pair_gates.reshape(-1))[:dump_slot]
    )
    pair_slots = slot_index.reshape(seq_len, top_count)
    layout = (local_experts, data_count, capacity)
    arrived_rows = to_experts(pack_second, slot_token, None, layout)
    expert_out, gated_all, lifted_all = lax.map(
        expert_forward, (arrived_rows, w_gate, w_up, w_down)
    )
    returned = from_experts(expert_out).reshape(-1, model_width)

    def combine_term(offset, row_count):
        return pair_sum(returned, pack_gates, pair_slots, row_count)

    outputs = middle + row_sum(combine_term, tok_rows)
    grad_arrived = to_experts(pack_cot, slot_token, slot_gate, layout)
    grad_rows_all, grad_w_gate, grad_w_up, grad_w_down = lax.map(
        expert_backward, (arrived_rows, grad_arrived, gated_all, lifted_all, w_gate, w_up, w_down)
    )
    returned_grad = from_experts(grad_rows_all).reshape(-1, model_width)
    unit_gates = jnp.ones_like(pack_gates)

    def dispatch_term(offset, row_count):
        return pair_sum(returned_grad, unit_gates, pair_slots, row_count)

    grad_second = row_sum(dispatch_term, tok_rows)
    return outputs, grad_second, grad_w_gate, grad_w_up, grad_w_down


class Folding:
    def __init__(self, order):
        self.order, self.planes, self.ready = order, {}, {}
        self.summed, self.passed, self.count = None, None, 0

    def begin(self, plane, own, other):
        self.planes[plane] = (0, (own, other))

    def turn(self, small, work):
        small, (planes, summed) = tied(
            small, ({plane: values for plane, (_, values) in self.planes.items()}, self.summed)
        )
        sent = {}
        for plane, values in planes.items():
            stage = self.planes[plane][0]
            if stage == 0:
                sent[plane] = (far_core(values[1]),)
            elif stage == 1:
                sent[plane] = (far_side(values[2]), far_pack(values[3]))
            else:
                sent[plane] = (far_pack(values[2]), far_side(values[3]))
        passed = self.passed
        if passed is None and summed is not None and not self.done():
            passed = next_plane(summed)
        sent, passed, result = lax.optimization_barrier((sent, passed, work(small)))
        self.passed = passed
        for plane, values in planes.items():
            stage, arrived = self.planes[plane][0], sent[plane]
            if stage == 0:
                made = fold_first(values[0], *arrived)
            elif stage == 1:
                upper, lower = added(values[0], arrived[0]), added(values[1], arrived[1])
                made = (upper[0], lower[0], upper[1], lower[1])
            else:
                self.ready[plane] = jnp.concatenate(
                    [added(values[0], arrived[0]), added(values[1], arrived[1])]
                )
            if stage < 2:
                self.planes[plane] = (stage + 1, made)
            else:
                del self.planes[plane]
        following = self.order[self.count] if self.count < len(self.order) else None
        if following in self.ready:
            last = self.count + 1 == len(self.order)
            self.summed = self.ready[following]
            if passed is not None:
                kind = jnp.float32 if last else jnp.bfloat16
                self.summed = added(passed, self.summed, kind)
            self.passed = None
            self.count += 1
        return result

    def done(self):
        return self.count == len(self.order)


def experts_by_gather(second_in, all_cot, places, gates, w_both, w_down, capacity):
    packs, local_experts, seq_len = places.shape
    tensor_count = lax.axis_size(TENSOR)
    planes = packs // 2
    pack_order = plane_order()
    side_index = lax.axis_index(TENSOR)
    quarter_order = side_index ^ jnp.arange(tensor_count, dtype=jnp.int32)

    def as_met(values, by_pack, by_quarter):
        split = values.reshape(packs, local_experts, tensor_count, -1)
        split = jnp.take(jnp.take(split, by_pack, axis=0), by_quarter, axis=2)
        return split.reshape(values.shape)

    near_places = as_met(places, pack_order, quarter_order)
    pairs = [slice(plane * 2, plane * 2 + 2) for plane in range(planes)]
    tables = [
        jnp.stack([lax.axis_index("pack"), (lax.axis_index("plane") + planes - plane) % planes])
        for plane in range(planes)
    ]
    prepared = [
        [table[pair] for pair in pairs] for table in (near_places, places, gates, pack_order)
    ]
    prepared, second_in = tied((prepared, tables, places, gates), second_in)
    (near_places, mix_places, mix_gates, pack_order), tables, places, gates = prepared

    def cot_work(plane, order):
        return cot_slots(order[plane], places, gates, all_cot, w_down, capacity)

    pieces, made = spread_all(second_in, pack_order, cot_work)
    order = [*range(1, planes), 0]
    kept, folding = {}, Folding(order)

    def row_work(plane, near):
        return row_slots(near, *pieces[plane], w_both, made[plane][1], capacity)

    for plane in order:
        if folding.planes:
            result = folding.turn(near_places[plane], functools.partial(row_work, plane))
        else:
            result = row_work(plane, near_places[plane])
        slots, hidden, above, *part = result
        folding.begin(plane, *part)
        kept[plane] = (slots, hidden, made[plane][0], above)
        if len(made) < planes:
            made.append(folding.turn(pack_order, functools.partial(cot_work, len(made))))
    hidden_all = jnp.concatenate([kept[plane][1] for plane in range(planes)])

    def mix_turn(some, given):
        table, mixed = given
        for plane in some:
            mixed = mix_rows(
                plane, planes, table[plane], mix_places[plane], mix_gates[plane], hidden_all, w_down,
                capacity, mixed,
            )
        return mixed

    mixed = ()
    for start in range(0, planes, 2):
        some = range(start, start + 2)
        mixed = folding.turn((tables, mixed), functools.partial(mix_turn, some))
    whole = mixed[0].reshape(planes, -1, mixed[0].shape[-1])
    whole = lax.psum_scatter(
        whole, ("pack", "side", "core"), scatter_dimension=1, tiled=True
    )
    kept = [kept[plane] for plane in range(planes)]
    weight_parts, next_expert = (), 0
    part_size = math.gcd(local_experts, GROUP)

    def weight_turn(count, small):
        state, (held, weights) = next_expert, small
        for _ in range(count):
            if state < local_experts:
                weights = weight_grads(state, part_size, *zip(*held), weights)
                state += part_size
        return weights

    for count in (2, 1, *[0] * planes):
        if folding.done():
            break
        weight_parts = folding.turn((kept, weight_parts), functools.partial(weight_turn, count))
        next_expert = min(next_expert + count * part_size, local_experts)
    rest = (kept, weight_parts, next_expert, part_size)
    return folding.summed, whole, rest


def shards(
    inputs,
    segment_ids,
    expert_ids,
    gate_values,
    attn_gain,
    query_gain,
    key_gain,
    w_query,
    w_key,
    w_value,
    w_output,
    ffn_gain,
    w_gate,
    w_up,
    w_down,
    cotangent,
):
    tok_rows, model_width = inputs.shape
    head_size = query_gain.shape[0]
    tensor_count = lax.axis_size(TENSOR)
    data_count = lax.axis_size(DP)
    local_experts = w_gate.shape[0]
    all_experts = local_experts * data_count
    top_count = expert_ids.shape[1]
    seq_len = tok_rows * tensor_count
    capacity = seq_len * top_count // all_experts
    inv_root = head_size ** (-0.5)
    by_gather = (
        seq_len <= local_experts * capacity
        and tensor_count == 4
        and data_count > 2
        and data_count & (data_count - 1) == 0
        and all_experts <= 256
    )
    if by_gather:
        axes = (*DP, *TENSOR)
        tables = jnp.concatenate(
            [expert_ids.T.astype(jnp.bfloat16), gate_values.T, segment_ids.astype(jnp.bfloat16)]
        )[None]
    inputs_f32 = inputs.astype(jnp.float32)
    normed_one, factor_one = norm_parts(inputs_f32)
    first_in = (normed_one * attn_gain).astype(jnp.bfloat16)
    if by_gather:
        side_sum, side_gather = fold_sides, gather_sides
        local_width = w_query.shape[1]
        w_in = jnp.concatenate([w_query, w_key, w_value], axis=1)
        full_in, full_output, pack_in, w_both, tables = gather_both(
            w_in, w_output, first_in, w_gate, w_up, tables
        )
        all_ids, all_gates, segments = read_tables(tables, top_count)
        places, gates = routing(all_ids, all_gates, local_experts, capacity)
        full_in, cotangent = tied(full_in, cotangent)
        all_cot = lax.all_gather(cotangent, axes, axis=0, tiled=True)
        all_cot = all_cot.reshape(data_count, seq_len, model_width)
        full_in = full_in.reshape(model_width, -1)
        full_query, full_key, full_value = (
            full_in[:, index * local_width : (index + 1) * local_width] for index in range(3)
        )
    else:
        side_sum, side_gather = lambda term: row_sum(lambda *_: term, tok_rows), gather_rows
        segments = lax.all_gather(segment_ids, TENSOR, axis=1, tiled=True)[0]
        full_query, full_key, full_value, full_output = (
            lax.all_gather(w_query, DP, axis=0, tiled=True),
            lax.all_gather(w_key, DP, axis=0, tiled=True),
            lax.all_gather(w_value, DP, axis=0, tiled=True),
            lax.all_gather(w_output, DP, axis=1, tiled=True),
        )
        pack_in = side_gather(first_in)
    query_pre = matmul(pack_in, full_query)
    key_pre = matmul(pack_in, full_key)
    value_low = matmul(pack_in, full_value).astype(jnp.bfloat16)
    head_count = query_pre.shape[1] // head_size
    cosine, sine_tab = rope_tables(seq_len, head_size)
    query_norm, query_factor = norm_parts(query_pre.reshape(seq_len, head_count, head_size))
    key_norm, key_factor = norm_parts(key_pre.reshape(seq_len, head_count, head_size))
    query_low = rotate(query_norm * query_gain, cosine, sine_tab).astype(jnp.bfloat16)
    key_low = rotate(key_norm * key_gain, cosine, sine_tab).astype(jnp.bfloat16)
    value_heads = value_low.reshape(seq_len, head_count, head_size)
    block_rows = min(512, seq_len)
    block_total = seq_len // block_rows
    masks = []
    mixture_parts = []
    lse_parts = []
    for block_index in range(block_total):
        offset = block_index * block_rows
        allowed = block_mask(segments, offset, block_rows, seq_len)
        masks.append(allowed)
        scores = block_scores(query_low[offset : offset + block_rows], key_low, allowed, inv_root)
        top_score = jnp.max(scores, axis=-1, keepdims=True)
        raw_weights = jnp.exp(scores - top_score)
        totals = jnp.sum(raw_weights, axis=-1, keepdims=True)
        weights_low = (raw_weights / totals).astype(jnp.bfloat16)
        mixture_parts.append(
            jnp.einsum(
                "hqk,khd->qhd", weights_low, value_heads, preferred_element_type=jnp.float32
            ).astype(jnp.bfloat16)
        )
        lse_parts.append(top_score + jnp.log(totals))
    mixture = jnp.concatenate(mixture_parts, axis=0).reshape(seq_len, head_count * head_size)

    middle = inputs_f32 + side_sum(matmul(mixture, full_output))
    normed_two, factor_two = norm_parts(middle)
    second_in = (normed_two * ffn_gain).astype(jnp.bfloat16)
    if by_gather:
        grad_second, mixed, rest = experts_by_gather(
            second_in, all_cot, places, gates, w_both, w_down, capacity
        )
    else:
        outputs, grad_second, grad_w_gate, grad_w_up, grad_w_down = experts_by_exchange(
            second_in, cotangent, expert_ids, gate_values, w_gate, w_up, w_down, middle, capacity
        )
    ffn_gain_part = jnp.sum(grad_second * normed_two, axis=0)
    grad_middle = cotangent.astype(jnp.float32) + norm_back(
        grad_second, normed_two, factor_two, ffn_gain
    )
    grad_attended = grad_middle.astype(jnp.bfloat16)
    if by_gather:
        kept, weight_parts, next_expert, part_size = rest
        (kept, weight_parts), grad_attended = tied((kept, weight_parts), grad_attended)
        moved = [far_core(grad_attended), far_side(grad_attended)]
        for first in range(next_expert, local_experts, part_size):
            weight_parts = weight_grads(first, part_size, *zip(*kept), weight_parts)
        grad_w_gate, grad_w_up, grad_w_down = weight_parts
        near, across, weight_parts = lax.optimization_barrier((*moved, weight_parts))
        grad_w_gate, grad_w_up, grad_w_down = weight_parts
        pack_grad = laid_sides([grad_attended, near, across, far_core(across)])
    else:
        pack_grad = side_gather(grad_attended)
    output_part = contract_first(mixture, pack_grad)
    fold_step = lambda other: other
    if by_gather:
        by_column = output_part.astype(jnp.bfloat16).reshape(local_width, data_count, -1)
        folded = FoldPacks(by_column.transpose(1, 0, 2))
        fold_step = folded.step
    grad_mixture = (
        contract_last(pack_grad, full_output)
        .astype(jnp.bfloat16)
        .reshape(seq_len, head_count, head_size)
    )
    grad_query_parts = []
    grad_key_sum = jnp.zeros((seq_len, head_count, head_size), jnp.float32)
    grad_value_sum = jnp.zeros((seq_len, head_count, head_size), jnp.float32)
    for block_index in range(block_total):
        offset = block_index * block_rows
        query_block = query_low[offset : offset + block_rows]
        if block_index:
            query_block = fold_step(query_block)
        grad_block = grad_mixture[offset : offset + block_rows]
        scores = block_scores(query_block, key_low, masks[block_index], inv_root)
        prob_rows = jnp.exp(scores - lse_parts[block_index])
        grad_probs = jnp.einsum(
            "qhd,khd->hqk", grad_block, value_heads, preferred_element_type=jnp.float32
        )
        row_delta = jnp.sum(grad_probs * prob_rows, axis=-1, keepdims=True)
        grad_scores = (prob_rows * (grad_probs - row_delta)).astype(jnp.bfloat16)
        grad_query_parts.append(
            jnp.einsum("hqk,khd->qhd", grad_scores, key_low, preferred_element_type=jnp.float32)
            * inv_root
        )
        grad_key_sum = (
            grad_key_sum
            + jnp.einsum(
                "hqk,qhd->khd", grad_scores, query_block, preferred_element_type=jnp.float32
            )
            * inv_root
        )
        grad_value_sum = grad_value_sum + jnp.einsum(
            "hqk,qhd->khd",
            prob_rows.astype(jnp.bfloat16),
            grad_block,
            preferred_element_type=jnp.float32,
        )
    grad_query_norm = rotate_back(jnp.concatenate(grad_query_parts, axis=0), cosine, sine_tab)
    grad_key_norm = rotate_back(grad_key_sum, cosine, sine_tab)
    grad_query_norm = fold_step(grad_query_norm)
    grad_key_norm = fold_step(grad_key_norm)
    query_gain_part = jnp.sum(grad_query_norm * query_norm, axis=(0, 1))
    key_gain_part = jnp.sum(grad_key_norm * key_norm, axis=(0, 1))
    grad_query_pre = (
        norm_back(grad_query_norm, query_norm, query_factor, query_gain)
        .reshape(seq_len, -1)
        .astype(jnp.bfloat16)
    )
    grad_key_pre = (
        norm_back(grad_key_norm, key_norm, key_factor, key_gain)
        .reshape(seq_len, -1)
        .astype(jnp.bfloat16)
    )
    grad_value_low = grad_value_sum.reshape(seq_len, -1).astype(jnp.bfloat16)
    query_part = contract_first(pack_in, grad_query_pre)
    key_part = contract_first(pack_in, grad_key_pre)
    value_part = contract_first(pack_in, grad_value_low)

    total_term = contract_last(grad_query_pre, full_query)
    total_term = total_term + contract_last(grad_key_pre, full_key)
    total_term = total_term + contract_last(grad_value_low, full_value)
    if by_gather:
        in_part = jnp.concatenate([query_part, key_part, value_part], axis=1)
        in_part = in_part.astype(jnp.bfloat16).reshape(data_count, -1, 3 * local_width)
        in_part = fold_step(in_part)
        grad_w_output = folded.finish()
        mixed, in_part = tied(mixed, in_part)
        mixed = lax.psum_scatter(mixed, "plane", scatter_dimension=0, tiled=True)
        grad_in, grad_first = fold_both(in_part, total_term)
        mixed, grad_in = tied(mixed, grad_in)
    else:
        grad_first = side_sum(total_term)
    attn_gain_part = jnp.sum(grad_first * normed_one, axis=0)
    grad_inputs = grad_middle + norm_back(grad_first, normed_one, factor_one, attn_gain)
    gain_parts = (attn_gain_part, ffn_gain_part, query_gain_part, key_gain_part)
    if by_gather:
        grad_w_query, grad_w_key, grad_w_value = (
            grad_in[:, index * local_width : (index + 1) * local_width] for index in range(3)
        )
        outputs = middle + mixed[0].astype(jnp.float32)
        splits = (model_width, 2 * model_width, 2 * model_width + head_size)
        gain_sums = jnp.split(sum_everywhere(jnp.concatenate(gain_parts)), splits)
    else:
        grad_w_query, grad_w_key, grad_w_value, grad_w_output = (
            lax.psum_scatter(
                part.astype(jnp.bfloat16), DP, scatter_dimension=along, tiled=True
            ).astype(jnp.float32)
            for part, along in ((query_part, 0), (key_part, 0), (value_part, 0), (output_part, 1))
        )
        gain_sums = lax.psum(gain_parts, (*DP, *TENSOR))
    grad_attn_gain, grad_ffn_gain, grad_query_gain, grad_key_gain = gain_sums
    return (
        outputs,
        grad_inputs,
        grad_attn_gain,
        grad_query_gain,
        grad_key_gain,
        grad_w_query,
        grad_w_key,
        grad_w_value,
        grad_w_output,
        grad_ffn_gain,
        grad_w_gate,
        grad_w_up,
        grad_w_down,
    )


def solution(mesh):
    rows, columns = mesh.devices.shape
    split = jax.sharding.Mesh(
        mesh.devices.reshape(rows // 2, 2, columns // 2, 2), (*DP, *TENSOR)
    )
    in_specs = (
        P((*DP, *TENSOR), None),
        P(DP, TENSOR),
        P((*DP, *TENSOR), None),
        P((*DP, *TENSOR), None),
        P(),
        P(),
        P(),
        P(DP, TENSOR),
        P(DP, TENSOR),
        P(DP, TENSOR),
        P(TENSOR, DP),
        P(),
        P(DP, None, TENSOR),
        P(DP, None, TENSOR),
        P(DP, TENSOR, None),
        P((*DP, *TENSOR), None),
    )
    out_specs = (
        P((*DP, *TENSOR), None),
        P((*DP, *TENSOR), None),
        P(),
        P(),
        P(),
        P(DP, TENSOR),
        P(DP, TENSOR),
        P(DP, TENSOR),
        P(TENSOR, DP),
        P(),
        P(DP, None, TENSOR),
        P(DP, None, TENSOR),
        P(DP, TENSOR, None),
    )
    return jax.shard_map(shards, mesh=split, in_specs=in_specs, out_specs=out_specs, check_vma=False)
```

```python
import jax
import jax.numpy as jnp
import functools
import math

from jax import lax
from jax.experimental import pallas as pl
from jax.experimental.pallas import tpu as pltpu
from jax.sharding import PartitionSpec as P

WINDOW = 1024
DP = ("plane", "pack")
TENSOR = ("side", "core")


EPSILON = 1e-06
THETA = 50000.0
NEG_FILL = -1e30


def matmul(left_side, right_side):
    return jnp.dot(left_side, right_side, preferred_element_type=jnp.float32)


def contract_last(left_side, right_side):
    return lax.dot_general(
        left_side, right_side, (((1,), (1,)), ((), ())), preferred_element_type=jnp.float32
    )


def contract_first(left_side, right_side):
    return lax.dot_general(
        left_side, right_side, (((0,), (0,)), ((), ())), preferred_element_type=jnp.float32
    )


def norm_parts(values):
    factor = lax.rsqrt(jnp.mean(values * values, axis=-1, keepdims=True) + EPSILON)
    return (values * factor, factor)


def norm_back(grad_out, normed, factor, gain_vec):
    scaled = grad_out * gain_vec
    return factor * (scaled - normed * jnp.mean(scaled * normed, axis=-1, keepdims=True))


def rope_tables(length, head_size):
    half_size = head_size // 2
    frequency = THETA ** (-(2.0 * jnp.arange(half_size, dtype=jnp.float32)) / head_size)
    angles = jnp.arange(length, dtype=jnp.float32)[:, None] * frequency[None, :]
    return (jnp.cos(angles)[:, None, :], jnp.sin(angles)[:, None, :])


def rotate(values, cosine, sine_tab):
    half_size = values.shape[-1] // 2
    first_half = values[..., :half_size]
    second_half = values[..., half_size:]
    return jnp.concatenate(
        [
            first_half * cosine - second_half * sine_tab,
            second_half * cosine + first_half * sine_tab,
        ],
        axis=-1,
    )


def rotate_back(grads_in, cosine, sine_tab):
    half_size = grads_in.shape[-1] // 2
    first_half = grads_in[..., :half_size]
    second_half = grads_in[..., half_size:]
    return jnp.concatenate(
        [
            first_half * cosine + second_half * sine_tab,
            second_half * cosine - first_half * sine_tab,
        ],
        axis=-1,
    )


def block_mask(segments, offset, block_rows, key_count):
    query_pos = offset + jnp.arange(block_rows)
    key_pos = jnp.arange(key_count)
    same_doc = segments[offset : offset + block_rows][:, None] == segments[None, :]
    near_pos = jnp.abs(query_pos[:, None] - key_pos[None, :]) < WINDOW // 2
    return same_doc & near_pos


def block_scores(query_block, key_low, allowed, inv_root):
    scores = (
        jnp.einsum("qhd,khd->hqk", query_block, key_low, preferred_element_type=jnp.float32)
        * inv_root
    )
    return jnp.where(allowed[None], scores, NEG_FILL)


def row_sum(term_fn, tok_rows):
    return lax.psum_scatter(
        term_fn(jnp.int32(0), lax.axis_size(TENSOR) * tok_rows),
        TENSOR,
        scatter_dimension=0,
        tiled=True,
    )


def gather_rows(values):
    return lax.all_gather(values, TENSOR, axis=0, tiled=True)


def from_experts(values):
    return lax.all_to_all(values, DP, split_axis=1, concat_axis=1, tiled=True)


def to_experts(source_rows, slot_token, slot_gate, layout):
    picked = jnp.take(source_rows, slot_token, axis=0, mode="fill", fill_value=0)
    if slot_gate is not None:
        picked = (picked.astype(jnp.float32) * slot_gate[:, None]).astype(jnp.bfloat16)
    picked = picked.reshape(layout + (picked.shape[1],))
    return lax.all_to_all(picked, DP, split_axis=1, concat_axis=1, tiled=True)


def pair_sum(table, weights_low, pair_slots, row_count):
    picked = jnp.take(table, pair_slots.reshape(-1), axis=0, mode="fill", fill_value=0)
    picked = picked.reshape(row_count, pair_slots.shape[1], table.shape[1])
    return jnp.einsum("rk,rkd->rd", weights_low, picked, preferred_element_type=jnp.float32)


def expert_forward(operands):
    rows_in, gate_mat, up_mat, down_mat = operands
    flat_rows = rows_in.reshape(-1, rows_in.shape[-1])
    gated = matmul(flat_rows, gate_mat)
    lifted = matmul(flat_rows, up_mat)
    hidden = (jax.nn.silu(gated) * lifted).astype(jnp.bfloat16)
    result = matmul(hidden, down_mat).astype(jnp.bfloat16)
    return (result.reshape(rows_in.shape), gated, lifted)


def expert_backward(operands):
    rows_in, grad_in, gated, lifted, gate_mat, up_mat, down_mat = operands
    flat_rows = rows_in.reshape(-1, rows_in.shape[-1])
    flat_grad = grad_in.reshape(-1, grad_in.shape[-1])
    gate_sig = jax.nn.sigmoid(gated)
    activated = jax.nn.silu(gated)
    hidden = (activated * lifted).astype(jnp.bfloat16)
    grad_hidden = contract_last(flat_grad, down_mat)
    grad_down = contract_first(hidden, flat_grad)
    grad_gated = (grad_hidden * lifted * gate_sig * (1.0 + gated * (1.0 - gate_sig))).astype(
        jnp.bfloat16
    )
    grad_lifted = (grad_hidden * activated).astype(jnp.bfloat16)
    grad_gate = contract_first(flat_rows, grad_gated)
    grad_up = contract_first(flat_rows, grad_lifted)
    grad_rows = (contract_last(grad_gated, gate_mat) + contract_last(grad_lifted, up_mat)).astype(
        jnp.bfloat16
    )
    return (grad_rows.reshape(rows_in.shape), grad_gate, grad_up, grad_down)


VMEM_BYTES = 60 * 1024 * 1024
COLUMN_CHUNK = 512
GROUP = 2


def select_rows(places_ref, gates_ref, pick_ref, capacity):
    expert_count, seq_len = places_ref.shape[1:]
    slot_range = lax.broadcasted_iota(jnp.int32, (capacity, seq_len), 0).astype(jnp.bfloat16)
    nothing = jnp.zeros((capacity, seq_len), jnp.bfloat16)
    for expert in range(expert_count):
        hit = places_ref[0, expert : expert + 1, :] == slot_range
        if gates_ref is None:
            weight = jnp.ones((capacity, seq_len), jnp.bfloat16)
        else:
            weight = jnp.broadcast_to(gates_ref[0, expert : expert + 1, :], (capacity, seq_len))
        rows = slice(expert * capacity, (expert + 1) * capacity)
        pick_ref[rows, :] = jnp.where(hit, weight, nothing)


def rows_to_slots(pick_ref, rows_ref, slots_ref, pack, capacity):
    width = rows_ref.shape[2]
    expert_count = slots_ref.shape[0]
    for start in range(0, width, COLUMN_CHUNK):
        columns = slice(start, start + COLUMN_CHUNK)
        picked = matmul(pick_ref[...], rows_ref[0, :, columns]).astype(jnp.bfloat16)
        slots_ref[:, pack, :, columns] = picked.reshape(expert_count, capacity, COLUMN_CHUNK)


def slots_to_rows(pick_ref, slots_ref, own_ref, other_ref, pack):
    width = own_ref.shape[3]
    for start in range(0, width, COLUMN_CHUNK):
        columns = slice(start, start + COLUMN_CHUNK)
        slots = slots_ref[:, pack, :, columns].reshape(-1, COLUMN_CHUNK)
        rows = contract_first(pick_ref[...], slots).astype(own_ref.dtype)
        rows = rows.reshape(2, 2, own_ref.shape[2], COLUMN_CHUNK)
        own_ref[0, :, :, columns] = rows[:, 0]
        other_ref[0, :, :, columns] = rows[:, 1]


def cot_kernel(
    packs, steps, capacity, table, places, gates, rows, down, slots_out, hidden_out, slots, pick
):
    step = pl.program_id(0)

    @pl.when(step < packs)
    def _():
        select_rows(places, gates, pick, capacity)
        rows_to_slots(pick, rows, slots, step, capacity)

    @pl.when(step >= packs)
    def _():
        for member in range(down.shape[0]):
            block = slots[(step - packs) * down.shape[0] + member].reshape(packs * capacity, -1)
            slots_out[member] = block
            hidden_out[member] = contract_last(block, down[member])


def piece_copies(own, other, rows, sems, pack):
    half_rows = own.shape[1]
    copies = []
    for far in range(2):
        for core, source in enumerate((own, other)):
            for half, index in enumerate((4 * far + pack, 2 + 4 * pack + far)):
                start = ((far * 2 + core) * 2 + half) * half_rows
                copies.append(
                    pltpu.make_async_copy(
                        source.at[index],
                        rows.at[pack, pl.ds(start, half_rows)],
                        sems.at[pack * 8 + len(copies)],
                    )
                )
    return copies


def row_kernel(
    packs, steps, capacity, places, own, other, both, grad_hidden,
    slots_out, hidden_out, grads_out, rows_own, rows_other,
    rows, slots, grads, pick, sems,
):
    step = pl.program_id(0)
    half = hidden_out.shape[2]

    @pl.when(step == 0)
    def _():
        for pack in range(packs):
            for copy in piece_copies(own, other, rows, sems, pack):
                copy.start()
        for pack in range(packs):
            select_rows(places.at[pl.ds(pack, 1)], None, pick.at[pack], capacity)

    for pack in range(packs):

        @pl.when(step == pack)
        def _(pack=pack):
            for copy in piece_copies(own, other, rows, sems, pack):
                copy.wait()
            rows_to_slots(pick.at[pack], rows.at[pl.ds(pack, 1)], slots, pack, capacity)

    @pl.when((step >= packs) & (step < packs + steps))
    def _():
        for member in range(both.shape[0]):
            expert = (step - packs) * both.shape[0] + member
            block = slots[expert].reshape(packs * capacity, -1)
            slots_out[member] = block
            product = matmul(block, both[member])
            gated, lifted = product[:, :half], product[:, half:]
            sig = 1.0 / (1.0 + jnp.exp(-gated))
            active = gated * sig
            hidden_out[member] = (active * lifted).astype(jnp.bfloat16)
            above = grad_hidden[member]
            grad_gated = above * lifted * sig * (1.0 + gated * (1.0 - sig))
            joined = jnp.concatenate([grad_gated, above * active], axis=1).astype(jnp.bfloat16)
            grads_out[member] = joined
            back = contract_last(joined, both[member])
            grads[expert] = back.astype(jnp.bfloat16).reshape(packs, capacity, -1)

    for pack in range(packs):

        @pl.when(step == packs + steps + pack)
        def _(pack=pack):
            slots_to_rows(pick.at[pack], grads, rows_own, rows_other, pack)


def mix_kernel(packs, steps, capacity, table, places, gates, hidden, down, *refs):
    rows, results, pick = refs[-3:]
    step = pl.program_id(0)

    @pl.when(step < steps)
    def _():
        for member in range(down.shape[0]):
            result = matmul(hidden[member], down[member]).astype(jnp.bfloat16)
            results[step * down.shape[0] + member] = result.reshape(packs, capacity, -1)

    @pl.when(step >= steps)
    def _():
        select_rows(places, gates, pick, capacity)
        pack = (step - steps) ^ table[0]
        for start in range(0, rows.shape[3], COLUMN_CHUNK):
            columns = slice(start, start + COLUMN_CHUNK)
            slots = results[:, pack, :, columns].reshape(-1, COLUMN_CHUNK)
            rows[0, 0, :, columns] = contract_first(pick[...], slots).astype(rows.dtype)


def weight_kernel(planes, *refs):
    slots, grads, hidden, above = (
        jnp.concatenate([ref[0] for ref in refs[i * planes : (i + 1) * planes]]) for i in range(4)
    )
    gate_out, up_out, down_out = refs[-3:]
    half = gate_out.shape[2]
    both = contract_first(slots, above)
    gate_out[0] = both[:, :half]
    up_out[0] = both[:, half:]
    down_out[0] = contract_first(hidden, grads)


def block(shape, place, count=1):
    tail = (0,) * (len(shape) - 1)
    return pl.BlockSpec((count,) + tuple(shape[1:]), lambda *ids: (place(*ids),) + tail)


def staged(first, count):
    return lambda step, *rest: jnp.clip(step - first, 0, count - 1)


def shape_of(shape, kind):
    return jax.ShapeDtypeStruct(shape, kind)


def call(kernel, steps, specs, out_specs, out_shape, scratch, flops, prefetch=0, aliases={}):
    return pl.pallas_call(
        kernel,
        grid_spec=pltpu.PrefetchScalarGridSpec(
            num_scalar_prefetch=prefetch,
            grid=(steps,),
            in_specs=specs,
            out_specs=out_specs,
            scratch_shapes=scratch,
        ),
        out_shape=out_shape,
        input_output_aliases=aliases,
        cost_estimate=pl.CostEstimate(
            flops=flops, transcendentals=0, bytes_accessed=flops // 500
        ),
        compiler_params=pltpu.CompilerParams(
            dimension_semantics=("arbitrary",), vmem_limit_bytes=VMEM_BYTES
        ),
    )


def cot_slots(table, places, gates, rows, down, capacity):
    packs = table.shape[0]
    _, seq_len, width = rows.shape
    experts, hidden_width, _ = down.shape
    slot_rows = packs * capacity
    group = math.gcd(experts, GROUP)
    steps = experts // group
    by_pack, by_expert = staged(0, packs), staged(packs, steps)
    listed = lambda step, numbers: numbers[by_pack(step)]
    out_shape = [
        shape_of((experts, slot_rows, width), jnp.bfloat16),
        shape_of((experts, slot_rows, hidden_width), jnp.float32),
    ]
    return call(
        functools.partial(cot_kernel, packs, steps, capacity),
        packs + steps,
        [
            block(places.shape, listed), block(gates.shape, listed), block(rows.shape, listed),
            block(down.shape, by_expert, group),
        ],
        [block(out.shape, by_expert, group) for out in out_shape],
        out_shape,
        [
            pltpu.VMEM((experts, packs, capacity, width), jnp.bfloat16),
            pltpu.VMEM((experts * capacity, seq_len), jnp.bfloat16),
        ],
        2 * experts * slot_rows * width * (seq_len + hidden_width),
        1,
    )(table, places, gates, rows, down)


def row_slots(places, own, other, both, grad_hidden, capacity):
    packs, _, seq_len = places.shape
    experts, width, hidden_width = both.shape
    slot_rows = packs * capacity
    group = math.gcd(experts, GROUP)
    steps = experts // group
    middle, last = staged(packs, steps), staged(packs + steps, packs)
    part = shape_of((packs, 2, seq_len // 4, width), jnp.bfloat16)
    out_shape = [
        shape_of((experts, slot_rows, width), jnp.bfloat16),
        shape_of((experts, slot_rows, hidden_width // 2), jnp.bfloat16),
        shape_of((experts, slot_rows, hidden_width), jnp.bfloat16),
        part, part,
    ]
    anywhere = pl.BlockSpec(memory_space=pl.ANY)
    return call(
        functools.partial(row_kernel, packs, steps, capacity),
        2 * packs + steps,
        [
            block(places.shape, lambda step: 0, packs), anywhere, anywhere,
            block(both.shape, middle, group), block(grad_hidden.shape, middle, group),
        ],
        [block(out.shape, middle, group) for out in out_shape[:3]] + [block(part.shape, last)] * 2,
        out_shape,
        [
            pltpu.VMEM((packs, seq_len, width), jnp.bfloat16),
            pltpu.VMEM((experts, packs, capacity, width), jnp.bfloat16),
            pltpu.VMEM((experts, packs, capacity, width), jnp.bfloat16),
            pltpu.VMEM((packs, experts * capacity, seq_len), jnp.bfloat16),
            pltpu.SemaphoreType.DMA((8 * packs,)),
        ],
        4 * experts * slot_rows * width * (seq_len + hidden_width),
    )(places, own, other, both, grad_hidden)


def mix_rows(plane, planes, table, places, gates, hidden, down, capacity, earlier=()):
    packs, _, seq_len = places.shape
    experts, hidden_width, width = down.shape
    group = math.gcd(experts, GROUP)
    steps = experts // group
    first, last = staged(0, steps), staged(steps, packs)
    listed = lambda step, numbers: numbers[1] * steps + first(step)
    return call(
        functools.partial(mix_kernel, packs, steps, capacity),
        packs + steps,
        [
            block(places.shape, last), block(gates.shape, last),
            block(hidden.shape, listed, group), block(down.shape, first, group),
        ]
        + [pl.BlockSpec(memory_space=pl.ANY)] * len(earlier),
        [pl.BlockSpec((1, 1, seq_len, width), lambda step, numbers: (plane, last(step), 0, 0))],
        [shape_of((planes, packs, seq_len, width), jnp.bfloat16)],
        [
            pltpu.VMEM((experts, packs, capacity, width), jnp.bfloat16),
            pltpu.VMEM((experts * capacity, seq_len), jnp.bfloat16),
        ],
        2 * experts * packs * capacity * width * (seq_len + hidden_width),
        1,
        aliases={5 + index: index for index in range(len(earlier))},
    )(table, places, gates, hidden, down, *earlier)


def weight_grads(first, count, slots, hidden, grads, above, earlier=()):
    planes = len(slots)
    operands = [*slots, *grads, *hidden, *above]
    experts, _, width = slots[0].shape
    hidden_width = hidden[0].shape[2]
    each = lambda step: step + first
    out_shape = [
        shape_of((experts, width, hidden_width), jnp.float32),
        shape_of((experts, width, hidden_width), jnp.float32),
        shape_of((experts, hidden_width, width), jnp.float32),
    ]
    return call(
        functools.partial(weight_kernel, planes),
        count,
        [block(operand.shape, each) for operand in operands]
        + [pl.BlockSpec(memory_space=pl.ANY)] * len(earlier),
        [block(out.shape, each) for out in out_shape],
        out_shape,
        [],
        6 * planes * slots[0].shape[1] * count * width * hidden_width,
        aliases={len(operands) + index: index for index in range(len(earlier))},
    )(*operands, *earlier)


def swapped(values, axis, bit):
    count = lax.axis_size(axis)
    return lax.ppermute(values, axis, [(i, i ^ bit) for i in range(count)])


def far_side(values):
    return swapped(values, TENSOR, 2)


def far_core(values):
    return swapped(values, TENSOR, 1)


def far_pack(values):
    return swapped(values, DP, 1)


def next_plane(values):
    count = lax.axis_size(DP)
    return lax.ppermute(values, DP, [(i, (i + 2) % count) for i in range(count)])


def spread_all(values, small, work):
    planes = lax.axis_size("plane")
    half_rows = values.shape[0] // 2
    first = lambda rows: (far_pack(rows[:half_rows]), far_side(rows[half_rows:]))
    small, values = tied(small, values)
    (across_pack, across_side), following = lax.optimization_barrier(
        (first(values), next_plane(values))
    )
    pieces, made = [], []
    for plane in range(planes):
        upper = jnp.stack([values[:half_rows], across_pack])
        lower = jnp.stack([values[half_rows:], across_side])
        small, (upper, lower, values) = tied(small, (upper, lower, following))
        moved = [
            far_side(upper),
            far_pack(lower),
            first(values) if plane + 1 < planes else ((), ()),
            next_plane(values) if plane + 2 < planes else (),
            far_core(pieces[-1]) if plane else (),
            work(plane - 1, small) if plane else (),
        ]
        upper_far, lower_far, (across_pack, across_side), following, other, result = (
            lax.optimization_barrier(moved)
        )
        if plane:
            pieces[-1] = (pieces[-1], other)
        if plane:
            made.append(result)
        pieces.append(jnp.concatenate([upper, lower, upper_far, lower_far]))
    pieces[-1] = (pieces[-1], far_core(pieces[-1]))
    return pieces, made


def plane_order():
    packs = lax.axis_size(DP)
    planes = packs // 2
    index = lax.axis_index(DP)
    return jnp.stack(
        [
            ((index // 2 + planes - plane) % planes) * 2 + (index % 2 ^ near)
            for plane in range(planes)
            for near in range(2)
        ]
    )


def place_kernel(by_column, order, *refs):
    *pieces, whole, sems = refs
    copies = []
    for index, piece in enumerate(pieces):
        target = None if by_column else whole.at[order[index]]
        if by_column:
            width = piece.shape[1]
            target = whole.at[:, pl.ds(pl.multiple_of(order[index] * width, 128), width)]
        copies.append(pltpu.make_async_copy(piece, target, sems.at[index]))
        copies[-1].start()
    for copy in copies:
        copy.wait()


def laid(pieces, order, by_column=False):
    count = len(pieces)
    rows, columns = pieces[0].shape
    shape = (rows, count * columns) if by_column else (count, rows, columns)
    anywhere = pl.BlockSpec(memory_space=pl.ANY)
    return call(
        functools.partial(place_kernel, by_column),
        1,
        [anywhere] * count,
        pl.BlockSpec(memory_space=pltpu.VMEM),
        shape_of(shape, pieces[0].dtype),
        [pltpu.SemaphoreType.DMA((count,))],
        1000,
        1,
    )(order, *pieces)


class FoldPacks:
    def __init__(self, values):
        order = plane_order()
        take = lambda index: lax.dynamic_index_in_dim(values, order[index], 0, keepdims=False)
        planes = values.shape[0] // 2
        self.turns = [*range(1, planes), 0]
        self.near = {plane: take(2 * plane) for plane in self.turns}
        self.moving = {plane: far_pack(take(2 * plane + 1)) for plane in self.turns}
        self.summed, self.count = None, 0

    def step(self, other):
        if self.count >= len(self.turns):
            return other
        self.moving, other = tied(self.moving, other)
        if self.summed is None:
            self.near = {plane: added(self.near[plane], self.moving[plane]) for plane in self.turns}
            self.summed = self.near[self.turns[0]]
        else:
            kind = jnp.float32 if self.count + 1 == len(self.turns) else jnp.bfloat16
            self.summed = added(self.moving, self.near[self.turns[self.count]], kind)
        self.count += 1
        if self.count < len(self.turns):
            self.moving = next_plane(self.summed)
        return other

    def finish(self):
        for plane in self.turns[self.count :]:
            kind = jnp.float32 if plane == 0 else jnp.bfloat16
            self.summed = added(self.moving, self.near[plane], kind)
            self.moving = next_plane(self.summed) if plane else None
        return self.summed


def laid_sides(pieces):
    order = lax.axis_index(TENSOR) ^ jnp.arange(len(pieces), dtype=jnp.int32)
    return laid(pieces, order).reshape((-1,) + pieces[0].shape[1:])


def gather_sides(values):
    across = far_side(values)
    return laid_sides([values, far_core(values), across, far_core(across)])


def fold_sides(values):
    split = values.astype(jnp.bfloat16).reshape((4, -1) + values.shape[1:])
    take = lambda bits: lax.dynamic_index_in_dim(
        split, lax.axis_index(TENSOR) ^ bits, 0, keepdims=False
    )
    far = added(take(2), far_core(take(3)))
    near = added(take(0), far_core(take(1)))
    return added(near, far_side(far), jnp.float32)


def fold_both(weights, rows, mixed):
    order = plane_order()
    planes = weights.shape[0] // 2
    take = lambda index: lax.dynamic_index_in_dim(weights, order[index], 0, keepdims=False)
    split = rows.astype(jnp.bfloat16).reshape((4, -1) + rows.shape[1:])
    mine = lax.axis_index(TENSOR)
    pick = lambda bits: lax.dynamic_index_in_dim(split, mine ^ bits, 0, keepdims=False)
    summed, total = None, None
    for turn, plane in enumerate([*range(1, planes), 0]):
        moved = [far_pack(take(2 * plane + 1)), () if summed is None else next_plane(summed)]
        if turn == 0:
            moved += [far_core(pick(3)), far_core(pick(1))]
        if turn == 1:
            moved += [far_side(far)]
        across, passed, *arrived = lax.optimization_barrier(moved)
        if turn == 0:
            far, close = added(pick(2), arrived[0]), added(pick(0), arrived[1])
            mixed, far = tied(mixed, far)
            mixed = lax.psum_scatter(mixed, "plane", scatter_dimension=0, tiled=True)
        if turn == 1:
            total = added(close, arrived[0], jnp.float32)
        near = added(take(2 * plane), across)
        kind = jnp.float32 if turn + 1 == planes else jnp.bfloat16
        summed = near if turn == 0 else added(passed, near, kind)
    return summed, total, mixed


def gather_both(weights, outer, rows, gate, up, tables):
    hops = table_hops()
    pieces, outer_pieces, row_pieces, values = [], [], [rows], (weights, outer)
    planes = lax.axis_size("plane")
    for plane in range(planes):
        moved = [tuple(far_pack(value) for value in values), ()]
        if plane + 1 < planes:
            moved[1] = tuple(next_plane(value) for value in values)
        if plane == 0:
            moved += [far_core(rows), far_side(rows)]
        if plane == 1:
            moved += [far_core(row_pieces[2])]
        if plane == 0:
            moved.insert(2, jnp.concatenate([gate, up], axis=2))
        moved.insert(2, swapped(tables, *hops[plane]) if plane < len(hops) else ())
        across, following, more, *arrived = lax.optimization_barrier(moved)
        if plane < len(hops):
            tables = jnp.concatenate([tables, more])
        if plane == 0:
            joined = arrived.pop(0)
        pieces += [values[0], across[0]]
        outer_pieces += [values[1], across[1]]
        row_pieces += arrived
        values = following
    order = plane_order()
    for hop in hops[planes:]:
        tables = jnp.concatenate([tables, swapped(tables, *hop)])
    laid_rows = laid_sides(row_pieces)
    return laid(pieces, order), laid(outer_pieces, order, True), laid_rows, joined, tables


def sum_everywhere(values):
    for axis in (TENSOR, DP):
        bit = 1
        while bit < lax.axis_size(axis):
            values = values + swapped(values, axis, bit)
            bit *= 2
    return values


def added(left, right, kind=jnp.bfloat16):
    return (left.astype(jnp.float32) + right.astype(jnp.float32)).astype(kind)


def fold_first(own, arrived):
    half_rows = own.shape[2] // 2
    upper, lower = slice(None, half_rows), slice(half_rows, None)
    return (
        added(own[:, 0, upper], arrived[:, 0, upper]),
        added(own[0, :, lower], arrived[0, :, lower]),
        added(own[:, 1, upper], arrived[:, 1, upper]),
        added(own[1, :, lower], arrived[1, :, lower]),
    )


def tied(small, values):
    return lax.optimization_barrier((small, values))


def table_hops():
    hops = []
    for axis in (TENSOR, DP):
        bit = 1
        while bit < lax.axis_size(axis):
            hops.append((axis, bit))
            bit *= 2
    return hops


def read_tables(tables, top_count):
    own = lax.axis_index(DP) * lax.axis_size(TENSOR) + lax.axis_index(TENSOR)
    sides = jnp.arange(lax.axis_size(TENSOR), dtype=jnp.int32) ^ lax.axis_index(TENSOR)
    segments = jnp.take(tables[: sides.shape[0], -1], sides, axis=0).reshape(-1)
    devices = jnp.arange(tables.shape[0], dtype=jnp.int32)
    tables = jnp.take(tables, devices ^ own, axis=0)
    all_ids, all_gates = tables[:, :top_count], tables[:, top_count : 2 * top_count]
    return all_ids.astype(jnp.int32), all_gates, segments.astype(jnp.int32)


def routing(all_ids, all_gates, local_experts, capacity):
    packs = lax.axis_size(DP)
    first = lax.axis_index(DP) * local_experts
    wanted = first + jnp.arange(local_experts, dtype=jnp.int32)

    def by_pack(values):
        top_count, tok_rows = values.shape[1:]
        ordered = values.reshape(packs, -1, top_count, tok_rows).transpose(0, 2, 1, 3)
        return ordered.reshape(packs, top_count, -1)

    matches = by_pack(all_ids)[:, :, None, :] == wanted[None, None, :, None]
    pair_gates = by_pack(all_gates).astype(jnp.float32)
    member = jnp.any(matches, axis=1)
    gates = jnp.sum(jnp.where(matches, pair_gates[:, :, None, :], 0.0), axis=1)
    order = jnp.arange(member.shape[2], dtype=jnp.int32)
    earlier = (order[:, None] < order[None, :]).astype(jnp.bfloat16)
    flat = member.reshape(packs * local_experts, -1).astype(jnp.bfloat16)
    before = matmul(flat, earlier).astype(jnp.int32).reshape(member.shape)
    places = jnp.where(member & (before < capacity), before, -1)
    return places.astype(jnp.bfloat16), gates.astype(jnp.bfloat16)


def experts_by_exchange(
    second_in, cotangent, expert_ids, gate_values, w_gate, w_up, w_down, middle, capacity
):
    tok_rows, model_width = second_in.shape
    tensor_count = lax.axis_size(TENSOR)
    data_count = lax.axis_size(DP)
    local_experts = w_gate.shape[0]
    all_experts = local_experts * data_count
    top_count = expert_ids.shape[1]
    seq_len = tok_rows * tensor_count
    pack_cot, pack_ids, pack_gates = (
        gather_rows(cotangent), gather_rows(expert_ids), gather_rows(gate_values)
    )
    pack_second = gather_rows(second_in)
    expert_range = jnp.arange(all_experts, dtype=jnp.int32)
    matches = pack_ids[:, :, None] == expert_range[None, None, :]
    token_counts = jnp.sum(matches.astype(jnp.float32), axis=1).astype(jnp.bfloat16)
    token_range = jnp.arange(seq_len, dtype=jnp.int32)
    earlier = (token_range[:, None] > token_range[None, :]).astype(jnp.bfloat16)
    before = matmul(earlier, token_counts)
    places = (
        jnp.sum(jnp.where(matches, before[:, None, :], 0.0), axis=2).astype(jnp.int32).reshape(-1)
    )
    flat_ids = pack_ids.reshape(-1)
    owners = flat_ids // local_experts
    local_index = flat_ids % local_experts
    dump_slot = all_experts * capacity
    slot_index = jnp.where(
        places < capacity,
        local_index * (data_count * capacity) + owners * capacity + places,
        dump_slot,
    ).astype(jnp.int32)
    pair_token = jnp.arange(seq_len * top_count) // top_count
    slot_token = (
        jnp.full((dump_slot + 1,), seq_len, jnp.int32).at[slot_index].set(pair_token)[:dump_slot]
    )
    pair_gates = pack_gates.astype(jnp.float32)
    slot_gate = (
        jnp.zeros((dump_slot + 1,), jnp.float32)
        .at[slot_index]
        .set(pair_gates.reshape(-1))[:dump_slot]
    )
    pair_slots = slot_index.reshape(seq_len, top_count)
    layout = (local_experts, data_count, capacity)
    arrived_rows = to_experts(pack_second, slot_token, None, layout)
    expert_out, gated_all, lifted_all = lax.map(
        expert_forward, (arrived_rows, w_gate, w_up, w_down)
    )
    returned = from_experts(expert_out).reshape(-1, model_width)

    def combine_term(offset, row_count):
        return pair_sum(returned, pack_gates, pair_slots, row_count)

    outputs = middle + row_sum(combine_term, tok_rows)
    grad_arrived = to_experts(pack_cot, slot_token, slot_gate, layout)
    grad_rows_all, grad_w_gate, grad_w_up, grad_w_down = lax.map(
        expert_backward, (arrived_rows, grad_arrived, gated_all, lifted_all, w_gate, w_up, w_down)
    )
    returned_grad = from_experts(grad_rows_all).reshape(-1, model_width)
    unit_gates = jnp.ones_like(pack_gates)

    def dispatch_term(offset, row_count):
        return pair_sum(returned_grad, unit_gates, pair_slots, row_count)

    grad_second = row_sum(dispatch_term, tok_rows)
    return outputs, grad_second, grad_w_gate, grad_w_up, grad_w_down


class Folding:
    def __init__(self, order):
        self.order, self.planes, self.ready = order, {}, {}
        self.summed, self.passed, self.count = None, None, 0

    def begin(self, plane, own, other):
        self.planes[plane] = (0, (own, other))

    def turn(self, small, work):
        small, (planes, summed) = tied(
            small, ({plane: values for plane, (_, values) in self.planes.items()}, self.summed)
        )
        sent = {}
        for plane, values in planes.items():
            stage = self.planes[plane][0]
            if stage == 0:
                sent[plane] = (far_core(values[1]),)
            elif stage == 1:
                sent[plane] = (far_side(values[2]), far_pack(values[3]))
            else:
                sent[plane] = (far_pack(values[2]), far_side(values[3]))
        passed = self.passed
        if passed is None and summed is not None and not self.done():
            passed = next_plane(summed)
        sent, passed, result = lax.optimization_barrier((sent, passed, work(small)))
        self.passed = passed
        for plane, values in planes.items():
            stage, arrived = self.planes[plane][0], sent[plane]
            if stage == 0:
                made = fold_first(values[0], *arrived)
            elif stage == 1:
                upper, lower = added(values[0], arrived[0]), added(values[1], arrived[1])
                made = (upper[0], lower[0], upper[1], lower[1])
            else:
                self.ready[plane] = jnp.concatenate(
                    [added(values[0], arrived[0]), added(values[1], arrived[1])]
                )
            if stage < 2:
                self.planes[plane] = (stage + 1, made)
            else:
                del self.planes[plane]
        following = self.order[self.count] if self.count < len(self.order) else None
        if following in self.ready:
            last = self.count + 1 == len(self.order)
            self.summed = self.ready[following]
            if passed is not None:
                kind = jnp.float32 if last else jnp.bfloat16
                self.summed = added(passed, self.summed, kind)
            self.passed = None
            self.count += 1
        return result

    def done(self):
        return self.count == len(self.order)


def experts_by_gather(second_in, all_cot, places, gates, w_both, w_down, capacity):
    packs, local_experts, seq_len = places.shape
    tensor_count = lax.axis_size(TENSOR)
    planes = packs // 2
    pack_order = plane_order()
    side_index = lax.axis_index(TENSOR)
    quarter_order = side_index ^ jnp.arange(tensor_count, dtype=jnp.int32)

    def as_met(values, by_pack, by_quarter):
        split = values.reshape(packs, local_experts, tensor_count, -1)
        split = jnp.take(jnp.take(split, by_pack, axis=0), by_quarter, axis=2)
        return split.reshape(values.shape)

    near_places = as_met(places, pack_order, quarter_order)
    pairs = [slice(plane * 2, plane * 2 + 2) for plane in range(planes)]
    tables = [
        jnp.stack([lax.axis_index("pack"), (lax.axis_index("plane") + planes - plane) % planes])
        for plane in range(planes)
    ]
    prepared = [
        [table[pair] for pair in pairs] for table in (near_places, places, gates, pack_order)
    ]
    prepared, second_in = tied((prepared, tables, places, gates), second_in)
    (near_places, mix_places, mix_gates, pack_order), tables, places, gates = prepared

    def cot_work(plane, order):
        return cot_slots(order[plane], places, gates, all_cot, w_down, capacity)

    pieces, made = spread_all(second_in, pack_order, cot_work)
    order = [*range(1, planes), 0]
    kept, folding = {}, Folding(order)

    def row_work(plane, near):
        return row_slots(near, *pieces[plane], w_both, made[plane][1], capacity)

    for plane in order:
        if folding.planes:
            result = folding.turn(near_places[plane], functools.partial(row_work, plane))
        else:
            result = row_work(plane, near_places[plane])
        slots, hidden, above, *part = result
        folding.begin(plane, *part)
        kept[plane] = (slots, hidden, made[plane][0], above)
        if len(made) < planes:
            made.append(folding.turn(pack_order, functools.partial(cot_work, len(made))))
    hidden_all = jnp.concatenate([kept[plane][1] for plane in range(planes)])

    def mix_turn(some, given):
        table, mixed = given
        for plane in some:
            mixed = mix_rows(
                plane, planes, table[plane], mix_places[plane], mix_gates[plane], hidden_all, w_down,
                capacity, mixed,
            )
        return mixed

    mixed = ()
    for start in range(0, planes, 2):
        some = range(start, start + 2)
        mixed = folding.turn((tables, mixed), functools.partial(mix_turn, some))
    whole = mixed[0].reshape(planes, -1, mixed[0].shape[-1])
    whole = lax.psum_scatter(
        whole, ("pack", "side", "core"), scatter_dimension=1, tiled=True
    )
    kept = [kept[plane] for plane in range(planes)]
    weight_parts, next_expert = (), 0
    part_size = math.gcd(local_experts, GROUP)

    def weight_turn(count, small):
        state, (held, weights) = next_expert, small
        for _ in range(count):
            if state < local_experts:
                weights = weight_grads(state, part_size, *zip(*held), weights)
                state += part_size
        return weights

    for count in (2, 1, *[0] * planes):
        if folding.done():
            break
        weight_parts = folding.turn((kept, weight_parts), functools.partial(weight_turn, count))
        next_expert = min(next_expert + count * part_size, local_experts)
    rest = (kept, weight_parts, next_expert, part_size)
    return folding.summed, whole, rest


def shards(
    inputs,
    segment_ids,
    expert_ids,
    gate_values,
    attn_gain,
    query_gain,
    key_gain,
    w_query,
    w_key,
    w_value,
    w_output,
    ffn_gain,
    w_gate,
    w_up,
    w_down,
    cotangent,
):
    tok_rows, model_width = inputs.shape
    head_size = query_gain.shape[0]
    tensor_count = lax.axis_size(TENSOR)
    data_count = lax.axis_size(DP)
    local_experts = w_gate.shape[0]
    all_experts = local_experts * data_count
    top_count = expert_ids.shape[1]
    seq_len = tok_rows * tensor_count
    capacity = seq_len * top_count // all_experts
    inv_root = head_size ** (-0.5)
    by_gather = (
        seq_len <= local_experts * capacity
        and tensor_count == 4
        and data_count > 2
        and data_count & (data_count - 1) == 0
        and all_experts <= 256
    )
    if by_gather:
        axes = (*DP, *TENSOR)
        tables = jnp.concatenate(
            [expert_ids.T.astype(jnp.bfloat16), gate_values.T, segment_ids.astype(jnp.bfloat16)]
        )[None]
    inputs_f32 = inputs.astype(jnp.float32)
    normed_one, factor_one = norm_parts(inputs_f32)
    first_in = (normed_one * attn_gain).astype(jnp.bfloat16)
    if by_gather:
        side_sum, side_gather = fold_sides, gather_sides
        local_width = w_query.shape[1]
        w_in = jnp.concatenate([w_query, w_key, w_value], axis=1)
        full_in, full_output, pack_in, w_both, tables = gather_both(
            w_in, w_output, first_in, w_gate, w_up, tables
        )
        all_ids, all_gates, segments = read_tables(tables, top_count)
        places, gates = routing(all_ids, all_gates, local_experts, capacity)
        full_in, cotangent = tied(full_in, cotangent)
        all_cot = lax.all_gather(cotangent, axes, axis=0, tiled=True)
        all_cot = all_cot.reshape(data_count, seq_len, model_width)
        full_in = full_in.reshape(model_width, -1)
        full_query, full_key, full_value = (
            full_in[:, index * local_width : (index + 1) * local_width] for index in range(3)
        )
    else:
        side_sum, side_gather = lambda term: row_sum(lambda *_: term, tok_rows), gather_rows
        segments = lax.all_gather(segment_ids, TENSOR, axis=1, tiled=True)[0]
        full_query, full_key, full_value, full_output = (
            lax.all_gather(w_query, DP, axis=0, tiled=True),
            lax.all_gather(w_key, DP, axis=0, tiled=True),
            lax.all_gather(w_value, DP, axis=0, tiled=True),
            lax.all_gather(w_output, DP, axis=1, tiled=True),
        )
        pack_in = side_gather(first_in)
    query_pre = matmul(pack_in, full_query)
    key_pre = matmul(pack_in, full_key)
    value_low = matmul(pack_in, full_value).astype(jnp.bfloat16)
    head_count = query_pre.shape[1] // head_size
    cosine, sine_tab = rope_tables(seq_len, head_size)
    query_norm, query_factor = norm_parts(query_pre.reshape(seq_len, head_count, head_size))
    key_norm, key_factor = norm_parts(key_pre.reshape(seq_len, head_count, head_size))
    query_low = rotate(query_norm * query_gain, cosine, sine_tab).astype(jnp.bfloat16)
    key_low = rotate(key_norm * key_gain, cosine, sine_tab).astype(jnp.bfloat16)
    value_heads = value_low.reshape(seq_len, head_count, head_size)
    block_rows = min(512, seq_len)
    block_total = seq_len // block_rows
    masks = []
    mixture_parts = []
    lse_parts = []
    for block_index in range(block_total):
        offset = block_index * block_rows
        allowed = block_mask(segments, offset, block_rows, seq_len)
        masks.append(allowed)
        scores = block_scores(query_low[offset : offset + block_rows], key_low, allowed, inv_root)
        top_score = jnp.max(scores, axis=-1, keepdims=True)
        raw_weights = jnp.exp(scores - top_score)
        totals = jnp.sum(raw_weights, axis=-1, keepdims=True)
        weights_low = (raw_weights / totals).astype(jnp.bfloat16)
        mixture_parts.append(
            jnp.einsum(
                "hqk,khd->qhd", weights_low, value_heads, preferred_element_type=jnp.float32
            ).astype(jnp.bfloat16)
        )
        lse_parts.append(top_score + jnp.log(totals))
    mixture = jnp.concatenate(mixture_parts, axis=0).reshape(seq_len, head_count * head_size)

    middle = inputs_f32 + side_sum(matmul(mixture, full_output))
    normed_two, factor_two = norm_parts(middle)
    second_in = (normed_two * ffn_gain).astype(jnp.bfloat16)
    if by_gather:
        grad_second, mixed, rest = experts_by_gather(
            second_in, all_cot, places, gates, w_both, w_down, capacity
        )
    else:
        outputs, grad_second, grad_w_gate, grad_w_up, grad_w_down = experts_by_exchange(
            second_in, cotangent, expert_ids, gate_values, w_gate, w_up, w_down, middle, capacity
        )
    ffn_gain_part = jnp.sum(grad_second * normed_two, axis=0)
    grad_middle = cotangent.astype(jnp.float32) + norm_back(
        grad_second, normed_two, factor_two, ffn_gain
    )
    grad_attended = grad_middle.astype(jnp.bfloat16)
    if by_gather:
        kept, weight_parts, next_expert, part_size = rest
        (kept, weight_parts), grad_attended = tied((kept, weight_parts), grad_attended)
        moved = [far_core(grad_attended), far_side(grad_attended)]
        for first in range(next_expert, local_experts, part_size):
            weight_parts = weight_grads(first, part_size, *zip(*kept), weight_parts)
        grad_w_gate, grad_w_up, grad_w_down = weight_parts
        near, across, weight_parts = lax.optimization_barrier((*moved, weight_parts))
        grad_w_gate, grad_w_up, grad_w_down = weight_parts
        pack_grad = laid_sides([grad_attended, near, across, far_core(across)])
    else:
        pack_grad = side_gather(grad_attended)
    output_part = contract_first(mixture, pack_grad)
    fold_step = lambda other: other
    if by_gather:
        by_column = output_part.astype(jnp.bfloat16).reshape(local_width, data_count, -1)
        folded = FoldPacks(by_column.transpose(1, 0, 2))
        fold_step = folded.step
    grad_mixture = (
        contract_last(pack_grad, full_output)
        .astype(jnp.bfloat16)
        .reshape(seq_len, head_count, head_size)
    )
    grad_query_parts = []
    grad_key_sum = jnp.zeros((seq_len, head_count, head_size), jnp.float32)
    grad_value_sum = jnp.zeros((seq_len, head_count, head_size), jnp.float32)
    for block_index in range(block_total):
        offset = block_index * block_rows
        query_block = query_low[offset : offset + block_rows]
        grad_block = grad_mixture[offset : offset + block_rows]
        scores = block_scores(query_block, key_low, masks[block_index], inv_root)
        prob_rows = jnp.exp(scores - lse_parts[block_index])
        grad_probs = jnp.einsum(
            "qhd,khd->hqk", grad_block, value_heads, preferred_element_type=jnp.float32
        )
        row_delta = jnp.sum(grad_probs * prob_rows, axis=-1, keepdims=True)
        grad_scores = (prob_rows * (grad_probs - row_delta)).astype(jnp.bfloat16)
        grad_query_parts.append(
            jnp.einsum("hqk,khd->qhd", grad_scores, key_low, preferred_element_type=jnp.float32)
            * inv_root
        )
        grad_key_sum = (
            grad_key_sum
            + jnp.einsum(
                "hqk,qhd->khd", grad_scores, query_block, preferred_element_type=jnp.float32
            )
            * inv_root
        )
        grad_value_sum = grad_value_sum + jnp.einsum(
            "hqk,qhd->khd",
            prob_rows.astype(jnp.bfloat16),
            grad_block,
            preferred_element_type=jnp.float32,
        )
    grad_query_norm = rotate_back(jnp.concatenate(grad_query_parts, axis=0), cosine, sine_tab)
    grad_key_norm = rotate_back(grad_key_sum, cosine, sine_tab)
    grad_query_norm = fold_step(grad_query_norm)
    query_gain_part = jnp.sum(grad_query_norm * query_norm, axis=(0, 1))
    key_gain_part = jnp.sum(grad_key_norm * key_norm, axis=(0, 1))
    grad_query_pre = (
        norm_back(grad_query_norm, query_norm, query_factor, query_gain)
        .reshape(seq_len, -1)
        .astype(jnp.bfloat16)
    )
    grad_key_pre = (
        norm_back(grad_key_norm, key_norm, key_factor, key_gain)
        .reshape(seq_len, -1)
        .astype(jnp.bfloat16)
    )
    grad_value_low = grad_value_sum.reshape(seq_len, -1).astype(jnp.bfloat16)
    query_part = contract_first(pack_in, grad_query_pre)
    key_part = contract_first(pack_in, grad_key_pre)
    value_part = contract_first(pack_in, grad_value_low)

    total_term = contract_last(grad_query_pre, full_query)
    total_term = total_term + contract_last(grad_key_pre, full_key)
    total_term = total_term + contract_last(grad_value_low, full_value)
    if by_gather:
        in_part = jnp.concatenate([query_part, key_part, value_part], axis=1)
        in_part = in_part.astype(jnp.bfloat16).reshape(data_count, -1, 3 * local_width)
        in_part = fold_step(in_part)
        grad_w_output = folded.finish()
        grad_in, grad_first, mixed = fold_both(in_part, total_term, mixed)
        mixed, grad_in = tied(mixed, grad_in)
    else:
        grad_first = side_sum(total_term)
    attn_gain_part = jnp.sum(grad_first * normed_one, axis=0)
    grad_inputs = grad_middle + norm_back(grad_first, normed_one, factor_one, attn_gain)
    gain_parts = (attn_gain_part, ffn_gain_part, query_gain_part, key_gain_part)
    if by_gather:
        grad_w_query, grad_w_key, grad_w_value = (
            grad_in[:, index * local_width : (index + 1) * local_width] for index in range(3)
        )
        outputs = middle + mixed[0].astype(jnp.float32)
        splits = (model_width, 2 * model_width, 2 * model_width + head_size)
        gain_sums = jnp.split(sum_everywhere(jnp.concatenate(gain_parts)), splits)
    else:
        grad_w_query, grad_w_key, grad_w_value, grad_w_output = (
            lax.psum_scatter(
                part.astype(jnp.bfloat16), DP, scatter_dimension=along, tiled=True
            ).astype(jnp.float32)
            for part, along in ((query_part, 0), (key_part, 0), (value_part, 0), (output_part, 1))
        )
        gain_sums = lax.psum(gain_parts, (*DP, *TENSOR))
    grad_attn_gain, grad_ffn_gain, grad_query_gain, grad_key_gain = gain_sums
    return (
        outputs,
        grad_inputs,
        grad_attn_gain,
        grad_query_gain,
        grad_key_gain,
        grad_w_query,
        grad_w_key,
        grad_w_value,
        grad_w_output,
        grad_ffn_gain,
        grad_w_gate,
        grad_w_up,
        grad_w_down,
    )


def solution(mesh):
    rows, columns = mesh.devices.shape
    split = jax.sharding.Mesh(
        mesh.devices.reshape(rows // 2, 2, columns // 2, 2), (*DP, *TENSOR)
    )
    in_specs = (
        P((*DP, *TENSOR), None),
        P(DP, TENSOR),
        P((*DP, *TENSOR), None),
        P((*DP, *TENSOR), None),
        P(),
        P(),
        P(),
        P(DP, TENSOR),
        P(DP, TENSOR),
        P(DP, TENSOR),
        P(TENSOR, DP),
        P(),
        P(DP, None, TENSOR),
        P(DP, None, TENSOR),
        P(DP, TENSOR, None),
        P((*DP, *TENSOR), None),
    )
    out_specs = (
        P((*DP, *TENSOR), None),
        P((*DP, *TENSOR), None),
        P(),
        P(),
        P(),
        P(DP, TENSOR),
        P(DP, TENSOR),
        P(DP, TENSOR),
        P(TENSOR, DP),
        P(),
        P(DP, None, TENSOR),
        P(DP, None, TENSOR),
        P(DP, TENSOR, None),
    )
    return jax.shard_map(shards, mesh=split, in_specs=in_specs, out_specs=out_specs, check_vma=False)
```

```python
import jax
import jax.numpy as jnp
import functools
import math

from jax import lax
from jax.experimental import pallas as pl
from jax.experimental.pallas import tpu as pltpu
from jax.sharding import PartitionSpec as P

WINDOW = 1024
DP = ("plane", "pack")
TENSOR = ("side", "core")


EPSILON = 1e-06
THETA = 50000.0
NEG_FILL = -1e30


def matmul(left_side, right_side):
    return jnp.dot(left_side, right_side, preferred_element_type=jnp.float32)


def contract_last(left_side, right_side):
    return lax.dot_general(
        left_side, right_side, (((1,), (1,)), ((), ())), preferred_element_type=jnp.float32
    )


def contract_first(left_side, right_side):
    return lax.dot_general(
        left_side, right_side, (((0,), (0,)), ((), ())), preferred_element_type=jnp.float32
    )


def norm_parts(values):
    factor = lax.rsqrt(jnp.mean(values * values, axis=-1, keepdims=True) + EPSILON)
    return (values * factor, factor)


def norm_back(grad_out, normed, factor, gain_vec):
    scaled = grad_out * gain_vec
    return factor * (scaled - normed * jnp.mean(scaled * normed, axis=-1, keepdims=True))


def rope_tables(length, head_size):
    half_size = head_size // 2
    frequency = THETA ** (-(2.0 * jnp.arange(half_size, dtype=jnp.float32)) / head_size)
    angles = jnp.arange(length, dtype=jnp.float32)[:, None] * frequency[None, :]
    return (jnp.cos(angles)[:, None, :], jnp.sin(angles)[:, None, :])


def rotate(values, cosine, sine_tab):
    half_size = values.shape[-1] // 2
    first_half = values[..., :half_size]
    second_half = values[..., half_size:]
    return jnp.concatenate(
        [
            first_half * cosine - second_half * sine_tab,
            second_half * cosine + first_half * sine_tab,
        ],
        axis=-1,
    )


def rotate_back(grads_in, cosine, sine_tab):
    half_size = grads_in.shape[-1] // 2
    first_half = grads_in[..., :half_size]
    second_half = grads_in[..., half_size:]
    return jnp.concatenate(
        [
            first_half * cosine + second_half * sine_tab,
            second_half * cosine - first_half * sine_tab,
        ],
        axis=-1,
    )


def block_mask(segments, offset, block_rows, key_count):
    query_pos = offset + jnp.arange(block_rows)
    key_pos = jnp.arange(key_count)
    same_doc = segments[offset : offset + block_rows][:, None] == segments[None, :]
    near_pos = jnp.abs(query_pos[:, None] - key_pos[None, :]) < WINDOW // 2
    return same_doc & near_pos


def block_scores(query_block, key_low, allowed, inv_root):
    scores = (
        jnp.einsum("qhd,khd->hqk", query_block, key_low, preferred_element_type=jnp.float32)
        * inv_root
    )
    return jnp.where(allowed[None], scores, NEG_FILL)


def row_sum(term_fn, tok_rows):
    return lax.psum_scatter(
        term_fn(jnp.int32(0), lax.axis_size(TENSOR) * tok_rows),
        TENSOR,
        scatter_dimension=0,
        tiled=True,
    )


def gather_rows(values):
    return lax.all_gather(values, TENSOR, axis=0, tiled=True)


def from_experts(values):
    return lax.all_to_all(values, DP, split_axis=1, concat_axis=1, tiled=True)


def to_experts(source_rows, slot_token, slot_gate, layout):
    picked = jnp.take(source_rows, slot_token, axis=0, mode="fill", fill_value=0)
    if slot_gate is not None:
        picked = (picked.astype(jnp.float32) * slot_gate[:, None]).astype(jnp.bfloat16)
    picked = picked.reshape(layout + (picked.shape[1],))
    return lax.all_to_all(picked, DP, split_axis=1, concat_axis=1, tiled=True)


def pair_sum(table, weights_low, pair_slots, row_count):
    picked = jnp.take(table, pair_slots.reshape(-1), axis=0, mode="fill", fill_value=0)
    picked = picked.reshape(row_count, pair_slots.shape[1], table.shape[1])
    return jnp.einsum("rk,rkd->rd", weights_low, picked, preferred_element_type=jnp.float32)


def expert_forward(operands):
    rows_in, gate_mat, up_mat, down_mat = operands
    flat_rows = rows_in.reshape(-1, rows_in.shape[-1])
    gated = matmul(flat_rows, gate_mat)
    lifted = matmul(flat_rows, up_mat)
    hidden = (jax.nn.silu(gated) * lifted).astype(jnp.bfloat16)
    result = matmul(hidden, down_mat).astype(jnp.bfloat16)
    return (result.reshape(rows_in.shape), gated, lifted)


def expert_backward(operands):
    rows_in, grad_in, gated, lifted, gate_mat, up_mat, down_mat = operands
    flat_rows = rows_in.reshape(-1, rows_in.shape[-1])
    flat_grad = grad_in.reshape(-1, grad_in.shape[-1])
    gate_sig = jax.nn.sigmoid(gated)
    activated = jax.nn.silu(gated)
    hidden = (activated * lifted).astype(jnp.bfloat16)
    grad_hidden = contract_last(flat_grad, down_mat)
    grad_down = contract_first(hidden, flat_grad)
    grad_gated = (grad_hidden * lifted * gate_sig * (1.0 + gated * (1.0 - gate_sig))).astype(
        jnp.bfloat16
    )
    grad_lifted = (grad_hidden * activated).astype(jnp.bfloat16)
    grad_gate = contract_first(flat_rows, grad_gated)
    grad_up = contract_first(flat_rows, grad_lifted)
    grad_rows = (contract_last(grad_gated, gate_mat) + contract_last(grad_lifted, up_mat)).astype(
        jnp.bfloat16
    )
    return (grad_rows.reshape(rows_in.shape), grad_gate, grad_up, grad_down)


VMEM_BYTES = 60 * 1024 * 1024
COLUMN_CHUNK = 512
GROUP = 2


def select_rows(places_ref, gates_ref, pick_ref, capacity):
    expert_count, seq_len = places_ref.shape[1:]
    slot_range = lax.broadcasted_iota(jnp.int32, (capacity, seq_len), 0).astype(jnp.bfloat16)
    nothing = jnp.zeros((capacity, seq_len), jnp.bfloat16)
    for expert in range(expert_count):
        hit = places_ref[0, expert : expert + 1, :] == slot_range
        if gates_ref is None:
            weight = jnp.ones((capacity, seq_len), jnp.bfloat16)
        else:
            weight = jnp.broadcast_to(gates_ref[0, expert : expert + 1, :], (capacity, seq_len))
        rows = slice(expert * capacity, (expert + 1) * capacity)
        pick_ref[rows, :] = jnp.where(hit, weight, nothing)


def rows_to_slots(pick_ref, rows_ref, slots_ref, pack, capacity):
    width = rows_ref.shape[2]
    expert_count = slots_ref.shape[0]
    for start in range(0, width, COLUMN_CHUNK):
        columns = slice(start, start + COLUMN_CHUNK)
        picked = matmul(pick_ref[...], rows_ref[0, :, columns]).astype(jnp.bfloat16)
        slots_ref[:, pack, :, columns] = picked.reshape(expert_count, capacity, COLUMN_CHUNK)


def slots_to_rows(pick_ref, slots_ref, own_ref, other_ref, pack):
    width = own_ref.shape[3]
    for start in range(0, width, COLUMN_CHUNK):
        columns = slice(start, start + COLUMN_CHUNK)
        slots = slots_ref[:, pack, :, columns].reshape(-1, COLUMN_CHUNK)
        rows = contract_first(pick_ref[...], slots).astype(own_ref.dtype)
        rows = rows.reshape(2, 2, own_ref.shape[2], COLUMN_CHUNK)
        own_ref[0, :, :, columns] = rows[:, 0]
        other_ref[0, :, :, columns] = rows[:, 1]


def cot_kernel(
    packs, steps, capacity, table, places, gates, rows, down, slots_out, hidden_out, slots, pick
):
    step = pl.program_id(0)

    @pl.when(step < packs)
    def _():
        select_rows(places, gates, pick, capacity)
        rows_to_slots(pick, rows, slots, step, capacity)

    @pl.when(step >= packs)
    def _():
        for member in range(down.shape[0]):
            block = slots[(step - packs) * down.shape[0] + member].reshape(packs * capacity, -1)
            slots_out[member] = block
            hidden_out[member] = contract_last(block, down[member])


def piece_copies(own, other, rows, sems, pack):
    half_rows = own.shape[1]
    copies = []
    for far in range(2):
        for core, source in enumerate((own, other)):
            for half, index in enumerate((4 * far + pack, 2 + 4 * pack + far)):
                start = ((far * 2 + core) * 2 + half) * half_rows
                copies.append(
                    pltpu.make_async_copy(
                        source.at[index],
                        rows.at[pack, pl.ds(start, half_rows)],
                        sems.at[pack * 8 + len(copies)],
                    )
                )
    return copies


def row_kernel(
    packs, steps, capacity, places, own, other, both, grad_hidden,
    slots_out, hidden_out, grads_out, rows_own, rows_other,
    rows, slots, grads, pick, sems,
):
    step = pl.program_id(0)
    half = hidden_out.shape[2]

    @pl.when(step == 0)
    def _():
        for pack in range(packs):
            for copy in piece_copies(own, other, rows, sems, pack):
                copy.start()
        for pack in range(packs):
            select_rows(places.at[pl.ds(pack, 1)], None, pick.at[pack], capacity)

    for pack in range(packs):

        @pl.when(step == pack)
        def _(pack=pack):
            for copy in piece_copies(own, other, rows, sems, pack):
                copy.wait()
            rows_to_slots(pick.at[pack], rows.at[pl.ds(pack, 1)], slots, pack, capacity)

    @pl.when((step >= packs) & (step < packs + steps))
    def _():
        for member in range(both.shape[0]):
            expert = (step - packs) * both.shape[0] + member
            block = slots[expert].reshape(packs * capacity, -1)
            slots_out[member] = block
            product = matmul(block, both[member])
            gated, lifted = product[:, :half], product[:, half:]
            sig = 1.0 / (1.0 + jnp.exp(-gated))
            active = gated * sig
            hidden_out[member] = (active * lifted).astype(jnp.bfloat16)
            above = grad_hidden[member]
            grad_gated = above * lifted * sig * (1.0 + gated * (1.0 - sig))
            joined = jnp.concatenate([grad_gated, above * active], axis=1).astype(jnp.bfloat16)
            grads_out[member] = joined
            back = contract_last(joined, both[member])
            grads[expert] = back.astype(jnp.bfloat16).reshape(packs, capacity, -1)

    for pack in range(packs):

        @pl.when(step == packs + steps + pack)
        def _(pack=pack):
            slots_to_rows(pick.at[pack], grads, rows_own, rows_other, pack)


def mix_kernel(packs, steps, capacity, table, places, gates, hidden, down, *refs):
    rows, results, pick = refs[-3:]
    step = pl.program_id(0)

    @pl.when(step < steps)
    def _():
        for member in range(down.shape[0]):
            result = matmul(hidden[member], down[member]).astype(jnp.bfloat16)
            results[step * down.shape[0] + member] = result.reshape(packs, capacity, -1)

    @pl.when(step >= steps)
    def _():
        select_rows(places, gates, pick, capacity)
        pack = (step - steps) ^ table[0]
        for start in range(0, rows.shape[3], COLUMN_CHUNK):
            columns = slice(start, start + COLUMN_CHUNK)
            slots = results[:, pack, :, columns].reshape(-1, COLUMN_CHUNK)
            rows[0, 0, :, columns] = contract_first(pick[...], slots).astype(rows.dtype)


def weight_kernel(planes, *refs):
    slots, grads, hidden, above = (
        jnp.concatenate([ref[0] for ref in refs[i * planes : (i + 1) * planes]]) for i in range(4)
    )
    gate_out, up_out, down_out = refs[-3:]
    half = gate_out.shape[2]
    both = contract_first(slots, above)
    gate_out[0] = both[:, :half]
    up_out[0] = both[:, half:]
    down_out[0] = contract_first(hidden, grads)


def block(shape, place, count=1):
    tail = (0,) * (len(shape) - 1)
    return pl.BlockSpec((count,) + tuple(shape[1:]), lambda *ids: (place(*ids),) + tail)


def staged(first, count):
    return lambda step, *rest: jnp.clip(step - first, 0, count - 1)


def shape_of(shape, kind):
    return jax.ShapeDtypeStruct(shape, kind)


def call(kernel, steps, specs, out_specs, out_shape, scratch, flops, prefetch=0, aliases={}):
    return pl.pallas_call(
        kernel,
        grid_spec=pltpu.PrefetchScalarGridSpec(
            num_scalar_prefetch=prefetch,
            grid=(steps,),
            in_specs=specs,
            out_specs=out_specs,
            scratch_shapes=scratch,
        ),
        out_shape=out_shape,
        input_output_aliases=aliases,
        cost_estimate=pl.CostEstimate(
            flops=flops, transcendentals=0, bytes_accessed=flops // 500
        ),
        compiler_params=pltpu.CompilerParams(
            dimension_semantics=("arbitrary",), vmem_limit_bytes=VMEM_BYTES
        ),
    )


def cot_slots(table, places, gates, rows, down, capacity):
    packs = table.shape[0]
    _, seq_len, width = rows.shape
    experts, hidden_width, _ = down.shape
    slot_rows = packs * capacity
    group = math.gcd(experts, GROUP)
    steps = experts // group
    by_pack, by_expert = staged(0, packs), staged(packs, steps)
    listed = lambda step, numbers: numbers[by_pack(step)]
    out_shape = [
        shape_of((experts, slot_rows, width), jnp.bfloat16),
        shape_of((experts, slot_rows, hidden_width), jnp.float32),
    ]
    return call(
        functools.partial(cot_kernel, packs, steps, capacity),
        packs + steps,
        [
            block(places.shape, listed), block(gates.shape, listed), block(rows.shape, listed),
            block(down.shape, by_expert, group),
        ],
        [block(out.shape, by_expert, group) for out in out_shape],
        out_shape,
        [
            pltpu.VMEM((experts, packs, capacity, width), jnp.bfloat16),
            pltpu.VMEM((experts * capacity, seq_len), jnp.bfloat16),
        ],
        2 * experts * slot_rows * width * (seq_len + hidden_width),
        1,
    )(table, places, gates, rows, down)


def row_slots(places, own, other, both, grad_hidden, capacity):
    packs, _, seq_len = places.shape
    experts, width, hidden_width = both.shape
    slot_rows = packs * capacity
    group = math.gcd(experts, GROUP)
    steps = experts // group
    middle, last = staged(packs, steps), staged(packs + steps, packs)
    part = shape_of((packs, 2, seq_len // 4, width), jnp.bfloat16)
    out_shape = [
        shape_of((experts, slot_rows, width), jnp.bfloat16),
        shape_of((experts, slot_rows, hidden_width // 2), jnp.bfloat16),
        shape_of((experts, slot_rows, hidden_width), jnp.bfloat16),
        part, part,
    ]
    anywhere = pl.BlockSpec(memory_space=pl.ANY)
    return call(
        functools.partial(row_kernel, packs, steps, capacity),
        2 * packs + steps,
        [
            block(places.shape, lambda step: 0, packs), anywhere, anywhere,
            block(both.shape, middle, group), block(grad_hidden.shape, middle, group),
        ],
        [block(out.shape, middle, group) for out in out_shape[:3]] + [block(part.shape, last)] * 2,
        out_shape,
        [
            pltpu.VMEM((packs, seq_len, width), jnp.bfloat16),
            pltpu.VMEM((experts, packs, capacity, width), jnp.bfloat16),
            pltpu.VMEM((experts, packs, capacity, width), jnp.bfloat16),
            pltpu.VMEM((packs, experts * capacity, seq_len), jnp.bfloat16),
            pltpu.SemaphoreType.DMA((8 * packs,)),
        ],
        4 * experts * slot_rows * width * (seq_len + hidden_width),
    )(places, own, other, both, grad_hidden)


def mix_rows(plane, planes, table, places, gates, hidden, down, capacity, earlier=()):
    packs, _, seq_len = places.shape
    experts, hidden_width, width = down.shape
    group = math.gcd(experts, GROUP)
    steps = experts // group
    first, last = staged(0, steps), staged(steps, packs)
    listed = lambda step, numbers: numbers[1] * steps + first(step)
    return call(
        functools.partial(mix_kernel, packs, steps, capacity),
        packs + steps,
        [
            block(places.shape, last), block(gates.shape, last),
            block(hidden.shape, listed, group), block(down.shape, first, group),
        ]
        + [pl.BlockSpec(memory_space=pl.ANY)] * len(earlier),
        [pl.BlockSpec((1, 1, seq_len, width), lambda step, numbers: (plane, last(step), 0, 0))],
        [shape_of((planes, packs, seq_len, width), jnp.bfloat16)],
        [
            pltpu.VMEM((experts, packs, capacity, width), jnp.bfloat16),
            pltpu.VMEM((experts * capacity, seq_len), jnp.bfloat16),
        ],
        2 * experts * packs * capacity * width * (seq_len + hidden_width),
        1,
        aliases={5 + index: index for index in range(len(earlier))},
    )(table, places, gates, hidden, down, *earlier)


def weight_grads(first, count, slots, hidden, grads, above, earlier=()):
    planes = len(slots)
    operands = [*slots, *grads, *hidden, *above]
    experts, _, width = slots[0].shape
    hidden_width = hidden[0].shape[2]
    each = lambda step: step + first
    out_shape = [
        shape_of((experts, width, hidden_width), jnp.float32),
        shape_of((experts, width, hidden_width), jnp.float32),
        shape_of((experts, hidden_width, width), jnp.float32),
    ]
    return call(
        functools.partial(weight_kernel, planes),
        count,
        [block(operand.shape, each) for operand in operands]
        + [pl.BlockSpec(memory_space=pl.ANY)] * len(earlier),
        [block(out.shape, each) for out in out_shape],
        out_shape,
        [],
        6 * planes * slots[0].shape[1] * count * width * hidden_width,
        aliases={len(operands) + index: index for index in range(len(earlier))},
    )(*operands, *earlier)


def swapped(values, axis, bit):
    count = lax.axis_size(axis)
    return lax.ppermute(values, axis, [(i, i ^ bit) for i in range(count)])


def far_side(values):
    return swapped(values, TENSOR, 2)


def far_core(values):
    return swapped(values, TENSOR, 1)


def far_pack(values):
    return swapped(values, DP, 1)


def next_plane(values):
    count = lax.axis_size(DP)
    return lax.ppermute(values, DP, [(i, (i + 2) % count) for i in range(count)])


def spread_all(values, small, work):
    planes = lax.axis_size("plane")
    half_rows = values.shape[0] // 2
    first = lambda rows: (far_pack(rows[:half_rows]), far_side(rows[half_rows:]))
    small, values = tied(small, values)
    (across_pack, across_side), following = lax.optimization_barrier(
        (first(values), next_plane(values))
    )
    pieces, made = [], []
    for plane in range(planes):
        upper = jnp.stack([values[:half_rows], across_pack])
        lower = jnp.stack([values[half_rows:], across_side])
        small, (upper, lower, values) = tied(small, (upper, lower, following))
        moved = [
            far_side(upper),
            far_pack(lower),
            first(values) if plane + 1 < planes else ((), ()),
            next_plane(values) if plane + 2 < planes else (),
            far_core(pieces[-1]) if plane else (),
            work(plane - 1, small) if plane else (),
        ]
        upper_far, lower_far, (across_pack, across_side), following, other, result = (
            lax.optimization_barrier(moved)
        )
        if plane:
            pieces[-1] = (pieces[-1], other)
        if plane:
            made.append(result)
        pieces.append(jnp.concatenate([upper, lower, upper_far, lower_far]))
    pieces[-1] = (pieces[-1], far_core(pieces[-1]))
    return pieces, made


def plane_order():
    packs = lax.axis_size(DP)
    planes = packs // 2
    index = lax.axis_index(DP)
    return jnp.stack(
        [
            ((index // 2 + planes - plane) % planes) * 2 + (index % 2 ^ near)
            for plane in range(planes)
            for near in range(2)
        ]
    )


def place_kernel(by_column, order, *refs):
    *pieces, whole, sems = refs
    copies = []
    for index, piece in enumerate(pieces):
        target = None if by_column else whole.at[order[index]]
        if by_column:
            width = piece.shape[1]
            target = whole.at[:, pl.ds(pl.multiple_of(order[index] * width, 128), width)]
        copies.append(pltpu.make_async_copy(piece, target, sems.at[index]))
        copies[-1].start()
    for copy in copies:
        copy.wait()


def laid(pieces, order, by_column=False):
    count = len(pieces)
    rows, columns = pieces[0].shape
    shape = (rows, count * columns) if by_column else (count, rows, columns)
    anywhere = pl.BlockSpec(memory_space=pl.ANY)
    return call(
        functools.partial(place_kernel, by_column),
        1,
        [anywhere] * count,
        pl.BlockSpec(memory_space=pltpu.VMEM),
        shape_of(shape, pieces[0].dtype),
        [pltpu.SemaphoreType.DMA((count,))],
        1000,
        1,
    )(order, *pieces)


class FoldPacks:
    def __init__(self, values):
        order = plane_order()
        take = lambda index: lax.dynamic_index_in_dim(values, order[index], 0, keepdims=False)
        planes = values.shape[0] // 2
        self.turns = [*range(1, planes), 0]
        self.near = {plane: take(2 * plane) for plane in self.turns}
        self.moving = {plane: far_pack(take(2 * plane + 1)) for plane in self.turns}
        self.summed, self.count = None, 0

    def step(self, other):
        if self.count >= len(self.turns):
            return other
        self.moving, other = tied(self.moving, other)
        if self.summed is None:
            self.near = {plane: added(self.near[plane], self.moving[plane]) for plane in self.turns}
            self.summed = self.near[self.turns[0]]
        else:
            kind = jnp.float32 if self.count + 1 == len(self.turns) else jnp.bfloat16
            self.summed = added(self.moving, self.near[self.turns[self.count]], kind)
        self.count += 1
        if self.count < len(self.turns):
            self.moving = next_plane(self.summed)
        return other

    def finish(self):
        for plane in self.turns[self.count :]:
            kind = jnp.float32 if plane == 0 else jnp.bfloat16
            self.summed = added(self.moving, self.near[plane], kind)
            self.moving = next_plane(self.summed) if plane else None
        return self.summed


def laid_sides(pieces):
    order = lax.axis_index(TENSOR) ^ jnp.arange(len(pieces), dtype=jnp.int32)
    return laid(pieces, order).reshape((-1,) + pieces[0].shape[1:])


def gather_sides(values):
    across = far_side(values)
    return laid_sides([values, far_core(values), across, far_core(across)])


def fold_sides(values):
    split = values.astype(jnp.bfloat16).reshape((4, -1) + values.shape[1:])
    take = lambda bits: lax.dynamic_index_in_dim(
        split, lax.axis_index(TENSOR) ^ bits, 0, keepdims=False
    )
    far = added(take(2), far_core(take(3)))
    near = added(take(0), far_core(take(1)))
    return added(near, far_side(far), jnp.float32)


def fold_both(weights, rows, mixed):
    order = plane_order()
    planes = weights.shape[0] // 2
    take = lambda index: lax.dynamic_index_in_dim(weights, order[index], 0, keepdims=False)
    split = rows.astype(jnp.bfloat16).reshape((4, -1) + rows.shape[1:])
    mine = lax.axis_index(TENSOR)
    pick = lambda bits: lax.dynamic_index_in_dim(split, mine ^ bits, 0, keepdims=False)
    summed, total = None, None
    for turn, plane in enumerate([*range(1, planes), 0]):
        moved = [far_pack(take(2 * plane + 1)), () if summed is None else next_plane(summed)]
        if turn == 0:
            moved += [far_core(pick(3)), far_core(pick(1))]
        if turn == 1:
            moved += [far_side(far)]
        across, passed, *arrived = lax.optimization_barrier(moved)
        if turn == 0:
            far, close = added(pick(2), arrived[0]), added(pick(0), arrived[1])
            mixed, far = tied(mixed, far)
            mixed = jnp.concatenate(mixed)
            mixed = lax.psum_scatter(mixed, "plane", scatter_dimension=0, tiled=True)
        if turn == 1:
            total = added(close, arrived[0], jnp.float32)
        near = added(take(2 * plane), across)
        kind = jnp.float32 if turn + 1 == planes else jnp.bfloat16
        summed = near if turn == 0 else added(passed, near, kind)
    return summed, total, mixed


def gather_both(weights, outer, rows, gate, up, tables):
    hops = table_hops()
    pieces, outer_pieces, row_pieces, values = [], [], [rows], (weights, outer)
    planes = lax.axis_size("plane")
    for plane in range(planes):
        moved = [tuple(far_pack(value) for value in values), ()]
        if plane + 1 < planes:
            moved[1] = tuple(next_plane(value) for value in values)
        if plane == 0:
            moved += [far_core(rows), far_side(rows)]
        if plane == 1:
            moved += [far_core(row_pieces[2])]
        if plane == 0:
            moved.insert(2, jnp.concatenate([gate, up], axis=2))
        moved.insert(2, swapped(tables, *hops[plane]) if plane < len(hops) else ())
        across, following, more, *arrived = lax.optimization_barrier(moved)
        if plane < len(hops):
            tables = jnp.concatenate([tables, more])
        if plane == 0:
            joined = arrived.pop(0)
        pieces += [values[0], across[0]]
        outer_pieces += [values[1], across[1]]
        row_pieces += arrived
        values = following
    order = plane_order()
    for hop in hops[planes:]:
        tables = jnp.concatenate([tables, swapped(tables, *hop)])
    laid_rows = laid_sides(row_pieces)
    return laid(pieces, order), laid(outer_pieces, order, True), laid_rows, joined, tables


def sum_everywhere(values):
    for axis in (TENSOR, DP):
        bit = 1
        while bit < lax.axis_size(axis):
            values = values + swapped(values, axis, bit)
            bit *= 2
    return values


def added(left, right, kind=jnp.bfloat16):
    return (left.astype(jnp.float32) + right.astype(jnp.float32)).astype(kind)


def fold_first(own, arrived):
    half_rows = own.shape[2] // 2
    upper, lower = slice(None, half_rows), slice(half_rows, None)
    return (
        added(own[:, 0, upper], arrived[:, 0, upper]),
        added(own[0, :, lower], arrived[0, :, lower]),
        added(own[:, 1, upper], arrived[:, 1, upper]),
        added(own[1, :, lower], arrived[1, :, lower]),
    )


def tied(small, values):
    return lax.optimization_barrier((small, values))


def table_hops():
    hops = []
    for axis in (TENSOR, DP):
        bit = 1
        while bit < lax.axis_size(axis):
            hops.append((axis, bit))
            bit *= 2
    return hops


def read_tables(tables, top_count):
    own = lax.axis_index(DP) * lax.axis_size(TENSOR) + lax.axis_index(TENSOR)
    sides = jnp.arange(lax.axis_size(TENSOR), dtype=jnp.int32) ^ lax.axis_index(TENSOR)
    segments = jnp.take(tables[: sides.shape[0], -1], sides, axis=0).reshape(-1)
    devices = jnp.arange(tables.shape[0], dtype=jnp.int32)
    tables = jnp.take(tables, devices ^ own, axis=0)
    all_ids, all_gates = tables[:, :top_count], tables[:, top_count : 2 * top_count]
    return all_ids.astype(jnp.int32), all_gates, segments.astype(jnp.int32)


def routing(all_ids, all_gates, local_experts, capacity):
    packs = lax.axis_size(DP)
    first = lax.axis_index(DP) * local_experts
    wanted = first + jnp.arange(local_experts, dtype=jnp.int32)

    def by_pack(values):
        top_count, tok_rows = values.shape[1:]
        ordered = values.reshape(packs, -1, top_count, tok_rows).transpose(0, 2, 1, 3)
        return ordered.reshape(packs, top_count, -1)

    matches = by_pack(all_ids)[:, :, None, :] == wanted[None, None, :, None]
    pair_gates = by_pack(all_gates).astype(jnp.float32)
    member = jnp.any(matches, axis=1)
    gates = jnp.sum(jnp.where(matches, pair_gates[:, :, None, :], 0.0), axis=1)
    order = jnp.arange(member.shape[2], dtype=jnp.int32)
    earlier = (order[:, None] < order[None, :]).astype(jnp.bfloat16)
    flat = member.reshape(packs * local_experts, -1).astype(jnp.bfloat16)
    before = matmul(flat, earlier).astype(jnp.int32).reshape(member.shape)
    places = jnp.where(member & (before < capacity), before, -1)
    return places.astype(jnp.bfloat16), gates.astype(jnp.bfloat16)


def experts_by_exchange(
    second_in, cotangent, expert_ids, gate_values, w_gate, w_up, w_down, middle, capacity
):
    tok_rows, model_width = second_in.shape
    tensor_count = lax.axis_size(TENSOR)
    data_count = lax.axis_size(DP)
    local_experts = w_gate.shape[0]
    all_experts = local_experts * data_count
    top_count = expert_ids.shape[1]
    seq_len = tok_rows * tensor_count
    pack_cot, pack_ids, pack_gates = (
        gather_rows(cotangent), gather_rows(expert_ids), gather_rows(gate_values)
    )
    pack_second = gather_rows(second_in)
    expert_range = jnp.arange(all_experts, dtype=jnp.int32)
    matches = pack_ids[:, :, None] == expert_range[None, None, :]
    token_counts = jnp.sum(matches.astype(jnp.float32), axis=1).astype(jnp.bfloat16)
    token_range = jnp.arange(seq_len, dtype=jnp.int32)
    earlier = (token_range[:, None] > token_range[None, :]).astype(jnp.bfloat16)
    before = matmul(earlier, token_counts)
    places = (
        jnp.sum(jnp.where(matches, before[:, None, :], 0.0), axis=2).astype(jnp.int32).reshape(-1)
    )
    flat_ids = pack_ids.reshape(-1)
    owners = flat_ids // local_experts
    local_index = flat_ids % local_experts
    dump_slot = all_experts * capacity
    slot_index = jnp.where(
        places < capacity,
        local_index * (data_count * capacity) + owners * capacity + places,
        dump_slot,
    ).astype(jnp.int32)
    pair_token = jnp.arange(seq_len * top_count) // top_count
    slot_token = (
        jnp.full((dump_slot + 1,), seq_len, jnp.int32).at[slot_index].set(pair_token)[:dump_slot]
    )
    pair_gates = pack_gates.astype(jnp.float32)
    slot_gate = (
        jnp.zeros((dump_slot + 1,), jnp.float32)
        .at[slot_index]
        .set(pair_gates.reshape(-1))[:dump_slot]
    )
    pair_slots = slot_index.reshape(seq_len, top_count)
    layout = (local_experts, data_count, capacity)
    arrived_rows = to_experts(pack_second, slot_token, None, layout)
    expert_out, gated_all, lifted_all = lax.map(
        expert_forward, (arrived_rows, w_gate, w_up, w_down)
    )
    returned = from_experts(expert_out).reshape(-1, model_width)

    def combine_term(offset, row_count):
        return pair_sum(returned, pack_gates, pair_slots, row_count)

    outputs = middle + row_sum(combine_term, tok_rows)
    grad_arrived = to_experts(pack_cot, slot_token, slot_gate, layout)
    grad_rows_all, grad_w_gate, grad_w_up, grad_w_down = lax.map(
        expert_backward, (arrived_rows, grad_arrived, gated_all, lifted_all, w_gate, w_up, w_down)
    )
    returned_grad = from_experts(grad_rows_all).reshape(-1, model_width)
    unit_gates = jnp.ones_like(pack_gates)

    def dispatch_term(offset, row_count):
        return pair_sum(returned_grad, unit_gates, pair_slots, row_count)

    grad_second = row_sum(dispatch_term, tok_rows)
    return outputs, grad_second, grad_w_gate, grad_w_up, grad_w_down


class Folding:
    def __init__(self, order):
        self.order, self.planes, self.ready = order, {}, {}
        self.summed, self.passed, self.count = None, None, 0

    def begin(self, plane, own, other):
        self.planes[plane] = (0, (own, other))

    def turn(self, small, work):
        small, (planes, summed) = tied(
            small, ({plane: values for plane, (_, values) in self.planes.items()}, self.summed)
        )
        sent = {}
        for plane, values in planes.items():
            stage = self.planes[plane][0]
            if stage == 0:
                sent[plane] = (far_core(values[1]),)
            elif stage == 1:
                sent[plane] = (far_side(values[2]), far_pack(values[3]))
            else:
                sent[plane] = (far_pack(values[2]), far_side(values[3]))
        passed = self.passed
        if passed is None and summed is not None and not self.done():
            passed = next_plane(summed)
        sent, passed, result = lax.optimization_barrier((sent, passed, work(small)))
        self.passed = passed
        for plane, values in planes.items():
            stage, arrived = self.planes[plane][0], sent[plane]
            if stage == 0:
                made = fold_first(values[0], *arrived)
            elif stage == 1:
                upper, lower = added(values[0], arrived[0]), added(values[1], arrived[1])
                made = (upper[0], lower[0], upper[1], lower[1])
            else:
                self.ready[plane] = jnp.concatenate(
                    [added(values[0], arrived[0]), added(values[1], arrived[1])]
                )
            if stage < 2:
                self.planes[plane] = (stage + 1, made)
            else:
                del self.planes[plane]
        following = self.order[self.count] if self.count < len(self.order) else None
        if following in self.ready:
            last = self.count + 1 == len(self.order)
            self.summed = self.ready[following]
            if passed is not None:
                kind = jnp.float32 if last else jnp.bfloat16
                self.summed = added(passed, self.summed, kind)
            self.passed = None
            self.count += 1
        return result

    def done(self):
        return self.count == len(self.order)


def experts_by_gather(second_in, all_cot, places, gates, w_both, w_down, capacity):
    packs, local_experts, seq_len = places.shape
    tensor_count = lax.axis_size(TENSOR)
    planes = packs // 2
    pack_order = plane_order()
    side_index = lax.axis_index(TENSOR)
    quarter_order = side_index ^ jnp.arange(tensor_count, dtype=jnp.int32)

    def as_met(values, by_pack, by_quarter):
        split = values.reshape(packs, local_experts, tensor_count, -1)
        split = jnp.take(jnp.take(split, by_pack, axis=0), by_quarter, axis=2)
        return split.reshape(values.shape)

    near_places = as_met(places, pack_order, quarter_order)
    pairs = [slice(plane * 2, plane * 2 + 2) for plane in range(planes)]
    tables = [
        jnp.stack([lax.axis_index("pack"), (lax.axis_index("plane") + planes - plane) % planes])
        for plane in range(planes)
    ]
    prepared = [
        [table[pair] for pair in pairs] for table in (near_places, places, gates, pack_order)
    ]
    prepared, second_in = tied((prepared, tables, places, gates), second_in)
    (near_places, mix_places, mix_gates, pack_order), tables, places, gates = prepared

    def cot_work(plane, order):
        return cot_slots(order[plane], places, gates, all_cot, w_down, capacity)

    pieces, made = spread_all(second_in, pack_order, cot_work)
    order = [*range(1, planes), 0]
    kept, folding = {}, Folding(order)

    def row_work(plane, near):
        return row_slots(near, *pieces[plane], w_both, made[plane][1], capacity)

    for plane in order:
        if folding.planes:
            result = folding.turn(near_places[plane], functools.partial(row_work, plane))
        else:
            result = row_work(plane, near_places[plane])
        slots, hidden, above, *part = result
        folding.begin(plane, *part)
        kept[plane] = (slots, hidden, made[plane][0], above)
        if len(made) < planes:
            made.append(folding.turn(pack_order, functools.partial(cot_work, len(made))))
    hidden_all = jnp.concatenate([kept[plane][1] for plane in range(planes)])

    def mix_turn(start, table):
        mixed = ()
        for index in range(2):
            plane = start + index
            mixed = mix_rows(
                index, 2, table[plane], mix_places[plane], mix_gates[plane], hidden_all, w_down,
                capacity, mixed,
            )
        return mixed[0].reshape(2, -1, mixed[0].shape[-1])

    mixed = []
    for start in range(0, planes, 2):
        part = folding.turn(tables, functools.partial(mix_turn, start))
        mixed.append(
            lax.psum_scatter(part, ("pack", "side", "core"), scatter_dimension=1, tiled=True)
        )
    kept = [kept[plane] for plane in range(planes)]
    weight_parts, next_expert = (), 0
    part_size = math.gcd(local_experts, GROUP)

    def weight_turn(count, small):
        state, (held, weights) = next_expert, small
        for _ in range(count):
            if state < local_experts:
                weights = weight_grads(state, part_size, *zip(*held), weights)
                state += part_size
        return weights

    for count in (2, 1, *[0] * planes):
        if folding.done():
            break
        weight_parts = folding.turn((kept, weight_parts), functools.partial(weight_turn, count))
        next_expert = min(next_expert + count * part_size, local_experts)
    rest = (kept, weight_parts, next_expert, part_size)
    return folding.summed, mixed, rest


def shards(
    inputs,
    segment_ids,
    expert_ids,
    gate_values,
    attn_gain,
    query_gain,
    key_gain,
    w_query,
    w_key,
    w_value,
    w_output,
    ffn_gain,
    w_gate,
    w_up,
    w_down,
    cotangent,
):
    tok_rows, model_width = inputs.shape
    head_size = query_gain.shape[0]
    tensor_count = lax.axis_size(TENSOR)
    data_count = lax.axis_size(DP)
    local_experts = w_gate.shape[0]
    all_experts = local_experts * data_count
    top_count = expert_ids.shape[1]
    seq_len = tok_rows * tensor_count
    capacity = seq_len * top_count // all_experts
    inv_root = head_size ** (-0.5)
    by_gather = (
        seq_len <= local_experts * capacity
        and tensor_count == 4
        and data_count > 2
        and data_count & (data_count - 1) == 0
        and all_experts <= 256
    )
    if by_gather:
        axes = (*DP, *TENSOR)
        tables = jnp.concatenate(
            [expert_ids.T.astype(jnp.bfloat16), gate_values.T, segment_ids.astype(jnp.bfloat16)]
        )[None]
    inputs_f32 = inputs.astype(jnp.float32)
    normed_one, factor_one = norm_parts(inputs_f32)
    first_in = (normed_one * attn_gain).astype(jnp.bfloat16)
    if by_gather:
        side_sum, side_gather = fold_sides, gather_sides
        local_width = w_query.shape[1]
        w_in = jnp.concatenate([w_query, w_key, w_value], axis=1)
        full_in, full_output, pack_in, w_both, tables = gather_both(
            w_in, w_output, first_in, w_gate, w_up, tables
        )
        all_ids, all_gates, segments = read_tables(tables, top_count)
        places, gates = routing(all_ids, all_gates, local_experts, capacity)
        full_in, cotangent = tied(full_in, cotangent)
        all_cot = lax.all_gather(cotangent, axes, axis=0, tiled=True)
        all_cot = all_cot.reshape(data_count, seq_len, model_width)
        full_in = full_in.reshape(model_width, -1)
        full_query, full_key, full_value = (
            full_in[:, index * local_width : (index + 1) * local_width] for index in range(3)
        )
    else:
        side_sum, side_gather = lambda term: row_sum(lambda *_: term, tok_rows), gather_rows
        segments = lax.all_gather(segment_ids, TENSOR, axis=1, tiled=True)[0]
        full_query, full_key, full_value, full_output = (
            lax.all_gather(w_query, DP, axis=0, tiled=True),
            lax.all_gather(w_key, DP, axis=0, tiled=True),
            lax.all_gather(w_value, DP, axis=0, tiled=True),
            lax.all_gather(w_output, DP, axis=1, tiled=True),
        )
        pack_in = side_gather(first_in)
    query_pre = matmul(pack_in, full_query)
    key_pre = matmul(pack_in, full_key)
    value_low = matmul(pack_in, full_value).astype(jnp.bfloat16)
    head_count = query_pre.shape[1] // head_size
    cosine, sine_tab = rope_tables(seq_len, head_size)
    query_norm, query_factor = norm_parts(query_pre.reshape(seq_len, head_count, head_size))
    key_norm, key_factor = norm_parts(key_pre.reshape(seq_len, head_count, head_size))
    query_low = rotate(query_norm * query_gain, cosine, sine_tab).astype(jnp.bfloat16)
    key_low = rotate(key_norm * key_gain, cosine, sine_tab).astype(jnp.bfloat16)
    value_heads = value_low.reshape(seq_len, head_count, head_size)
    block_rows = min(512, seq_len)
    block_total = seq_len // block_rows
    masks = []
    mixture_parts = []
    lse_parts = []
    for block_index in range(block_total):
        offset = block_index * block_rows
        allowed = block_mask(segments, offset, block_rows, seq_len)
        masks.append(allowed)
        scores = block_scores(query_low[offset : offset + block_rows], key_low, allowed, inv_root)
        top_score = jnp.max(scores, axis=-1, keepdims=True)
        raw_weights = jnp.exp(scores - top_score)
        totals = jnp.sum(raw_weights, axis=-1, keepdims=True)
        weights_low = (raw_weights / totals).astype(jnp.bfloat16)
        mixture_parts.append(
            jnp.einsum(
                "hqk,khd->qhd", weights_low, value_heads, preferred_element_type=jnp.float32
            ).astype(jnp.bfloat16)
        )
        lse_parts.append(top_score + jnp.log(totals))
    mixture = jnp.concatenate(mixture_parts, axis=0).reshape(seq_len, head_count * head_size)

    middle = inputs_f32 + side_sum(matmul(mixture, full_output))
    normed_two, factor_two = norm_parts(middle)
    second_in = (normed_two * ffn_gain).astype(jnp.bfloat16)
    if by_gather:
        grad_second, mixed, rest = experts_by_gather(
            second_in, all_cot, places, gates, w_both, w_down, capacity
        )
    else:
        outputs, grad_second, grad_w_gate, grad_w_up, grad_w_down = experts_by_exchange(
            second_in, cotangent, expert_ids, gate_values, w_gate, w_up, w_down, middle, capacity
        )
    ffn_gain_part = jnp.sum(grad_second * normed_two, axis=0)
    grad_middle = cotangent.astype(jnp.float32) + norm_back(
        grad_second, normed_two, factor_two, ffn_gain
    )
    grad_attended = grad_middle.astype(jnp.bfloat16)
    if by_gather:
        kept, weight_parts, next_expert, part_size = rest
        (kept, weight_parts), grad_attended = tied((kept, weight_parts), grad_attended)
        moved = [far_core(grad_attended), far_side(grad_attended)]
        for first in range(next_expert, local_experts, part_size):
            weight_parts = weight_grads(first, part_size, *zip(*kept), weight_parts)
        grad_w_gate, grad_w_up, grad_w_down = weight_parts
        near, across, weight_parts = lax.optimization_barrier((*moved, weight_parts))
        grad_w_gate, grad_w_up, grad_w_down = weight_parts
        pack_grad = laid_sides([grad_attended, near, across, far_core(across)])
    else:
        pack_grad = side_gather(grad_attended)
    output_part = contract_first(mixture, pack_grad)
    fold_step = lambda other: other
    if by_gather:
        by_column = output_part.astype(jnp.bfloat16).reshape(local_width, data_count, -1)
        folded = FoldPacks(by_column.transpose(1, 0, 2))
        fold_step = folded.step
    grad_mixture = (
        contract_last(pack_grad, full_output)
        .astype(jnp.bfloat16)
        .reshape(seq_len, head_count, head_size)
    )
    grad_query_parts = []
    grad_key_sum = jnp.zeros((seq_len, head_count, head_size), jnp.float32)
    grad_value_sum = jnp.zeros((seq_len, head_count, head_size), jnp.float32)
    for block_index in range(block_total):
        offset = block_index * block_rows
        query_block = query_low[offset : offset + block_rows]
        grad_block = grad_mixture[offset : offset + block_rows]
        scores = block_scores(query_block, key_low, masks[block_index], inv_root)
        prob_rows = jnp.exp(scores - lse_parts[block_index])
        grad_probs = jnp.einsum(
            "qhd,khd->hqk", grad_block, value_heads, preferred_element_type=jnp.float32
        )
        row_delta = jnp.sum(grad_probs * prob_rows, axis=-1, keepdims=True)
        grad_scores = (prob_rows * (grad_probs - row_delta)).astype(jnp.bfloat16)
        grad_query_parts.append(
            jnp.einsum("hqk,khd->qhd", grad_scores, key_low, preferred_element_type=jnp.float32)
            * inv_root
        )
        grad_key_sum = (
            grad_key_sum
            + jnp.einsum(
                "hqk,qhd->khd", grad_scores, query_block, preferred_element_type=jnp.float32
            )
            * inv_root
        )
        grad_value_sum = grad_value_sum + jnp.einsum(
            "hqk,qhd->khd",
            prob_rows.astype(jnp.bfloat16),
            grad_block,
            preferred_element_type=jnp.float32,
        )
    grad_query_norm = rotate_back(jnp.concatenate(grad_query_parts, axis=0), cosine, sine_tab)
    grad_key_norm = rotate_back(grad_key_sum, cosine, sine_tab)
    grad_query_norm = fold_step(grad_query_norm)
    query_gain_part = jnp.sum(grad_query_norm * query_norm, axis=(0, 1))
    key_gain_part = jnp.sum(grad_key_norm * key_norm, axis=(0, 1))
    grad_query_pre = (
        norm_back(grad_query_norm, query_norm, query_factor, query_gain)
        .reshape(seq_len, -1)
        .astype(jnp.bfloat16)
    )
    grad_key_pre = (
        norm_back(grad_key_norm, key_norm, key_factor, key_gain)
        .reshape(seq_len, -1)
        .astype(jnp.bfloat16)
    )
    grad_value_low = grad_value_sum.reshape(seq_len, -1).astype(jnp.bfloat16)
    query_part = contract_first(pack_in, grad_query_pre)
    key_part = contract_first(pack_in, grad_key_pre)
    value_part = contract_first(pack_in, grad_value_low)

    total_term = contract_last(grad_query_pre, full_query)
    total_term = total_term + contract_last(grad_key_pre, full_key)
    total_term = total_term + contract_last(grad_value_low, full_value)
    if by_gather:
        in_part = jnp.concatenate([query_part, key_part, value_part], axis=1)
        in_part = in_part.astype(jnp.bfloat16).reshape(data_count, -1, 3 * local_width)
        in_part = fold_step(in_part)
        grad_w_output = folded.finish()
        grad_in, grad_first, mixed = fold_both(in_part, total_term, mixed)
        mixed, grad_in = tied(mixed, grad_in)
    else:
        grad_first = side_sum(total_term)
    attn_gain_part = jnp.sum(grad_first * normed_one, axis=0)
    grad_inputs = grad_middle + norm_back(grad_first, normed_one, factor_one, attn_gain)
    gain_parts = (attn_gain_part, ffn_gain_part, query_gain_part, key_gain_part)
    if by_gather:
        grad_w_query, grad_w_key, grad_w_value = (
            grad_in[:, index * local_width : (index + 1) * local_width] for index in range(3)
        )
        outputs = middle + mixed[0].astype(jnp.float32)
        splits = (model_width, 2 * model_width, 2 * model_width + head_size)
        gain_sums = jnp.split(sum_everywhere(jnp.concatenate(gain_parts)), splits)
    else:
        grad_w_query, grad_w_key, grad_w_value, grad_w_output = (
            lax.psum_scatter(
                part.astype(jnp.bfloat16), DP, scatter_dimension=along, tiled=True
            ).astype(jnp.float32)
            for part, along in ((query_part, 0), (key_part, 0), (value_part, 0), (output_part, 1))
        )
        gain_sums = lax.psum(gain_parts, (*DP, *TENSOR))
    grad_attn_gain, grad_ffn_gain, grad_query_gain, grad_key_gain = gain_sums
    return (
        outputs,
        grad_inputs,
        grad_attn_gain,
        grad_query_gain,
        grad_key_gain,
        grad_w_query,
        grad_w_key,
        grad_w_value,
        grad_w_output,
        grad_ffn_gain,
        grad_w_gate,
        grad_w_up,
        grad_w_down,
    )


def solution(mesh):
    rows, columns = mesh.devices.shape
    split = jax.sharding.Mesh(
        mesh.devices.reshape(rows // 2, 2, columns // 2, 2), (*DP, *TENSOR)
    )
    in_specs = (
        P((*DP, *TENSOR), None),
        P(DP, TENSOR),
        P((*DP, *TENSOR), None),
        P((*DP, *TENSOR), None),
        P(),
        P(),
        P(),
        P(DP, TENSOR),
        P(DP, TENSOR),
        P(DP, TENSOR),
        P(TENSOR, DP),
        P(),
        P(DP, None, TENSOR),
        P(DP, None, TENSOR),
        P(DP, TENSOR, None),
        P((*DP, *TENSOR), None),
    )
    out_specs = (
        P((*DP, *TENSOR), None),
        P((*DP, *TENSOR), None),
        P(),
        P(),
        P(),
        P(DP, TENSOR),
        P(DP, TENSOR),
        P(DP, TENSOR),
        P(TENSOR, DP),
        P(),
        P(DP, None, TENSOR),
        P(DP, None, TENSOR),
        P(DP, TENSOR, None),
    )
    return jax.shard_map(shards, mesh=split, in_specs=in_specs, out_specs=out_specs, check_vma=False)
```

```python
import jax
import jax.numpy as jnp
import functools
import math

from jax import lax
from jax.experimental import pallas as pl
from jax.experimental.pallas import tpu as pltpu
from jax.sharding import PartitionSpec as P

WINDOW = 1024
DP = ("plane", "pack")
TENSOR = ("side", "core")


EPSILON = 1e-06
THETA = 50000.0
NEG_FILL = -1e30


def matmul(left_side, right_side):
    return jnp.dot(left_side, right_side, preferred_element_type=jnp.float32)


def contract_last(left_side, right_side):
    return lax.dot_general(
        left_side, right_side, (((1,), (1,)), ((), ())), preferred_element_type=jnp.float32
    )


def contract_first(left_side, right_side):
    return lax.dot_general(
        left_side, right_side, (((0,), (0,)), ((), ())), preferred_element_type=jnp.float32
    )


def norm_parts(values):
    factor = lax.rsqrt(jnp.mean(values * values, axis=-1, keepdims=True) + EPSILON)
    return (values * factor, factor)


def norm_back(grad_out, normed, factor, gain_vec):
    scaled = grad_out * gain_vec
    return factor * (scaled - normed * jnp.mean(scaled * normed, axis=-1, keepdims=True))


def rope_tables(length, head_size):
    half_size = head_size // 2
    frequency = THETA ** (-(2.0 * jnp.arange(half_size, dtype=jnp.float32)) / head_size)
    angles = jnp.arange(length, dtype=jnp.float32)[:, None] * frequency[None, :]
    return (jnp.cos(angles)[:, None, :], jnp.sin(angles)[:, None, :])


def rotate(values, cosine, sine_tab):
    half_size = values.shape[-1] // 2
    first_half = values[..., :half_size]
    second_half = values[..., half_size:]
    return jnp.concatenate(
        [
            first_half * cosine - second_half * sine_tab,
            second_half * cosine + first_half * sine_tab,
        ],
        axis=-1,
    )


def rotate_back(grads_in, cosine, sine_tab):
    half_size = grads_in.shape[-1] // 2
    first_half = grads_in[..., :half_size]
    second_half = grads_in[..., half_size:]
    return jnp.concatenate(
        [
            first_half * cosine + second_half * sine_tab,
            second_half * cosine - first_half * sine_tab,
        ],
        axis=-1,
    )


def block_mask(segments, offset, block_rows, key_count):
    query_pos = offset + jnp.arange(block_rows)
    key_pos = jnp.arange(key_count)
    same_doc = segments[offset : offset + block_rows][:, None] == segments[None, :]
    near_pos = jnp.abs(query_pos[:, None] - key_pos[None, :]) < WINDOW // 2
    return same_doc & near_pos


def block_scores(query_block, key_low, allowed, inv_root):
    scores = (
        jnp.einsum("qhd,khd->hqk", query_block, key_low, preferred_element_type=jnp.float32)
        * inv_root
    )
    return jnp.where(allowed[None], scores, NEG_FILL)


def row_sum(term_fn, tok_rows):
    return lax.psum_scatter(
        term_fn(jnp.int32(0), lax.axis_size(TENSOR) * tok_rows),
        TENSOR,
        scatter_dimension=0,
        tiled=True,
    )


def gather_rows(values):
    return lax.all_gather(values, TENSOR, axis=0, tiled=True)


def from_experts(values):
    return lax.all_to_all(values, DP, split_axis=1, concat_axis=1, tiled=True)


def to_experts(source_rows, slot_token, slot_gate, layout):
    picked = jnp.take(source_rows, slot_token, axis=0, mode="fill", fill_value=0)
    if slot_gate is not None:
        picked = (picked.astype(jnp.float32) * slot_gate[:, None]).astype(jnp.bfloat16)
    picked = picked.reshape(layout + (picked.shape[1],))
    return lax.all_to_all(picked, DP, split_axis=1, concat_axis=1, tiled=True)


def pair_sum(table, weights_low, pair_slots, row_count):
    picked = jnp.take(table, pair_slots.reshape(-1), axis=0, mode="fill", fill_value=0)
    picked = picked.reshape(row_count, pair_slots.shape[1], table.shape[1])
    return jnp.einsum("rk,rkd->rd", weights_low, picked, preferred_element_type=jnp.float32)


def expert_forward(operands):
    rows_in, gate_mat, up_mat, down_mat = operands
    flat_rows = rows_in.reshape(-1, rows_in.shape[-1])
    gated = matmul(flat_rows, gate_mat)
    lifted = matmul(flat_rows, up_mat)
    hidden = (jax.nn.silu(gated) * lifted).astype(jnp.bfloat16)
    result = matmul(hidden, down_mat).astype(jnp.bfloat16)
    return (result.reshape(rows_in.shape), gated, lifted)


def expert_backward(operands):
    rows_in, grad_in, gated, lifted, gate_mat, up_mat, down_mat = operands
    flat_rows = rows_in.reshape(-1, rows_in.shape[-1])
    flat_grad = grad_in.reshape(-1, grad_in.shape[-1])
    gate_sig = jax.nn.sigmoid(gated)
    activated = jax.nn.silu(gated)
    hidden = (activated * lifted).astype(jnp.bfloat16)
    grad_hidden = contract_last(flat_grad, down_mat)
    grad_down = contract_first(hidden, flat_grad)
    grad_gated = (grad_hidden * lifted * gate_sig * (1.0 + gated * (1.0 - gate_sig))).astype(
        jnp.bfloat16
    )
    grad_lifted = (grad_hidden * activated).astype(jnp.bfloat16)
    grad_gate = contract_first(flat_rows, grad_gated)
    grad_up = contract_first(flat_rows, grad_lifted)
    grad_rows = (contract_last(grad_gated, gate_mat) + contract_last(grad_lifted, up_mat)).astype(
        jnp.bfloat16
    )
    return (grad_rows.reshape(rows_in.shape), grad_gate, grad_up, grad_down)


VMEM_BYTES = 60 * 1024 * 1024
COLUMN_CHUNK = 512
GROUP = 2


def select_rows(places_ref, gates_ref, pick_ref, capacity):
    expert_count, seq_len = places_ref.shape[1:]
    slot_range = lax.broadcasted_iota(jnp.int32, (capacity, seq_len), 0).astype(jnp.bfloat16)
    nothing = jnp.zeros((capacity, seq_len), jnp.bfloat16)
    for expert in range(expert_count):
        hit = places_ref[0, expert : expert + 1, :] == slot_range
        if gates_ref is None:
            weight = jnp.ones((capacity, seq_len), jnp.bfloat16)
        else:
            weight = jnp.broadcast_to(gates_ref[0, expert : expert + 1, :], (capacity, seq_len))
        rows = slice(expert * capacity, (expert + 1) * capacity)
        pick_ref[rows, :] = jnp.where(hit, weight, nothing)


def rows_to_slots(pick_ref, rows_ref, slots_ref, pack, capacity):
    width = rows_ref.shape[2]
    expert_count = slots_ref.shape[0]
    for start in range(0, width, COLUMN_CHUNK):
        columns = slice(start, start + COLUMN_CHUNK)
        picked = matmul(pick_ref[...], rows_ref[0, :, columns]).astype(jnp.bfloat16)
        slots_ref[:, pack, :, columns] = picked.reshape(expert_count, capacity, COLUMN_CHUNK)


def slots_to_rows(pick_ref, slots_ref, own_ref, other_ref, pack):
    width = own_ref.shape[3]
    for start in range(0, width, COLUMN_CHUNK):
        columns = slice(start, start + COLUMN_CHUNK)
        slots = slots_ref[:, pack, :, columns].reshape(-1, COLUMN_CHUNK)
        rows = contract_first(pick_ref[...], slots).astype(own_ref.dtype)
        rows = rows.reshape(2, 2, own_ref.shape[2], COLUMN_CHUNK)
        own_ref[0, :, :, columns] = rows[:, 0]
        other_ref[0, :, :, columns] = rows[:, 1]


def cot_kernel(
    packs, steps, capacity, table, places, gates, rows, down, slots_out, hidden_out, slots, pick
):
    step = pl.program_id(0)

    @pl.when(step < packs)
    def _():
        select_rows(places, gates, pick, capacity)
        rows_to_slots(pick, rows, slots, step, capacity)

    @pl.when(step >= packs)
    def _():
        for member in range(down.shape[0]):
            block = slots[(step - packs) * down.shape[0] + member].reshape(packs * capacity, -1)
            slots_out[member] = block
            hidden_out[member] = contract_last(block, down[member])


def piece_copies(own, other, rows, sems, pack):
    half_rows = own.shape[1]
    copies = []
    for far in range(2):
        for core, source in enumerate((own, other)):
            for half, index in enumerate((4 * far + pack, 2 + 4 * pack + far)):
                start = ((far * 2 + core) * 2 + half) * half_rows
                copies.append(
                    pltpu.make_async_copy(
                        source.at[index],
                        rows.at[pack, pl.ds(start, half_rows)],
                        sems.at[pack * 8 + len(copies)],
                    )
                )
    return copies


def row_kernel(
    packs, steps, capacity, places, own, other, both, grad_hidden,
    slots_out, hidden_out, grads_out, rows_own, rows_other,
    rows, slots, grads, pick, sems,
):
    step = pl.program_id(0)
    half = hidden_out.shape[2]

    @pl.when(step == 0)
    def _():
        for pack in range(packs):
            for copy in piece_copies(own, other, rows, sems, pack):
                copy.start()
        for pack in range(packs):
            select_rows(places.at[pl.ds(pack, 1)], None, pick.at[pack], capacity)

    for pack in range(packs):

        @pl.when(step == pack)
        def _(pack=pack):
            for copy in piece_copies(own, other, rows, sems, pack):
                copy.wait()
            rows_to_slots(pick.at[pack], rows.at[pl.ds(pack, 1)], slots, pack, capacity)

    @pl.when((step >= packs) & (step < packs + steps))
    def _():
        for member in range(both.shape[0]):
            expert = (step - packs) * both.shape[0] + member
            block = slots[expert].reshape(packs * capacity, -1)
            slots_out[member] = block
            product = matmul(block, both[member])
            gated, lifted = product[:, :half], product[:, half:]
            sig = 1.0 / (1.0 + jnp.exp(-gated))
            active = gated * sig
            hidden_out[member] = (active * lifted).astype(jnp.bfloat16)
            above = grad_hidden[member]
            grad_gated = above * lifted * sig * (1.0 + gated * (1.0 - sig))
            joined = jnp.concatenate([grad_gated, above * active], axis=1).astype(jnp.bfloat16)
            grads_out[member] = joined
            back = contract_last(joined, both[member])
            grads[expert] = back.astype(jnp.bfloat16).reshape(packs, capacity, -1)

    for pack in range(packs):

        @pl.when(step == packs + steps + pack)
        def _(pack=pack):
            slots_to_rows(pick.at[pack], grads, rows_own, rows_other, pack)


def mix_kernel(packs, steps, capacity, table, places, gates, hidden, down, *refs):
    rows, results, pick = refs[-3:]
    step = pl.program_id(0)

    @pl.when(step < steps)
    def _():
        for member in range(down.shape[0]):
            result = matmul(hidden[member], down[member]).astype(jnp.bfloat16)
            results[step * down.shape[0] + member] = result.reshape(packs, capacity, -1)

    @pl.when(step >= steps)
    def _():
        select_rows(places, gates, pick, capacity)
        pack = (step - steps) ^ table[0]
        for start in range(0, rows.shape[3], COLUMN_CHUNK):
            columns = slice(start, start + COLUMN_CHUNK)
            slots = results[:, pack, :, columns].reshape(-1, COLUMN_CHUNK)
            rows[0, 0, :, columns] = contract_first(pick[...], slots).astype(rows.dtype)


def weight_kernel(planes, *refs):
    slots, grads, hidden, above = (
        jnp.concatenate([ref[0] for ref in refs[i * planes : (i + 1) * planes]]) for i in range(4)
    )
    gate_out, up_out, down_out = refs[-3:]
    half = gate_out.shape[2]
    both = contract_first(slots, above)
    gate_out[0] = both[:, :half]
    up_out[0] = both[:, half:]
    down_out[0] = contract_first(hidden, grads)


def block(shape, place, count=1):
    tail = (0,) * (len(shape) - 1)
    return pl.BlockSpec((count,) + tuple(shape[1:]), lambda *ids: (place(*ids),) + tail)


def staged(first, count):
    return lambda step, *rest: jnp.clip(step - first, 0, count - 1)


def shape_of(shape, kind):
    return jax.ShapeDtypeStruct(shape, kind)


def call(kernel, steps, specs, out_specs, out_shape, scratch, flops, prefetch=0, aliases={}):
    return pl.pallas_call(
        kernel,
        grid_spec=pltpu.PrefetchScalarGridSpec(
            num_scalar_prefetch=prefetch,
            grid=(steps,),
            in_specs=specs,
            out_specs=out_specs,
            scratch_shapes=scratch,
        ),
        out_shape=out_shape,
        input_output_aliases=aliases,
        cost_estimate=pl.CostEstimate(
            flops=flops, transcendentals=0, bytes_accessed=flops // 500
        ),
        compiler_params=pltpu.CompilerParams(
            dimension_semantics=("arbitrary",), vmem_limit_bytes=VMEM_BYTES
        ),
    )


def cot_slots(table, places, gates, rows, down, capacity):
    packs = table.shape[0]
    _, seq_len, width = rows.shape
    experts, hidden_width, _ = down.shape
    slot_rows = packs * capacity
    group = math.gcd(experts, GROUP)
    steps = experts // group
    by_pack, by_expert = staged(0, packs), staged(packs, steps)
    listed = lambda step, numbers: numbers[by_pack(step)]
    out_shape = [
        shape_of((experts, slot_rows, width), jnp.bfloat16),
        shape_of((experts, slot_rows, hidden_width), jnp.float32),
    ]
    return call(
        functools.partial(cot_kernel, packs, steps, capacity),
        packs + steps,
        [
            block(places.shape, listed), block(gates.shape, listed), block(rows.shape, listed),
            block(down.shape, by_expert, group),
        ],
        [block(out.shape, by_expert, group) for out in out_shape],
        out_shape,
        [
            pltpu.VMEM((experts, packs, capacity, width), jnp.bfloat16),
            pltpu.VMEM((experts * capacity, seq_len), jnp.bfloat16),
        ],
        2 * experts * slot_rows * width * (seq_len + hidden_width),
        1,
    )(table, places, gates, rows, down)


def row_slots(places, own, other, both, grad_hidden, capacity):
    packs, _, seq_len = places.shape
    experts, width, hidden_width = both.shape
    slot_rows = packs * capacity
    group = math.gcd(experts, GROUP)
    steps = experts // group
    middle, last = staged(packs, steps), staged(packs + steps, packs)
    part = shape_of((packs, 2, seq_len // 4, width), jnp.bfloat16)
    out_shape = [
        shape_of((experts, slot_rows, width), jnp.bfloat16),
        shape_of((experts, slot_rows, hidden_width // 2), jnp.bfloat16),
        shape_of((experts, slot_rows, hidden_width), jnp.bfloat16),
        part, part,
    ]
    anywhere = pl.BlockSpec(memory_space=pl.ANY)
    return call(
        functools.partial(row_kernel, packs, steps, capacity),
        2 * packs + steps,
        [
            block(places.shape, lambda step: 0, packs), anywhere, anywhere,
            block(both.shape, middle, group), block(grad_hidden.shape, middle, group),
        ],
        [block(out.shape, middle, group) for out in out_shape[:3]] + [block(part.shape, last)] * 2,
        out_shape,
        [
            pltpu.VMEM((packs, seq_len, width), jnp.bfloat16),
            pltpu.VMEM((experts, packs, capacity, width), jnp.bfloat16),
            pltpu.VMEM((experts, packs, capacity, width), jnp.bfloat16),
            pltpu.VMEM((packs, experts * capacity, seq_len), jnp.bfloat16),
            pltpu.SemaphoreType.DMA((8 * packs,)),
        ],
        4 * experts * slot_rows * width * (seq_len + hidden_width),
    )(places, own, other, both, grad_hidden)


def mix_rows(plane, planes, table, places, gates, hidden, down, capacity, earlier=()):
    packs, _, seq_len = places.shape
    experts, hidden_width, width = down.shape
    group = math.gcd(experts, GROUP)
    steps = experts // group
    first, last = staged(0, steps), staged(steps, packs)
    listed = lambda step, numbers: numbers[1] * steps + first(step)
    return call(
        functools.partial(mix_kernel, packs, steps, capacity),
        packs + steps,
        [
            block(places.shape, last), block(gates.shape, last),
            block(hidden.shape, listed, group), block(down.shape, first, group),
        ]
        + [pl.BlockSpec(memory_space=pl.ANY)] * len(earlier),
        [pl.BlockSpec((1, 1, seq_len, width), lambda step, numbers: (plane, last(step), 0, 0))],
        [shape_of((planes, packs, seq_len, width), jnp.bfloat16)],
        [
            pltpu.VMEM((experts, packs, capacity, width), jnp.bfloat16),
            pltpu.VMEM((experts * capacity, seq_len), jnp.bfloat16),
        ],
        2 * experts * packs * capacity * width * (seq_len + hidden_width),
        1,
        aliases={5 + index: index for index in range(len(earlier))},
    )(table, places, gates, hidden, down, *earlier)


def weight_grads(first, count, slots, hidden, grads, above, earlier=()):
    planes = len(slots)
    operands = [*slots, *grads, *hidden, *above]
    experts, _, width = slots[0].shape
    hidden_width = hidden[0].shape[2]
    each = lambda step: step + first
    out_shape = [
        shape_of((experts, width, hidden_width), jnp.float32),
        shape_of((experts, width, hidden_width), jnp.float32),
        shape_of((experts, hidden_width, width), jnp.float32),
    ]
    return call(
        functools.partial(weight_kernel, planes),
        count,
        [block(operand.shape, each) for operand in operands]
        + [pl.BlockSpec(memory_space=pl.ANY)] * len(earlier),
        [block(out.shape, each) for out in out_shape],
        out_shape,
        [],
        6 * planes * slots[0].shape[1] * count * width * hidden_width,
        aliases={len(operands) + index: index for index in range(len(earlier))},
    )(*operands, *earlier)


def swapped(values, axis, bit):
    count = lax.axis_size(axis)
    return lax.ppermute(values, axis, [(i, i ^ bit) for i in range(count)])


def far_side(values):
    return swapped(values, TENSOR, 2)


def far_core(values):
    return swapped(values, TENSOR, 1)


def far_pack(values):
    return swapped(values, DP, 1)


def next_plane(values):
    count = lax.axis_size(DP)
    return lax.ppermute(values, DP, [(i, (i + 2) % count) for i in range(count)])


def spread_all(values, small, work):
    planes = lax.axis_size("plane")
    half_rows = values.shape[0] // 2
    first = lambda rows: (far_pack(rows[:half_rows]), far_side(rows[half_rows:]))
    small, values = tied(small, values)
    (across_pack, across_side), following = lax.optimization_barrier(
        (first(values), next_plane(values))
    )
    pieces, made = [], []
    for plane in range(planes):
        upper = jnp.stack([values[:half_rows], across_pack])
        lower = jnp.stack([values[half_rows:], across_side])
        small, (upper, lower, values) = tied(small, (upper, lower, following))
        moved = [
            far_side(upper),
            far_pack(lower),
            first(values) if plane + 1 < planes else ((), ()),
            next_plane(values) if plane + 2 < planes else (),
            far_core(pieces[-1]) if plane else (),
            work(plane - 1, small) if plane else (),
        ]
        upper_far, lower_far, (across_pack, across_side), following, other, result = (
            lax.optimization_barrier(moved)
        )
        if plane:
            pieces[-1] = (pieces[-1], other)
        if plane:
            made.append(result)
        pieces.append(jnp.concatenate([upper, lower, upper_far, lower_far]))
    pieces[-1] = (pieces[-1], far_core(pieces[-1]))
    return pieces, made


def plane_order():
    packs = lax.axis_size(DP)
    planes = packs // 2
    index = lax.axis_index(DP)
    return jnp.stack(
        [
            ((index // 2 + planes - plane) % planes) * 2 + (index % 2 ^ near)
            for plane in range(planes)
            for near in range(2)
        ]
    )


def place_kernel(by_column, order, *refs):
    *pieces, whole, sems = refs
    copies = []
    for index, piece in enumerate(pieces):
        target = None if by_column else whole.at[order[index]]
        if by_column:
            width = piece.shape[1]
            target = whole.at[:, pl.ds(pl.multiple_of(order[index] * width, 128), width)]
        copies.append(pltpu.make_async_copy(piece, target, sems.at[index]))
        copies[-1].start()
    for copy in copies:
        copy.wait()


def laid(pieces, order, by_column=False):
    count = len(pieces)
    rows, columns = pieces[0].shape
    shape = (rows, count * columns) if by_column else (count, rows, columns)
    anywhere = pl.BlockSpec(memory_space=pl.ANY)
    return call(
        functools.partial(place_kernel, by_column),
        1,
        [anywhere] * count,
        pl.BlockSpec(memory_space=pltpu.VMEM),
        shape_of(shape, pieces[0].dtype),
        [pltpu.SemaphoreType.DMA((count,))],
        1000,
        1,
    )(order, *pieces)


class FoldPacks:
    def __init__(self, values):
        order = plane_order()
        take = lambda index: lax.dynamic_index_in_dim(values, order[index], 0, keepdims=False)
        planes = values.shape[0] // 2
        self.turns = [*range(1, planes), 0]
        self.near = {plane: take(2 * plane) for plane in self.turns}
        self.moving = {plane: far_pack(take(2 * plane + 1)) for plane in self.turns}
        self.summed, self.count = None, 0

    def step(self, other):
        if self.count >= len(self.turns):
            return other
        self.moving, other = tied(self.moving, other)
        if self.summed is None:
            self.near = {plane: added(self.near[plane], self.moving[plane]) for plane in self.turns}
            self.summed = self.near[self.turns[0]]
        else:
            kind = jnp.float32 if self.count + 1 == len(self.turns) else jnp.bfloat16
            self.summed = added(self.moving, self.near[self.turns[self.count]], kind)
        self.count += 1
        if self.count < len(self.turns):
            self.moving = next_plane(self.summed)
        return other

    def finish(self):
        for plane in self.turns[self.count :]:
            kind = jnp.float32 if plane == 0 else jnp.bfloat16
            self.summed = added(self.moving, self.near[plane], kind)
            self.moving = next_plane(self.summed) if plane else None
        return self.summed


def laid_sides(pieces):
    order = lax.axis_index(TENSOR) ^ jnp.arange(len(pieces), dtype=jnp.int32)
    return laid(pieces, order).reshape((-1,) + pieces[0].shape[1:])


def gather_sides(values):
    across = far_side(values)
    return laid_sides([values, far_core(values), across, far_core(across)])


def fold_sides(values):
    split = values.astype(jnp.bfloat16).reshape((4, -1) + values.shape[1:])
    take = lambda bits: lax.dynamic_index_in_dim(
        split, lax.axis_index(TENSOR) ^ bits, 0, keepdims=False
    )
    far = added(take(2), far_core(take(3)))
    near = added(take(0), far_core(take(1)))
    return added(near, far_side(far), jnp.float32)


def fold_both(weights, rows, mixed):
    order = plane_order()
    planes = weights.shape[0] // 2
    take = lambda index: lax.dynamic_index_in_dim(weights, order[index], 0, keepdims=False)
    split = rows.astype(jnp.bfloat16).reshape((4, -1) + rows.shape[1:])
    mine = lax.axis_index(TENSOR)
    pick = lambda bits: lax.dynamic_index_in_dim(split, mine ^ bits, 0, keepdims=False)
    summed, total = None, None
    for turn, plane in enumerate([*range(1, planes), 0]):
        moved = [far_pack(take(2 * plane + 1)), () if summed is None else next_plane(summed)]
        if turn == 0:
            moved += [far_core(pick(3)), far_core(pick(1))]
        if turn == 1:
            moved += [far_side(far)]
        across, passed, *arrived = lax.optimization_barrier(moved)
        if turn == 0:
            far, close = added(pick(2), arrived[0]), added(pick(0), arrived[1])
            mixed, far = tied(mixed, far)
            mixed = jnp.concatenate(mixed)
            mixed = lax.psum_scatter(mixed, "plane", scatter_dimension=0, tiled=True)
        if turn == 1:
            total = added(close, arrived[0], jnp.float32)
        near = added(take(2 * plane), across)
        kind = jnp.float32 if turn + 1 == planes else jnp.bfloat16
        summed = near if turn == 0 else added(passed, near, kind)
    return summed, total, mixed


def gather_both(weights, outer, rows, gate, up, tables):
    hops = table_hops()
    pieces, outer_pieces, row_pieces, values = [], [], [rows], (weights, outer)
    planes = lax.axis_size("plane")
    for plane in range(planes):
        moved = [tuple(far_pack(value) for value in values), ()]
        if plane + 1 < planes:
            moved[1] = tuple(next_plane(value) for value in values)
        if plane == 0:
            moved += [far_core(rows), far_side(rows)]
        if plane == 1:
            moved += [far_core(row_pieces[2])]
        if plane == 0:
            moved.insert(2, jnp.concatenate([gate, up], axis=2))
        moved.insert(2, swapped(tables, *hops[plane]) if plane < len(hops) else ())
        across, following, more, *arrived = lax.optimization_barrier(moved)
        if plane < len(hops):
            tables = jnp.concatenate([tables, more])
        if plane == 0:
            joined = arrived.pop(0)
        pieces += [values[0], across[0]]
        outer_pieces += [values[1], across[1]]
        row_pieces += arrived
        values = following
    order = plane_order()
    for hop in hops[planes:]:
        tables = jnp.concatenate([tables, swapped(tables, *hop)])
    laid_rows = laid_sides(row_pieces)
    return laid(pieces, order), laid(outer_pieces, order, True), laid_rows, joined, tables


def sum_everywhere(values):
    for axis in (TENSOR, DP):
        bit = 1
        while bit < lax.axis_size(axis):
            values = values + swapped(values, axis, bit)
            bit *= 2
    return values


def added(left, right, kind=jnp.bfloat16):
    return (left.astype(jnp.float32) + right.astype(jnp.float32)).astype(kind)


def fold_first(own, arrived):
    half_rows = own.shape[2] // 2
    upper, lower = slice(None, half_rows), slice(half_rows, None)
    return (
        added(own[:, 0, upper], arrived[:, 0, upper]),
        added(own[0, :, lower], arrived[0, :, lower]),
        added(own[:, 1, upper], arrived[:, 1, upper]),
        added(own[1, :, lower], arrived[1, :, lower]),
    )


def tied(small, values):
    return lax.optimization_barrier((small, values))


def table_hops():
    hops = []
    for axis in (TENSOR, DP):
        bit = 1
        while bit < lax.axis_size(axis):
            hops.append((axis, bit))
            bit *= 2
    return hops


def read_tables(tables, top_count):
    own = lax.axis_index(DP) * lax.axis_size(TENSOR) + lax.axis_index(TENSOR)
    sides = jnp.arange(lax.axis_size(TENSOR), dtype=jnp.int32) ^ lax.axis_index(TENSOR)
    segments = jnp.take(tables[: sides.shape[0], -1], sides, axis=0).reshape(-1)
    devices = jnp.arange(tables.shape[0], dtype=jnp.int32)
    tables = jnp.take(tables, devices ^ own, axis=0)
    all_ids, all_gates = tables[:, :top_count], tables[:, top_count : 2 * top_count]
    return all_ids.astype(jnp.int32), all_gates, segments.astype(jnp.int32)


def routing(all_ids, all_gates, local_experts, capacity):
    packs = lax.axis_size(DP)
    first = lax.axis_index(DP) * local_experts
    wanted = first + jnp.arange(local_experts, dtype=jnp.int32)

    def by_pack(values):
        top_count, tok_rows = values.shape[1:]
        ordered = values.reshape(packs, -1, top_count, tok_rows).transpose(0, 2, 1, 3)
        return ordered.reshape(packs, top_count, -1)

    matches = by_pack(all_ids)[:, :, None, :] == wanted[None, None, :, None]
    pair_gates = by_pack(all_gates).astype(jnp.float32)
    member = jnp.any(matches, axis=1)
    gates = jnp.sum(jnp.where(matches, pair_gates[:, :, None, :], 0.0), axis=1)
    order = jnp.arange(member.shape[2], dtype=jnp.int32)
    earlier = (order[:, None] < order[None, :]).astype(jnp.bfloat16)
    flat = member.reshape(packs * local_experts, -1).astype(jnp.bfloat16)
    before = matmul(flat, earlier).astype(jnp.int32).reshape(member.shape)
    places = jnp.where(member & (before < capacity), before, -1)
    return places.astype(jnp.bfloat16), gates.astype(jnp.bfloat16)


def experts_by_exchange(
    second_in, cotangent, expert_ids, gate_values, w_gate, w_up, w_down, middle, capacity
):
    tok_rows, model_width = second_in.shape
    tensor_count = lax.axis_size(TENSOR)
    data_count = lax.axis_size(DP)
    local_experts = w_gate.shape[0]
    all_experts = local_experts * data_count
    top_count = expert_ids.shape[1]
    seq_len = tok_rows * tensor_count
    pack_cot, pack_ids, pack_gates = (
        gather_rows(cotangent), gather_rows(expert_ids), gather_rows(gate_values)
    )
    pack_second = gather_rows(second_in)
    expert_range = jnp.arange(all_experts, dtype=jnp.int32)
    matches = pack_ids[:, :, None] == expert_range[None, None, :]
    token_counts = jnp.sum(matches.astype(jnp.float32), axis=1).astype(jnp.bfloat16)
    token_range = jnp.arange(seq_len, dtype=jnp.int32)
    earlier = (token_range[:, None] > token_range[None, :]).astype(jnp.bfloat16)
    before = matmul(earlier, token_counts)
    places = (
        jnp.sum(jnp.where(matches, before[:, None, :], 0.0), axis=2).astype(jnp.int32).reshape(-1)
    )
    flat_ids = pack_ids.reshape(-1)
    owners = flat_ids // local_experts
    local_index = flat_ids % local_experts
    dump_slot = all_experts * capacity
    slot_index = jnp.where(
        places < capacity,
        local_index * (data_count * capacity) + owners * capacity + places,
        dump_slot,
    ).astype(jnp.int32)
    pair_token = jnp.arange(seq_len * top_count) // top_count
    slot_token = (
        jnp.full((dump_slot + 1,), seq_len, jnp.int32).at[slot_index].set(pair_token)[:dump_slot]
    )
    pair_gates = pack_gates.astype(jnp.float32)
    slot_gate = (
        jnp.zeros((dump_slot + 1,), jnp.float32)
        .at[slot_index]
        .set(pair_gates.reshape(-1))[:dump_slot]
    )
    pair_slots = slot_index.reshape(seq_len, top_count)
    layout = (local_experts, data_count, capacity)
    arrived_rows = to_experts(pack_second, slot_token, None, layout)
    expert_out, gated_all, lifted_all = lax.map(
        expert_forward, (arrived_rows, w_gate, w_up, w_down)
    )
    returned = from_experts(expert_out).reshape(-1, model_width)

    def combine_term(offset, row_count):
        return pair_sum(returned, pack_gates, pair_slots, row_count)

    outputs = middle + row_sum(combine_term, tok_rows)
    grad_arrived = to_experts(pack_cot, slot_token, slot_gate, layout)
    grad_rows_all, grad_w_gate, grad_w_up, grad_w_down = lax.map(
        expert_backward, (arrived_rows, grad_arrived, gated_all, lifted_all, w_gate, w_up, w_down)
    )
    returned_grad = from_experts(grad_rows_all).reshape(-1, model_width)
    unit_gates = jnp.ones_like(pack_gates)

    def dispatch_term(offset, row_count):
        return pair_sum(returned_grad, unit_gates, pair_slots, row_count)

    grad_second = row_sum(dispatch_term, tok_rows)
    return outputs, grad_second, grad_w_gate, grad_w_up, grad_w_down


class Folding:
    def __init__(self, order):
        self.order, self.planes, self.ready = order, {}, {}
        self.summed, self.passed, self.count = None, None, 0

    def begin(self, plane, own, other):
        self.planes[plane] = (0, (own, other))

    def turn(self, small, work):
        small, (planes, summed) = tied(
            small, ({plane: values for plane, (_, values) in self.planes.items()}, self.summed)
        )
        sent = {}
        for plane, values in planes.items():
            stage = self.planes[plane][0]
            if stage == 0:
                sent[plane] = (far_core(values[1]),)
            elif stage == 1:
                sent[plane] = (far_side(values[2]), far_pack(values[3]))
            else:
                sent[plane] = (far_pack(values[2]), far_side(values[3]))
        passed = self.passed
        if passed is None and summed is not None and not self.done():
            passed = next_plane(summed)
        sent, passed, result = lax.optimization_barrier((sent, passed, work(small)))
        self.passed = passed
        for plane, values in planes.items():
            stage, arrived = self.planes[plane][0], sent[plane]
            if stage == 0:
                made = fold_first(values[0], *arrived)
            elif stage == 1:
                upper, lower = added(values[0], arrived[0]), added(values[1], arrived[1])
                made = (upper[0], lower[0], upper[1], lower[1])
            else:
                self.ready[plane] = jnp.concatenate(
                    [added(values[0], arrived[0]), added(values[1], arrived[1])]
                )
            if stage < 2:
                self.planes[plane] = (stage + 1, made)
            else:
                del self.planes[plane]
        following = self.order[self.count] if self.count < len(self.order) else None
        if following in self.ready:
            last = self.count + 1 == len(self.order)
            self.summed = self.ready[following]
            if passed is not None:
                kind = jnp.float32 if last else jnp.bfloat16
                self.summed = added(passed, self.summed, kind)
            self.passed = None
            self.count += 1
        return result

    def done(self):
        return self.count == len(self.order)


def experts_by_gather(second_in, all_cot, places, gates, w_both, w_down, capacity):
    packs, local_experts, seq_len = places.shape
    tensor_count = lax.axis_size(TENSOR)
    planes = packs // 2
    pack_order = plane_order()
    side_index = lax.axis_index(TENSOR)
    quarter_order = side_index ^ jnp.arange(tensor_count, dtype=jnp.int32)

    def as_met(values, by_pack, by_quarter):
        split = values.reshape(packs, local_experts, tensor_count, -1)
        split = jnp.take(jnp.take(split, by_pack, axis=0), by_quarter, axis=2)
        return split.reshape(values.shape)

    near_places = as_met(places, pack_order, quarter_order)
    pairs = [slice(plane * 2, plane * 2 + 2) for plane in range(planes)]
    tables = [
        jnp.stack([lax.axis_index("pack"), (lax.axis_index("plane") + planes - plane) % planes])
        for plane in range(planes)
    ]
    prepared = [
        [table[pair] for pair in pairs] for table in (near_places, places, gates, pack_order)
    ]
    prepared, second_in = tied((prepared, tables, places, gates), second_in)
    (near_places, mix_places, mix_gates, pack_order), tables, places, gates = prepared

    def cot_work(plane, order):
        return cot_slots(order[plane], places, gates, all_cot, w_down, capacity)

    pieces, made = spread_all(second_in, pack_order, cot_work)
    order = [*range(1, planes), 0]
    kept, folding = {}, Folding(order)

    def row_work(plane, near):
        return row_slots(near, *pieces[plane], w_both, made[plane][1], capacity)

    for plane in order:
        if folding.planes:
            result = folding.turn(near_places[plane], functools.partial(row_work, plane))
        else:
            result = row_work(plane, near_places[plane])
        slots, hidden, above, *part = result
        folding.begin(plane, *part)
        kept[plane] = (slots, hidden, made[plane][0], above)
        if len(made) < planes:
            made.append(folding.turn(pack_order, functools.partial(cot_work, len(made))))
    hidden_all = jnp.concatenate([kept[plane][1] for plane in range(planes)])

    def mix_turn(start, table):
        mixed = ()
        for index in range(2):
            plane = start + index
            mixed = mix_rows(
                index, 2, table[plane], mix_places[plane], mix_gates[plane], hidden_all, w_down,
                capacity, mixed,
            )
        return mixed[0].reshape(2, -1, mixed[0].shape[-1])

    mixed = []
    for start in range(0, planes, 2):
        part = folding.turn(tables, functools.partial(mix_turn, start))
        mixed.append(
            lax.psum_scatter(part, ("pack", "side", "core"), scatter_dimension=1, tiled=True)
        )
    kept = [kept[plane] for plane in range(planes)]
    weight_parts, next_expert = (), 0
    part_size = math.gcd(local_experts, GROUP)

    def weight_turn(count, small):
        state, (held, weights) = next_expert, small
        for _ in range(count):
            if state < local_experts:
                weights = weight_grads(state, part_size, *zip(*held), weights)
                state += part_size
        return weights

    for count in (2, 1, *[0] * planes):
        if folding.done():
            break
        weight_parts = folding.turn((kept, weight_parts), functools.partial(weight_turn, count))
        next_expert = min(next_expert + count * part_size, local_experts)
    rest = (kept, weight_parts, next_expert, part_size)
    return folding.summed, mixed, rest


def shards(
    inputs,
    segment_ids,
    expert_ids,
    gate_values,
    attn_gain,
    query_gain,
    key_gain,
    w_query,
    w_key,
    w_value,
    w_output,
    ffn_gain,
    w_gate,
    w_up,
    w_down,
    cotangent,
):
    tok_rows, model_width = inputs.shape
    head_size = query_gain.shape[0]
    tensor_count = lax.axis_size(TENSOR)
    data_count = lax.axis_size(DP)
    local_experts = w_gate.shape[0]
    all_experts = local_experts * data_count
    top_count = expert_ids.shape[1]
    seq_len = tok_rows * tensor_count
    capacity = seq_len * top_count // all_experts
    inv_root = head_size ** (-0.5)
    by_gather = (
        seq_len <= local_experts * capacity
        and tensor_count == 4
        and data_count > 2
        and data_count & (data_count - 1) == 0
        and all_experts <= 256
    )
    if by_gather:
        axes = (*DP, *TENSOR)
        tables = jnp.concatenate(
            [expert_ids.T.astype(jnp.bfloat16), gate_values.T, segment_ids.astype(jnp.bfloat16)]
        )[None]
    inputs_f32 = inputs.astype(jnp.float32)
    normed_one, factor_one = norm_parts(inputs_f32)
    first_in = (normed_one * attn_gain).astype(jnp.bfloat16)
    if by_gather:
        side_sum, side_gather = fold_sides, gather_sides
        local_width = w_query.shape[1]
        w_in = jnp.concatenate([w_query, w_key, w_value], axis=1)
        full_in, full_output, pack_in, w_both, tables = gather_both(
            w_in, w_output, first_in, w_gate, w_up, tables
        )
        all_ids, all_gates, segments = read_tables(tables, top_count)
        places, gates = routing(all_ids, all_gates, local_experts, capacity)
        full_in, cotangent = tied(full_in, cotangent)
        all_cot = lax.all_gather(cotangent, axes, axis=0, tiled=True)
        all_cot = all_cot.reshape(data_count, seq_len, model_width)
        full_in = full_in.reshape(model_width, -1)
        full_query, full_key, full_value = (
            full_in[:, index * local_width : (index + 1) * local_width] for index in range(3)
        )
    else:
        side_sum, side_gather = lambda term: row_sum(lambda *_: term, tok_rows), gather_rows
        segments = lax.all_gather(segment_ids, TENSOR, axis=1, tiled=True)[0]
        full_query, full_key, full_value, full_output = (
            lax.all_gather(w_query, DP, axis=0, tiled=True),
            lax.all_gather(w_key, DP, axis=0, tiled=True),
            lax.all_gather(w_value, DP, axis=0, tiled=True),
            lax.all_gather(w_output, DP, axis=1, tiled=True),
        )
        pack_in = side_gather(first_in)
    query_pre = matmul(pack_in, full_query)
    key_pre = matmul(pack_in, full_key)
    value_low = matmul(pack_in, full_value).astype(jnp.bfloat16)
    head_count = query_pre.shape[1] // head_size
    cosine, sine_tab = rope_tables(seq_len, head_size)
    query_norm, query_factor = norm_parts(query_pre.reshape(seq_len, head_count, head_size))
    key_norm, key_factor = norm_parts(key_pre.reshape(seq_len, head_count, head_size))
    query_low = rotate(query_norm * query_gain, cosine, sine_tab).astype(jnp.bfloat16)
    key_low = rotate(key_norm * key_gain, cosine, sine_tab).astype(jnp.bfloat16)
    value_heads = value_low.reshape(seq_len, head_count, head_size)
    block_rows = min(512, seq_len)
    block_total = seq_len // block_rows
    masks = []
    mixture_parts = []
    lse_parts = []
    for block_index in range(block_total):
        offset = block_index * block_rows
        allowed = block_mask(segments, offset, block_rows, seq_len)
        masks.append(allowed)
        scores = block_scores(query_low[offset : offset + block_rows], key_low, allowed, inv_root)
        top_score = jnp.max(scores, axis=-1, keepdims=True)
        raw_weights = jnp.exp(scores - top_score)
        totals = jnp.sum(raw_weights, axis=-1, keepdims=True)
        weights_low = (raw_weights / totals).astype(jnp.bfloat16)
        mixture_parts.append(
            jnp.einsum(
                "hqk,khd->qhd", weights_low, value_heads, preferred_element_type=jnp.float32
            ).astype(jnp.bfloat16)
        )
        lse_parts.append(top_score + jnp.log(totals))
    mixture = jnp.concatenate(mixture_parts, axis=0).reshape(seq_len, head_count * head_size)

    middle = inputs_f32 + side_sum(matmul(mixture, full_output))
    normed_two, factor_two = norm_parts(middle)
    second_in = (normed_two * ffn_gain).astype(jnp.bfloat16)
    if by_gather:
        grad_second, mixed, rest = experts_by_gather(
            second_in, all_cot, places, gates, w_both, w_down, capacity
        )
    else:
        outputs, grad_second, grad_w_gate, grad_w_up, grad_w_down = experts_by_exchange(
            second_in, cotangent, expert_ids, gate_values, w_gate, w_up, w_down, middle, capacity
        )
    ffn_gain_part = jnp.sum(grad_second * normed_two, axis=0)
    grad_middle = cotangent.astype(jnp.float32) + norm_back(
        grad_second, normed_two, factor_two, ffn_gain
    )
    grad_attended = grad_middle.astype(jnp.bfloat16)
    if by_gather:
        kept, weight_parts, next_expert, part_size = rest
        (kept, weight_parts), grad_attended = tied((kept, weight_parts), grad_attended)
        moved = [far_core(grad_attended), far_side(grad_attended)]
        for first in range(next_expert, local_experts, part_size):
            weight_parts = weight_grads(first, part_size, *zip(*kept), weight_parts)
        grad_w_gate, grad_w_up, grad_w_down = weight_parts
        near, across, weight_parts = lax.optimization_barrier((*moved, weight_parts))
        grad_w_gate, grad_w_up, grad_w_down = weight_parts
        pack_grad = laid_sides([grad_attended, near, across, far_core(across)])
    else:
        pack_grad = side_gather(grad_attended)
    output_part = contract_first(mixture, pack_grad)
    fold_step = lambda other: other
    if by_gather:
        by_column = output_part.astype(jnp.bfloat16).reshape(local_width, data_count, -1)
        folded = FoldPacks(by_column.transpose(1, 0, 2))
        fold_step = folded.step
    grad_mixture = (
        contract_last(pack_grad, full_output)
        .astype(jnp.bfloat16)
        .reshape(seq_len, head_count, head_size)
    )
    grad_query_parts = []
    grad_key_sum = jnp.zeros((seq_len, head_count, head_size), jnp.float32)
    grad_value_sum = jnp.zeros((seq_len, head_count, head_size), jnp.float32)
    for block_index in range(block_total):
        offset = block_index * block_rows
        query_block = query_low[offset : offset + block_rows]
        if block_index:
            query_block = fold_step(query_block)
        grad_block = grad_mixture[offset : offset + block_rows]
        scores = block_scores(query_block, key_low, masks[block_index], inv_root)
        prob_rows = jnp.exp(scores - lse_parts[block_index])
        grad_probs = jnp.einsum(
            "qhd,khd->hqk", grad_block, value_heads, preferred_element_type=jnp.float32
        )
        row_delta = jnp.sum(grad_probs * prob_rows, axis=-1, keepdims=True)
        grad_scores = (prob_rows * (grad_probs - row_delta)).astype(jnp.bfloat16)
        grad_query_parts.append(
            jnp.einsum("hqk,khd->qhd", grad_scores, key_low, preferred_element_type=jnp.float32)
            * inv_root
        )
        grad_key_sum = (
            grad_key_sum
            + jnp.einsum(
                "hqk,qhd->khd", grad_scores, query_block, preferred_element_type=jnp.float32
            )
            * inv_root
        )
        grad_value_sum = grad_value_sum + jnp.einsum(
            "hqk,qhd->khd",
            prob_rows.astype(jnp.bfloat16),
            grad_block,
            preferred_element_type=jnp.float32,
        )
    grad_query_norm = rotate_back(jnp.concatenate(grad_query_parts, axis=0), cosine, sine_tab)
    grad_key_norm = rotate_back(grad_key_sum, cosine, sine_tab)
    grad_query_norm = fold_step(grad_query_norm)
    grad_key_norm = fold_step(grad_key_norm)
    query_gain_part = jnp.sum(grad_query_norm * query_norm, axis=(0, 1))
    key_gain_part = jnp.sum(grad_key_norm * key_norm, axis=(0, 1))
    grad_query_pre = (
        norm_back(grad_query_norm, query_norm, query_factor, query_gain)
        .reshape(seq_len, -1)
        .astype(jnp.bfloat16)
    )
    grad_key_pre = (
        norm_back(grad_key_norm, key_norm, key_factor, key_gain)
        .reshape(seq_len, -1)
        .astype(jnp.bfloat16)
    )
    grad_value_low = grad_value_sum.reshape(seq_len, -1).astype(jnp.bfloat16)
    query_part = contract_first(pack_in, grad_query_pre)
    key_part = contract_first(pack_in, grad_key_pre)
    value_part = contract_first(pack_in, grad_value_low)

    total_term = contract_last(grad_query_pre, full_query)
    total_term = total_term + contract_last(grad_key_pre, full_key)
    total_term = total_term + contract_last(grad_value_low, full_value)
    if by_gather:
        in_part = jnp.concatenate([query_part, key_part, value_part], axis=1)
        in_part = in_part.astype(jnp.bfloat16).reshape(data_count, -1, 3 * local_width)
        in_part = fold_step(in_part)
        grad_w_output = folded.finish()
        grad_in, grad_first, mixed = fold_both(in_part, total_term, mixed)
        mixed, grad_in = tied(mixed, grad_in)
    else:
        grad_first = side_sum(total_term)
    attn_gain_part = jnp.sum(grad_first * normed_one, axis=0)
    grad_inputs = grad_middle + norm_back(grad_first, normed_one, factor_one, attn_gain)
    gain_parts = (attn_gain_part, ffn_gain_part, query_gain_part, key_gain_part)
    if by_gather:
        grad_w_query, grad_w_key, grad_w_value = (
            grad_in[:, index * local_width : (index + 1) * local_width] for index in range(3)
        )
        outputs = middle + mixed[0].astype(jnp.float32)
        splits = (model_width, 2 * model_width, 2 * model_width + head_size)
        gain_sums = jnp.split(sum_everywhere(jnp.concatenate(gain_parts)), splits)
    else:
        grad_w_query, grad_w_key, grad_w_value, grad_w_output = (
            lax.psum_scatter(
                part.astype(jnp.bfloat16), DP, scatter_dimension=along, tiled=True
            ).astype(jnp.float32)
            for part, along in ((query_part, 0), (key_part, 0), (value_part, 0), (output_part, 1))
        )
        gain_sums = lax.psum(gain_parts, (*DP, *TENSOR))
    grad_attn_gain, grad_ffn_gain, grad_query_gain, grad_key_gain = gain_sums
    return (
        outputs,
        grad_inputs,
        grad_attn_gain,
        grad_query_gain,
        grad_key_gain,
        grad_w_query,
        grad_w_key,
        grad_w_value,
        grad_w_output,
        grad_ffn_gain,
        grad_w_gate,
        grad_w_up,
        grad_w_down,
    )


def solution(mesh):
    rows, columns = mesh.devices.shape
    split = jax.sharding.Mesh(
        mesh.devices.reshape(rows // 2, 2, columns // 2, 2), (*DP, *TENSOR)
    )
    in_specs = (
        P((*DP, *TENSOR), None),
        P(DP, TENSOR),
        P((*DP, *TENSOR), None),
        P((*DP, *TENSOR), None),
        P(),
        P(),
        P(),
        P(DP, TENSOR),
        P(DP, TENSOR),
        P(DP, TENSOR),
        P(TENSOR, DP),
        P(),
        P(DP, None, TENSOR),
        P(DP, None, TENSOR),
        P(DP, TENSOR, None),
        P((*DP, *TENSOR), None),
    )
    out_specs = (
        P((*DP, *TENSOR), None),
        P((*DP, *TENSOR), None),
        P(),
        P(),
        P(),
        P(DP, TENSOR),
        P(DP, TENSOR),
        P(DP, TENSOR),
        P(TENSOR, DP),
        P(),
        P(DP, None, TENSOR),
        P(DP, None, TENSOR),
        P(DP, TENSOR, None),
    )
    return jax.shard_map(shards, mesh=split, in_specs=in_specs, out_specs=out_specs, check_vma=False)
```
